32 devices in a mesh: wide: 8 (over y, x, core), narrow: 4 (over z).
Axes of the slice: x: 2, y: 2, z: 4, core: 2. Of those that a mesh axis runs over, the one named last changes fastest.
Arguments:
- tokens: bfloat16 [12288, 2048], P(('wide', 'narrow')), may hold values from -6 to 6
- cotangent: bfloat16 [12288, 2048], P(('wide', 'narrow')), may hold values from -6 to 6
- lengths: int32 [8], replicated, may hold values from 768 to 1536, as said below
- owners: int32 [116], replicated, may hold values from 0 to 7, as said below
- master: float32 [208, 4, 1024, 128], P('wide', 'narrow'), as said below
- moment_one: float32 [208, 4, 1024, 128], P('wide', 'narrow'), as said below
- moment_two: float32 [208, 4, 1024, 128], P('wide', 'narrow'), as said below
- norm_gains: float32 [2, 2048], replicated, may hold values from 0.5 to 1.5
- gain_first: float32 [2, 2048], replicated, may hold values from -640 to 640
- gain_second: float32 [2, 2048], replicated, may hold values from 12288 to 49152
Outputs:
- output: bfloat16 [12288, 2048], P(('wide', 'narrow'))
- input_grad: bfloat16 [12288, 2048], P(('wide', 'narrow'))
- weight_grads: float32 [208, 4, 1024, 128], P('wide', 'narrow')
- new_master: float32 [208, 4, 1024, 128], P('wide', 'narrow')
- new_copy: bfloat16 [208, 4, 1024, 128], P('wide', 'narrow')
- new_first: float32 [208, 4, 1024, 128], P('wide', 'narrow')
- new_second: float32 [208, 4, 1024, 128], P('wide', 'narrow')
- gain_grads: float32 [2, 2048], replicated
- gain_second_new: float32 [2, 2048], replicated
- new_gains: float32 [2, 2048], replicated
The draws below stay inside these ranges and needn't reach their ends.
Inputs may be any that keep to these rules, and one draw needn't show every extreme that they name: `owners`: each owner holds at most 26 units and some owner holds exactly 26. `lengths`: some sequence has length exactly 1536. `master`: slots that hold no unit are zero. `moment_one`: slots that hold no unit are zero. `moment_two`: slots that hold no unit are zero, the others positive.
All inputs are finite; a program needn't handle non-finite values.
Results may differ from the reference program's by a relative error of at most 0.025.
Values may be sent and summed in bfloat16 or wider, within the bound.
A program may use at most 704 MiB of HBM per device.

```python
import math
import jax
import jax.numpy as jnp
from jax import lax

D = 2048
H = 32
KV = 8
HD = 64
FF = 8192
SEQ_PAD = 1536
UR = 1024
CB = 128
STEP = 5
SEQS = 8
TOKENS = 12288
UNITS = 116
CAP = 26
N_WIDE = 8
N_NARROW = 4


def owner_list(key):
    key = jax.random.fold_in(key, 7)
    first_key, second_key, third_key = jax.random.split(key, 3)
    busiest = jax.random.randint(first_key, (), 0, N_WIDE)
    spare = jax.random.permutation(second_key, (N_WIDE - 1) * CAP)[:UNITS - CAP]
    others = (spare // CAP + busiest + 1) % N_WIDE
    listing = jnp.concatenate([jnp.full((CAP,), busiest, jnp.int32), others.astype(jnp.int32)])
    return jax.random.permutation(third_key, listing).astype(jnp.int32)


def slot_tables(owners, table):
    onehot = (owners[:, None] == jnp.arange(N_WIDE, dtype=jnp.int32)[None, :]).astype(jnp.int32)
    before = jnp.cumsum(onehot, axis=0) - onehot
    slot_place = owners * CAP + jnp.sum(before * onehot, axis=1)
    unit_of = jnp.zeros((N_WIDE * CAP,), jnp.int32).at[slot_place].set(jnp.arange(UNITS, dtype=jnp.int32))
    filled = jnp.zeros((N_WIDE * CAP,), jnp.float32).at[slot_place].set(1.0)
    col_blocks = UNITS // (D // UR)
    column = (unit_of % col_blocks)[:, None] * CB + jnp.arange(CB, dtype=jnp.int32)[None, :]
    query_width = H * HD // N_NARROW
    kv_width = KV * HD // N_NARROW
    ff_width = FF // N_NARROW
    edges = [query_width, query_width + kv_width, query_width + 2 * kv_width, 2 * query_width + 2 * kv_width, 2 * query_width + 2 * kv_width + ff_width, 2 * query_width + 2 * kv_width + 2 * ff_width]
    kind = jnp.zeros(column.shape, jnp.int32)
    for edge_col in edges:
        kind = kind + (column >= edge_col).astype(jnp.int32)
    scales = jnp.sum((kind[..., None] == jnp.arange(7, dtype=jnp.int32)).astype(jnp.float32) * jnp.array(table, jnp.float32), axis=-1)
    return scales * filled[:, None]


def draw_owners(key, part):
    return owner_list(key)


def draw_lengths(key, part):
    key = jax.random.fold_in(key, 31)
    first_key, second_key = jax.random.split(key)
    drawn = jax.random.randint(first_key, (N_WIDE,), SEQ_PAD // 2, SEQ_PAD + 1)
    longest = jax.random.randint(second_key, (), 0, N_WIDE)
    return jnp.where(jnp.arange(N_WIDE) == longest, SEQ_PAD, drawn).astype(jnp.int32)


def draw_master(key, part):
    owners = owner_list(key)
    key = jax.random.fold_in(key, 41)
    factor = D ** (-0.5)
    scales = slot_tables(owners, [1.7 * factor, 1.7 * factor, factor, 2.0 * factor, factor, factor, factor])
    noise = jax.random.normal(key, (N_WIDE * CAP, N_NARROW, UR, CB), jnp.float32)
    return noise * scales[:, None, None, :]


def draw_moment_one(key, part):
    owners = owner_list(key)
    key = jax.random.fold_in(key, 53)
    size = TOKENS ** 0.5
    scales = slot_tables(owners, [0.3 * size, 0.3 * size, 0.5 * size, 0.4 * size, 0.4 * size, 0.4 * size, 0.5 * size])
    noise = jax.random.normal(key, (N_WIDE * CAP, N_NARROW, UR, CB), jnp.float32)
    return noise * scales[:, None, None, :]


def draw_moment_two(key, part):
    owners = owner_list(key)
    key = jax.random.fold_in(key, 67)
    size = TOKENS ** 0.5
    scales = slot_tables(owners, [0.3 * size, 0.3 * size, 0.5 * size, 0.4 * size, 0.4 * size, 0.4 * size, 0.5 * size])
    spread = jnp.exp(jax.random.uniform(key, (N_WIDE * CAP, N_NARROW, UR, CB), jnp.float32, 0.0, math.log(4.0)))
    return spread * (scales * scales)[:, None, None, :]


def steps_of(rng, shape, cuts, least, largest):
    level = 1.0
    for dim, blocks in cuts:
        steps = jax.random.uniform(jax.random.fold_in(jax.random.fold_in(rng, 6), dim), (blocks,), jnp.float32, least / len(cuts), largest / len(cuts))
        level = level * jnp.repeat(jnp.exp(steps), shape[dim] // blocks).reshape((-1,) + (1,) * (len(shape) - 1 - dim))
    return level


def scatter_about(own_key, dims, scale, most, shards=(), kind=jnp.bfloat16):
    entries = jax.random.normal(own_key, dims, jnp.float32) * scale
    if len(shards) > 0:
        entries = steps_of(own_key, dims, shards, -0.22, 0.18) * entries
    return jnp.clip(entries, min=-most, max=most).astype(kind)


def setup_inputs(seed: int = 0) -> dict:
    key_list = jax.random.split(jax.random.key(seed), 11)
    tokens = scatter_about(key_list[0], (TOKENS, D), 1.0, 6.0, ((0, 32),))
    cotangent = scatter_about(key_list[1], (TOKENS, D), 1.0, 6.0, ((0, 32),))
    lengths = draw_lengths(jax.random.fold_in(key_list[10], 71), 0)
    owners = draw_owners(jax.random.fold_in(key_list[10], 71), 0)
    master = draw_master(jax.random.fold_in(key_list[10], 71), 0)
    moment_one = draw_moment_one(jax.random.fold_in(key_list[10], 71), 0)
    moment_two = draw_moment_two(jax.random.fold_in(key_list[10], 71), 0)
    norm_gains = jnp.clip(1.0 + 0.1 * jax.random.normal(key_list[7], (2, D), jnp.float32), 0.5, 1.5)
    gain_first = scatter_about(key_list[8], (2, D), (TOKENS ** 0.5), 640.0, (), jnp.float32)
    gain_second = jnp.clip(jnp.exp(jax.random.uniform(key_list[9], (2, D), jnp.float32, math.log(12288.0), math.log(49152.0))), 12288.0, 49152.0)
    return {"tokens": tokens, "cotangent": cotangent, "lengths": lengths, "owners": owners, "master": master, "moment_one": moment_one, "moment_two": moment_two, "norm_gains": norm_gains, "gain_first": gain_first, "gain_second": gain_second}


@jax.custom_vjp
def low(v):
    return lax.optimization_barrier(v.astype(jnp.bfloat16)).astype(jnp.float32)

@jax.custom_vjp
def low_back(v):
    return v

def low_keep(v):
    return (low(v), None)

def low_pass(kept, grad):
    return (grad,)

def back_keep(v):
    return (v, None)

def back_low(kept, grad):
    return (low(grad),)
low.defvjp(low_keep, low_pass)
low_back.defvjp(back_keep, back_low)
precise_mode = lax.Precision.HIGHEST

def matmul(first_op, second_op):
    return jnp.dot(first_op, second_op, precision=precise_mode, preferred_element_type=jnp.float32)

def rotate(values, cos_table, sin_table):
    middle = values.shape[-1] // 2
    turned = jnp.concatenate([-values[..., middle:], values[..., :middle]], axis=-1)
    return values * cos_table + turned * sin_table

def tables(length_all, head_size):
    inverse = 500000.0 ** (-jnp.arange(0, head_size, 2, dtype=jnp.float32) / head_size)
    angles = jnp.arange(length_all, dtype=jnp.float32)[:, None] * inverse[None, :]
    angles = jnp.concatenate([angles, angles], axis=1)
    return (jnp.cos(angles), jnp.sin(angles))

def rmsnorm(values, weight_gain):
    return values * lax.rsqrt(lax.optimization_barrier(jnp.mean(values * values, axis=-1, keepdims=True)) + 1e-05) * weight_gain

def positions(owners, wide_count, capacity):
    onehot = (owners[:, None] == jnp.arange(wide_count, dtype=jnp.int32)[None, :]).astype(jnp.int32)
    before = jnp.cumsum(onehot, axis=0) - onehot
    return (owners * capacity + lax.optimization_barrier(jnp.sum(before * onehot, axis=1))).astype(jnp.int32)

def to_packed(unit_data):
    row_blocks = D // UR
    col_blocks = unit_data.shape[0] // row_blocks
    shaped = unit_data.reshape(row_blocks, col_blocks, N_NARROW, UR, CB)
    return jnp.transpose(shaped, (2, 0, 3, 1, 4)).reshape(N_NARROW, D, col_blocks * CB)

def from_packed(packed):
    row_blocks = D // UR
    col_blocks = packed.shape[2] // CB
    shaped = packed.reshape(N_NARROW, row_blocks, UR, col_blocks, CB)
    return jnp.transpose(shaped, (1, 3, 0, 2, 4)).reshape(row_blocks * col_blocks, N_NARROW, UR, CB)

def split_packed(packed):
    query_width = H * HD // N_NARROW
    kv_width = KV * HD // N_NARROW
    ff_width = FF // N_NARROW
    extents = [query_width, kv_width, kv_width, query_width, ff_width, ff_width, ff_width]
    pieces = []
    offset = 0
    for extent in extents:
        section = packed[:, :, offset:offset + extent]
        pieces.append(jnp.transpose(section, (1, 0, 2)).reshape(D, N_NARROW * extent))
        offset = offset + extent
    return pieces

def sequence_layer(packed, norm_gains, inputs, length):
    w_query, w_key, w_value, w_out_t, w_gate, w_upper, w_down_t = split_packed(packed)
    cos_table, sin_table = tables(SEQ_PAD, HD)
    cos_heads = cos_table[:, None, :]
    sin_heads = sin_table[:, None, :]
    normed = low(rmsnorm(inputs, norm_gains[0]))
    query_heads = low(rotate(low_back(matmul(normed, w_query)).reshape(SEQ_PAD, H, HD), cos_heads, sin_heads))
    key_heads = low(rotate(low_back(matmul(normed, w_key)).reshape(SEQ_PAD, KV, HD), cos_heads, sin_heads))
    value_heads = low(low_back(matmul(normed, w_value))).reshape(SEQ_PAD, KV, HD)
    query_heads = jnp.transpose(query_heads, (1, 0, 2))
    key_heads = jnp.repeat(jnp.transpose(key_heads, (1, 0, 2)), H // KV, axis=0)
    value_heads = jnp.repeat(jnp.transpose(value_heads, (1, 0, 2)), H // KV, axis=0)
    block_rows = min(512, SEQ_PAD)
    block_count = SEQ_PAD // block_rows
    query_blocks = jnp.transpose(query_heads.reshape(H, block_count, block_rows, HD), (1, 0, 2, 3))
    row_starts = (jnp.arange(block_count) * block_rows).astype(jnp.int32)

    def attend(scanned):
        query_block, row_start = scanned
        scores = low_back(jnp.einsum('hqd,hkd->hqk', query_block, key_heads, precision=precise_mode)) * HD ** (-0.5)
        row_pos = row_start + jnp.arange(block_rows, dtype=jnp.int32)
        key_pos = jnp.arange(SEQ_PAD, dtype=jnp.int32)
        allowed = (key_pos[None, :] <= row_pos[:, None]) & (key_pos[None, :] < length)
        scores = jnp.where(allowed[None], scores, -1e+30)
        row_peak = lax.optimization_barrier(jnp.max(scores, axis=-1, keepdims=True))
        raised = jnp.exp(scores - row_peak)
        attn_probs = raised / lax.optimization_barrier(jnp.sum(raised, axis=-1, keepdims=True))
        return jnp.einsum('hqk,hkd->hqd', low(attn_probs), value_heads, precision=precise_mode)
    attended = lax.map(jax.checkpoint(attend), (query_blocks, row_starts))
    attended = jnp.transpose(attended, (0, 2, 1, 3)).reshape(SEQ_PAD, H * HD)
    attended = low(low_back(attended))
    residual = inputs + low_back(matmul(attended, w_out_t.T))
    normed_two = low(rmsnorm(residual, norm_gains[1]))
    gate_proj = low_back(matmul(normed_two, w_gate))
    upward = low_back(matmul(normed_two, w_upper))
    hidden = low(jax.nn.silu(gate_proj) * upward)
    return residual + low_back(matmul(hidden, w_down_t.T))

def whole(packed, norm_gains, inputs, lengths):
    checked_layer = jax.checkpoint(sequence_layer)

    def one_sequence(unused_state, scanned):
        seq_rows, length = scanned
        return (unused_state, checked_layer(packed, norm_gains, seq_rows, length))
    _, outputs = lax.scan(one_sequence, jnp.zeros((), jnp.float32), (inputs.reshape(SEQS, SEQ_PAD, D), lengths))
    return outputs.reshape(TOKENS, D)

def adamw(weight, gradient, moment_one, moment_two, rate, decay):
    moment_one = 0.5 * moment_one + 0.5 * gradient
    moment_two = 0.5 * moment_two + 0.5 * gradient * gradient
    correct = 1.0 - 0.5 ** STEP
    update = moment_one / correct / (jnp.sqrt(moment_two / correct) + 1e-08)
    return (weight - rate * (update + decay * weight), moment_one, moment_two)

def reference(tokens, cotangent, lengths, owners, master, moment_one, moment_two, norm_gains, gain_first, gain_second):
    slot_place = positions(owners, N_WIDE, CAP)
    master_units = master[slot_place]
    weights = to_packed(lax.optimization_barrier(master_units.astype(jnp.bfloat16)).astype(jnp.float32))
    inputs = tokens.astype(jnp.float32)

    def forward(packed, gain_pair, layer_input):
        return whole(packed, gain_pair, layer_input, lengths)
    output, pullback = jax.vjp(forward, weights, norm_gains, inputs)
    grad_packed, grad_gains, grad_inputs = pullback(cotangent.astype(jnp.float32))
    grad_units = from_packed(grad_packed)
    new_units, first_units, second_units = adamw(master_units, grad_units, moment_one[slot_place], moment_two[slot_place], 0.02, 0.1)
    zero_slots = jnp.zeros(master.shape, jnp.float32)
    grad_slots = zero_slots.at[slot_place].set(grad_units)
    new_slots = zero_slots.at[slot_place].set(new_units)
    first_slots = zero_slots.at[slot_place].set(first_units)
    second_slots = zero_slots.at[slot_place].set(second_units)
    new_gains, unused, gain_second_new = adamw(norm_gains, grad_gains, gain_first, gain_second, 0.5, 0.0)
    return (output.astype(jnp.bfloat16), grad_inputs.astype(jnp.bfloat16), grad_slots, new_slots, new_slots.astype(jnp.bfloat16), first_slots, second_slots, grad_gains, gain_second_new, new_gains)
```

```python
import functools

import jax
import jax.numpy as jnp
from jax import lax
from jax.experimental import pallas as pl
from jax.experimental.pallas import tpu as pltpu
from jax.sharding import PartitionSpec as P

D = 2048
H = 32
KV = 8
HD = 64
FF = 8192
STEP = 5
LANES = 128
MIB = 1 << 20

f32 = jnp.float32
bf16 = jnp.bfloat16


def dot(first_op, second_op, first_dim, second_dim):
    return lax.dot_general(
        first_op,
        second_op,
        (((first_dim,), (second_dim,)), ((), ())),
        preferred_element_type=f32,
    )


def params(mib):
    return pltpu.CompilerParams(vmem_limit_bytes=mib * MIB)


def cost(flops, moved, transcendentals=0):
    return pl.CostEstimate(
        flops=int(flops), bytes_accessed=int(moved), transcendentals=int(transcendentals)
    )


def tables(length_all, head_size):
    inverse = 500000.0 ** (-jnp.arange(0, head_size, 2, dtype=f32) / head_size)
    angles = jnp.arange(length_all, dtype=f32)[:, None] * inverse[None, :]
    angles = jnp.concatenate([angles, angles], axis=1)
    return (jnp.cos(angles), jnp.sin(angles))


def rmsnorm(values, weight_gain):
    return (
        values * lax.rsqrt(jnp.mean(values * values, axis=-1, keepdims=True) + 1e-05) * weight_gain
    )


def positions(owners, wide_count, capacity):
    onehot = (owners[:, None] == jnp.arange(wide_count, dtype=jnp.int32)[None, :]).astype(jnp.int32)
    before = jnp.cumsum(onehot, axis=0) - onehot
    return (owners * capacity + jnp.sum(before * onehot, axis=1), jnp.sum(onehot, axis=0))


def adamw(weight, gradient, moment_one, moment_two, rate, decay):
    moment_one = 0.5 * moment_one + 0.5 * gradient
    moment_two = 0.5 * moment_two + 0.5 * gradient * gradient
    correct = 1.0 - 0.5**STEP
    update = moment_one / correct / (jnp.sqrt(moment_two / correct) + 1e-08)
    return (weight - rate * (update + decay * weight), moment_one, moment_two)


def turn_kernel(unit_ref, out_ref):
    for k in range(out_ref.shape[0]):
        out_ref[k] = jnp.transpose(unit_ref[k, 0], (1, 0)).astype(bf16)


def turn_units(master):
    capacity, _, unit_rows, unit_cols = master.shape
    step = 2 if capacity % 2 == 0 else 1
    return pl.pallas_call(
        turn_kernel,
        grid=(capacity // step,),
        in_specs=[pl.BlockSpec((step, 1, unit_rows, unit_cols), lambda s: (s, 0, 0, 0))],
        out_specs=pl.BlockSpec((step, unit_cols, unit_rows), lambda s: (s, 0, 0)),
        out_shape=jax.ShapeDtypeStruct((capacity, unit_cols, unit_rows), bf16),
        compiler_params=params(32),
        cost_estimate=cost(0, master.size * 6),
        name="turn_units",
    )(master)


def pick_kernel(place_ref, got_ref, out_ref, sem, *, col_blocks, piece, unit_rows):
    def start(unit, carry):
        half = unit // col_blocks
        block = unit - half * col_blocks
        pltpu.make_async_copy(
            got_ref.at[place_ref[unit]],
            out_ref.at[
                pl.ds(pl.multiple_of(block * piece, piece), piece),
                pl.ds(pl.multiple_of(half * unit_rows, unit_rows), unit_rows),
            ],
            sem,
        ).start()
        return carry

    lax.fori_loop(0, place_ref.shape[0], start, 0)
    pltpu.make_async_copy(out_ref, out_ref, sem).wait()


def pick_units(got, slot_place, row_blocks):
    _, piece, unit_rows = got.shape
    unit_count = slot_place.shape[0]
    col_blocks = unit_count // row_blocks
    if piece % 16 == 0:
        return pl.pallas_call(
            functools.partial(
                pick_kernel, col_blocks=col_blocks, piece=piece, unit_rows=unit_rows
            ),
            in_specs=[
                pl.BlockSpec(memory_space=pltpu.SMEM),
                pl.BlockSpec(memory_space=pl.ANY),
            ],
            out_specs=pl.BlockSpec(memory_space=pl.ANY),
            out_shape=jax.ShapeDtypeStruct((col_blocks * piece, row_blocks * unit_rows), bf16),
            scratch_shapes=[pltpu.SemaphoreType.DMA],
            cost_estimate=cost(0, unit_count * piece * unit_rows * 4),
            name="pick_units",
        )(slot_place, got)
    units = jnp.take(got, slot_place, axis=0).reshape(row_blocks, col_blocks, piece, unit_rows)
    return jnp.transpose(units, (1, 2, 0, 3)).reshape(col_blocks * piece, row_blocks * unit_rows)


def unpick_kernel(unit_ref, rows_ref, out_ref, sem, *, col_blocks, piece, unit_rows):
    def start(slot, carry):
        unit = unit_ref[slot]
        half = unit // col_blocks
        block = unit - half * col_blocks
        pltpu.make_async_copy(
            rows_ref.at[
                pl.ds(pl.multiple_of(block * piece, piece), piece),
                pl.ds(pl.multiple_of(half * unit_rows, unit_rows), unit_rows),
            ],
            out_ref.at[slot],
            sem,
        ).start()
        return carry

    lax.fori_loop(0, unit_ref.shape[0], start, 0)
    pltpu.make_async_copy(out_ref, out_ref, sem).wait()


def unpick_units(rows, unit_of, unit_count, piece, unit_rows):
    row_blocks = rows.shape[1] // unit_rows
    col_blocks = unit_count // row_blocks
    slots = unit_of.shape[0]
    if piece % 16 == 0:
        return pl.pallas_call(
            functools.partial(
                unpick_kernel, col_blocks=col_blocks, piece=piece, unit_rows=unit_rows
            ),
            in_specs=[
                pl.BlockSpec(memory_space=pltpu.SMEM),
                pl.BlockSpec(memory_space=pl.ANY),
            ],
            out_specs=pl.BlockSpec(memory_space=pl.ANY),
            out_shape=jax.ShapeDtypeStruct((slots, piece, unit_rows), bf16),
            scratch_shapes=[pltpu.SemaphoreType.DMA],
            cost_estimate=cost(0, slots * piece * unit_rows * 4),
            name="unpick_units",
        )(unit_of, rows)
    units = jnp.transpose(
        rows.reshape(col_blocks, piece, row_blocks, unit_rows), (2, 0, 1, 3)
    ).reshape(unit_count, piece, unit_rows)
    return jnp.take(units, unit_of, axis=0)


def update_kernel(
    count_ref, grad_ref, master_ref, one_ref, two_ref,
    grad_out, master_out, copy_out, one_out, two_out,
):
    filled = pl.program_id(0) < count_ref[0]
    parts, _, piece, unit_rows = grad_ref.shape
    turned = grad_ref[:, 0].astype(f32).reshape(parts * piece, unit_rows)
    gradient = jnp.where(filled, jnp.transpose(turned, (1, 0)), 0.0)
    weight, one, two = adamw(master_ref[0, 0], gradient, one_ref[0, 0], two_ref[0, 0], 0.02, 0.1)
    grad_out[0, 0] = gradient
    master_out[0, 0] = weight
    copy_out[0, 0] = weight.astype(bf16)
    one_out[0, 0] = one
    two_out[0, 0] = two


def update_units(count, grads, master, moment_one, moment_two):
    capacity, _, unit_rows, unit_cols = master.shape
    parts, _, piece, _ = grads.shape
    unit = pl.BlockSpec((1, 1, unit_rows, unit_cols), lambda s: (s, 0, 0, 0))
    whole = jax.ShapeDtypeStruct(master.shape, f32)
    return pl.pallas_call(
        update_kernel,
        grid=(capacity,),
        in_specs=[
            pl.BlockSpec(memory_space=pltpu.SMEM),
            pl.BlockSpec((parts, 1, piece, unit_rows), lambda s: (0, s, 0, 0)),
            unit,
            unit,
            unit,
        ],
        out_specs=[unit] * 5,
        out_shape=[whole, whole, jax.ShapeDtypeStruct(master.shape, bf16), whole, whole],
        compiler_params=params(40),
        cost_estimate=cost(master.size * 12, master.size * 32),
        name="update_units",
    )(count, grads, master, moment_one, moment_two)


def lane_index(shape):
    return lax.broadcasted_iota(jnp.int32, shape, 1)


def rope(tile, cos_tile, sin_tile):
    lower = lane_index(tile.shape) % HD < HD // 2
    ahead = pltpu.roll(tile, LANES - HD // 2, 1)
    behind = pltpu.roll(tile, HD // 2, 1)
    return tile * cos_tile + jnp.where(lower, -ahead, behind) * sin_tile


def unrope(tile, cos_tile, sin_tile):
    lower = lane_index(tile.shape) % HD < HD // 2
    weighted = tile * sin_tile
    ahead = pltpu.roll(weighted, LANES - HD // 2, 1)
    behind = pltpu.roll(weighted, HD // 2, 1)
    return tile * cos_tile + jnp.where(lower, ahead, -behind)


def project_kernel(rows_ref, w_ref, cos_ref, sin_ref, out_ref, *, query_width, kv_width):
    product = dot(rows_ref[...], w_ref[...], 1, 1)
    roped_end = query_width + kv_width
    for start in range(0, out_ref.shape[1], LANES):
        tile = product[:, start : start + LANES]
        if start < roped_end:
            turned = rope(tile, cos_ref[...], sin_ref[...])
            if start + LANES > roped_end:
                tile = jnp.where(lane_index(tile.shape) < roped_end - start, turned, tile)
            else:
                tile = turned
        tile = tile.astype(bf16)
        if start < query_width:
            tile = tile * HD ** (-0.5)
        out_ref[:, start : start + LANES] = tile


def project(rows, w_qkv, cos_rows, sin_rows, query_width, kv_width):
    count = rows.shape[0]
    width = w_qkv.shape[0]
    return pl.pallas_call(
        functools.partial(project_kernel, query_width=query_width, kv_width=kv_width),
        out_shape=jax.ShapeDtypeStruct((count, width), bf16),
        compiler_params=params(40),
        cost_estimate=cost(2 * count * width * D, 2 * (count + width) * D),
        name="project",
    )(rows, w_qkv, cos_rows, sin_rows)


def extend(tile_ref, offset, out_ref):
    tile = tile_ref[...].astype(f32)
    other = pltpu.roll(tile, HD, 1)
    low = lane_index(tile.shape) < HD
    at_low = offset == 0
    out_ref[0] = jnp.where(low, jnp.where(at_low, tile, other), 0.0).astype(bf16)
    out_ref[1] = jnp.where(low, 0.0, jnp.where(at_low, other, tile)).astype(bf16)


def forward_kernel(
    length_ref, q_ref, k_ref, v_ref, out_ref, log_ref, kx, vx, *, block, pairs_per, k_start, v_start
):
    pair = pl.program_id(0)
    kv_head = pair // pairs_per
    length = length_ref[0]
    seq_len = q_ref.shape[0]

    @pl.when(pair % pairs_per == 0)
    def _():
        extend(k_ref, (k_start + kv_head * HD) % LANES, kx)
        extend(v_ref, (v_start + kv_head * HD) % LANES, vx)

    row = lax.broadcasted_iota(jnp.int32, (block, block), 0)
    col = lax.broadcasted_iota(jnp.int32, (block, block), 1)
    causal = col <= row
    key_row = lax.broadcasted_iota(jnp.int32, (1, seq_len), 1)
    bias = jnp.where(key_row < length, 0.0, -1e30).astype(f32)
    low = lane_index((block, LANES)) < HD
    for start in range(0, seq_len, block):
        query = q_ref[start : start + block, :]
        total = None
        logs = []
        for half in range(2):
            diagonal = dot(query, kx[half, start : start + block, :], 1, 1)
            diagonal = jnp.where(causal, diagonal + bias[:, start : start + block], -1e30)
            peak = jnp.max(diagonal, axis=1, keepdims=True)
            if start:
                before = dot(query, kx[half, :start, :], 1, 1) + bias[:, :start]
                peak = jnp.maximum(peak, jnp.max(before, axis=1, keepdims=True))
                before = jnp.exp(before - peak)
            diagonal = jnp.exp(diagonal - peak)
            row_sum = jnp.sum(diagonal, axis=1, keepdims=True)
            part = dot(diagonal.astype(bf16), vx[half, start : start + block, :], 1, 0)
            if start:
                row_sum = row_sum + jnp.sum(before, axis=1, keepdims=True)
                part = part + dot(before.astype(bf16), vx[half, :start, :], 1, 0)
            part = part / row_sum
            total = part if total is None else total + part
            logs.append(peak + jnp.log(row_sum))
        out_ref[start : start + block, :] = total.astype(bf16)
        tile = jnp.transpose(jnp.where(low, logs[0], logs[1]), (1, 0))
        log_ref[0, 0:1, start : start + block] = tile[0:1]
        log_ref[0, 1:2, start : start + block] = tile[HD : HD + 1]


def attend_forward(length, qkv, query_width, kv_width, block):
    seq_len = qkv.shape[0]
    pairs = query_width // LANES
    pairs_per = H // KV // 2
    k_start = query_width
    v_start = query_width + kv_width
    column = functools.partial(pl.BlockSpec, (seq_len, LANES))
    return pl.pallas_call(
        functools.partial(
            forward_kernel, block=block, pairs_per=pairs_per, k_start=k_start, v_start=v_start
        ),
        grid=(pairs,),
        in_specs=[
            pl.BlockSpec(memory_space=pltpu.SMEM),
            column(lambda p: (0, p)),
            column(lambda p: (0, (k_start + p // pairs_per * HD) // LANES)),
            column(lambda p: (0, (v_start + p // pairs_per * HD) // LANES)),
        ],
        out_specs=[
            column(lambda p: (0, p)),
            pl.BlockSpec((1, 8, seq_len), lambda p: (p, 0, 0)),
        ],
        out_shape=[
            jax.ShapeDtypeStruct((seq_len, query_width), bf16),
            jax.ShapeDtypeStruct((pairs, 8, seq_len), f32),
        ],
        scratch_shapes=[
            pltpu.VMEM((2, seq_len, LANES), bf16),
            pltpu.VMEM((2, seq_len, LANES), bf16),
        ],
        compiler_params=params(56),
        cost_estimate=cost(pairs * seq_len * seq_len * 1024, seq_len * 768 * 4),
        name="attend_forward",
    )(length, qkv, qkv, qkv)


def backward_kernel(
    length_ref, q_ref, k_ref, v_ref, back_ref, out_ref, log_ref, cos_ref, sin_ref, grad_ref,
    kx, vx, dk, dv, *, block, pairs_per, k_start, v_start,
):
    pair = pl.program_id(0)
    kv_head = pair // pairs_per
    length = length_ref[0]
    seq_len = q_ref.shape[0]
    k_offset = (k_start + kv_head * HD) % LANES
    v_offset = (v_start + kv_head * HD) % LANES

    @pl.when(pair == 0)
    def _():
        grad_ref[:, k_start // LANES * LANES :] = jnp.zeros(
            (seq_len, grad_ref.shape[1] - k_start // LANES * LANES), bf16
        )

    @pl.when(pair % pairs_per == 0)
    def _():
        extend(k_ref, k_offset, kx)
        extend(v_ref, v_offset, vx)
        dk[...] = jnp.zeros(dk.shape, f32)
        dv[...] = jnp.zeros(dv.shape, f32)

    key = lax.broadcasted_iota(jnp.int32, (block, block), 0)
    row = lax.broadcasted_iota(jnp.int32, (block, block), 1)
    causal = key <= row
    for start in range(0, seq_len, block):
        here = slice(start, start + block)
        query = q_ref[here, :]
        back = back_ref[here, :]
        turned = jnp.transpose(back.astype(f32) * out_ref[here, :].astype(f32), (1, 0))
        query_grad = None
        for half in range(2):
            log_row = log_ref[0, half : half + 1, here]
            shift = jnp.sum(turned[half * HD : half * HD + HD], axis=0, keepdims=True)
            for first in range(0, start + block, block):
                keys = slice(first, first + block)
                scores = dot(kx[half, keys, :], query, 1, 1)
                probs = jnp.exp(scores - log_row)
                if first + block > seq_len // 2:
                    probs = jnp.where(key + first < length, probs, 0.0)
                if first == start:
                    probs = jnp.where(causal, probs, 0.0)
                probs_back = dot(vx[half, keys, :], back, 1, 1)
                scores_back = (probs * (probs_back - shift)).astype(bf16)
                dv[half, keys, :] += dot(probs.astype(bf16), back, 1, 0)
                dk[half, keys, :] += dot(scores_back, query, 1, 0)
                part = dot(scores_back, kx[half, keys, :], 0, 0)
                query_grad = part if query_grad is None else query_grad + part
        query_grad = unrope(query_grad * HD ** (-0.5), cos_ref[here, :], sin_ref[here, :])
        grad_ref[here, pl.ds(pl.multiple_of(pair * LANES, LANES), LANES)] = query_grad.astype(bf16)

    @pl.when(pair % pairs_per == pairs_per - 1)
    def _():
        low = lane_index((seq_len, LANES)) < HD

        def place(sums, offset, start, roped):
            joined = jnp.where(low, sums[0], 0.0) + pltpu.roll(
                jnp.where(low, 0.0, sums[1]), HD, 1
            )
            if roped:
                joined = unrope(joined, cos_ref[...], sin_ref[...])
            joined = jnp.where(offset == 0, joined, pltpu.roll(joined, HD, 1))
            tile = pl.ds(
                pl.multiple_of((start + kv_head * HD) // LANES * LANES, LANES), LANES
            )
            grad_ref[:, tile] = (grad_ref[:, tile].astype(f32) + joined).astype(bf16)

        place(dk[...], k_offset, k_start, True)
        place(dv[...], v_offset, v_start, False)


def attend_backward(length, qkv, back, out, logs, cos_all, sin_all, query_width, kv_width, block):
    seq_len, width = qkv.shape
    pairs = query_width // LANES
    pairs_per = H // KV // 2
    k_start = query_width
    v_start = query_width + kv_width
    column = functools.partial(pl.BlockSpec, (seq_len, LANES))
    return pl.pallas_call(
        functools.partial(
            backward_kernel, block=block, pairs_per=pairs_per, k_start=k_start, v_start=v_start
        ),
        grid=(pairs,),
        in_specs=[
            pl.BlockSpec(memory_space=pltpu.SMEM),
            column(lambda p: (0, p)),
            column(lambda p: (0, (k_start + p // pairs_per * HD) // LANES)),
            column(lambda p: (0, (v_start + p // pairs_per * HD) // LANES)),
            column(lambda p: (0, p)),
            column(lambda p: (0, p)),
            pl.BlockSpec((1, 8, seq_len), lambda p: (p, 0, 0)),
            column(lambda p: (0, 0)),
            column(lambda p: (0, 0)),
        ],
        out_specs=pl.BlockSpec((seq_len, width), lambda p: (0, 0)),
        out_shape=jax.ShapeDtypeStruct((seq_len, width), bf16),
        scratch_shapes=[
            pltpu.VMEM((2, seq_len, LANES), bf16),
            pltpu.VMEM((2, seq_len, LANES), bf16),
            pltpu.VMEM((2, seq_len, LANES), f32),
            pltpu.VMEM((2, seq_len, LANES), f32),
        ],
        compiler_params=params(56),
        cost_estimate=cost(pairs * seq_len * seq_len * 2560, seq_len * 768 * 6),
        name="attend_backward",
    )(length, qkv, qkv, qkv, back, out, logs, cos_all, sin_all)


def hidden_kernel(rows_ref, back_ref, wg_ref, wu_ref, wd_ref, hid_ref, dgate_ref, dup_ref):
    gate = dot(rows_ref[...], wg_ref[...], 1, 1)
    up = dot(rows_ref[...], wu_ref[...], 1, 1)
    hidden_back = dot(back_ref[...], wd_ref[...], 1, 1)
    sig = 1.0 / (1.0 + jnp.exp(-gate))
    silu = gate * sig
    hid_ref[...] = (silu * up).astype(bf16)
    dgate_ref[...] = (hidden_back * up * (sig * (1.0 + gate * (1.0 - sig)))).astype(bf16)
    dup_ref[...] = (hidden_back * silu).astype(bf16)


def hidden_pass(rows, back, wg, wu, wd):
    count = rows.shape[0]
    ff_width = wg.shape[0]
    step = 256
    resident = pl.BlockSpec((count, D), lambda i: (0, 0))
    weight = pl.BlockSpec((step, D), lambda i: (i, 0))
    given = pl.BlockSpec((count, step), lambda i: (0, i))
    shape = jax.ShapeDtypeStruct((count, ff_width), bf16)
    return pl.pallas_call(
        hidden_kernel,
        grid=(ff_width // step,),
        in_specs=[resident, resident, weight, weight, weight],
        out_specs=[given] * 3,
        out_shape=[shape] * 3,
        compiler_params=params(48),
        cost_estimate=cost(6 * count * ff_width * D, 6 * ff_width * D, count * ff_width),
        name="hidden_pass",
    )(rows, back, wg, wu, wd)


def outer_kernel(*refs):
    out_ref = refs[-1]
    count = (len(refs) - 1) // 2
    total = None
    for k in range(count):
        part = dot(refs[k][...], refs[count + k][...], 0, 0)
        total = part if total is None else total + part
    out_ref[...] = total.astype(bf16)


def outer(firsts, seconds):
    rows, height = firsts[0].shape
    width = seconds[0].shape[1]
    step = 512 if height % 512 == 0 else 256 if height % 256 == 0 else LANES
    chunks = len(firsts)
    return pl.pallas_call(
        outer_kernel,
        grid=(height // step,),
        in_specs=[pl.BlockSpec((rows, step), lambda i: (0, i))] * chunks
        + [pl.BlockSpec((rows, width), lambda i: (0, 0))] * chunks,
        out_specs=pl.BlockSpec((step, width), lambda i: (i, 0)),
        out_shape=jax.ShapeDtypeStruct((height, width), bf16),
        compiler_params=params(56),
        cost_estimate=cost(
            2 * chunks * rows * height * width,
            2 * (chunks * rows * (height + width) + height * width),
        ),
        name="outer",
    )(*firsts, *seconds)


def cycle(count, step=1):
    return [(i, (i + step) % count) for i in range(count)]


def ring_gather(own, count):
    blocks = [own]
    for _ in range(count - 1):
        blocks.append(lax.ppermute(blocks[-1], "narrow", cycle(count)))
    return blocks


def ring_reduce(parts, count):
    total = parts[1]().astype(bf16)
    for s in range(2, count):
        total = (parts[s]() + lax.ppermute(total, "narrow", cycle(count)).astype(f32)).astype(bf16)
    return parts[0]() + lax.ppermute(total, "narrow", cycle(count)).astype(f32)


def square_pairs(step):
    order = (0, 1, 3, 2)
    pairs = []
    for place, chip in enumerate(order):
        target = order[(place + step) % 4]
        pairs += [(chip * 2 + core, target * 2 + core) for core in range(2)]
    return pairs


def swap_pairs():
    return [(i, i ^ 1) for i in range(8)]


def plane_gather(halves):
    first, second = halves
    blocks = [first, second]
    for _ in range(3):
        first = lax.ppermute(first, "wide", square_pairs(1))
        second = lax.ppermute(second, "wide", square_pairs(-1))
        blocks += [first, second]
    return blocks + [lax.ppermute(block, "wide", swap_pairs()) for block in blocks]


def plane_reduce(grad):
    half = grad.shape[0] // 2
    own = grad[:half].astype(f32) + lax.ppermute(grad[half:], "wide", swap_pairs()).astype(f32)
    own = own.astype(bf16)
    size = half // 8
    blocks = [own[k * size : (k + 1) * size] for k in range(8)]
    ends = []
    for side, step in ((0, 1), (1, -1)):
        total = blocks[2 + side]
        for s in (2, 3, 0):
            total = (
                blocks[2 * s + side].astype(f32)
                + lax.ppermute(total, "wide", square_pairs(step)).astype(f32)
            ).astype(bf16)
        ends.append(total)
    return ends


def local(
    tokens, cotangent, lengths, owners, master, moment_one, moment_two, norm_gains, gain_first,
    gain_second,
):
    wide_count = lax.axis_size("wide")
    narrow_count = lax.axis_size("narrow")
    capacity, _, unit_rows, unit_cols = master.shape
    unit_count = owners.shape[0]
    row_count = tokens.shape[0]
    seq_len = row_count * narrow_count
    row_blocks = D // unit_rows
    piece = unit_cols // wide_count
    query_width = H // narrow_count * HD
    kv_width = KV // narrow_count * HD
    ff_width = FF // narrow_count
    qkv_width = query_width + 2 * kv_width
    wide_index = lax.axis_index("wide")
    narrow_index = lax.axis_index("narrow")
    length = lax.dynamic_slice(lengths, (wide_index,), (1,))
    block = min(256, seq_len)

    inputs = tokens.astype(f32)
    normed = rmsnorm(inputs, norm_gains[0]).astype(bf16)
    normed_blocks = ring_gather(normed, narrow_count)

    slot_place, counts = positions(owners, wide_count, capacity)
    turned = turn_units(master).reshape(capacity, wide_count, piece, unit_rows)
    got = lax.all_to_all(turned, "wide", split_axis=1, concat_axis=0)
    got = got.reshape(wide_count * capacity, piece, unit_rows)
    rows = pick_units(got, slot_place, row_blocks)
    qkv_end = qkv_width // wide_count
    out_end = qkv_end + query_width // wide_count
    ff_rows = ff_width // wide_count

    def plane_all(part, width):
        gathered = lax.all_gather(part, "wide", axis=0)
        gathered = gathered.reshape(wide_count, width // unit_cols, piece, D)
        return jnp.transpose(gathered, (1, 0, 2, 3)).reshape(width, D)

    w_qkv = plane_all(rows[:qkv_end], qkv_width)
    out_part = lax.all_gather(rows[qkv_end:out_end], "narrow", axis=0)
    w_out = lax.all_gather(out_part, "wide", axis=0)
    w_out = jnp.transpose(
        w_out.reshape(wide_count, narrow_count, query_width // unit_cols, piece, D),
        (1, 2, 0, 3, 4),
    ).reshape(D, D)
    ff_parts = [rows[out_end + k * ff_rows : out_end + (k + 1) * ff_rows] for k in range(3)]
    if wide_count == 8:
        half = ff_rows // 2
        halves = [
            jnp.concatenate([part[:half] for part in ff_parts], axis=0),
            jnp.concatenate([part[half:] for part in ff_parts], axis=0),
        ]
        ff_blocks = plane_gather(halves)
        w_gate, w_upper, w_down = [
            jnp.concatenate([b[k * half : (k + 1) * half] for b in ff_blocks], axis=0)
            for k in range(3)
        ]
    else:
        w_gate, w_upper, w_down = [
            lax.all_gather(part, "wide", axis=0, tiled=True) for part in ff_parts
        ]

    cos_table, sin_table = tables(seq_len, HD)
    cos_all = jnp.concatenate([cos_table] * (LANES // HD), axis=1)
    sin_all = jnp.concatenate([sin_table] * (LANES // HD), axis=1)
    projected = []
    for s in range(narrow_count):
        first_row = (narrow_index - s) % narrow_count * row_count
        projected.append(
            project(
                normed_blocks[s],
                w_qkv,
                lax.dynamic_slice(cos_all, (first_row, 0), (row_count, LANES)),
                lax.dynamic_slice(sin_all, (first_row, 0), (row_count, LANES)),
                query_width,
                kv_width,
            )
        )
    back_by = (narrow_index - jnp.arange(narrow_count, dtype=jnp.int32)) % narrow_count
    qkv = jnp.take(jnp.stack(projected), back_by, axis=0).reshape(seq_len, qkv_width)
    attended, logs = attend_forward(length, qkv, query_width, kv_width, block)
    attended_rows = lax.all_to_all(
        attended.reshape(narrow_count, row_count, query_width), "narrow", 0, 0
    )
    attended_rows = jnp.transpose(attended_rows, (1, 0, 2)).reshape(row_count, D)
    residual = inputs + dot(attended_rows, w_out, 1, 0)

    normed_two = rmsnorm(residual, norm_gains[1]).astype(bf16)
    mlp_blocks = ring_gather(normed_two, narrow_count)
    back_blocks = ring_gather(cotangent, narrow_count)
    passes = [
        hidden_pass(mlp_blocks[s], back_blocks[s], w_gate, w_upper, w_down)
        for s in range(narrow_count)
    ]

    def norm_back_part(s):
        return lambda: dot(passes[s][1], w_gate, 1, 0) + dot(passes[s][2], w_upper, 1, 0)

    norm_two_back = ring_reduce([norm_back_part(s) for s in range(narrow_count)], narrow_count)
    output = residual + ring_reduce(
        [functools.partial(dot, passes[s][0], w_down, 1, 0) for s in range(narrow_count)],
        narrow_count,
    )
    ff_grads = [
        outer([p[1] for p in passes], mlp_blocks),
        outer([p[2] for p in passes], mlp_blocks),
        outer([p[0] for p in passes], back_blocks),
    ]

    def plane_sum(grad):
        if wide_count == 8:
            return plane_reduce(grad)
        return [lax.psum_scatter(grad, "wide", scatter_dimension=0, tiled=True)]

    ff_sums = [part for grad in ff_grads for part in plane_sum(grad)]

    _, norm_two_pull = jax.vjp(rmsnorm, residual, norm_gains[1])
    resid_part, gain_two = norm_two_pull(norm_two_back)
    resid_back = cotangent.astype(f32) + resid_part
    attn_back = resid_back.astype(bf16)
    out_back = dot(attn_back, w_out, 1, 1).astype(bf16)
    out_back = jnp.transpose(out_back.reshape(row_count, narrow_count, query_width), (1, 0, 2))
    out_back = lax.all_to_all(out_back, "narrow", 0, 0).reshape(seq_len, query_width)
    grad_out = outer([attended_rows], [attn_back])
    qkv_back = attend_backward(
        length, qkv, out_back, attended, logs, cos_all, sin_all, query_width, kv_width, block
    )
    qkv_blocks = [
        lax.dynamic_slice(
            qkv_back, ((narrow_index - s) % narrow_count * row_count, 0), (row_count, qkv_width)
        )
        for s in range(narrow_count)
    ]
    grad_qkv = outer(qkv_blocks, normed_blocks)

    def plane_split(grad, width, lead):
        shaped = grad.reshape(lead, width // unit_cols, wide_count, piece, D)
        shaped = jnp.transpose(shaped, (2, 0, 1, 3, 4)).reshape(wide_count * lead * width // wide_count, D)
        return lax.psum_scatter(shaped, "wide", scatter_dimension=0, tiled=True)

    grad_out = plane_split(grad_out, query_width, narrow_count)
    grad_out = lax.psum_scatter(grad_out, "narrow", scatter_dimension=0, tiled=True)
    grad_qkv = plane_split(grad_qkv, qkv_width, 1)

    grad_rows = jnp.concatenate([grad_qkv, grad_out] + ff_sums, axis=0)
    slots = wide_count * capacity
    unit_of = jnp.zeros((slots,), jnp.int32).at[slot_place].set(
        jnp.arange(unit_count, dtype=jnp.int32)
    )
    sent = unpick_units(grad_rows, unit_of, unit_count, piece, unit_rows)
    sent = sent.reshape(wide_count, capacity, piece, unit_rows)
    owned = lax.all_to_all(sent, "wide", split_axis=0, concat_axis=0)
    count = lax.dynamic_slice(counts, (wide_index,), (1,))
    owned_grads, new_master, new_copy, new_first, new_second = update_units(
        count, owned, master, moment_one, moment_two
    )

    norm_one_back = ring_reduce(
        [functools.partial(dot, qkv_blocks[s], w_qkv, 1, 0) for s in range(narrow_count)],
        narrow_count,
    )
    _, norm_one_pull = jax.vjp(rmsnorm, inputs, norm_gains[0])
    input_part, gain_one = norm_one_pull(norm_one_back)
    input_grad = (resid_back + input_part).astype(bf16)
    gain_grads = lax.psum(jnp.stack([gain_one, gain_two]), ("wide", "narrow"))
    new_gains, _, gain_second_new = adamw(
        norm_gains, gain_grads, gain_first, gain_second, 0.5, 0.0
    )
    return (
        output.astype(bf16),
        input_grad,
        owned_grads,
        new_master,
        new_copy,
        new_first,
        new_second,
        gain_grads,
        gain_second_new,
        new_gains,
    )


def solution(mesh):
    rows = P(("wide", "narrow"), None)
    units = P("wide", "narrow", None, None)
    return jax.shard_map(
        local,
        mesh=mesh,
        in_specs=(rows, rows, P(), P(), units, units, units, P(), P(), P()),
        out_specs=(rows, rows, units, units, units, units, units, P(), P(), P()),
        check_vma=False,
    )
```

```python
import functools

import jax
import jax.numpy as jnp
from jax import lax
from jax.experimental import pallas as pl
from jax.experimental.pallas import tpu as pltpu
from jax.sharding import PartitionSpec as P

D = 2048
H = 32
KV = 8
HD = 64
FF = 8192
STEP = 5
LANES = 128
MIB = 1 << 20

f32 = jnp.float32
bf16 = jnp.bfloat16


def dot(first_op, second_op, first_dim, second_dim):
    return lax.dot_general(
        first_op,
        second_op,
        (((first_dim,), (second_dim,)), ((), ())),
        preferred_element_type=f32,
    )


def params(mib):
    return pltpu.CompilerParams(vmem_limit_bytes=mib * MIB)


def cost(flops, moved, transcendentals=0):
    return pl.CostEstimate(
        flops=int(flops), bytes_accessed=int(moved), transcendentals=int(transcendentals)
    )


def tables(length_all, head_size):
    inverse = 500000.0 ** (-jnp.arange(0, head_size, 2, dtype=f32) / head_size)
    angles = jnp.arange(length_all, dtype=f32)[:, None] * inverse[None, :]
    angles = jnp.concatenate([angles, angles], axis=1)
    return (jnp.cos(angles), jnp.sin(angles))


def rmsnorm(values, weight_gain):
    return (
        values * lax.rsqrt(jnp.mean(values * values, axis=-1, keepdims=True) + 1e-05) * weight_gain
    )


def positions(owners, wide_count, capacity):
    onehot = (owners[:, None] == jnp.arange(wide_count, dtype=jnp.int32)[None, :]).astype(jnp.int32)
    before = jnp.cumsum(onehot, axis=0) - onehot
    return (owners * capacity + jnp.sum(before * onehot, axis=1), jnp.sum(onehot, axis=0))


def adamw(weight, gradient, moment_one, moment_two, rate, decay):
    moment_one = 0.5 * moment_one + 0.5 * gradient
    moment_two = 0.5 * moment_two + 0.5 * gradient * gradient
    correct = 1.0 - 0.5**STEP
    update = moment_one / correct / (jnp.sqrt(moment_two / correct) + 1e-08)
    return (weight - rate * (update + decay * weight), moment_one, moment_two)


def turn_kernel(unit_ref, out_ref):
    for k in range(out_ref.shape[0]):
        out_ref[k] = jnp.transpose(unit_ref[k, 0], (1, 0)).astype(bf16)


def turn_units(master):
    capacity, _, unit_rows, unit_cols = master.shape
    step = 2 if capacity % 2 == 0 else 1
    return pl.pallas_call(
        turn_kernel,
        grid=(capacity // step,),
        in_specs=[pl.BlockSpec((step, 1, unit_rows, unit_cols), lambda s: (s, 0, 0, 0))],
        out_specs=pl.BlockSpec((step, unit_cols, unit_rows), lambda s: (s, 0, 0)),
        out_shape=jax.ShapeDtypeStruct((capacity, unit_cols, unit_rows), bf16),
        compiler_params=params(32),
        cost_estimate=cost(0, master.size * 6),
        name="turn_units",
    )(master)


def pick_kernel(place_ref, got_ref, out_ref, sem, *, col_blocks, piece, unit_rows):
    def start(unit, carry):
        half = unit // col_blocks
        block = unit - half * col_blocks
        pltpu.make_async_copy(
            got_ref.at[place_ref[unit]],
            out_ref.at[
                pl.ds(pl.multiple_of(block * piece, piece), piece),
                pl.ds(pl.multiple_of(half * unit_rows, unit_rows), unit_rows),
            ],
            sem,
        ).start()
        return carry

    lax.fori_loop(0, place_ref.shape[0], start, 0)
    pltpu.make_async_copy(out_ref, out_ref, sem).wait()


def pick_units(got, slot_place, row_blocks):
    _, piece, unit_rows = got.shape
    unit_count = slot_place.shape[0]
    col_blocks = unit_count // row_blocks
    if piece % 16 == 0:
        return pl.pallas_call(
            functools.partial(
                pick_kernel, col_blocks=col_blocks, piece=piece, unit_rows=unit_rows
            ),
            in_specs=[
                pl.BlockSpec(memory_space=pltpu.SMEM),
                pl.BlockSpec(memory_space=pl.ANY),
            ],
            out_specs=pl.BlockSpec(memory_space=pltpu.VMEM),
            out_shape=jax.ShapeDtypeStruct((col_blocks * piece, row_blocks * unit_rows), bf16),
            scratch_shapes=[pltpu.SemaphoreType.DMA],
            compiler_params=params(24),
            cost_estimate=cost(0, unit_count * piece * unit_rows * 12),
            name="pick_units",
        )(slot_place, got)
    units = jnp.take(got, slot_place, axis=0).reshape(row_blocks, col_blocks, piece, unit_rows)
    return jnp.transpose(units, (1, 2, 0, 3)).reshape(col_blocks * piece, row_blocks * unit_rows)


def unpick_kernel(block_ref, half_ref, rows_ref, out_ref, sem, *, piece, unit_rows):
    def start(slot, carry):
        pltpu.make_async_copy(
            rows_ref.at[
                pl.ds(pl.multiple_of(block_ref[slot] * piece, piece), piece),
                pl.ds(pl.multiple_of(half_ref[slot] * unit_rows, unit_rows), unit_rows),
            ],
            out_ref.at[slot],
            sem,
        ).start()
        return carry

    lax.fori_loop(0, block_ref.shape[0], start, 0)
    pltpu.make_async_copy(out_ref, out_ref, sem).wait()


def unpick_units(rows, block_of, half_of, piece, unit_rows):
    slots = block_of.shape[0]
    if piece % 16 == 0:
        return pl.pallas_call(
            functools.partial(unpick_kernel, piece=piece, unit_rows=unit_rows),
            in_specs=[
                pl.BlockSpec(memory_space=pltpu.SMEM),
                pl.BlockSpec(memory_space=pltpu.SMEM),
                pl.BlockSpec(memory_space=pltpu.VMEM),
            ],
            out_specs=pl.BlockSpec(memory_space=pl.ANY),
            out_shape=jax.ShapeDtypeStruct((slots, piece, unit_rows), bf16),
            scratch_shapes=[pltpu.SemaphoreType.DMA],
            compiler_params=params(24),
            cost_estimate=cost(0, slots * piece * unit_rows * 8),
            name="unpick_units",
        )(block_of, half_of, rows)
    row_blocks = rows.shape[1] // unit_rows
    units = jnp.transpose(rows.reshape(-1, piece, row_blocks, unit_rows), (0, 2, 1, 3))
    units = units.reshape(-1, piece, unit_rows)
    return jnp.take(units, block_of * row_blocks + half_of, axis=0)


def update_kernel(
    block_ref, half_ref, count_ref, grad_ref, attn_ref, master_ref, one_ref, two_ref,
    grad_out, master_out, copy_out, one_out, two_out, *, attn_blocks,
):
    slot = pl.program_id(0)
    filled = slot < count_ref[0]
    from_attn = block_ref[slot] < attn_blocks
    parts, _, piece, unit_rows = grad_ref.shape
    mine = jnp.where(from_attn, attn_ref[:, 0].astype(f32), grad_ref[:, 0].astype(f32))
    mine = mine.reshape(parts * piece, unit_rows)
    gradient = jnp.where(filled, jnp.transpose(mine, (1, 0)), 0.0)
    weight, one, two = adamw(master_ref[0, 0], gradient, one_ref[0, 0], two_ref[0, 0], 0.02, 0.1)
    grad_out[0, 0] = gradient
    master_out[0, 0] = weight
    copy_out[0, 0] = weight.astype(bf16)
    one_out[0, 0] = one
    two_out[0, 0] = two


def update_units(block_of, half_of, count, grads, attn, master, moment_one, moment_two):
    capacity, _, unit_rows, unit_cols = master.shape
    parts, _, piece, _ = grads.shape
    attn_blocks = attn.shape[1]
    unit = pl.BlockSpec((1, 1, unit_rows, unit_cols), lambda s, *refs: (s, 0, 0, 0))
    whole = jax.ShapeDtypeStruct(master.shape, f32)

    def attn_place(s, block_ref, half_ref, count_ref):
        block = block_ref[s]
        inside = block < attn_blocks
        return (0, jnp.where(inside, block, 0), 0, jnp.where(inside, half_ref[s], 0))

    return pl.pallas_call(
        functools.partial(update_kernel, attn_blocks=attn_blocks),
        grid_spec=pltpu.PrefetchScalarGridSpec(
            num_scalar_prefetch=3,
            grid=(capacity,),
            in_specs=[
                pl.BlockSpec((parts, 1, piece, unit_rows), lambda s, *refs: (0, s, 0, 0)),
                pl.BlockSpec((parts, 1, piece, unit_rows), attn_place),
                unit,
                unit,
                unit,
            ],
            out_specs=[unit] * 5,
        ),
        out_shape=[whole, whole, jax.ShapeDtypeStruct(master.shape, bf16), whole, whole],
        compiler_params=params(40),
        cost_estimate=cost(master.size * 12, master.size * 32),
        name="update_units",
    )(block_of, half_of, count, grads, attn, master, moment_one, moment_two)


def lane_index(shape):
    return lax.broadcasted_iota(jnp.int32, shape, 1)


def rope(tile, cos_tile, sin_tile):
    lower = lane_index(tile.shape) % HD < HD // 2
    ahead = pltpu.roll(tile, LANES - HD // 2, 1)
    behind = pltpu.roll(tile, HD // 2, 1)
    return tile * cos_tile + jnp.where(lower, -ahead, behind) * sin_tile


def unrope(tile, cos_tile, sin_tile):
    lower = lane_index(tile.shape) % HD < HD // 2
    weighted = tile * sin_tile
    ahead = pltpu.roll(weighted, LANES - HD // 2, 1)
    behind = pltpu.roll(weighted, HD // 2, 1)
    return tile * cos_tile + jnp.where(lower, ahead, -behind)


def project_kernel(rows_ref, w_ref, cos_ref, sin_ref, out_ref, *, query_width, kv_width):
    product = dot(rows_ref[...], w_ref[...], 1, 1)
    roped_end = query_width + kv_width
    for start in range(0, out_ref.shape[1], LANES):
        tile = product[:, start : start + LANES]
        if start < roped_end:
            turned = rope(tile, cos_ref[...], sin_ref[...])
            if start + LANES > roped_end:
                tile = jnp.where(lane_index(tile.shape) < roped_end - start, turned, tile)
            else:
                tile = turned
        tile = tile.astype(bf16)
        if start < query_width:
            tile = tile * HD ** (-0.5)
        out_ref[:, start : start + LANES] = tile


def project(rows, w_qkv, cos_all, sin_all, query_width, kv_width, step):
    count = rows.shape[0]
    width = w_qkv.shape[0]
    return pl.pallas_call(
        functools.partial(project_kernel, query_width=query_width, kv_width=kv_width),
        grid=(count // step,),
        in_specs=[
            pl.BlockSpec((step, D), lambda i: (i, 0)),
            pl.BlockSpec((width, D), lambda i: (0, 0)),
            pl.BlockSpec((step, LANES), lambda i: (i, 0)),
            pl.BlockSpec((step, LANES), lambda i: (i, 0)),
        ],
        out_specs=pl.BlockSpec((step, width), lambda i: (i, 0)),
        out_shape=jax.ShapeDtypeStruct((count, width), bf16),
        compiler_params=params(40),
        cost_estimate=cost(2 * count * width * D, 2 * (count + width) * D),
        name="project",
    )(rows, w_qkv, cos_all, sin_all)


def extend(tile_ref, offset, out_ref):
    tile = tile_ref[...].astype(f32)
    other = pltpu.roll(tile, HD, 1)
    low = lane_index(tile.shape) < HD
    at_low = offset == 0
    out_ref[0] = jnp.where(low, jnp.where(at_low, tile, other), 0.0).astype(bf16)
    out_ref[1] = jnp.where(low, 0.0, jnp.where(at_low, other, tile)).astype(bf16)


def forward_kernel(
    length_ref, q_ref, k_ref, v_ref, out_ref, log_ref, kx, vx, *, block, pairs_per, k_start, v_start
):
    pair = pl.program_id(0)
    kv_head = pair // pairs_per
    length = length_ref[0]
    seq_len = q_ref.shape[0]

    @pl.when(pair % pairs_per == 0)
    def _():
        extend(k_ref, (k_start + kv_head * HD) % LANES, kx)
        extend(v_ref, (v_start + kv_head * HD) % LANES, vx)

    row = lax.broadcasted_iota(jnp.int32, (block, block), 0)
    col = lax.broadcasted_iota(jnp.int32, (block, block), 1)
    causal = col <= row
    key_row = lax.broadcasted_iota(jnp.int32, (1, seq_len), 1)
    bias = jnp.where(key_row < length, 0.0, -1e30).astype(f32)
    low = lane_index((block, LANES)) < HD
    for start in range(0, seq_len, block):
        query = q_ref[start : start + block, :]
        total = None
        logs = []
        for half in range(2):
            diagonal = dot(query, kx[half, start : start + block, :], 1, 1)
            diagonal = jnp.where(causal, diagonal + bias[:, start : start + block], -1e30)
            peak = jnp.max(diagonal, axis=1, keepdims=True)
            if start:
                before = dot(query, kx[half, :start, :], 1, 1) + bias[:, :start]
                peak = jnp.maximum(peak, jnp.max(before, axis=1, keepdims=True))
                before = jnp.exp(before - peak)
            diagonal = jnp.exp(diagonal - peak)
            row_sum = jnp.sum(diagonal, axis=1, keepdims=True)
            part = dot(diagonal.astype(bf16), vx[half, start : start + block, :], 1, 0)
            if start:
                row_sum = row_sum + jnp.sum(before, axis=1, keepdims=True)
                part = part + dot(before.astype(bf16), vx[half, :start, :], 1, 0)
            part = part / row_sum
            total = part if total is None else total + part
            logs.append(peak + jnp.log(row_sum))
        out_ref[start : start + block, :] = total.astype(bf16)
        tile = jnp.transpose(jnp.where(low, logs[0], logs[1]), (1, 0))
        log_ref[0, 0:1, start : start + block] = tile[0:1]
        log_ref[0, 1:2, start : start + block] = tile[HD : HD + 1]


def attend_forward(length, qkv, query_width, kv_width, block):
    seq_len = qkv.shape[0]
    pairs = query_width // LANES
    pairs_per = H // KV // 2
    k_start = query_width
    v_start = query_width + kv_width
    column = functools.partial(pl.BlockSpec, (seq_len, LANES))
    return pl.pallas_call(
        functools.partial(
            forward_kernel, block=block, pairs_per=pairs_per, k_start=k_start, v_start=v_start
        ),
        grid=(pairs,),
        in_specs=[
            pl.BlockSpec(memory_space=pltpu.SMEM),
            column(lambda p: (0, p)),
            column(lambda p: (0, (k_start + p // pairs_per * HD) // LANES)),
            column(lambda p: (0, (v_start + p // pairs_per * HD) // LANES)),
        ],
        out_specs=[
            column(lambda p: (0, p)),
            pl.BlockSpec((1, 8, seq_len), lambda p: (p, 0, 0)),
        ],
        out_shape=[
            jax.ShapeDtypeStruct((seq_len, query_width), bf16),
            jax.ShapeDtypeStruct((pairs, 8, seq_len), f32),
        ],
        scratch_shapes=[
            pltpu.VMEM((2, seq_len, LANES), bf16),
            pltpu.VMEM((2, seq_len, LANES), bf16),
        ],
        compiler_params=params(56),
        cost_estimate=cost(pairs * seq_len * seq_len * 1024, seq_len * 768 * 4),
        name="attend_forward",
    )(length, qkv, qkv, qkv)


def backward_kernel(
    length_ref, q_ref, k_ref, v_ref, back_ref, out_ref, log_ref, cos_ref, sin_ref, grad_ref,
    kx, vx, dk, dv, *, block, pairs_per, k_start, v_start,
):
    pair = pl.program_id(0)
    kv_head = pair // pairs_per
    length = length_ref[0]
    seq_len = q_ref.shape[0]
    k_offset = (k_start + kv_head * HD) % LANES
    v_offset = (v_start + kv_head * HD) % LANES

    @pl.when(pair == 0)
    def _():
        grad_ref[:, k_start // LANES * LANES :] = jnp.zeros(
            (seq_len, grad_ref.shape[1] - k_start // LANES * LANES), bf16
        )

    @pl.when(pair % pairs_per == 0)
    def _():
        extend(k_ref, k_offset, kx)
        extend(v_ref, v_offset, vx)
        dk[...] = jnp.zeros(dk.shape, f32)
        dv[...] = jnp.zeros(dv.shape, f32)

    key = lax.broadcasted_iota(jnp.int32, (block, block), 0)
    row = lax.broadcasted_iota(jnp.int32, (block, block), 1)
    causal = key <= row
    for start in range(0, seq_len, block):
        here = slice(start, start + block)
        query = q_ref[here, :]
        back = back_ref[here, :]
        turned = jnp.transpose(back.astype(f32) * out_ref[here, :].astype(f32), (1, 0))
        query_grad = None
        for half in range(2):
            log_row = log_ref[0, half : half + 1, here]
            shift = jnp.sum(turned[half * HD : half * HD + HD], axis=0, keepdims=True)
            for first in range(0, start + block, block):
                keys = slice(first, first + block)
                scores = dot(kx[half, keys, :], query, 1, 1)
                probs = jnp.exp(scores - log_row)
                if first + block > seq_len // 2:
                    probs = jnp.where(key + first < length, probs, 0.0)
                if first == start:
                    probs = jnp.where(causal, probs, 0.0)
                probs_back = dot(vx[half, keys, :], back, 1, 1)
                scores_back = (probs * (probs_back - shift)).astype(bf16)
                dv[half, keys, :] += dot(probs.astype(bf16), back, 1, 0)
                dk[half, keys, :] += dot(scores_back, query, 1, 0)
                part = dot(scores_back, kx[half, keys, :], 0, 0)
                query_grad = part if query_grad is None else query_grad + part
        query_grad = unrope(query_grad * HD ** (-0.5), cos_ref[here, :], sin_ref[here, :])
        grad_ref[here, pl.ds(pl.multiple_of(pair * LANES, LANES), LANES)] = query_grad.astype(bf16)

    @pl.when(pair % pairs_per == pairs_per - 1)
    def _():
        low = lane_index((seq_len, LANES)) < HD

        def place(sums, offset, start, roped):
            joined = jnp.where(low, sums[0], 0.0) + pltpu.roll(
                jnp.where(low, 0.0, sums[1]), HD, 1
            )
            if roped:
                joined = unrope(joined, cos_ref[...], sin_ref[...])
            joined = jnp.where(offset == 0, joined, pltpu.roll(joined, HD, 1))
            tile = pl.ds(
                pl.multiple_of((start + kv_head * HD) // LANES * LANES, LANES), LANES
            )
            grad_ref[:, tile] = (grad_ref[:, tile].astype(f32) + joined).astype(bf16)

        place(dk[...], k_offset, k_start, True)
        place(dv[...], v_offset, v_start, False)


def attend_backward(length, qkv, back, out, logs, cos_all, sin_all, query_width, kv_width, block):
    seq_len, width = qkv.shape
    pairs = query_width // LANES
    pairs_per = H // KV // 2
    k_start = query_width
    v_start = query_width + kv_width
    column = functools.partial(pl.BlockSpec, (seq_len, LANES))
    return pl.pallas_call(
        functools.partial(
            backward_kernel, block=block, pairs_per=pairs_per, k_start=k_start, v_start=v_start
        ),
        grid=(pairs,),
        in_specs=[
            pl.BlockSpec(memory_space=pltpu.SMEM),
            column(lambda p: (0, p)),
            column(lambda p: (0, (k_start + p // pairs_per * HD) // LANES)),
            column(lambda p: (0, (v_start + p // pairs_per * HD) // LANES)),
            column(lambda p: (0, p)),
            column(lambda p: (0, p)),
            pl.BlockSpec((1, 8, seq_len), lambda p: (p, 0, 0)),
            column(lambda p: (0, 0)),
            column(lambda p: (0, 0)),
        ],
        out_specs=pl.BlockSpec((seq_len, width), lambda p: (0, 0)),
        out_shape=jax.ShapeDtypeStruct((seq_len, width), bf16),
        scratch_shapes=[
            pltpu.VMEM((2, seq_len, LANES), bf16),
            pltpu.VMEM((2, seq_len, LANES), bf16),
            pltpu.VMEM((2, seq_len, LANES), f32),
            pltpu.VMEM((2, seq_len, LANES), f32),
        ],
        compiler_params=params(56),
        cost_estimate=cost(pairs * seq_len * seq_len * 2560, seq_len * 768 * 6),
        name="attend_backward",
    )(length, qkv, qkv, qkv, back, out, logs, cos_all, sin_all)


def branch_kernel(attended_ref, w_ref, tokens_ref, gain_ref, residual_ref, normed_ref):
    total = tokens_ref[...].astype(f32)
    groups, _, width = attended_ref.shape
    for n in range(groups):
        total = total + dot(attended_ref[n], w_ref[n * width : (n + 1) * width, :], 1, 0)
    residual_ref[...] = total
    normed_ref[...] = rmsnorm(total, gain_ref[...]).astype(bf16)


def branch(attended, w_out, tokens, gain):
    groups, count, width = attended.shape
    step = 128 if count % 128 == 0 else 64
    return pl.pallas_call(
        branch_kernel,
        grid=(count // step,),
        in_specs=[
            pl.BlockSpec((groups, step, width), lambda i: (0, i, 0)),
            pl.BlockSpec((D, D), lambda i: (0, 0)),
            pl.BlockSpec((step, D), lambda i: (i, 0)),
            pl.BlockSpec((1, D), lambda i: (0, 0)),
        ],
        out_specs=[pl.BlockSpec((step, D), lambda i: (i, 0))] * 2,
        out_shape=[
            jax.ShapeDtypeStruct((count, D), f32),
            jax.ShapeDtypeStruct((count, D), bf16),
        ],
        compiler_params=params(56),
        cost_estimate=cost(2 * count * D * D, 2 * D * D + 8 * count * D),
        name="branch",
    )(attended, w_out, tokens, gain)


def spread_kernel(back_ref, w_ref, out_ref):
    out_ref[0] = dot(back_ref[...], w_ref[...], 1, 1).astype(bf16)


def spread(back, w_out, groups):
    count = back.shape[0]
    width = D // groups
    return pl.pallas_call(
        spread_kernel,
        grid=(groups,),
        in_specs=[
            pl.BlockSpec((count, D), lambda i: (0, 0)),
            pl.BlockSpec((width, D), lambda i: (i, 0)),
        ],
        out_specs=pl.BlockSpec((1, count, width), lambda i: (i, 0, 0)),
        out_shape=jax.ShapeDtypeStruct((groups, count, width), bf16),
        compiler_params=params(40),
        cost_estimate=cost(2 * count * D * D, 2 * D * D + 4 * count * D),
        name="spread",
    )(back, w_out)


def hidden_kernel(place_ref, rows_ref, back_ref, wg_ref, wu_ref, wd_ref, *refs):
    hid_ref, dgate_ref, dup_ref, keep_ref = refs[-4:]

    @pl.when(pl.program_id(0) == 0)
    def _():
        keep_ref[...] = rows_ref[...]

    gate = dot(rows_ref[...], wg_ref[...], 1, 1)
    up = dot(rows_ref[...], wu_ref[...], 1, 1)
    hidden_back = dot(back_ref[...], wd_ref[...], 1, 1)
    sig = 1.0 / (1.0 + jnp.exp(-gate))
    silu = gate * sig
    hid_ref[...] = (silu * up).astype(bf16)
    dgate_ref[...] = (hidden_back * up * (sig * (1.0 + gate * (1.0 - sig)))).astype(bf16)
    dup_ref[...] = (hidden_back * silu).astype(bf16)


def hidden_pass(place, rows, back, wg, wu, wd, kept):
    count = rows.shape[0]
    seq_len = back.shape[0]
    ff_width = wg.shape[0]
    step = 256
    weight = pl.BlockSpec((step, D), lambda i, p: (i, 0))
    wide_rows = jax.ShapeDtypeStruct((seq_len, ff_width), bf16)
    given = pl.BlockSpec((count, step), lambda i, p: (p[0], i))
    return pl.pallas_call(
        hidden_kernel,
        grid_spec=pltpu.PrefetchScalarGridSpec(
            num_scalar_prefetch=1,
            grid=(ff_width // step,),
            in_specs=[
                pl.BlockSpec((count, D), lambda i, p: (0, 0)),
                pl.BlockSpec((count, D), lambda i, p: (p[0], 0)),
                weight,
                weight,
                weight,
            ]
            + [pl.BlockSpec(memory_space=pl.ANY)] * len(kept),
            out_specs=[given] * 3 + [pl.BlockSpec((count, D), lambda i, p: (p[0], 0))],
        ),
        out_shape=[wide_rows] * 3 + [jax.ShapeDtypeStruct((seq_len, D), bf16)],
        input_output_aliases={6 + k: k for k in range(len(kept))},
        compiler_params=params(48),
        cost_estimate=cost(6 * count * ff_width * D, 6 * ff_width * D, count * ff_width),
        name="hidden_pass",
    )(place, rows, back, wg, wu, wd, *kept)


def norm_back_kernel(place_ref, dgate_ref, dup_ref, wg_ref, wu_ref, *refs):
    out_ref = refs[-1]
    total = dot(dgate_ref[...], wg_ref[...], 1, 0) + dot(dup_ref[...], wu_ref[...], 1, 0)
    if len(refs) > 1:
        total = total + refs[0][...].astype(f32)
    out_ref[...] = total.astype(out_ref.dtype)


def norm_back(place, dgate, dup, wg, wu, count, before, kind):
    ff_width = wg.shape[0]
    step = 512
    taken = pl.BlockSpec((count, ff_width), lambda i, p: (p[0], 0))
    weight = pl.BlockSpec((ff_width, step), lambda i, p: (0, i))
    given = pl.BlockSpec((count, step), lambda i, p: (0, i))
    extra = [] if before is None else [before]
    return pl.pallas_call(
        norm_back_kernel,
        grid_spec=pltpu.PrefetchScalarGridSpec(
            num_scalar_prefetch=1,
            grid=(D // step,),
            in_specs=[taken, taken, weight, weight] + [given] * len(extra),
            out_specs=given,
        ),
        out_shape=jax.ShapeDtypeStruct((count, D), kind),
        compiler_params=params(48),
        cost_estimate=cost(4 * count * ff_width * D, 4 * ff_width * D),
        name="norm_back",
    )(place, dgate, dup, wg, wu, *extra)


def outer_kernel(first_ref, second_ref, out_ref):
    first = first_ref[...]
    if len(first.shape) == 3:
        first = first[0]
    out_ref[...] = dot(first, second_ref[...], 0, 0).astype(bf16)


def outer(first, second):
    rows, width = second.shape
    if len(first.shape) == 3:
        groups, _, step = first.shape
        height = groups * step
        taken = pl.BlockSpec((1, rows, step), lambda i: (i, 0, 0))
    else:
        height = first.shape[1]
        step = next(k for k in (512, 384, 256, 192, LANES) if height % k == 0)
        taken = pl.BlockSpec((rows, step), lambda i: (0, i))
    return pl.pallas_call(
        outer_kernel,
        grid=(height // step,),
        in_specs=[taken, pl.BlockSpec((rows, width), lambda i: (0, 0))],
        out_specs=pl.BlockSpec((step, width), lambda i: (i, 0)),
        out_shape=jax.ShapeDtypeStruct((height, width), bf16),
        compiler_params=params(56),
        cost_estimate=cost(
            2 * rows * height * width, 2 * (rows * (height + width) + height * width)
        ),
        name="outer",
    )(first, second)


def cycle(count, step=1):
    return [(i, (i + step) % count) for i in range(count)]


def ring_gather(own, count):
    blocks = [own]
    for _ in range(count - 1):
        blocks.append(lax.ppermute(blocks[-1], "narrow", cycle(count)))
    return blocks


def butterfly(value):
    for axis in ("wide", "narrow"):
        count = lax.axis_size(axis)
        step = 1
        while step < count:
            value = value + lax.ppermute(value, axis, [(i, i ^ step) for i in range(count)])
            step *= 2
    return value


ORDER = (0, 1, 3, 2)


def square_pairs(step):
    pairs = []
    for place, chip in enumerate(ORDER):
        target = ORDER[(place + step) % 4]
        pairs += [(chip * 2 + core, target * 2 + core) for core in range(2)]
    return pairs


def swap_pairs():
    return [(i, i ^ 1) for i in range(8)]


def plane_ring(first, second):
    firsts, seconds = [first], [second]
    for _ in range(3):
        firsts.append(lax.ppermute(firsts[-1], "wide", square_pairs(1)))
        seconds.append(lax.ppermute(seconds[-1], "wide", square_pairs(-1)))
    firsts += [lax.ppermute(part, "wide", swap_pairs()) for part in firsts]
    seconds += [lax.ppermute(part, "wide", swap_pairs()) for part in seconds]
    return firsts, seconds


def plane_ring_back(firsts, seconds):
    ends = []
    for parts, step in ((firsts, 1), (seconds, -1)):
        total = parts[1]
        for s in (2, 3, 0):
            total = (
                parts[s].astype(f32)
                + lax.ppermute(total, "wide", square_pairs(step)).astype(f32)
            ).astype(bf16)
        ends.append(total)
    return ends


def ring_orders():
    wide_index = lax.axis_index("wide")
    order = jnp.array(ORDER, jnp.int32)
    core = wide_index % 2
    place = order[wide_index // 2]
    entry = jnp.arange(8, dtype=jnp.int32)
    device = entry
    entry_core = (core + entry // 4) % 2
    apart = order[device // 2] - place
    away = 4 * ((device % 2 + core) % 2)
    return (
        order[(place - entry) % 4] * 2 + entry_core,
        order[(place + entry) % 4] * 2 + entry_core,
        (-apart) % 4 + away,
        apart % 4 + away,
    )


def plane_all(part):
    count = lax.axis_size("wide")
    if count != 8:
        return lax.all_gather(part, "wide", axis=0)
    half = part.shape[0] // 2
    firsts, seconds = plane_ring(part[:half], part[half:])
    _, _, at_first, at_second = ring_orders()
    return jnp.concatenate(
        [
            jnp.take(jnp.stack(firsts), at_first, axis=0),
            jnp.take(jnp.stack(seconds), at_second, axis=0),
        ],
        axis=1,
    )


def plane_sum(grad):
    count = lax.axis_size("wide")
    if count != 8:
        return lax.psum_scatter(grad, "wide", scatter_dimension=0, tiled=False)
    half = grad.shape[1] // 2
    from_first, from_second, _, _ = ring_orders()
    firsts = jnp.take(grad[:, :half], from_first, axis=0)
    seconds = jnp.take(grad[:, half:], from_second, axis=0)
    joined = jnp.stack([firsts, seconds])
    own = (
        joined[:, :4].astype(f32)
        + lax.ppermute(joined[:, 4:], "wide", swap_pairs()).astype(f32)
    ).astype(bf16)
    return jnp.concatenate(
        plane_ring_back([own[0, s] for s in range(4)], [own[1, s] for s in range(4)]), axis=0
    )


def ff_gather(parts):
    if lax.axis_size("wide") != 8:
        return [lax.all_gather(part, "wide", axis=0, tiled=True) for part in parts]
    half = parts[0].shape[0] // 2
    firsts, seconds = plane_ring(
        jnp.concatenate([part[:half] for part in parts], axis=0),
        jnp.concatenate([part[half:] for part in parts], axis=0),
    )
    blocks = [block for pair in zip(firsts, seconds) for block in pair]
    return [
        jnp.concatenate([block[k * half : (k + 1) * half] for block in blocks], axis=0)
        for k in range(3)
    ]


def ff_sum(grad):
    if lax.axis_size("wide") != 8:
        return [lax.psum_scatter(grad, "wide", scatter_dimension=0, tiled=True)]
    middle = grad.shape[0] // 2
    own = (
        grad[:middle].astype(f32)
        + lax.ppermute(grad[middle:], "wide", swap_pairs()).astype(f32)
    ).astype(bf16)
    size = middle // 8
    blocks = [own[k * size : (k + 1) * size] for k in range(8)]
    return plane_ring_back(blocks[0::2], blocks[1::2])


def local(
    tokens, cotangent, lengths, owners, master, moment_one, moment_two, norm_gains, gain_first,
    gain_second,
):
    wide_count = lax.axis_size("wide")
    narrow_count = lax.axis_size("narrow")
    capacity, _, unit_rows, unit_cols = master.shape
    unit_count = owners.shape[0]
    row_count = tokens.shape[0]
    seq_len = row_count * narrow_count
    row_blocks = D // unit_rows
    col_blocks = unit_count // row_blocks
    piece = unit_cols // wide_count
    query_width = H // narrow_count * HD
    kv_width = KV // narrow_count * HD
    ff_width = FF // narrow_count
    qkv_width = query_width + 2 * kv_width
    wide_index = lax.axis_index("wide")
    narrow_index = lax.axis_index("narrow")
    length = lax.dynamic_slice(lengths, (wide_index,), (1,))
    block = min(256, seq_len)
    qkv_blocks = qkv_width // unit_cols
    out_blocks = query_width // unit_cols
    attn_blocks = qkv_blocks + out_blocks

    inputs = tokens.astype(f32)
    normed = rmsnorm(inputs, norm_gains[0]).astype(bf16)
    normed_all = lax.all_gather(normed, "narrow", axis=0, tiled=True)

    slot_place, counts = positions(owners, wide_count, capacity)
    turned = turn_units(master).reshape(capacity, wide_count, piece, unit_rows)
    got = lax.all_to_all(turned, "wide", split_axis=1, concat_axis=0)
    got = got.reshape(wide_count * capacity, piece, unit_rows)
    rows = pick_units(got, slot_place, row_blocks)
    qkv_end = qkv_blocks * piece
    out_end = attn_blocks * piece
    ff_rows = ff_width // wide_count

    w_qkv = plane_all(rows[:qkv_end]).reshape(wide_count, qkv_blocks, piece, D)
    w_qkv = jnp.transpose(w_qkv, (1, 0, 2, 3)).reshape(qkv_width, D)
    out_part = jnp.stack(ring_gather(rows[qkv_end:out_end], narrow_count))
    by_place = (narrow_index - jnp.arange(narrow_count, dtype=jnp.int32)) % narrow_count
    out_part = jnp.take(out_part, by_place, axis=0)
    w_out = plane_all(out_part.reshape(narrow_count * out_blocks * piece, D))
    w_out = w_out.reshape(wide_count, narrow_count * out_blocks, piece, D)
    w_out = jnp.transpose(w_out, (1, 0, 2, 3)).reshape(D, D)
    ff_parts = [rows[out_end + k * ff_rows : out_end + (k + 1) * ff_rows] for k in range(3)]
    w_gate, w_upper, w_down = ff_gather(ff_parts)

    cos_table, sin_table = tables(seq_len, HD)
    cos_all = jnp.concatenate([cos_table] * (LANES // HD), axis=1)
    sin_all = jnp.concatenate([sin_table] * (LANES // HD), axis=1)
    cotangent_later, normed_all = lax.optimization_barrier((cotangent, normed_all))
    back_all = lax.all_gather(cotangent_later, "narrow", axis=0, tiled=True)
    qkv = project(normed_all, w_qkv, cos_all, sin_all, query_width, kv_width, row_count)
    attended, logs = attend_forward(length, qkv, query_width, kv_width, block)
    attended_rows = lax.all_to_all(
        attended.reshape(narrow_count, row_count, query_width), "narrow", 0, 0
    )
    residual, normed_two = branch(attended_rows, w_out, tokens, norm_gains[1:2])

    mlp_blocks = ring_gather(normed_two, narrow_count)
    places = [((narrow_index - s) % narrow_count).reshape(1) for s in range(narrow_count)]
    kept = ()
    for s in range(narrow_count):
        kept = hidden_pass(places[s], mlp_blocks[s], back_all, w_gate, w_upper, w_down, kept)
    hidden, dgate, dup, mlp_all = kept
    total = None
    for s in range(1, narrow_count + 1):
        last = s == narrow_count
        total = norm_back(
            places[s % narrow_count], dgate, dup, w_gate, w_upper, row_count, total,
            f32 if last else bf16,
        )
        if not last:
            total = lax.ppermute(total, "narrow", cycle(narrow_count))
    norm_two_back = total

    _, norm_two_pull = jax.vjp(rmsnorm, residual, norm_gains[1])
    resid_part, gain_two = norm_two_pull(norm_two_back)
    resid_back = cotangent.astype(f32) + resid_part
    attn_back = resid_back.astype(bf16)
    out_back = lax.all_to_all(spread(attn_back, w_out, narrow_count), "narrow", 0, 0)
    out_back = out_back.reshape(seq_len, query_width)

    ff_term = dot(hidden, w_down, 1, 0).astype(bf16)
    output = residual + lax.psum_scatter(
        ff_term, "narrow", scatter_dimension=0, tiled=True
    ).astype(f32)
    ff_grads = [outer(hidden, back_all), outer(dgate, mlp_all), outer(dup, mlp_all)]
    ff_sums = [ff_sum(grad) for grad in ff_grads]
    ff_sums = ff_sums[1] + ff_sums[2] + ff_sums[0]

    slots = wide_count * capacity
    unit_of = jnp.zeros((slots,), jnp.int32).at[slot_place].set(
        jnp.arange(unit_count, dtype=jnp.int32)
    )
    half_of = unit_of // col_blocks
    block_of = unit_of - half_of * col_blocks
    sent = unpick_units(
        jnp.concatenate(ff_sums, axis=0),
        jnp.maximum(block_of - attn_blocks, 0),
        half_of,
        piece,
        unit_rows,
    )
    sent = sent.reshape(wide_count, capacity, piece, unit_rows)
    owned = lax.all_to_all(sent, "wide", split_axis=0, concat_axis=0)

    grad_out = outer(attended_rows, attn_back)
    grad_out = grad_out.reshape(narrow_count * out_blocks, wide_count, piece, D)
    grad_out = jnp.transpose(grad_out, (1, 0, 2, 3))
    grad_out = plane_sum(grad_out.reshape(wide_count, narrow_count * out_blocks * piece, D))
    grad_out = lax.psum_scatter(grad_out, "narrow", scatter_dimension=0, tiled=True)
    qkv_back = attend_backward(
        length, qkv, out_back, attended, logs, cos_all, sin_all, query_width, kv_width, block
    )
    grad_qkv = outer(qkv_back, normed_all)
    gain_one = jnp.sum(w_qkv.astype(f32) * grad_qkv.astype(f32), axis=0) / norm_gains[0]
    gain_grads = butterfly(jnp.stack([gain_one, gain_two]))
    grad_qkv = jnp.transpose(grad_qkv.reshape(qkv_blocks, wide_count, piece, D), (1, 0, 2, 3))
    grad_qkv = plane_sum(grad_qkv.reshape(wide_count, qkv_blocks * piece, D))
    attn_grads = plane_all(jnp.concatenate([grad_qkv, grad_out], axis=0))
    attn_grads = attn_grads.reshape(wide_count, attn_blocks, piece, D)

    first_slot = wide_index * capacity
    owned_grads, new_master, new_copy, new_first, new_second = update_units(
        lax.dynamic_slice(block_of, (first_slot,), (capacity,)),
        lax.dynamic_slice(half_of, (first_slot,), (capacity,)),
        lax.dynamic_slice(counts, (wide_index,), (1,)),
        owned,
        attn_grads,
        master,
        moment_one,
        moment_two,
    )

    norm_one_back = lax.psum_scatter(
        dot(qkv_back, w_qkv, 1, 0).astype(bf16), "narrow", scatter_dimension=0, tiled=True
    ).astype(f32)
    _, norm_one_pull = jax.vjp(lambda values: rmsnorm(values, norm_gains[0]), inputs)
    (input_part,) = norm_one_pull(norm_one_back)
    input_grad = (resid_back + input_part).astype(bf16)
    new_gains, _, gain_second_new = adamw(
        norm_gains, gain_grads, gain_first, gain_second, 0.5, 0.0
    )
    return (
        output.astype(bf16),
        input_grad,
        owned_grads,
        new_master,
        new_copy,
        new_first,
        new_second,
        gain_grads,
        gain_second_new,
        new_gains,
    )


def solution(mesh):
    rows = P(("wide", "narrow"), None)
    units = P("wide", "narrow", None, None)
    return jax.shard_map(
        local,
        mesh=mesh,
        in_specs=(rows, rows, P(), P(), units, units, units, P(), P(), P()),
        out_specs=(rows, rows, units, units, units, units, units, P(), P(), P()),
        check_vma=False,
    )
```

```python
import functools

import jax
import jax.numpy as jnp
from jax import lax
from jax.experimental import pallas as pl
from jax.experimental.pallas import tpu as pltpu
from jax.sharding import PartitionSpec as P

D = 2048
H = 32
KV = 8
HD = 64
FF = 8192
STEP = 5
LANES = 128
MIB = 1 << 20
ANY = pl.BlockSpec(memory_space=pl.ANY)
VMEM = pl.BlockSpec(memory_space=pltpu.VMEM)
SMEM = pl.BlockSpec(memory_space=pltpu.SMEM)

f32 = jnp.float32
bf16 = jnp.bfloat16


def dot(first_op, second_op, first_dim, second_dim):
    return lax.dot_general(
        first_op,
        second_op,
        (((first_dim,), (second_dim,)), ((), ())),
        preferred_element_type=f32,
    )


def shaped(shape, kind=bf16):
    return jax.ShapeDtypeStruct(shape, kind)


def blocks(shape, place):
    return pl.BlockSpec(shape, place)


class Send:
    def __init__(self, source, land, axis, step, source_at=None, land_at=None, landed=False, needs=()):
        self.source, self.land, self.axis, self.step = source, land, axis, step
        self.source_at, self.land_at = source_at, land_at
        self.landed, self.needs = landed, needs


COLLECTIVE = [0]


def run_sends(sends, sources, lands, send_sem, recv_sem):
    count = lax.axis_size("narrow")
    wide, narrow = lax.axis_index("wide"), lax.axis_index("narrow")

    def target(axis, step):
        if axis == "wide":
            return {"wide": jnp.bitwise_xor(wide, step)}
        return {"narrow": lax.rem(narrow + step, count)}

    copies = []
    for k, send in enumerate(sends):
        ref = (lands if send.landed else sources)[send.source]
        if send.source_at is not None:
            ref = ref.at[send.source_at(wide, narrow)]
        land = lands[send.land]
        if send.land_at is not None:
            land = land.at[send.land_at(wide, narrow)]
        copies.append(
            pltpu.make_async_remote_copy(
                src_ref=ref,
                dst_ref=land,
                send_sem=send_sem.at[k],
                recv_sem=recv_sem.at[k],
                device_id=target(send.axis, send.step),
                device_id_type=pl.DeviceIdType.MESH,
            )
        )

    def start():
        partners = set()
        for send in sends:
            if send.axis == "wide":
                partners.add(("wide", send.step))
            else:
                partners.add(("narrow", send.step % count))
                partners.add(("narrow", -send.step % count))
        barrier = pltpu.get_barrier_semaphore()
        for axis, step in sorted(partners):
            pl.semaphore_signal(
                barrier, inc=1, device_id=target(axis, step), device_id_type=pl.DeviceIdType.MESH
            )
        pl.semaphore_wait(barrier, len(partners))
        for send, copy in zip(sends, copies):
            if not send.needs:
                copy.start()

    def finish():
        arrived = set()
        for send, copy in zip(sends, copies):
            for k in send.needs:
                if k not in arrived:
                    copies[k].wait_recv()
                    arrived.add(k)
            if send.needs:
                copy.start()
        for k, copy in enumerate(copies):
            copy.wait_send()
            if k not in arrived:
                copy.wait_recv()

    return start, finish


def call(
    body, ins, in_specs, out_shape, out_specs, *, name, grid=(), prefetch=(), scratch=(), deps=(),
    aliases=None, mib=56, flops=0, moved=0, sends=(), sources=(), lands=(), closing=None,
):
    first = len(prefetch) + len(ins)
    single = not isinstance(out_shape, (list, tuple))
    out_shapes = [out_shape] if single else list(out_shape)
    specs = [out_specs] if single else list(out_specs)
    out_count = len(out_shapes)
    land_count = len(lands)

    def wrapped(*refs):
        given = refs[:first]
        refs = refs[first:]
        source_refs = refs[: len(sources)]
        refs = refs[len(sources) + len(deps) :]
        outs, refs = refs[:out_count], refs[out_count:]
        land_refs, refs = refs[:land_count], refs[land_count:]
        if not sends:
            body(*given, *outs, *refs)
            return
        own, (send_sem, recv_sem) = refs[:-2], refs[-2:]
        start, finish = run_sends(sends, source_refs, land_refs, send_sem, recv_sem)

        def last():
            finish()
            if closing is not None:
                closing(land_refs, (*given, *outs, *own))

        if grid:
            steps = [pl.program_id(k) for k in range(len(grid))]
            begins = functools.reduce(jnp.logical_and, [step == 0 for step in steps])
            ends = functools.reduce(
                jnp.logical_and, [step == size - 1 for step, size in zip(steps, grid)]
            )
            pl.when(begins)(start)
            body(*given, *outs, *own)
            pl.when(ends)(last)
        else:
            start()
            body(*given, *outs, *own)
            last()

    extra = {}
    if sends:
        COLLECTIVE[0] += 1
        extra = {"collective_id": COLLECTIVE[0], "has_side_effects": True}
        scratch = [*scratch] + [pltpu.SemaphoreType.DMA((len(sends),))] * 2
    results = pl.pallas_call(
        wrapped,
        grid_spec=pltpu.PrefetchScalarGridSpec(
            num_scalar_prefetch=len(prefetch),
            grid=grid,
            in_specs=list(in_specs) + [ANY] * (len(sources) + len(deps)),
            out_specs=specs + [ANY] * land_count,
            scratch_shapes=list(scratch),
        ),
        out_shape=out_shapes + [shaped(*land) if isinstance(land[0], tuple) else shaped(land) for land in lands],
        input_output_aliases=aliases or {},
        compiler_params=pltpu.CompilerParams(vmem_limit_bytes=mib * MIB, **extra),
        cost_estimate=pl.CostEstimate(
            flops=int(flops), bytes_accessed=int(moved), transcendentals=0
        ),
        name=name,
    )(*prefetch, *ins, *sources, *deps)
    return results[0] if single and not sends else list(results)


def tables(length_all, head_size):
    inverse = 500000.0 ** (-jnp.arange(0, head_size, 2, dtype=f32) / head_size)
    angles = jnp.arange(length_all, dtype=f32)[:, None] * inverse[None, :]
    angles = jnp.concatenate([angles, angles], axis=1)
    return (jnp.cos(angles), jnp.sin(angles))


def rmsnorm(values, weight_gain):
    return (
        values * lax.rsqrt(jnp.mean(values * values, axis=-1, keepdims=True) + 1e-05) * weight_gain
    )


def positions(owners, wide_count, capacity):
    onehot = (owners[:, None] == jnp.arange(wide_count, dtype=jnp.int32)[None, :]).astype(jnp.int32)
    before = jnp.cumsum(onehot, axis=0) - onehot
    return (owners * capacity + jnp.sum(before * onehot, axis=1), jnp.sum(onehot, axis=0))


def adamw(weight, gradient, moment_one, moment_two, rate, decay):
    moment_one = 0.5 * moment_one + 0.5 * gradient
    moment_two = 0.5 * moment_two + 0.5 * gradient * gradient
    correct = 1.0 - 0.5**STEP
    update = moment_one / correct / (jnp.sqrt(moment_two / correct) + 1e-08)
    return (weight - rate * (update + decay * weight), moment_one, moment_two)


def turn_kernel(unit_ref, out_ref):
    parts, step, piece, unit_rows = out_ref.shape
    for k in range(step):
        out_ref[:, k] = (
            jnp.transpose(unit_ref[k, 0], (1, 0)).reshape(parts, piece, unit_rows).astype(bf16)
        )


def turn_units(master, parts, deps):
    capacity, _, unit_rows, unit_cols = master.shape
    piece = unit_cols // parts
    step = 2 if capacity % 2 == 0 else 1
    return call(
        turn_kernel,
        [master],
        [blocks((step, 1, unit_rows, unit_cols), lambda s: (s, 0, 0, 0))],
        shaped((parts, capacity, piece, unit_rows)),
        blocks((parts, step, piece, unit_rows), lambda s: (0, s, 0, 0)),
        grid=(capacity // step,),
        deps=deps,
        mib=20,
        moved=master.size * 6,
        name="turn_units",
    )


def pick_kernel(turn_ref, place_ref, own_ref, got_ref, out_ref, sem, *, col_blocks):
    _, capacity, piece, unit_rows = got_ref.shape

    def start(unit, carry):
        half = unit // col_blocks
        block = unit - half * col_blocks
        owner = place_ref[unit] // capacity
        slot = place_ref[unit] - owner * capacity
        target = out_ref.at[
            pl.ds(pl.multiple_of(block * piece, piece), piece),
            pl.ds(pl.multiple_of(half * unit_rows, unit_rows), unit_rows),
        ]

        @pl.when(owner == turn_ref[0])
        def _():
            pltpu.make_async_copy(own_ref.at[owner, slot], target, sem).start()

        @pl.when(owner != turn_ref[0])
        def _():
            pltpu.make_async_copy(got_ref.at[owner, slot], target, sem).start()

        return carry

    lax.fori_loop(0, place_ref.shape[0], start, 0)
    pltpu.make_async_copy(out_ref, out_ref, sem).wait()


def pick_units(turn, slot_place, own, got, row_blocks):
    _, _, piece, unit_rows = got.shape
    unit_count = slot_place.shape[0]
    col_blocks = unit_count // row_blocks
    return call(
        functools.partial(pick_kernel, col_blocks=col_blocks),
        [turn, slot_place, own, got],
        [SMEM, SMEM, ANY, ANY],
        shaped((col_blocks * piece, row_blocks * unit_rows)),
        VMEM,
        scratch=[pltpu.SemaphoreType.DMA],
        moved=unit_count * piece * unit_rows * 12,
        name="pick_units",
    )


def unpick_kernel(block_ref, half_ref, rows_ref, low_ref, high_ref, sems, *, piece, unit_rows):
    owners, part, _, _ = low_ref.shape

    def start(owner, carry):
        for slot in range(2 * part):
            out_ref = high_ref if slot >= part else low_ref
            place = owner * 2 * part + slot
            pltpu.make_async_copy(
                rows_ref.at[
                    pl.ds(pl.multiple_of(block_ref[place] * piece, piece), piece),
                    pl.ds(pl.multiple_of(half_ref[place] * unit_rows, unit_rows), unit_rows),
                ],
                out_ref.at[owner, slot % part],
                sems.at[slot // part],
            ).start()
        return carry

    lax.fori_loop(0, owners, start, 0)
    pltpu.make_async_copy(low_ref, low_ref, sems.at[0]).wait()
    pltpu.make_async_copy(high_ref, high_ref, sems.at[1]).wait()


def unpick_units(rows, block_of, half_of, owners, piece, unit_rows):
    slots = block_of.shape[0]
    shape = shaped((owners, slots // owners // 2, piece, unit_rows))
    return call(
        functools.partial(unpick_kernel, piece=piece, unit_rows=unit_rows),
        [block_of, half_of, rows],
        [SMEM, SMEM, VMEM],
        [shape, shape],
        [ANY, ANY],
        scratch=[pltpu.SemaphoreType.DMA((2,))],
        moved=slots * piece * unit_rows * 8,
        name="unpick_units",
    )


def apply_update(gradient, master_ref, one_ref, two_ref, outs):
    grad_out, master_out, copy_out, one_out, two_out = outs
    weight, one, two = adamw(master_ref[0, 0], gradient, one_ref[0, 0], two_ref[0, 0], 0.02, 0.1)
    grad_out[0, 0] = gradient
    master_out[0, 0] = weight
    copy_out[0, 0] = weight.astype(bf16)
    one_out[0, 0] = one
    two_out[0, 0] = two


def unit_gradient(parts, piece, unit_rows):
    return jnp.transpose(parts.astype(f32).reshape(-1, unit_rows), (1, 0))


def update_kernel(count_ref, grad_ref, master_ref, one_ref, two_ref, *refs, first):
    filled = pl.program_id(0) + first < count_ref[0]
    piece, unit_rows = grad_ref.shape[2:]
    gradient = jnp.where(filled, unit_gradient(grad_ref[:, 0], piece, unit_rows), 0.0)
    apply_update(gradient, master_ref, one_ref, two_ref, refs[-5:])


def update_outs(master):
    whole = shaped(master.shape, f32)
    return [whole, whole, shaped(master.shape), whole, whole]


def update_units(count, grads, first, master, moment_one, moment_two, done):
    _, _, unit_rows, unit_cols = master.shape
    parts, slots, piece, _ = grads.shape
    unit = blocks((1, 1, unit_rows, unit_cols), lambda s, *refs: (s + first, 0, 0, 0))
    return call(
        functools.partial(update_kernel, first=first),
        [grads, master, moment_one, moment_two, *done],
        [blocks((parts, 1, piece, unit_rows), lambda s, *refs: (0, s, 0, 0)), unit, unit, unit]
        + [ANY] * len(done),
        update_outs(master),
        [unit] * 5,
        grid=(slots,),
        prefetch=[count],
        aliases={5 + k: k for k in range(len(done))},
        moved=master.size * 16,
        name="update_units",
    )


def update_attn_kernel(
    slot_ref, block_ref, half_ref, count_ref, qkv_ref, out_ref, grad_ref, master_ref, one_ref,
    two_ref, *refs, qkv_blocks,
):
    entry = pl.program_id(0)
    parts, _, piece, unit_rows = grad_ref.shape

    @pl.when((entry == 0) | (entry < count_ref[0]))
    def _():
        from_qkv = block_ref[entry] < qkv_blocks
        turn = count_ref[2]
        taken = []
        for j in range(parts):
            place = jnp.bitwise_xor(turn, j)
            taken.append(
                jnp.where(
                    from_qkv,
                    qkv_ref[pl.ds(place, 1), 0].astype(f32),
                    out_ref[pl.ds(place, 1), 0].astype(f32),
                )
            )
        attn = jnp.concatenate(taken, axis=0)
        gradient = jnp.where(count_ref[0] > 0, attn, grad_ref[:, 0].astype(f32))
        gradient = unit_gradient(gradient, piece, unit_rows)
        gradient = jnp.where(slot_ref[entry] < count_ref[1], gradient, 0.0)
        apply_update(gradient, master_ref, one_ref, two_ref, refs[-5:])


def update_attn(
    slots, places, halves, count, qkv, out, grads, master, moment_one, moment_two, done
):
    _, _, unit_rows, unit_cols = master.shape
    parts, _, piece, _ = grads.shape
    qkv_blocks, out_blocks = qkv.shape[1], out.shape[1]
    unit = blocks((1, 1, unit_rows, unit_cols), lambda k, slot, *refs: (slot[k], 0, 0, 0))
    piece_of = (parts, 1, piece, unit_rows)
    return call(
        functools.partial(update_attn_kernel, qkv_blocks=qkv_blocks),
        [qkv, out, grads, master, moment_one, moment_two, *done],
        [
            blocks(
                piece_of,
                lambda k, slot, block, half, count: (
                    0, jnp.minimum(block[k], qkv_blocks - 1), 0, half[k]
                ),
            ),
            blocks(
                piece_of,
                lambda k, slot, block, half, count: (
                    0, jnp.clip(block[k] - qkv_blocks, 0, out_blocks - 1), 0, half[k]
                ),
            ),
            blocks(
                piece_of, lambda k, slot, *refs: (0, jnp.minimum(slot[k], grads.shape[1] - 1), 0, 0)
            ),
            unit,
            unit,
            unit,
        ]
        + [ANY] * 5,
        update_outs(master),
        [unit] * 5,
        grid=(slots.shape[0],),
        prefetch=[slots, places, halves, count],
        aliases={10 + k: k for k in range(5)},
        moved=master.size * 6,
        name="update_attn",
    )


def lane_index(shape):
    return lax.broadcasted_iota(jnp.int32, shape, 1)


def rope(tile, cos_tile, sin_tile):
    lower = lane_index(tile.shape) % HD < HD // 2
    ahead = pltpu.roll(tile, LANES - HD // 2, 1)
    behind = pltpu.roll(tile, HD // 2, 1)
    return tile * cos_tile + jnp.where(lower, -ahead, behind) * sin_tile


def unrope(tile, cos_tile, sin_tile):
    lower = lane_index(tile.shape) % HD < HD // 2
    weighted = tile * sin_tile
    ahead = pltpu.roll(weighted, LANES - HD // 2, 1)
    behind = pltpu.roll(weighted, HD // 2, 1)
    return tile * cos_tile + jnp.where(lower, ahead, -behind)


def project_kernel(rows_ref, w_ref, cos_ref, sin_ref, out_ref, *, group_width):
    product = dot(rows_ref[...], w_ref[...], 1, 1)
    for start in range(0, out_ref.shape[1], LANES):
        tile = product[:, start : start + LANES]
        turned = rope(tile, cos_ref[...], sin_ref[...])
        if (start + LANES) % group_width == 0:
            tile = jnp.where(lane_index(tile.shape) < HD, turned, tile).astype(bf16)
        else:
            tile = turned.astype(bf16) * HD ** (-0.5)
        out_ref[:, start : start + LANES] = tile


def project(rows, w_qkv, cos_all, sin_all, group_width, step, deps):
    count = rows.shape[0]
    width = w_qkv.shape[0]
    return call(
        functools.partial(project_kernel, group_width=group_width),
        [rows, w_qkv, cos_all, sin_all],
        [
            blocks((step, D), lambda i: (i, 0)),
            blocks((width, D), lambda i: (0, 0)),
            blocks((step, LANES), lambda i: (i, 0)),
            blocks((step, LANES), lambda i: (i, 0)),
        ],
        shaped((count, width)),
        blocks((step, width), lambda i: (i, 0)),
        grid=(count // step,),
        deps=deps,
        flops=2 * count * width * D,
        name="project",
    )


def extend(tile, kx, vx):
    tile = tile.astype(f32)
    other = pltpu.roll(tile, HD, 1)
    low = lane_index(tile.shape) < HD
    kx[0] = jnp.where(low, tile, 0.0).astype(bf16)
    kx[1] = jnp.where(low, 0.0, other).astype(bf16)
    vx[0] = jnp.where(low, other, 0.0).astype(bf16)
    vx[1] = jnp.where(low, 0.0, tile).astype(bf16)


def forward_kernel(length_ref, qkv_ref, out_ref, log_ref, kx, vx, *, block):
    length = length_ref[0]
    seq_len, group_width = qkv_ref.shape
    pairs = group_width // LANES - 1
    extend(qkv_ref[:, pairs * LANES :], kx, vx)
    row = lax.broadcasted_iota(jnp.int32, (block, block), 0)
    col = lax.broadcasted_iota(jnp.int32, (block, block), 1)
    causal = col <= row
    key_row = lax.broadcasted_iota(jnp.int32, (1, seq_len), 1)
    bias = jnp.where(key_row < length, 0.0, -1e30).astype(f32)
    low = lane_index((block, LANES)) < HD
    for pair in range(pairs):
        lanes = slice(pair * LANES, (pair + 1) * LANES)
        for start in range(0, seq_len, block):
            query = qkv_ref[start : start + block, lanes]
            total = None
            logs = []
            for half in range(2):
                diagonal = dot(query, kx[half, start : start + block, :], 1, 1)
                diagonal = jnp.where(causal, diagonal + bias[:, start : start + block], -1e30)
                peak = jnp.max(diagonal, axis=1, keepdims=True)
                if start:
                    before = dot(query, kx[half, :start, :], 1, 1) + bias[:, :start]
                    peak = jnp.maximum(peak, jnp.max(before, axis=1, keepdims=True))
                    before = jnp.exp(before - peak)
                diagonal = jnp.exp(diagonal - peak)
                row_sum = jnp.sum(diagonal, axis=1, keepdims=True)
                part = dot(diagonal.astype(bf16), vx[half, start : start + block, :], 1, 0)
                if start:
                    row_sum = row_sum + jnp.sum(before, axis=1, keepdims=True)
                    part = part + dot(before.astype(bf16), vx[half, :start, :], 1, 0)
                part = part / row_sum
                total = part if total is None else total + part
                logs.append(peak + jnp.log(row_sum))
            out_ref[start : start + block, lanes] = total.astype(bf16)
            tile = jnp.transpose(jnp.where(low, logs[0], logs[1]), (1, 0))
            log_ref[0, 2 * pair : 2 * pair + 1, start : start + block] = tile[0:1]
            log_ref[0, 2 * pair + 1 : 2 * pair + 2, start : start + block] = tile[HD : HD + 1]


def attend_forward(length, qkv, groups, block, deps=(), **beside):
    seq_len, width = qkv.shape
    group_width = width // groups
    query_width = group_width - LANES
    return call(
        functools.partial(forward_kernel, block=block),
        [length, qkv],
        [SMEM, blocks((seq_len, group_width), lambda g: (0, g))],
        [shaped((seq_len, groups * query_width)), shaped((groups, 8, seq_len), f32)],
        [
            blocks((seq_len, query_width), lambda g: (0, g)),
            blocks((1, 8, seq_len), lambda g: (g, 0, 0)),
        ],
        grid=(groups,),
        scratch=[pltpu.VMEM((2, seq_len, LANES), bf16), pltpu.VMEM((2, seq_len, LANES), bf16)],
        deps=deps,
        mib=48,
        flops=groups * seq_len * seq_len * 2048,
        **beside,
        name="attend_forward",
    )


def backward_kernel(
    length_ref, qkv_ref, back_ref, out_ref, log_ref, cos_ref, sin_ref, *refs, block
):
    grad_ref, kx, vx, dk, dv = refs
    length = length_ref[0]
    seq_len, group_width = qkv_ref.shape
    pairs = group_width // LANES - 1
    extend(qkv_ref[:, pairs * LANES :], kx, vx)
    dk[...] = jnp.zeros(dk.shape, f32)
    dv[...] = jnp.zeros(dv.shape, f32)
    key = lax.broadcasted_iota(jnp.int32, (block, block), 0)
    row = lax.broadcasted_iota(jnp.int32, (block, block), 1)
    causal = key <= row
    for pair in range(pairs):
        lanes = slice(pair * LANES, (pair + 1) * LANES)
        for start in range(0, seq_len, block):
            here = slice(start, start + block)
            query = qkv_ref[here, lanes]
            back = back_ref[here, lanes]
            turned = jnp.transpose(back.astype(f32) * out_ref[here, lanes].astype(f32), (1, 0))
            query_grad = None
            for half in range(2):
                log_row = log_ref[0, 2 * pair + half : 2 * pair + half + 1, here]
                shift = jnp.sum(turned[half * HD : half * HD + HD], axis=0, keepdims=True)
                for first in range(0, start + block, block):
                    keys = slice(first, first + block)
                    scores = dot(kx[half, keys, :], query, 1, 1)
                    probs = jnp.exp(scores - log_row)
                    if first + block > seq_len // 2:
                        probs = jnp.where(key + first < length, probs, 0.0)
                    if first == start:
                        probs = jnp.where(causal, probs, 0.0)
                    probs_back = dot(vx[half, keys, :], back, 1, 1)
                    scores_back = (probs * (probs_back - shift)).astype(bf16)
                    dv[half, keys, :] += dot(probs.astype(bf16), back, 1, 0)
                    dk[half, keys, :] += dot(scores_back, query, 1, 0)
                    part = dot(scores_back, kx[half, keys, :], 0, 0)
                    query_grad = part if query_grad is None else query_grad + part
            query_grad = unrope(query_grad * HD ** (-0.5), cos_ref[here, :], sin_ref[here, :])
            grad_ref[here, lanes] = query_grad.astype(bf16)

    low = lane_index((seq_len, LANES)) < HD
    key_grad = jnp.where(low, dk[0] + pltpu.roll(dk[1], HD, 1), 0.0)
    key_grad = unrope(key_grad, cos_ref[...], sin_ref[...])
    value_grad = pltpu.roll(dv[0], HD, 1) + dv[1]
    grad_ref[:, pairs * LANES :] = jnp.where(low, key_grad, value_grad).astype(bf16)


def attend_backward(group, groups, length, qkv, back, out, logs, cos_all, sin_all, block, deps=(), **beside):
    seq_len, width = qkv.shape
    group_width = width // groups
    query_width = group_width - LANES
    given = blocks((seq_len, query_width), lambda i: (0, group))
    table = blocks((seq_len, LANES), lambda i: (0, 0))
    return call(
        functools.partial(backward_kernel, block=block),
        [length, qkv, back, out, logs, cos_all, sin_all],
        [
            SMEM,
            blocks((seq_len, group_width), lambda i: (0, group)),
            given,
            given,
            blocks((1, 8, seq_len), lambda i: (group, 0, 0)),
            table,
            table,
        ],
        shaped((seq_len, group_width)),
        blocks((seq_len, group_width), lambda i: (0, 0)),
        grid=(1,),
        scratch=[
            pltpu.VMEM((2, seq_len, LANES), bf16),
            pltpu.VMEM((2, seq_len, LANES), bf16),
            pltpu.VMEM((2, seq_len, LANES), f32),
            pltpu.VMEM((2, seq_len, LANES), f32),
        ],
        deps=deps,
        mib=48,
        flops=seq_len * seq_len * 5120,
        **beside,
        name="attend_backward",
    )


def branch_kernel(
    attended_ref, others_ref, w_ref, tokens_ref, gain_ref, residual_ref, normed_ref
):
    parts = others_ref.shape[0] + 1
    step, width = others_ref.shape[1:]
    here = lax.axis_index("narrow")
    first = here * (attended_ref.shape[0] // parts) + pl.program_id(0) * step
    total = tokens_ref[...].astype(f32)
    for k in range(parts):
        part = (
            others_ref[k - 1]
            if k
            else attended_ref[pl.ds(pl.multiple_of(first, step), step), :]
        )
        place = lax.rem(here - k + parts, parts) * width
        total = total + dot(part, w_ref[pl.ds(pl.multiple_of(place, width), width), :], 1, 0)
    residual_ref[...] = total
    normed_ref[...] = rmsnorm(total, gain_ref[...]).astype(bf16)


def branch(attended, others, w_out, tokens, gain, **beside):
    groups, count, width = others.shape
    step = 128
    rows = blocks((step, D), lambda i: (i, 0))
    return call(
        branch_kernel,
        [attended, others, w_out, tokens, gain],
        [
            blocks(attended.shape, lambda i: (0, 0)),
            blocks((groups, step, width), lambda i: (0, i, 0)),
            blocks((D, D), lambda i: (0, 0)),
            rows,
            blocks((1, D), lambda i: (0, 0)),
        ],
        [shaped((count, D), f32), shaped((count, D))],
        [rows, rows],
        grid=(count // step,),
        flops=2 * count * D * D,
        name="branch",
        **beside,
    )


def spread_kernel(turn_ref, back_ref, w_ref, out_ref):
    out_ref[0] = dot(back_ref[...], w_ref[...], 1, 1).astype(bf16)


def spread(turn, back, w_out, groups, deps=()):
    count = back.shape[0]
    width = D // groups
    return call(
        spread_kernel,
        [back, w_out],
        [
            blocks((count, D), lambda i, t: (0, 0)),
            blocks((width, D), lambda i, t: (lax.rem(t[1] + i, groups), 0)),
        ],
        shaped((groups, count, width)),
        blocks((1, count, width), lambda i, t: (i, 0, 0)),
        grid=(groups,),
        prefetch=[turn],
        deps=deps,
        flops=2 * count * D * D,
        name="spread",
    )


def first_back_kernel(*refs):
    groups = (len(refs) - 1) // 2
    total = sum(dot(refs[g][...], refs[groups + g][...], 1, 0) for g in range(groups))
    refs[-1][...] = total.astype(bf16)


def first_back(qkv_back, w_qkv, step, deps=()):
    groups = len(qkv_back)
    seq_len, width = qkv_back[0].shape
    return call(
        first_back_kernel,
        [*qkv_back, *([w_qkv] * groups)],
        [blocks((step, width), lambda i: (i, 0))] * groups
        + [blocks((width, D), lambda i, g=g: (g, 0)) for g in range(groups)],
        shaped((seq_len, D)),
        blocks((step, D), lambda i: (i, 0)),
        grid=(seq_len // step,),
        deps=deps,
        flops=2 * seq_len * width * groups * D,
        name="first_back",
    )


def stream(entry_refs, layout, low, high, buffer, sems, use):
    def copies(i):
        found = []
        for part, (ref, start, end, offset) in enumerate(layout[i]):
            first, last = max(start, low), min(end, high)
            if first < last:
                found.append(
                    pltpu.make_async_copy(
                        entry_refs[ref].at[pl.ds(first - start + offset, last - first)],
                        buffer.at[i % 2, pl.ds(first - low, last - first)],
                        sems.at[i % 2, part],
                    )
                )
        return found

    for copy in copies(0):
        copy.start()
    for i in range(len(layout)):
        if i + 1 < len(layout):
            for copy in copies(i + 1):
                copy.start()
        for copy in copies(i):
            copy.wait()
        use(i, buffer.at[i % 2])


def stream_scratch(rows):
    return [pltpu.VMEM((2, rows, D), bf16), pltpu.SemaphoreType.DMA((2, 3))]


def entry_layout(entries):
    arrays, layout = [], []
    for entry in entries:
        start, parts = 0, []
        for array, offset, count in entry:
            known = [k for k, other in enumerate(arrays) if other is array]
            if not known:
                known = [len(arrays)]
                arrays.append(array)
            parts.append((known[0], start, start + count, offset))
            start += count
        layout.append(parts)
    return arrays, layout, start // 3


def ff_kernel(rows_ref, back_all_ref, *refs, layout, size, s, parts):
    hid_ref, dgate_ref, dup_ref, keep_ref, keep_back_ref, _, total, buffer, sems = refs[-12:-3]
    back_ref, sem = refs[-3], refs[-1]
    count = rows_ref.shape[0]
    place = lax.rem(lax.axis_index("narrow") - s + parts, parts) * count
    copy = pltpu.make_async_copy(
        back_all_ref.at[pl.ds(pl.multiple_of(place, count), count)], back_ref, sem
    )
    copy.start()
    keep_ref[...] = rows_ref[...]
    copy.wait()
    keep_back_ref[...] = back_ref[...]

    def use(i, weights):
        gate = dot(rows_ref[...], weights[:size], 1, 1)
        up = dot(rows_ref[...], weights[size : 2 * size], 1, 1)
        hidden_back = dot(back_ref[...], weights[2 * size :], 1, 1)
        sig = 1.0 / (1.0 + jnp.exp(-gate))
        silu = gate * sig
        here = slice(i * size, (i + 1) * size)
        hid_ref[:, here] = (silu * up).astype(bf16)
        dgate = (hidden_back * up * (sig * (1.0 + gate * (1.0 - sig)))).astype(bf16)
        dup = (hidden_back * silu).astype(bf16)
        dgate_ref[:, here] = dgate
        dup_ref[:, here] = dup
        part = dot(dgate, weights[:size], 1, 0) + dot(dup, weights[size : 2 * size], 1, 0)
        if i:
            part = part + total[...]
        total[...] = part

    stream(refs, layout, 0, 3 * size, buffer, sems, use)


def ff_close(lands, refs, *, added):
    out_ref, total, _, _, _, arrived, sem = refs[-7:]
    value = total[...]
    if added:
        copy = pltpu.make_async_copy(lands[0], arrived, sem)
        copy.start()
        copy.wait()
        value = value + arrived[...].astype(f32)
    out_ref[...] = value.astype(out_ref.dtype)


def ff_step(s, rows, back_all, entries, kept, moving, before=None, last=False):
    count = rows.shape[0]
    seq_len = back_all.shape[0]
    arrays, layout, size = entry_layout(entries)
    ff_width = size * len(entries)
    wide_rows = shaped((seq_len, ff_width))
    given = blocks((count, ff_width), lambda i: (s, 0))
    here = blocks((count, D), lambda i: (s, 0))
    whole = blocks((count, D), lambda i: (0, 0))
    order = sorted(range(1, seq_len // count)) + [0]
    first = order[0] == s
    return call(
        functools.partial(
            ff_kernel, layout=layout, size=size, s=s, parts=seq_len // count
        ),
        [rows, back_all, *arrays, *kept],
        [whole, ANY] + [ANY] * (len(arrays) + len(kept)),
        [wide_rows] * 3
        + [shaped((seq_len, D))] * 2
        + [shaped((count, D), f32 if last else bf16)],
        [given] * 3 + [here, here, whole],
        grid=(1,),
        scratch=[pltpu.VMEM((count, D), f32)]
        + stream_scratch(3 * size)
        + [pltpu.VMEM((count, D), bf16)] * 2
        + [pltpu.SemaphoreType.DMA],
        aliases={2 + len(arrays) + k: k for k in range(len(kept))},
        mib=56,
        flops=10 * count * ff_width * D,
        name="ff_step",
        sends=[Send(0, 0, "narrow", 1)],
        sources=[moving],
        lands=[moving.shape],
        closing=functools.partial(ff_close, added=not first),
    )


def down_kernel(hid_ref, *refs, layout, size):
    out_ref, weights, sems = refs[-3:]

    @pl.when(pl.program_id(0) == 0)
    def _():
        copies = []
        for i, parts in enumerate(layout):
            for ref, start, end, offset in parts:
                begin = max(start, 2 * size)
                if begin < end:
                    copies.append(
                        pltpu.make_async_copy(
                            refs[ref].at[pl.ds(begin - start + offset, end - begin)],
                            weights.at[pl.ds(i * size + begin - 2 * size, end - begin)],
                            sems.at[len(copies)],
                        )
                    )
        for copy in copies:
            copy.start()
        for copy in copies:
            copy.wait()

    out_ref[...] = dot(hid_ref[...], weights[...], 1, 0).astype(bf16)


def down_pass(hidden, entries, count, deps=(), **beside):
    arrays, layout, size = entry_layout(entries)
    seq_len, ff_width = hidden.shape
    parts = seq_len // count
    return call(
        functools.partial(down_kernel, layout=layout, size=size),
        [hidden, *arrays],
        [blocks((count, ff_width), lambda i: (i, 0))] + [ANY] * len(arrays),
        shaped((seq_len, D)),
        blocks(
            (count, D), lambda i: (lax.rem(lax.axis_index("narrow") - i + parts, parts), 0)
        ),
        grid=(parts,),
        scratch=[
            pltpu.VMEM((ff_width, D), bf16),
            pltpu.SemaphoreType.DMA((2 * len(entries),)),
        ],
        deps=deps,
        flops=2 * seq_len * ff_width * D,
        name="down_pass",
        **beside,
    )


def add_kernel(*refs):
    refs[-1][...] = sum(ref[...].astype(f32) for ref in refs[:-1]).astype(refs[-1].dtype)


def add(terms, kind=bf16, deps=()):
    count, width = terms[0].shape
    step = 128 if count % 128 == 0 else 64 if count % 64 == 0 else count
    given = blocks((step, width), lambda i: (i, 0))
    return call(
        add_kernel,
        terms,
        [given] * len(terms),
        shaped((count, width), kind),
        given,
        grid=(count // step,),
        deps=deps,
        moved=count * width * 8,
        name="add",
    )


def outer_kernel(first_ref, second_ref, *outs):
    first = first_ref[...]
    if len(first.shape) == 3:
        first = first[0]
    product = dot(first, second_ref[...], 0, 0).astype(bf16)
    each = pl.num_programs(0) // len(outs)
    for k, out_ref in enumerate(outs):

        @pl.when(pl.program_id(0) // each == k)
        def _(out_ref=out_ref):
            out_ref[...] = product


def outer(first, second, split=1, deps=(), **beside):
    rows, width = second.shape
    if len(first.shape) == 3:
        groups, _, step = first.shape
        height = groups * step
        taken = blocks((1, rows, step), lambda i: (i, 0, 0))
    else:
        height = first.shape[1]
        step = next(k for k in (512, 384, 256, 192, LANES) if height % (k * split) == 0)
        taken = blocks((rows, step), lambda i: (0, i))
    each = height // step // split
    return call(
        outer_kernel,
        [first, second],
        [taken, blocks((rows, width), lambda i: (0, 0))],
        [shaped((height // split, width))] * split,
        [
            blocks((step, width), lambda i, k=k: (jnp.clip(i - k * each, 0, each - 1), 0))
            for k in range(split)
        ],
        grid=(height // step,),
        deps=deps,
        mib=56,
        flops=2 * rows * height * width,
        **beside,
        name="outer",
    )


def pass_kernel(*refs):
    pass


def after(value, *deps):
    return call(
        pass_kernel, [value], [ANY], shaped(value.shape, value.dtype), ANY, deps=deps,
        aliases={0: 0}, name="after",
    )


def shift(count, step=1):
    return [(i, (i + step) % count) for i in range(count)]


def butterfly(value):
    for axis in ("wide", "narrow"):
        count = lax.axis_size(axis)
        step = 1
        while step < count:
            value = value + lax.ppermute(value, axis, [(i, i ^ step) for i in range(count)])
            step *= 2
    return value


def nothing(*refs):
    pass


def sum_places_kernel(place_ref, own_ref, others_ref, out_ref):
    total = jnp.zeros(own_ref.shape, f32)
    for k in range(others_ref.shape[0]):
        total = total + jnp.where(place_ref[0] == k, own_ref[...], others_ref[k])
    out_ref[...] = total


def sum_places(place, own, others):
    return call(
        sum_places_kernel,
        [place, own, others],
        [SMEM, VMEM, VMEM],
        shaped(own.shape, f32),
        VMEM,
        name="sum_places",
    )


def move(sends, sources, lands, deps=()):
    return call(
        nothing, [], [], [], [], sends=sends, sources=sources, lands=lands, deps=deps, name="move"
    )


def rows_at(first, count):
    return lambda wide, narrow: pl.ds(first, count)


def exchange_units(turned):
    return move(
        [
            Send(
                0, 0, "wide", e,
                lambda wide, narrow, e=e: jnp.bitwise_xor(wide, e),
                lambda wide, narrow: wide,
            )
            for e in range(1, turned.shape[0])
        ],
        [turned],
        [turned.shape],
    )[0]


def near_and_across(source, land, at=None, needs=()):
    return [
        Send(source, land, "wide", 2, at, needs=needs),
        Send(source, land + 1, "wide", 4, at, needs=needs),
    ]


def sum_entries_kernel(first_ref, second_ref, *outs):
    total = (first_ref[0].astype(f32) + second_ref[0].astype(f32)).astype(bf16)
    for r, out_ref in enumerate(outs):

        @pl.when(pl.program_id(0) == r)
        def _(out_ref=out_ref):
            out_ref[...] = total


def sum_entries(first, second):
    count, rows, width = first.shape
    given = blocks((1, rows, width), lambda i: (i, 0, 0))
    return call(
        sum_entries_kernel,
        [first, second],
        [given, given],
        [shaped((rows, width))] * count,
        [blocks((rows, width), lambda i: (0, 0))] * count,
        grid=(count,),
        moved=first.size * 6,
        name="sum_entries",
    )


def ff_meet_kernel(own_ref, other_ref, *outs):
    total = (own_ref[...].astype(f32) + other_ref[...].astype(f32)).astype(bf16)
    half = total.shape[0] // 2
    for r in range(3):

        @pl.when(pl.program_id(0) == r)
        def _(r=r):
            outs[r][...] = total

    @pl.when(pl.program_id(0) == 3)
    def _():
        outs[3][...] = total[:half]
        outs[4][...] = total[half:]


def ff_meet(own, other, deps=()):
    height, width = own.shape
    rows = height // 4
    given = blocks((rows, width), lambda i: (i, 0))
    sizes = [rows, rows, rows, rows // 2, rows // 2]
    return call(
        ff_meet_kernel,
        [own, other],
        [given, given],
        [shaped((size, width)) for size in sizes],
        [blocks((size, width), lambda i: (0, 0)) for size in sizes],
        grid=(4,),
        deps=deps,
        moved=own.size * 6,
        name="ff_meet",
    )


def ff_join_kernel(x_ref, first_ref, y_ref, second_ref, x_out, y_out):
    half = first_ref.shape[0]
    x_out[:half] = (x_ref[:half].astype(f32) + first_ref[...].astype(f32)).astype(bf16)
    x_out[half:] = x_ref[half:]
    y_out[:half] = y_ref[:half]
    y_out[half:] = (y_ref[half:].astype(f32) + second_ref[...].astype(f32)).astype(bf16)


def ff_join(met, first, second, deps=()):
    shape = shaped(met[1].shape)
    return call(
        ff_join_kernel,
        [met[1], first, met[2], second],
        [VMEM] * 4,
        [shape, shape],
        [VMEM] * 2,
        deps=deps,
        moved=met[1].size * 8,
        name="ff_join",
    )


def across_sends(source, land):
    return [Send(source, land, "wide", 4), Send(source + 1, land + 1, "wide", 2)]


def near_sends(source, land):
    return [Send(source, land, "wide", 2), Send(source + 1, land + 1, "wide", 4)]


def unit_row(col, query_width, kv_width, by_head, group_width):
    start, offset = col
    if start < query_width:
        return start // by_head * group_width + start % by_head + offset
    start -= query_width
    last = start >= kv_width
    if last:
        start -= kv_width
    head = (start + offset) // HD
    return head * group_width + by_head + last * HD + (start + offset) % HD


def assemble_qkv_kernel(
    turn_ref, own_ref, near_ref, other_ref, out_ref, *, piece, unit_cols, sizes
):
    height = near_ref.shape[1]
    for e in range(8):
        j = jnp.bitwise_xor(turn_ref[0], e)
        for c in range(height // piece):
            here = slice(c * piece, (c + 1) * piece)
            row = unit_row((c * unit_cols, j * piece), *sizes)
            if e % 2:
                value = other_ref[e // 2, here, :]
            elif e:
                value = near_ref[e // 2 - 1, here, :]
            else:
                value = own_ref[here, :]
            out_ref[pl.ds(pl.multiple_of(row, piece), piece), :] = value


def assemble_qkv(turn, rows, near, other, piece, unit_cols, sizes):
    _, height, _ = near.shape
    return call(
        functools.partial(
            assemble_qkv_kernel, piece=piece, unit_cols=unit_cols, sizes=sizes
        ),
        [turn, rows, near, other],
        [SMEM, blocks((height, D), lambda i: (0, 0)), whole_block(near), whole_block(other)],
        shaped((height * 8, D)),
        blocks((height * 8, D), lambda i: (0, 0)),
        grid=(1,),
        mib=32,
        moved=height * 8 * D * 4,
        name="assemble_qkv",
    )


def whole_block(array):
    return blocks(array.shape, lambda i: (0,) * len(array.shape))


def arrange_qkv_kernel(turn_ref, *refs, piece, unit_cols, sizes):
    own_ref, other_ref = refs[-2:]
    group_width = sizes[3]
    for j in range(unit_cols // piece):
        e = jnp.bitwise_xor(turn_ref[0], j)
        for core, out_ref in enumerate((own_ref, other_ref)):

            @pl.when(e % 2 == core)
            def _(j=j, e=e, out_ref=out_ref):
                for c in range(out_ref.shape[1] // piece):
                    row = unit_row((c * unit_cols, j * piece), *sizes)
                    grad_ref = refs[row // group_width]
                    first = row % group_width
                    out_ref[e // 2, c * piece : (c + 1) * piece, :] = grad_ref[
                        first : first + piece, :
                    ]


def arrange_qkv(turn, grads, piece, unit_cols, sizes):
    count = unit_cols // piece
    rows = sizes[3] * len(grads) // count
    shape = shaped((count // 2, rows, D))
    return call(
        functools.partial(arrange_qkv_kernel, piece=piece, unit_cols=unit_cols, sizes=sizes),
        [turn, *grads],
        [SMEM] + [VMEM] * len(grads),
        [shape, shape],
        [VMEM] * 2,
        moved=rows * count * D * 4,
        name="arrange_qkv",
    )


def out_row(turn_ref, k, c, j, parts, piece, unit_cols, sign):
    n = lax.rem(turn_ref[1] + sign * k + parts, parts)
    return n * (D // parts) + c * unit_cols + j * piece


def assemble_out_kernel(
    turn_ref, rows_ref, z_ref, x_ref, y_ref, across_ref, other_ref, out_ref, *, first, piece,
    unit_cols, parts,
):
    height = z_ref.shape[1]
    for e in range(8):
        j = jnp.bitwise_xor(turn_ref[0], e)
        for k in range(parts):
            for c in range(height // piece):
                here = slice(c * piece, (c + 1) * piece)
                row = out_row(turn_ref, k, c, j, parts, piece, unit_cols, -1)
                if e % 2:
                    value = other_ref[e // 2, k, here, :]
                elif e:
                    value = (x_ref, y_ref, across_ref)[e // 2 - 1][k, here, :]
                elif k:
                    value = z_ref[k - 1, here, :]
                else:
                    value = rows_ref[first + c * piece : first + (c + 1) * piece, :]
                out_ref[pl.ds(pl.multiple_of(row, piece), piece), :] = value


def assemble_out(turn, rows, first, given, piece, unit_cols, parts, deps=()):
    height = given[0].shape[1]
    return call(
        functools.partial(
            assemble_out_kernel, first=first, piece=piece, unit_cols=unit_cols, parts=parts
        ),
        [turn, rows, *given],
        [SMEM, blocks((first + height, D), lambda i: (0, 0))] + [whole_block(a) for a in given],
        shaped((D, D)),
        blocks((D, D), lambda i: (0, 0)),
        grid=(1,),
        mib=52,
        deps=deps,
        moved=D * D * 4,
        name="assemble_out",
    )


def arrange_out_kernel(grad_ref, own_ref, other_ref, *, piece, unit_cols, parts):
    per = own_ref.shape[1] // piece // parts
    for j in range(unit_cols // piece):
        e = jnp.bitwise_xor(lax.axis_index("wide"), j)
        for core, out_ref in enumerate((own_ref, other_ref)):

            @pl.when(e % 2 == core)
            def _(j=j, e=e, out_ref=out_ref):
                for k in range(parts):
                    for c in range(per):
                        row = (parts - k) % parts * (grad_ref.shape[0] // parts) + c * unit_cols + j * piece
                        first = (k * per + c) * piece
                        out_ref[e // 2, first : first + piece, :] = grad_ref[
                            row : row + piece, :
                        ]


def arrange_out(grad, piece, unit_cols, parts, **beside):
    count = unit_cols // piece
    shape = shaped((count // 2, D // count, D))
    return call(
        functools.partial(arrange_out_kernel, piece=piece, unit_cols=unit_cols, parts=parts),
        [grad],
        [VMEM],
        [shape, shape],
        [VMEM] * 2,
        moved=D * D * 4,
        name="arrange_out",
        **beside,
    )


def local(
    tokens, cotangent, lengths, owners, master, moment_one, moment_two, norm_gains, gain_first,
    gain_second,
):
    wide_count = lax.axis_size("wide")
    narrow_count = lax.axis_size("narrow")
    capacity, _, unit_rows, unit_cols = master.shape
    unit_count = owners.shape[0]
    row_count = tokens.shape[0]
    seq_len = row_count * narrow_count
    row_blocks = D // unit_rows
    col_blocks = unit_count // row_blocks
    piece = unit_cols // wide_count
    query_width = H // narrow_count * HD
    kv_width = KV // narrow_count * HD
    ff_width = FF // narrow_count
    qkv_width = query_width + 2 * kv_width
    groups = KV // narrow_count
    group_width = qkv_width // groups
    by_head = group_width - 2 * HD
    wide_index = lax.axis_index("wide")
    narrow_index = lax.axis_index("narrow")
    turn = jnp.stack([wide_index, narrow_index]).astype(jnp.int32)
    length = lax.dynamic_slice(lengths, (wide_index,), (1,))
    block = min(256, seq_len)
    qkv_blocks = qkv_width // unit_cols
    out_blocks = query_width // unit_cols
    attn_blocks = qkv_blocks + out_blocks
    sizes = (query_width, kv_width, by_head, group_width)
    back_by = (narrow_index - jnp.arange(narrow_count, dtype=jnp.int32)) % narrow_count

    inputs = tokens.astype(f32)
    normed = rmsnorm(inputs, norm_gains[0]).astype(bf16)
    normed_all = lax.all_gather(normed, "narrow", axis=0, tiled=True)

    slot_place, counts = positions(owners, wide_count, capacity)
    turned = turn_units(master, wide_count, (normed,))
    got = exchange_units(turned)
    rows = pick_units(turn, slot_place, turned, got, row_blocks)
    qkv_rows = qkv_blocks * piece
    out_rows = out_blocks * piece
    ff_first = qkv_rows + out_rows
    ff_rows = 3 * ff_width // wide_count

    qkv_at, out_at = rows_at(0, qkv_rows), rows_at(qkv_rows, out_rows)

    def entry(k):
        return lambda wide, narrow: k

    near_qkv, other_qkv, narrow_out = move(
        [Send(0, 0, "wide", 2 * r, qkv_at, entry(r - 1)) for r in (1, 2, 3)]
        + [Send(0, 1, "wide", 1, qkv_at, entry(0))]
        + [Send(0, 2, "narrow", k, out_at, entry(k - 1)) for k in range(1, narrow_count)]
        + [
            Send(0, 1, "wide", 1, entry(r - 1), entry(r), landed=True, needs=(r - 1,))
            for r in (1, 2, 3)
        ],
        [rows],
        [
            (3, qkv_rows, D),
            (4, qkv_rows, D),
            (narrow_count - 1, out_rows, D),
        ],
    )
    w_qkv = assemble_qkv(turn, rows, near_qkv, other_qkv, piece, unit_cols, sizes)

    cos_table, sin_table = tables(seq_len, HD)
    cos_all = jnp.concatenate([cos_table] * (LANES // HD), axis=1)
    sin_all = jnp.concatenate([sin_table] * (LANES // HD), axis=1)
    cotangent_then = after(cotangent, normed_all, w_qkv)
    back_all = lax.all_gather(cotangent_then, "narrow", axis=0, tiled=True)
    qkv = project(
        normed_all, w_qkv, cos_all, sin_all, group_width, row_count, (cotangent_then,)
    )
    out_shape = (narrow_count, out_rows, D)

    def first_entry(wide, narrow):
        return 0

    def later_entries(wide, narrow):
        return pl.ds(1, narrow_count - 1)

    attended, logs, out_x, out_y = attend_forward(
        length, qkv, groups, block,
        sends=[
            Send(0, 0, "wide", 2, out_at, first_entry),
            Send(0, 1, "wide", 4, out_at, first_entry),
            Send(1, 0, "wide", 2, None, later_entries),
            Send(1, 1, "wide", 4, None, later_entries),
        ],
        sources=[rows, narrow_out],
        lands=[out_shape, out_shape],
    )
    out_x, out_y = out_x, out_y

    half = narrow_count // 2
    third = ff_rows // 3

    def heads_of(k):
        return lambda wide, narrow: pl.ds(
            pl.multiple_of(lax.rem(narrow + k, narrow_count) * row_count, row_count), row_count
        )

    def part_of(k, at):
        return lambda wide, narrow: (k, at)

    low_part, high_part = pl.ds(0, half), pl.ds(half, narrow_count - half)
    attended_others, out_across, out_other, x_first, y_first = move(
        [Send(0, 0, "narrow", k, heads_of(k), entry(k - 1)) for k in range(1, narrow_count)]
        + [
            Send(2, 1, "wide", 4, lambda w, n: low_part, lambda w, n: low_part),
            Send(3, 1, "wide", 2, lambda w, n: high_part, lambda w, n: high_part),
            Send(1, 2, "wide", 1, out_at, lambda w, n: (0, 0)),
            Send(4, 2, "wide", 1, None, lambda w, n: (0, pl.ds(1, narrow_count - 1))),
            Send(2, 2, "wide", 1, None, entry(1)),
            Send(3, 2, "wide", 1, None, entry(2)),
            Send(1, 3, "wide", 2, rows_at(ff_first, third)),
            Send(1, 4, "wide", 4, rows_at(ff_first, third)),
            Send(
                1, 2, "wide", 1, None, entry(3), landed=True,
                needs=(narrow_count - 1, narrow_count),
            ),
        ],
        [attended, rows, out_x, out_y, narrow_out],
        [
            (narrow_count - 1, row_count, query_width),
            out_shape,
            (4, *out_shape),
            (third, D),
            (third, D),
        ],
    )
    w_out = assemble_out(
        turn, rows, qkv_rows, [narrow_out, out_x, out_y, out_across, out_other], piece,
        unit_cols, narrow_count,
    )
    sixth = third // 2
    residual, normed_two, x_second, y_second = branch(
        attended, attended_others, w_out, tokens, norm_gains[1:2],
        sends=near_and_across(0, 0, rows_at(ff_first + third, sixth)),
        sources=[rows],
        lands=[(sixth, D), (sixth, D)],
    )

    rest = ff_rows - third - sixth
    block_one, x_third, y_third, *swapped = move(
        [Send(0, 0, "narrow", 1)]
        + near_and_across(1, 1, rows_at(ff_first + third + sixth, rest))
        + [Send(1, 3, "wide", 1, rows_at(ff_first, ff_rows))]
        + [Send(2 + k, 4 + k, "wide", 1) for k in range(4)],
        [normed_two, rows, x_first, x_second, y_first, y_second],
        [normed_two.shape, (rest, D), (rest, D), (ff_rows, D)]
        + [(third, D), (sixth, D), (third, D), (sixth, D)],
    )
    own_swap, x_first_swap, x_second_swap, y_first_swap, y_second_swap = swapped
    block_two, across_first, across_second, across_third, *swapped = move(
        [
            Send(0, 0, "narrow", 1),
            Send(1, 1, "wide", 4),
            Send(2, 2, "wide", 4),
            Send(4, 3, "wide", 2),
            Send(3, 4, "wide", 1),
            Send(4, 5, "wide", 1),
            Send(1, 6, "wide", 1, landed=True, needs=(1,)),
            Send(2, 7, "wide", 1, landed=True, needs=(2,)),
            Send(3, 8, "wide", 1, landed=True, needs=(3,)),
        ],
        [block_one, x_first, x_second, x_third, y_third],
        [block_one.shape, (third, D), (sixth, D), (rest, D), (rest, D), (rest, D)]
        + [(third, D), (sixth, D), (rest, D)],
    )
    x_third_swap, y_third_swap, *across_swap = swapped

    def pieces(first, second, last):
        return [(first, 0, third), (second, 0, sixth), (last, 0, rest)]

    entries = [
        [(rows, ff_first, ff_rows)],
        pieces(x_first, x_second, x_third),
        pieces(y_first, y_second, y_third),
        pieces(across_first, across_second, across_third),
        [(own_swap, 0, ff_rows)],
        pieces(x_first_swap, x_second_swap, x_third_swap),
        pieces(y_first_swap, y_second_swap, y_third_swap),
        pieces(*across_swap),
    ]

    *kept, total, block_three = ff_step(1, block_one, back_all, entries, (), block_two)
    *kept, total, _ = ff_step(2, block_two, back_all, entries, kept, total, True)
    *kept, total, _ = ff_step(3, block_three, back_all, entries, kept, total, True)
    *kept, norm_two_back, _ = ff_step(0, normed_two, back_all, entries, kept, total, True, True)
    hidden, dgate, dup, mlp_all, back_kept = kept

    _, norm_two_pull = jax.vjp(rmsnorm, residual, norm_gains[1])
    resid_part, gain_two = norm_two_pull(norm_two_back)
    resid_back = cotangent.astype(f32) + resid_part
    attn_back = resid_back.astype(bf16)
    by_heads = spread(turn, attn_back, w_out, narrow_count)

    def heads_send(k, land):
        return Send(0, land, "narrow", k, entry(k))

    heads_shape = (row_count, query_width)
    attended_rows = jnp.concatenate(
        [
            lax.dynamic_slice(attended, (narrow_index * row_count, 0), (row_count, query_width))[
                None
            ],
            attended_others,
        ],
        axis=0,
    )
    grad_out, heads_one = outer(
        attended_rows, attn_back, 1,
        sends=[heads_send(1, 0)], sources=[by_heads], lands=[heads_shape],
    )
    own_out, other_out, heads_three = arrange_out(
        grad_out, piece, unit_cols, narrow_count,
        sends=[heads_send(3, 0)], sources=[by_heads], lands=[heads_shape],
    )
    *grad_down, heads_two, out_swap = outer(
        hidden, back_kept, 2, (own_out,),
        sends=[heads_send(2, 0), Send(1, 1, "wide", 1)],
        sources=[by_heads, other_out],
        lands=[heads_shape, other_out.shape],
    )
    out_back = jnp.stack([by_heads[0], heads_one, heads_two, heads_three])
    out_back = jnp.take(out_back, back_by, axis=0).reshape(seq_len, query_width)
    met_out = sum_entries(own_out, out_swap)
    met_shape = met_out[0].shape
    ff_term, out_x, out_y, down_swap = down_pass(
        hidden, entries, row_count,
        sends=[Send(0, 0, "wide", 2), Send(1, 1, "wide", 4), Send(2, 2, "wide", 1)],
        sources=[met_out[1], met_out[2], grad_down[1]],
        lands=[met_shape, met_shape, grad_down[1].shape],
    )
    output = residual + lax.psum_scatter(
        ff_term, "narrow", scatter_dimension=0, tiled=True
    ).astype(f32)
    met_down = ff_meet(grad_down[0], down_swap)
    half_shape, near_shape = met_down[3].shape, met_down[1].shape
    *grad_gate, down_a, down_b = outer(
        dgate, mlp_all, 2,
        sends=across_sends(0, 0), sources=met_down[3:], lands=[half_shape] * 2,
    )
    joined_down = ff_join(met_down, down_a, down_b)
    *grad_upper, gate_swap, down_x, down_y = outer(
        dup, mlp_all, 2, (joined_down[0],),
        sends=[Send(0, 0, "wide", 1)] + near_sends(1, 1),
        sources=[grad_gate[1], *joined_down],
        lands=[grad_gate[1].shape, near_shape, near_shape],
    )
    met_gate = ff_meet(grad_gate[0], gate_swap)

    qkv_back = [None, None]
    qkv_back[0], upper_swap, gate_a, gate_b, out_across = attend_backward(
        0, groups, length, qkv, out_back, attended, logs, cos_all, sin_all, block,
        sends=[Send(0, 0, "wide", 1)] + across_sends(1, 1) + [Send(3, 3, "wide", 6)],
        sources=[grad_upper[1], *met_gate[3:], met_out[3]],
        lands=[grad_upper[1].shape, half_shape, half_shape, met_shape],
    )
    joined_gate = ff_join(met_gate, gate_a, gate_b)
    met_upper = ff_meet(grad_upper[0], upper_swap)
    out_sum = add([met_out[0], out_x, out_y, out_across])
    qkv_back[1], upper_a, upper_b, gate_x, gate_y = attend_backward(
        1, groups, length, qkv, out_back, attended, logs, cos_all, sin_all, block,
        sends=across_sends(0, 0) + near_sends(2, 2),
        sources=[*met_upper[3:], *joined_gate],
        lands=[half_shape] * 2 + [near_shape] * 2,
        deps=(out_sum,),
    )
    joined_upper = ff_join(met_upper, upper_a, upper_b)
    norm_one_term = first_back(qkv_back, w_qkv, row_count, (joined_upper[0],))
    first_qkv, upper_x, upper_y = outer(
        qkv_back[0], normed_all, 1, (norm_one_term,),
        sends=near_sends(0, 0), sources=list(joined_upper), lands=[near_shape] * 2,
    )
    ff_sums = [
        add([met_gate[0], gate_x, gate_y]),
        add([met_upper[0], upper_x, upper_y]),
        add([met_down[0], down_x, down_y]),
    ]

    slots = wide_count * capacity
    unit_of = jnp.zeros((slots,), jnp.int32).at[slot_place].set(
        jnp.arange(unit_count, dtype=jnp.int32)
    )
    half_of = unit_of // col_blocks
    block_of = unit_of - half_of * col_blocks
    sent = unpick_units(
        jnp.concatenate(ff_sums, axis=0),
        jnp.maximum(block_of - attn_blocks, 0),
        half_of,
        wide_count,
        piece,
        unit_rows,
    )
    owned = [lax.all_to_all(part, "wide", split_axis=0, concat_axis=0) for part in sent]
    count = lax.dynamic_slice(counts, (wide_index,), (1,))

    (second_qkv,) = outer(qkv_back[1], normed_all, 1, tuple(sent))
    grad_qkv = [first_qkv, second_qkv]
    gain_one = sum(
        jnp.sum(
            w_qkv[g * group_width : (g + 1) * group_width].astype(f32) * grad_qkv[g].astype(f32),
            axis=0,
        )
        for g in range(groups)
    )
    gain_terms = jnp.stack([gain_one / norm_gains[0], gain_two])
    own_qkv, other_qkv = arrange_qkv(turn, grad_qkv, piece, unit_cols, sizes)

    def by_wide(wide, narrow):
        return wide

    def by_narrow(wide, narrow):
        return narrow

    qkv_swap, gain_others, *out_parts = move(
        [Send(0, 0, "wide", 1)]
        + [Send(1, 1, "wide", e, None, by_wide) for e in range(1, wide_count)]
        + [
            Send(2, k + 1, "narrow", k, rows_at(k * out_rows, out_rows))
            for k in range(1, narrow_count)
        ],
        [other_qkv, gain_terms, out_sum],
        [other_qkv.shape, ((wide_count, *gain_terms.shape), f32)]
        + [(out_rows, D)] * (narrow_count - 1),
    )
    met_qkv = sum_entries(own_qkv, qkv_swap)
    gain_plane = sum_places(wide_index.reshape(1), gain_terms, gain_others)
    out_sum = add([out_sum[:out_rows]] + list(out_parts))
    *arrived, gain_others = move(
        [Send(r - 1, r - 1, "wide", 2 * r) for r in (1, 2, 3)]
        + [Send(3, 3, "narrow", k, None, by_narrow) for k in range(1, narrow_count)],
        [*met_qkv[1:], gain_plane],
        [met_qkv[0].shape] * 3 + [((narrow_count, *gain_terms.shape), f32)],
    )
    gain_grads = sum_places(narrow_index.reshape(1), gain_plane, gain_others)
    qkv_sum = add([met_qkv[0]] + list(arrived))
    near_qkv, near_out, other_qkv, other_out = move(
        [Send(0, 0, "wide", 2 * r, None, entry(r)) for r in (1, 2, 3)]
        + [Send(1, 1, "wide", 2 * r, None, entry(r)) for r in (1, 2, 3)]
        + [
            Send(0, 2, "wide", 1, None, entry(0)),
            Send(1, 3, "wide", 1, None, entry(0)),
        ]
        + [
            Send(0, 2, "wide", 1, entry(r), entry(r), landed=True, needs=(r - 1,))
            for r in (1, 2, 3)
        ]
        + [
            Send(1, 3, "wide", 1, entry(r), entry(r), landed=True, needs=(r + 2,))
            for r in (1, 2, 3)
        ],
        [qkv_sum, out_sum],
        [(4, qkv_rows, D), (4, out_rows, D)] * 2,
    )

    def by_device(own, near, other):
        return jnp.stack(
            [
                other[e // 2] if e % 2 else near[e // 2] if e else own
                for e in range(wide_count)
            ]
        )

    qkv_grads = by_device(qkv_sum, near_qkv, other_qkv)
    out_grads = by_device(out_sum, near_out, other_out)
    qkv_grads = qkv_grads.reshape(wide_count, qkv_blocks, piece, D)
    out_grads = out_grads.reshape(wide_count, out_blocks, piece, D)

    updated = ()
    for k in range(2):
        updated = update_units(
            count, owned[k], k * (capacity // 2), master, moment_one, moment_two, updated
        )
    first_slot = wide_index * capacity
    own_block = lax.dynamic_slice(block_of, (first_slot,), (capacity,))
    own_half = lax.dynamic_slice(half_of, (first_slot,), (capacity,))
    slot = jnp.arange(capacity, dtype=jnp.int32)
    is_attn = (own_block < attn_blocks) & (slot < count[0])
    attn_count = jnp.sum(is_attn.astype(jnp.int32))
    rank = jnp.cumsum(is_attn.astype(jnp.int32)) - 1
    listed = min(capacity, attn_blocks * row_blocks)
    wanted = jnp.minimum(jnp.arange(listed, dtype=jnp.int32), jnp.maximum(attn_count - 1, 0))
    chosen = is_attn[None, :] & (rank[None, :] == wanted[:, None])

    def entries_of(values):
        return jnp.sum(jnp.where(chosen, values[None, :], 0), axis=1)

    owned_grads, new_master, new_copy, new_first, new_second = update_attn(
        entries_of(slot), entries_of(own_block), entries_of(own_half),
        jnp.stack([attn_count, count[0], wide_index]).astype(jnp.int32),
        qkv_grads, out_grads, owned[0], master, moment_one, moment_two, updated,
    )

    norm_one_back = lax.psum_scatter(
        norm_one_term, "narrow", scatter_dimension=0, tiled=True
    ).astype(f32)
    _, norm_one_pull = jax.vjp(lambda values: rmsnorm(values, norm_gains[0]), inputs)
    (input_part,) = norm_one_pull(norm_one_back)
    input_grad = (resid_back + input_part).astype(bf16)
    new_gains, _, gain_second_new = adamw(
        norm_gains, gain_grads, gain_first, gain_second, 0.5, 0.0
    )
    return (
        output.astype(bf16),
        input_grad,
        owned_grads,
        new_master,
        new_copy,
        new_first,
        new_second,
        gain_grads,
        gain_second_new,
        new_gains,
    )


def rotate(values, cos_table, sin_table):
    middle = values.shape[-1] // 2
    turned = jnp.concatenate([-values[..., middle:], values[..., :middle]], axis=-1)
    return values * cos_table + turned * sin_table


def unrotate(gradient, cos_table, sin_table):
    middle = gradient.shape[-1] // 2
    weighted = gradient * sin_table
    turned = jnp.concatenate([weighted[..., middle:], -weighted[..., :middle]], axis=-1)
    return gradient * cos_table + turned


def matmul_rows(first_op, second_op):
    return lax.dot_general(
        first_op, second_op, (((0,), (0,)), ((), ())), preferred_element_type=jnp.float32
    )


def matmul_cols(first_op, second_op):
    return lax.dot_general(
        first_op, second_op, (((1,), (1,)), ((), ())), preferred_element_type=jnp.float32
    )


def project_any(normed_all, w_qkv, cos_heads, sin_heads, heads_here, kv_here):
    seq_len = normed_all.shape[0]
    projected = jnp.dot(normed_all, w_qkv, preferred_element_type=jnp.float32)
    query_width = heads_here * HD
    kv_width = kv_here * HD
    group_size = heads_here // kv_here
    query_heads = rotate(
        projected[:, :query_width].reshape(seq_len, heads_here, HD), cos_heads, sin_heads
    )
    key_heads = rotate(
        projected[:, query_width : query_width + kv_width].reshape(seq_len, kv_here, HD),
        cos_heads,
        sin_heads,
    )
    value_heads = projected[:, query_width + kv_width :].reshape(seq_len, kv_here, HD)
    query_heads = jnp.transpose(query_heads.astype(jnp.bfloat16), (1, 0, 2)).reshape(
        kv_here, group_size, seq_len, HD
    )
    key_heads = jnp.transpose(key_heads.astype(jnp.bfloat16), (1, 0, 2))
    value_heads = jnp.transpose(value_heads.astype(jnp.bfloat16), (1, 0, 2))
    return (query_heads, key_heads, value_heads)


def masked_scores(query_block, key_heads, row_start, length):
    block_rows = query_block.shape[2]
    seq_len = key_heads.shape[1]
    scores = jnp.einsum(
        "kgqd,ksd->kgqs", query_block, key_heads, preferred_element_type=jnp.float32
    ) * HD ** (-0.5)
    row_pos = row_start + jnp.arange(block_rows, dtype=jnp.int32)
    key_pos = jnp.arange(seq_len, dtype=jnp.int32)
    allowed = (key_pos[None, :] <= row_pos[:, None]) & (key_pos[None, :] < length)
    return jnp.where(allowed, scores, -1e30)


def attend_forward_any(query_heads, key_heads, value_heads, length, block_rows):
    seq_len = query_heads.shape[2]
    outputs = []
    log_sums = []
    for row_start in range(0, seq_len, block_rows):
        query_block = query_heads[:, :, row_start : row_start + block_rows]
        scores = masked_scores(query_block, key_heads, row_start, length)
        row_peak = jnp.max(scores, axis=-1, keepdims=True)
        raised = jnp.exp(scores - row_peak)
        row_total = jnp.sum(raised, axis=-1, keepdims=True)
        attn_probs = (raised / row_total).astype(jnp.bfloat16)
        outputs.append(
            jnp.einsum(
                "kgqs,ksd->kgqd", attn_probs, value_heads, preferred_element_type=jnp.float32
            )
        )
        log_sums.append((row_peak + jnp.log(row_total))[..., 0])
    return (jnp.concatenate(outputs, axis=2), jnp.concatenate(log_sums, axis=2))


def attend_backward_any(query_heads, key_heads, value_heads, out_back, log_sums, length, block_rows):
    seq_len = query_heads.shape[2]
    query_grads = []
    key_grad = jnp.zeros(key_heads.shape, jnp.float32)
    value_grad = jnp.zeros(value_heads.shape, jnp.float32)
    for row_start in range(0, seq_len, block_rows):
        query_block = query_heads[:, :, row_start : row_start + block_rows]
        back_block = out_back[:, :, row_start : row_start + block_rows]
        scores = masked_scores(query_block, key_heads, row_start, length)
        attn_probs = jnp.exp(scores - log_sums[:, :, row_start : row_start + block_rows, None])
        probs_back = jnp.einsum(
            "kgqd,ksd->kgqs", back_block, value_heads, preferred_element_type=jnp.float32
        )
        row_shift = jnp.sum(attn_probs * probs_back, axis=-1, keepdims=True)
        scores_back = (HD ** (-0.5) * attn_probs * (probs_back - row_shift)).astype(jnp.bfloat16)
        query_grads.append(
            jnp.einsum("kgqs,ksd->kgqd", scores_back, key_heads, preferred_element_type=jnp.float32)
        )
        key_grad = key_grad + jnp.einsum(
            "kgqs,kgqd->ksd", scores_back, query_block, preferred_element_type=jnp.float32
        )
        value_grad = value_grad + jnp.einsum(
            "kgqs,kgqd->ksd",
            attn_probs.astype(jnp.bfloat16),
            back_block,
            preferred_element_type=jnp.float32,
        )
    return (jnp.concatenate(query_grads, axis=2), key_grad, value_grad)


def local_any(
    tokens,
    cotangent,
    lengths,
    owners,
    master,
    moment_one,
    moment_two,
    norm_gains,
    gain_first,
    gain_second,
):
    wide_count = lax.axis_size("wide")
    narrow_count = lax.axis_size("narrow")
    capacity = master.shape[0]
    unit_rows = master.shape[2]
    unit_cols = master.shape[3]
    unit_count = owners.shape[0]
    row_count = tokens.shape[0]
    seq_len = row_count * narrow_count
    slot_place, _ = positions(owners, wide_count, capacity)
    own_slots = master[:, 0].astype(jnp.bfloat16)
    all_slots = lax.all_gather(own_slots, "wide", axis=0, tiled=True)
    unit_data = jnp.take(all_slots, slot_place, axis=0)
    row_blocks = D // unit_rows
    col_blocks = unit_count // row_blocks
    packed = jnp.transpose(
        unit_data.reshape(row_blocks, col_blocks, unit_rows, unit_cols), (0, 2, 1, 3)
    ).reshape(D, col_blocks * unit_cols)
    heads_here = H // narrow_count
    kv_here = KV // narrow_count
    group_size = heads_here // kv_here
    query_width = heads_here * HD
    kv_width = kv_here * HD
    ff_width = FF // narrow_count
    qkv_end = query_width + 2 * kv_width
    out_end = qkv_end + query_width
    gate_end = out_end + 2 * ff_width
    w_qkv = packed[:, :qkv_end]
    w_out_t = packed[:, qkv_end:out_end]
    w_gate_up = packed[:, out_end:gate_end]
    w_down_t = packed[:, gate_end:]
    cos_table, sin_table = tables(seq_len, HD)
    cos_heads = cos_table[:, None, :]
    sin_heads = sin_table[:, None, :]
    block_rows = min(512, seq_len)
    wide_index = lax.axis_index("wide")
    length = lengths[wide_index]
    inputs = tokens.astype(jnp.float32)
    normed = rmsnorm(inputs, norm_gains[0]).astype(jnp.bfloat16)
    normed_all = lax.all_gather(normed, "narrow", axis=0, tiled=True)
    query_heads, key_heads, value_heads = project_any(
        normed_all, w_qkv, cos_heads, sin_heads, heads_here, kv_here
    )
    attended, log_sums = attend_forward_any(query_heads, key_heads, value_heads, length, block_rows)
    attended = (
        jnp.transpose(attended.reshape(heads_here, seq_len, HD), (1, 0, 2))
        .reshape(seq_len, query_width)
        .astype(jnp.bfloat16)
    )
    residual = inputs + lax.psum_scatter(
        matmul_cols(attended, w_out_t), "narrow", scatter_dimension=0, tiled=True
    )
    normed_two = rmsnorm(residual, norm_gains[1]).astype(jnp.bfloat16)
    mlp_input = lax.all_gather(normed_two, "narrow", axis=0, tiled=True)
    gate_up = jnp.dot(mlp_input, w_gate_up, preferred_element_type=jnp.float32)
    hidden = (jax.nn.silu(gate_up[:, :ff_width]) * gate_up[:, ff_width:]).astype(jnp.bfloat16)
    output = residual + lax.psum_scatter(
        matmul_cols(hidden, w_down_t).astype(jnp.bfloat16),
        "narrow",
        scatter_dimension=0,
        tiled=True,
    ).astype(jnp.float32)
    down_back = lax.all_gather(cotangent, "narrow", axis=0, tiled=True)
    mlp_again = lax.all_gather(normed_two, "narrow", axis=0, tiled=True)
    gate_up = jnp.dot(mlp_again, w_gate_up, preferred_element_type=jnp.float32)
    hidden_back = jnp.dot(down_back, w_down_t, preferred_element_type=jnp.float32)
    grad_down_t = matmul_rows(down_back, hidden)
    _, swiglu_pull = jax.vjp(
        lambda gate_in, upper_in: jax.nn.silu(gate_in) * upper_in,
        gate_up[:, :ff_width],
        gate_up[:, ff_width:],
    )
    gate_back, upper_back = swiglu_pull(hidden_back)
    gate_up_back = jnp.concatenate([gate_back, upper_back], axis=1).astype(jnp.bfloat16)
    grad_gate_up = matmul_rows(mlp_again, gate_up_back)
    norm_two_back = lax.psum_scatter(
        matmul_cols(gate_up_back, w_gate_up).astype(jnp.bfloat16),
        "narrow",
        scatter_dimension=0,
        tiled=True,
    ).astype(jnp.float32)
    _, norm_two_pull = jax.vjp(rmsnorm, residual, norm_gains[1])
    resid_part, gain_two = norm_two_pull(norm_two_back)
    resid_back = cotangent.astype(jnp.float32) + resid_part
    attn_back = lax.all_gather(resid_back.astype(jnp.bfloat16), "narrow", axis=0, tiled=True)
    normed_again = lax.all_gather(normed, "narrow", axis=0, tiled=True)
    query_heads, key_heads, value_heads = project_any(
        normed_again, w_qkv, cos_heads, sin_heads, heads_here, kv_here
    )
    out_back = jnp.dot(attn_back, w_out_t, preferred_element_type=jnp.float32).astype(jnp.bfloat16)
    grad_out_t = matmul_rows(attn_back, attended)
    out_back = jnp.transpose(out_back.reshape(seq_len, heads_here, HD), (1, 0, 2)).reshape(
        kv_here, group_size, seq_len, HD
    )
    query_grad, key_grad, value_grad = attend_backward_any(
        query_heads, key_heads, value_heads, out_back, log_sums, length, block_rows
    )
    query_grad = jnp.transpose(query_grad.reshape(heads_here, seq_len, HD), (1, 0, 2))
    query_grad = unrotate(query_grad, cos_heads, sin_heads).reshape(seq_len, query_width)
    key_grad = unrotate(jnp.transpose(key_grad, (1, 0, 2)), cos_heads, sin_heads).reshape(
        seq_len, kv_width
    )
    value_grad = jnp.transpose(value_grad, (1, 0, 2)).reshape(seq_len, kv_width)
    qkv_back = jnp.concatenate([query_grad, key_grad, value_grad], axis=1).astype(jnp.bfloat16)
    grad_qkv = matmul_rows(normed_again, qkv_back)
    norm_one_back = lax.psum_scatter(
        matmul_cols(qkv_back, w_qkv).astype(jnp.bfloat16), "narrow", scatter_dimension=0, tiled=True
    ).astype(jnp.float32)
    _, norm_one_pull = jax.vjp(rmsnorm, inputs, norm_gains[0])
    input_part, gain_one = norm_one_pull(norm_one_back)
    input_grad = (resid_back + input_part).astype(jnp.bfloat16)
    grad_packed = jnp.concatenate([grad_qkv, grad_out_t, grad_gate_up, grad_down_t], axis=1)
    grad_units = jnp.transpose(
        grad_packed.reshape(row_blocks, unit_rows, col_blocks, unit_cols), (0, 2, 1, 3)
    ).reshape(unit_count, unit_rows, unit_cols)
    grad_slots = (
        jnp.zeros((wide_count * capacity, unit_rows, unit_cols), jnp.float32)
        .at[slot_place]
        .set(grad_units)
    )
    owned_grads = lax.psum_scatter(
        grad_slots.astype(jnp.bfloat16), "wide", scatter_dimension=0, tiled=True
    ).astype(jnp.float32)[:, None]
    new_master, new_first, new_second = adamw(
        master, owned_grads, moment_one, moment_two, 0.02, 0.1
    )
    gain_grads = lax.psum(jnp.stack([gain_one, gain_two]), ("wide", "narrow"))
    new_gains, unused, gain_second_new = adamw(
        norm_gains, gain_grads, gain_first, gain_second, 0.5, 0.0
    )
    return (
        output.astype(jnp.bfloat16),
        input_grad,
        owned_grads,
        new_master,
        new_master.astype(jnp.bfloat16),
        new_first,
        new_second,
        gain_grads,
        gain_second_new,
        new_gains,
    )


def solution(mesh):
    COLLECTIVE[0] = 0
    rows = P(("wide", "narrow"), None)
    units = P("wide", "narrow", None, None)
    return jax.shard_map(
        local if mesh.shape["wide"] == 8 and mesh.shape["narrow"] == 4 else local_any,
        mesh=mesh,
        in_specs=(rows, rows, P(), P(), units, units, units, P(), P(), P()),
        out_specs=(rows, rows, units, units, units, units, units, P(), P(), P()),
        check_vma=False,
    )
```

```python
import functools

import jax
import jax.numpy as jnp
from jax import lax
from jax.experimental import pallas as pl
from jax.experimental.pallas import tpu as pltpu
from jax.sharding import PartitionSpec as P

D = 2048
H = 32
KV = 8
HD = 64
FF = 8192
STEP = 5
LANES = 128
MIB = 1 << 20
ANY = pl.BlockSpec(memory_space=pl.ANY)
VMEM = pl.BlockSpec(memory_space=pltpu.VMEM)
SMEM = pl.BlockSpec(memory_space=pltpu.SMEM)

f32 = jnp.float32
bf16 = jnp.bfloat16


def dot(first_op, second_op, first_dim, second_dim):
    return lax.dot_general(
        first_op,
        second_op,
        (((first_dim,), (second_dim,)), ((), ())),
        preferred_element_type=f32,
    )


def shaped(shape, kind=bf16):
    return jax.ShapeDtypeStruct(shape, kind)


def blocks(shape, place):
    return pl.BlockSpec(shape, place)


class Send:
    def __init__(self, source, land, axis, step, source_at=None, land_at=None, landed=False, needs=()):
        self.source, self.land, self.axis, self.step = source, land, axis, step
        self.source_at, self.land_at = source_at, land_at
        self.landed, self.needs = landed, needs


COLLECTIVE = [0]


def run_sends(sends, sources, lands, send_sem, recv_sem):
    count = lax.axis_size("narrow")
    wide, narrow = lax.axis_index("wide"), lax.axis_index("narrow")

    def target(axis, step):
        if axis == "wide":
            return {"wide": jnp.bitwise_xor(wide, step)}
        return {"narrow": lax.rem(narrow + step, count)}

    copies = []
    for k, send in enumerate(sends):
        ref = (lands if send.landed else sources)[send.source]
        if send.source_at is not None:
            ref = ref.at[send.source_at(wide, narrow)]
        land = lands[send.land]
        if send.land_at is not None:
            land = land.at[send.land_at(wide, narrow)]
        copies.append(
            pltpu.make_async_remote_copy(
                src_ref=ref,
                dst_ref=land,
                send_sem=send_sem.at[k],
                recv_sem=recv_sem.at[k],
                device_id=target(send.axis, send.step),
                device_id_type=pl.DeviceIdType.MESH,
            )
        )

    def start():
        partners = set()
        for send in sends:
            if send.axis == "wide":
                partners.add(("wide", send.step))
            else:
                partners.add(("narrow", send.step % count))
                partners.add(("narrow", -send.step % count))
        barrier = pltpu.get_barrier_semaphore()
        for axis, step in sorted(partners):
            pl.semaphore_signal(
                barrier, inc=1, device_id=target(axis, step), device_id_type=pl.DeviceIdType.MESH
            )
        pl.semaphore_wait(barrier, len(partners))
        for send, copy in zip(sends, copies):
            if not send.needs and not send.landed:
                copy.start()

    def finish():
        arrived = set()
        for send, copy in zip(sends, copies):
            for k in send.needs:
                if k not in arrived:
                    copies[k].wait_recv()
                    arrived.add(k)
            if send.needs or send.landed:
                copy.start()
        for k, copy in enumerate(copies):
            copy.wait_send()
            if k not in arrived:
                copy.wait_recv()

    return start, finish


def call(
    body, ins, in_specs, out_shape, out_specs, *, name, grid=(), prefetch=(), scratch=(), deps=(),
    aliases=None, mib=56, flops=0, moved=0, sends=(), sources=(), lands=(), inner=(), closing=None,
):
    first = len(prefetch) + len(ins)
    single = not isinstance(out_shape, (list, tuple))
    out_shapes = [out_shape] if single else list(out_shape)
    specs = [out_specs] if single else list(out_specs)
    out_count = len(out_shapes)
    land_count = len(lands)

    def wrapped(*refs):
        given = refs[:first]
        refs = refs[first:]
        source_refs = refs[: len(sources)]
        refs = refs[len(sources) + len(deps) :]
        outs, refs = refs[:out_count], refs[out_count:]
        land_refs, refs = refs[:land_count], refs[land_count:]
        if not sends:
            body(*given, *outs, *refs)
            return
        own, (send_sem, recv_sem) = refs[:-2], refs[-2:]
        start, finish = run_sends(
            sends, source_refs, [*land_refs, *[own[k] for k in inner]], send_sem, recv_sem
        )

        def last():
            finish()
            if closing is not None:
                closing(land_refs, (*given, *outs, *own))

        if grid:
            steps = [pl.program_id(k) for k in range(len(grid))]
            begins = functools.reduce(jnp.logical_and, [step == 0 for step in steps])
            ends = functools.reduce(
                jnp.logical_and, [step == size - 1 for step, size in zip(steps, grid)]
            )
            pl.when(begins)(start)
            body(*given, *outs, *own)
            pl.when(ends)(last)
        else:
            start()
            body(*given, *outs, *own)
            last()

    extra = {}
    if sends:
        COLLECTIVE[0] += 1
        extra = {"collective_id": COLLECTIVE[0], "has_side_effects": True}
        scratch = [*scratch] + [pltpu.SemaphoreType.DMA((len(sends),))] * 2
    results = pl.pallas_call(
        wrapped,
        grid_spec=pltpu.PrefetchScalarGridSpec(
            num_scalar_prefetch=len(prefetch),
            grid=grid,
            in_specs=list(in_specs) + [ANY] * (len(sources) + len(deps)),
            out_specs=specs + [ANY] * land_count,
            scratch_shapes=list(scratch),
        ),
        out_shape=out_shapes + [shaped(*land) if isinstance(land[0], tuple) else shaped(land) for land in lands],
        input_output_aliases=aliases or {},
        compiler_params=pltpu.CompilerParams(vmem_limit_bytes=mib * MIB, **extra),
        cost_estimate=pl.CostEstimate(
            flops=int(flops), bytes_accessed=int(moved), transcendentals=0
        ),
        name=name,
    )(*prefetch, *ins, *sources, *deps)
    return results[0] if single and not sends else list(results)


def tables(length_all, head_size):
    inverse = 500000.0 ** (-jnp.arange(0, head_size, 2, dtype=f32) / head_size)
    angles = jnp.arange(length_all, dtype=f32)[:, None] * inverse[None, :]
    angles = jnp.concatenate([angles, angles], axis=1)
    return (jnp.cos(angles), jnp.sin(angles))


def rmsnorm(values, weight_gain):
    return (
        values * lax.rsqrt(jnp.mean(values * values, axis=-1, keepdims=True) + 1e-05) * weight_gain
    )


def positions(owners, wide_count, capacity):
    onehot = (owners[:, None] == jnp.arange(wide_count, dtype=jnp.int32)[None, :]).astype(jnp.int32)
    before = jnp.cumsum(onehot, axis=0) - onehot
    return (owners * capacity + jnp.sum(before * onehot, axis=1), jnp.sum(onehot, axis=0))


def adamw(weight, gradient, moment_one, moment_two, rate, decay):
    moment_one = 0.5 * moment_one + 0.5 * gradient
    moment_two = 0.5 * moment_two + 0.5 * gradient * gradient
    correct = 1.0 - 0.5**STEP
    update = moment_one / correct / (jnp.sqrt(moment_two / correct) + 1e-08)
    return (weight - rate * (update + decay * weight), moment_one, moment_two)


def turn_kernel(unit_ref, out_ref):
    parts, step, piece, unit_rows = out_ref.shape
    for k in range(step):
        out_ref[:, k] = (
            jnp.transpose(unit_ref[k, 0], (1, 0)).reshape(parts, piece, unit_rows).astype(bf16)
        )


def turn_units(master, parts, deps):
    capacity, _, unit_rows, unit_cols = master.shape
    piece = unit_cols // parts
    step = 2 if capacity % 2 == 0 else 1
    return call(
        turn_kernel,
        [master],
        [blocks((step, 1, unit_rows, unit_cols), lambda s: (s, 0, 0, 0))],
        shaped((parts, capacity, piece, unit_rows)),
        blocks((parts, step, piece, unit_rows), lambda s: (0, s, 0, 0)),
        grid=(capacity // step,),
        deps=deps,
        mib=20,
        moved=master.size * 6,
        name="turn_units",
    )


def pick_kernel(turn_ref, place_ref, own_ref, got_ref, out_ref, sem, *, col_blocks):
    _, capacity, piece, unit_rows = got_ref.shape

    def start(unit, carry):
        half = unit // col_blocks
        block = unit - half * col_blocks
        owner = place_ref[unit] // capacity
        slot = place_ref[unit] - owner * capacity
        target = out_ref.at[
            pl.ds(pl.multiple_of(block * piece, piece), piece),
            pl.ds(pl.multiple_of(half * unit_rows, unit_rows), unit_rows),
        ]

        @pl.when(owner == turn_ref[0])
        def _():
            pltpu.make_async_copy(own_ref.at[owner, slot], target, sem).start()

        @pl.when(owner != turn_ref[0])
        def _():
            pltpu.make_async_copy(got_ref.at[owner, slot], target, sem).start()

        return carry

    lax.fori_loop(0, place_ref.shape[0], start, 0)
    pltpu.make_async_copy(out_ref, out_ref, sem).wait()


def pick_units(turn, slot_place, own, got, row_blocks):
    _, _, piece, unit_rows = got.shape
    unit_count = slot_place.shape[0]
    col_blocks = unit_count // row_blocks
    return call(
        functools.partial(pick_kernel, col_blocks=col_blocks),
        [turn, slot_place, own, got],
        [SMEM, SMEM, ANY, ANY],
        shaped((col_blocks * piece, row_blocks * unit_rows)),
        VMEM,
        scratch=[pltpu.SemaphoreType.DMA],
        moved=unit_count * piece * unit_rows * 12,
        name="pick_units",
    )


def unpick_kernel(block_ref, half_ref, rows_ref, low_ref, high_ref, sems, *, piece, unit_rows):
    owners, part, _, _ = low_ref.shape

    def start(owner, carry):
        for slot in range(2 * part):
            out_ref = high_ref if slot >= part else low_ref
            place = owner * 2 * part + slot
            pltpu.make_async_copy(
                rows_ref.at[
                    pl.ds(pl.multiple_of(block_ref[place] * piece, piece), piece),
                    pl.ds(pl.multiple_of(half_ref[place] * unit_rows, unit_rows), unit_rows),
                ],
                out_ref.at[owner, slot % part],
                sems.at[slot // part],
            ).start()
        return carry

    lax.fori_loop(0, owners, start, 0)
    pltpu.make_async_copy(low_ref, low_ref, sems.at[0]).wait()
    pltpu.make_async_copy(high_ref, high_ref, sems.at[1]).wait()


def unpick_units(rows, block_of, half_of, owners, piece, unit_rows):
    slots = block_of.shape[0]
    shape = shaped((owners, slots // owners // 2, piece, unit_rows))
    return call(
        functools.partial(unpick_kernel, piece=piece, unit_rows=unit_rows),
        [block_of, half_of, rows],
        [SMEM, SMEM, VMEM],
        [shape, shape],
        [ANY, ANY],
        scratch=[pltpu.SemaphoreType.DMA((2,))],
        moved=slots * piece * unit_rows * 8,
        name="unpick_units",
    )


def apply_update(gradient, master_ref, one_ref, two_ref, outs):
    grad_out, master_out, copy_out, one_out, two_out = outs
    weight, one, two = adamw(master_ref[0, 0], gradient, one_ref[0, 0], two_ref[0, 0], 0.02, 0.1)
    grad_out[0, 0] = gradient
    master_out[0, 0] = weight
    copy_out[0, 0] = weight.astype(bf16)
    one_out[0, 0] = one
    two_out[0, 0] = two


def unit_gradient(parts, piece, unit_rows):
    return jnp.transpose(parts.astype(f32).reshape(-1, unit_rows), (1, 0))


def all_pieces(grad_ref, own_ref, turn):
    place = lax.broadcasted_iota(jnp.int32, (grad_ref.shape[0], 1, 1), 0)
    return jnp.where(place == turn, own_ref[0].astype(f32), grad_ref[:, 0].astype(f32))


def update_kernel(filled_ref, grad_ref, own_ref, master_ref, one_ref, two_ref, *refs, first):
    piece, unit_rows = grad_ref.shape[2:]
    pieces = all_pieces(grad_ref, own_ref, lax.axis_index("wide"))
    empty = lax.broadcasted_iota(jnp.int32, (unit_rows, 128), 0) * 0 + pl.program_id(0) + first
    gradient = jnp.where(
        empty < filled_ref[0], unit_gradient(pieces, piece, unit_rows), 0.0
    )
    apply_update(gradient, master_ref, one_ref, two_ref, refs[-5:])


def update_outs(master):
    whole = shaped(master.shape, f32)
    return [whole, whole, shaped(master.shape), whole, whole]


def update_units(filled, grads, own, first, master, moment_one, moment_two, done, deps=()):
    _, _, unit_rows, unit_cols = master.shape
    parts, slots, piece, _ = grads.shape
    unit = blocks((1, 1, unit_rows, unit_cols), lambda s, *refs: (s + first, 0, 0, 0))
    return call(
        functools.partial(update_kernel, first=first),
        [filled, grads, own, master, moment_one, moment_two, *done],
        [
            SMEM,
            blocks((parts, 1, piece, unit_rows), lambda s: (0, s, 0, 0)),
            blocks((1, 1, piece, unit_rows), lambda s: (lax.axis_index("wide"), s, 0, 0)),
            unit,
            unit,
            unit,
        ]
        + [ANY] * len(done),
        update_outs(master),
        [unit] * 5,
        grid=(slots,),
        aliases={6 + k: k for k in range(len(done))},
        moved=master.size * 16,
        mib=40,
        deps=deps,
        name="update_units",
    )


def update_attn_kernel(
    slot_ref, block_ref, half_ref, count_ref, mine_ref, near_ref, other_ref, grad_ref, own_ref,
    master_ref, one_ref, two_ref, *refs,
):
    entry = pl.program_id(0)
    parts, _, piece, unit_rows = grad_ref.shape

    @pl.when((entry == 0) | (entry < count_ref[0]))
    def _():
        turn = count_ref[2]
        taken = []
        for j in range(parts):
            e = jnp.bitwise_xor(turn, j)
            near = jnp.where(
                e == 0, mine_ref[...].astype(f32), near_ref[pl.ds(e // 2, 1), 0].astype(f32)
            )
            other = other_ref[pl.ds(e // 2, 1), 0].astype(f32)
            taken.append(jnp.where(e % 2 == 0, near, other))
        attn = jnp.concatenate(taken, axis=0)
        gradient = jnp.where(count_ref[0] > 0, attn, all_pieces(grad_ref, own_ref, turn))
        gradient = unit_gradient(gradient, piece, unit_rows)
        gradient = jnp.where(slot_ref[entry] < count_ref[1], gradient, 0.0)
        apply_update(gradient, master_ref, one_ref, two_ref, refs[-5:])


def update_attn(
    slots, places, halves, count, attn, grads, own, master, moment_one, moment_two, done
):
    _, _, unit_rows, unit_cols = master.shape
    parts, low, piece, _ = grads.shape
    unit = blocks((1, 1, unit_rows, unit_cols), lambda k, slot, *refs: (slot[k], 0, 0, 0))
    given = blocks(
        (parts // 2, 1, piece, unit_rows),
        lambda k, slot, block, half, count: (0, block[k], 0, half[k]),
    )
    return call(
        update_attn_kernel,
        [*attn, grads, own, master, moment_one, moment_two, *done],
        [
            blocks(
                (1, piece, unit_rows),
                lambda k, slot, block, half, count: (block[k], 0, half[k]),
            ),
            given,
            given,
            blocks(
                (parts, 1, piece, unit_rows),
                lambda k, slot, *refs: (0, jnp.minimum(slot[k], low - 1), 0, 0),
            ),
            blocks(
                (1, 1, piece, unit_rows),
                lambda k, slot, block, half, count: (
                    count[2], jnp.minimum(slot[k], low - 1), 0, 0
                ),
            ),
            unit,
            unit,
            unit,
        ]
        + [ANY] * 5,
        update_outs(master),
        [unit] * 5,
        grid=(slots.shape[0],),
        prefetch=[slots, places, halves, count],
        aliases={12 + k: k for k in range(5)},
        moved=master.size * 6,
        mib=40,
        name="update_attn",
    )


def lane_index(shape):
    return lax.broadcasted_iota(jnp.int32, shape, 1)


def rope(tile, cos_tile, sin_tile):
    lower = lane_index(tile.shape) % HD < HD // 2
    ahead = pltpu.roll(tile, LANES - HD // 2, 1)
    behind = pltpu.roll(tile, HD // 2, 1)
    return tile * cos_tile + jnp.where(lower, -ahead, behind) * sin_tile


def unrope(tile, cos_tile, sin_tile):
    lower = lane_index(tile.shape) % HD < HD // 2
    weighted = tile * sin_tile
    ahead = pltpu.roll(weighted, LANES - HD // 2, 1)
    behind = pltpu.roll(weighted, HD // 2, 1)
    return tile * cos_tile + jnp.where(lower, ahead, -behind)


def project_kernel(rows_ref, w_ref, cos_ref, sin_ref, out_ref, *, group_width):
    product = dot(rows_ref[...], w_ref[...], 1, 1)
    for start in range(0, out_ref.shape[1], LANES):
        tile = product[:, start : start + LANES]
        turned = rope(tile, cos_ref[...], sin_ref[...])
        if (start + LANES) % group_width == 0:
            tile = jnp.where(lane_index(tile.shape) < HD, turned, tile).astype(bf16)
        else:
            tile = turned.astype(bf16) * HD ** (-0.5)
        out_ref[:, start : start + LANES] = tile


def project(rows, w_qkv, cos_all, sin_all, group_width, step, deps):
    count = rows.shape[0]
    width = w_qkv.shape[0]
    return call(
        functools.partial(project_kernel, group_width=group_width),
        [rows, w_qkv, cos_all, sin_all],
        [
            blocks((step, D), lambda i: (i, 0)),
            blocks((width, D), lambda i: (0, 0)),
            blocks((step, LANES), lambda i: (i, 0)),
            blocks((step, LANES), lambda i: (i, 0)),
        ],
        shaped((count, width)),
        blocks((step, width), lambda i: (i, 0)),
        grid=(count // step,),
        deps=deps,
        flops=2 * count * width * D,
        name="project",
    )


def extend(tile, kx, vx):
    tile = tile.astype(f32)
    other = pltpu.roll(tile, HD, 1)
    low = lane_index(tile.shape) < HD
    kx[0] = jnp.where(low, tile, 0.0).astype(bf16)
    kx[1] = jnp.where(low, 0.0, other).astype(bf16)
    vx[0] = jnp.where(low, other, 0.0).astype(bf16)
    vx[1] = jnp.where(low, 0.0, tile).astype(bf16)


def forward_kernel(length_ref, qkv_ref, out_ref, log_ref, kx, vx, *, block):
    length = length_ref[0]
    seq_len, group_width = qkv_ref.shape
    pairs = group_width // LANES - 1
    extend(qkv_ref[:, pairs * LANES :], kx, vx)
    row = lax.broadcasted_iota(jnp.int32, (block, block), 0)
    col = lax.broadcasted_iota(jnp.int32, (block, block), 1)
    causal = col <= row
    key_row = lax.broadcasted_iota(jnp.int32, (1, seq_len), 1)
    bias = jnp.where(key_row < length, 0.0, -1e30).astype(f32)
    low = lane_index((block, LANES)) < HD
    for pair in range(pairs):
        lanes = slice(pair * LANES, (pair + 1) * LANES)
        for start in range(0, seq_len, block):
            query = qkv_ref[start : start + block, lanes]
            total = None
            logs = []
            for half in range(2):
                diagonal = dot(query, kx[half, start : start + block, :], 1, 1)
                diagonal = jnp.where(causal, diagonal + bias[:, start : start + block], -1e30)
                peak = jnp.max(diagonal, axis=1, keepdims=True)
                if start:
                    before = dot(query, kx[half, :start, :], 1, 1) + bias[:, :start]
                    peak = jnp.maximum(peak, jnp.max(before, axis=1, keepdims=True))
                    before = jnp.exp(before - peak)
                diagonal = jnp.exp(diagonal - peak)
                row_sum = jnp.sum(diagonal, axis=1, keepdims=True)
                part = dot(diagonal.astype(bf16), vx[half, start : start + block, :], 1, 0)
                if start:
                    row_sum = row_sum + jnp.sum(before, axis=1, keepdims=True)
                    part = part + dot(before.astype(bf16), vx[half, :start, :], 1, 0)
                part = part / row_sum
                total = part if total is None else total + part
                logs.append(peak + jnp.log(row_sum))
            out_ref[start : start + block, lanes] = total.astype(bf16)
            tile = jnp.transpose(jnp.where(low, logs[0], logs[1]), (1, 0))
            log_ref[0, 2 * pair : 2 * pair + 1, start : start + block] = tile[0:1]
            log_ref[0, 2 * pair + 1 : 2 * pair + 2, start : start + block] = tile[HD : HD + 1]


def attend_forward(length, qkv, groups, block, deps=(), **beside):
    seq_len, width = qkv.shape
    group_width = width // groups
    query_width = group_width - LANES
    return call(
        functools.partial(forward_kernel, block=block),
        [length, qkv],
        [SMEM, blocks((seq_len, group_width), lambda g: (0, g))],
        [shaped((seq_len, groups * query_width)), shaped((groups, 8, seq_len), f32)],
        [
            blocks((seq_len, query_width), lambda g: (0, g)),
            blocks((1, 8, seq_len), lambda g: (g, 0, 0)),
        ],
        grid=(groups,),
        scratch=[pltpu.VMEM((2, seq_len, LANES), bf16), pltpu.VMEM((2, seq_len, LANES), bf16)],
        deps=deps,
        mib=48,
        flops=groups * seq_len * seq_len * 2048,
        **beside,
        name="attend_forward",
    )


def backward_kernel(
    length_ref, qkv_ref, back_ref, out_ref, log_ref, cos_ref, sin_ref, *refs, block
):
    grad_ref, kx, vx, dk, dv = refs
    length = length_ref[0]
    seq_len, group_width = qkv_ref.shape
    pairs = group_width // LANES - 1
    extend(qkv_ref[:, pairs * LANES :], kx, vx)
    dk[...] = jnp.zeros(dk.shape, f32)
    dv[...] = jnp.zeros(dv.shape, f32)
    key = lax.broadcasted_iota(jnp.int32, (block, block), 0)
    row = lax.broadcasted_iota(jnp.int32, (block, block), 1)
    causal = key <= row
    for pair in range(pairs):
        lanes = slice(pair * LANES, (pair + 1) * LANES)
        for start in range(0, seq_len, block):
            here = slice(start, start + block)
            query = qkv_ref[here, lanes]
            back = back_ref[here, lanes]
            turned = jnp.transpose(back.astype(f32) * out_ref[here, lanes].astype(f32), (1, 0))
            query_grad = None
            for half in range(2):
                log_row = log_ref[0, 2 * pair + half : 2 * pair + half + 1, here]
                shift = jnp.sum(turned[half * HD : half * HD + HD], axis=0, keepdims=True)
                for first in range(0, start + block, block):
                    keys = slice(first, first + block)
                    scores = dot(kx[half, keys, :], query, 1, 1)
                    probs = jnp.exp(scores - log_row)
                    if first + block > seq_len // 2:
                        probs = jnp.where(key + first < length, probs, 0.0)
                    if first == start:
                        probs = jnp.where(causal, probs, 0.0)
                    probs_back = dot(vx[half, keys, :], back, 1, 1)
                    scores_back = (probs * (probs_back - shift)).astype(bf16)
                    dv[half, keys, :] += dot(probs.astype(bf16), back, 1, 0)
                    dk[half, keys, :] += dot(scores_back, query, 1, 0)
                    part = dot(scores_back, kx[half, keys, :], 0, 0)
                    query_grad = part if query_grad is None else query_grad + part
            query_grad = unrope(query_grad * HD ** (-0.5), cos_ref[here, :], sin_ref[here, :])
            grad_ref[here, lanes] = query_grad.astype(bf16)

    low = lane_index((seq_len, LANES)) < HD
    key_grad = jnp.where(low, dk[0] + pltpu.roll(dk[1], HD, 1), 0.0)
    key_grad = unrope(key_grad, cos_ref[...], sin_ref[...])
    value_grad = pltpu.roll(dv[0], HD, 1) + dv[1]
    grad_ref[:, pairs * LANES :] = jnp.where(low, key_grad, value_grad).astype(bf16)


def attend_backward(group, groups, length, qkv, back, out, logs, cos_all, sin_all, block, deps=(), **beside):
    seq_len, width = qkv.shape
    group_width = width // groups
    query_width = group_width - LANES
    given = blocks((seq_len, query_width), lambda i: (0, group))
    table = blocks((seq_len, LANES), lambda i: (0, 0))
    return call(
        functools.partial(backward_kernel, block=block),
        [length, qkv, back, out, logs, cos_all, sin_all],
        [
            SMEM,
            blocks((seq_len, group_width), lambda i: (0, group)),
            given,
            given,
            blocks((1, 8, seq_len), lambda i: (group, 0, 0)),
            table,
            table,
        ],
        shaped((seq_len, group_width)),
        blocks((seq_len, group_width), lambda i: (0, 0)),
        grid=(1,),
        scratch=[
            pltpu.VMEM((2, seq_len, LANES), bf16),
            pltpu.VMEM((2, seq_len, LANES), bf16),
            pltpu.VMEM((2, seq_len, LANES), f32),
            pltpu.VMEM((2, seq_len, LANES), f32),
        ],
        deps=deps,
        mib=48,
        flops=seq_len * seq_len * 5120,
        **beside,
        name="attend_backward",
    )


def branch_kernel(
    attended_ref, others_ref, w_ref, tokens_ref, gain_ref, residual_ref, normed_ref
):
    parts = others_ref.shape[0] + 1
    step, width = others_ref.shape[1:]
    here = lax.axis_index("narrow")
    first = here * (attended_ref.shape[0] // parts) + pl.program_id(0) * step
    total = tokens_ref[...].astype(f32)
    for k in range(parts):
        part = (
            others_ref[k - 1]
            if k
            else attended_ref[pl.ds(pl.multiple_of(first, step), step), :]
        )
        place = lax.rem(here - k + parts, parts) * width
        total = total + dot(part, w_ref[pl.ds(pl.multiple_of(place, width), width), :], 1, 0)
    residual_ref[...] = total
    normed_ref[...] = rmsnorm(total, gain_ref[...]).astype(bf16)


def branch(attended, others, w_out, tokens, gain, **beside):
    groups, count, width = others.shape
    step = 128
    rows = blocks((step, D), lambda i: (i, 0))
    return call(
        branch_kernel,
        [attended, others, w_out, tokens, gain],
        [
            blocks(attended.shape, lambda i: (0, 0)),
            blocks((groups, step, width), lambda i: (0, i, 0)),
            blocks((D, D), lambda i: (0, 0)),
            rows,
            blocks((1, D), lambda i: (0, 0)),
        ],
        [shaped((count, D), f32), shaped((count, D))],
        [rows, rows],
        grid=(count // step,),
        flops=2 * count * D * D,
        name="branch",
        **beside,
    )


def spread_kernel(turn_ref, back_ref, w_ref, out_ref):
    out_ref[0] = dot(back_ref[...], w_ref[...], 1, 1).astype(bf16)


def spread(turn, back, w_out, groups, deps=()):
    count = back.shape[0]
    width = D // groups
    return call(
        spread_kernel,
        [back, w_out],
        [
            blocks((count, D), lambda i, t: (0, 0)),
            blocks((width, D), lambda i, t: (lax.rem(t[1] + i, groups), 0)),
        ],
        shaped((groups, count, width)),
        blocks((1, count, width), lambda i, t: (i, 0, 0)),
        grid=(groups,),
        prefetch=[turn],
        deps=deps,
        flops=2 * count * D * D,
        mib=32,
        name="spread",
    )


def first_back_kernel(*refs):
    groups = (len(refs) - 1) // 2
    total = sum(dot(refs[g][...], refs[groups + g][...], 1, 0) for g in range(groups))
    refs[-1][...] = total.astype(bf16)


def first_back(qkv_back, w_qkv, step, deps=(), **beside):
    groups = len(qkv_back)
    seq_len, width = qkv_back[0].shape
    return call(
        first_back_kernel,
        [*qkv_back, *([w_qkv] * groups)],
        [blocks((step, width), lambda i: (i, 0))] * groups
        + [blocks((width, D), lambda i, g=g: (g, 0)) for g in range(groups)],
        shaped((seq_len, D)),
        blocks((step, D), lambda i: (i, 0)),
        grid=(seq_len // step,),
        deps=deps,
        flops=2 * seq_len * width * groups * D,
        name="first_back",
        mib=60,
        **beside,
    )


def stream(entry_refs, layout, low, high, buffer, sems, use):
    def copies(i):
        found = []
        for part, (ref, start, end, offset) in enumerate(layout[i]):
            first, last = max(start, low), min(end, high)
            if first < last:
                found.append(
                    pltpu.make_async_copy(
                        entry_refs[ref].at[pl.ds(first - start + offset, last - first)],
                        buffer.at[i % 2, pl.ds(first - low, last - first)],
                        sems.at[i % 2, part],
                    )
                )
        return found

    for copy in copies(0):
        copy.start()
    for i in range(len(layout)):
        if i + 1 < len(layout):
            for copy in copies(i + 1):
                copy.start()
        for copy in copies(i):
            copy.wait()
        use(i, buffer.at[i % 2])


def stream_scratch(rows):
    return [pltpu.VMEM((2, rows, D), bf16), pltpu.SemaphoreType.DMA((2, 3))]


def entry_layout(entries):
    arrays, layout = [], []
    for entry in entries:
        start, parts = 0, []
        for array, offset, count in entry:
            known = [k for k, other in enumerate(arrays) if other is array]
            if not known:
                known = [len(arrays)]
                arrays.append(array)
            parts.append((known[0], start, start + count, offset))
            start += count
        layout.append(parts)
    return arrays, layout, start // 3


def ff_kernel(rows_all_ref, low_ref, high_ref, *refs, layout, size, s, parts):
    hid_all, dgate_all, dup_all, rows_kept, back_kept, term_all, _ = refs[-18:-11]
    total, down, rows_ref, back_ref, hid_ref, dgate_ref, dup_ref, _, buffer, sems, own = refs[-11:]
    count = rows_ref.shape[0]
    half = count // 2
    place = lax.rem(lax.axis_index("narrow") - s + parts, parts)
    low_place = pl.ds(pl.multiple_of(place * half, half), half)
    place = pl.ds(pl.multiple_of(place * count, count), count)
    here = pl.ds(s * count, count)
    copies = [
        pltpu.make_async_copy(rows_all_ref, rows_ref, own.at[0]),
        pltpu.make_async_copy(low_ref.at[low_place], back_ref.at[:half], own.at[1]),
        pltpu.make_async_copy(high_ref.at[low_place], back_ref.at[half:], own.at[4]),
    ]
    for copy in copies:
        copy.start()
    kept = [
        pltpu.make_async_copy(rows_ref, rows_kept.at[here], own.at[2]),
        pltpu.make_async_copy(back_ref, back_kept.at[here], own.at[3]),
    ]

    def use(i, weights):
        if i == 0:
            for copy in copies:
                copy.wait()
            for copy in kept:
                copy.start()
        gate = dot(rows_ref[...], weights[:size], 1, 1)
        up = dot(rows_ref[...], weights[size : 2 * size], 1, 1)
        hidden_back = dot(back_ref[...], weights[2 * size :], 1, 1)
        sig = 1.0 / (1.0 + jnp.exp(-gate))
        silu = gate * sig
        cols = slice(i * size, (i + 1) * size)
        hid = (silu * up).astype(bf16)
        dgate = (hidden_back * up * (sig * (1.0 + gate * (1.0 - sig)))).astype(bf16)
        dup = (hidden_back * silu).astype(bf16)
        hid_ref[:, cols] = hid
        dgate_ref[:, cols] = dgate
        dup_ref[:, cols] = dup
        part = dot(dgate, weights[:size], 1, 0) + dot(dup, weights[size : 2 * size], 1, 0)
        term = dot(hid, weights[2 * size :], 1, 0)
        if i:
            part = part + total[...]
            term = term + down[...]
        total[...] = part
        down[...] = term

    stream(refs, layout, 0, 3 * size, buffer, sems, use)
    for copy in kept:
        copy.wait()
    rows_ref[...] = down[...].astype(bf16)
    copies = [
        pltpu.make_async_copy(hid_ref, hid_all.at[here], own.at[0]),
        pltpu.make_async_copy(dgate_ref, dgate_all.at[here], own.at[1]),
        pltpu.make_async_copy(dup_ref, dup_all.at[here], own.at[2]),
        pltpu.make_async_copy(rows_ref, term_all.at[place], own.at[3]),
    ]
    for copy in copies:
        copy.start()
    for copy in copies:
        copy.wait()


def ff_close(lands, refs, *, added):
    out_ref, total = refs[-12:-10]
    arrived = refs[-4]
    value = total[...]
    if added:
        value = value + arrived[...].astype(f32)
    out_ref[...] = value.astype(out_ref.dtype)


def ff_step(s, rows, back_low, back_high, entries, kept, moving, added=False, last=False):
    count = rows.shape[0]
    seq_len = back_low.shape[0] + back_high.shape[0]
    arrays, layout, size = entry_layout(entries)
    ff_width = size * len(entries)
    return call(
        functools.partial(
            ff_kernel, layout=layout, size=size, s=s, parts=seq_len // count
        ),
        [rows, back_low, back_high, *arrays, *kept],
        [ANY] * (3 + len(arrays) + len(kept)),
        [shaped((seq_len, ff_width))] * 3
        + [shaped((seq_len, D))] * 3
        + [shaped((count, D), f32 if last else bf16)],
        [ANY] * 6 + [VMEM],
        scratch=[pltpu.VMEM((count, D), f32)] * 2
        + [pltpu.VMEM((count, D), bf16)] * 2
        + [pltpu.VMEM((count, ff_width), bf16)] * 3
        + [pltpu.VMEM((count, D), bf16)]
        + stream_scratch(3 * size)
        + [pltpu.SemaphoreType.DMA((5,))],
        aliases={3 + len(arrays) + k: k for k in range(len(kept))},
        mib=60,
        flops=10 * count * ff_width * D,
        name="ff_step",
        sends=[Send(0, 0, "narrow", 1)],
        sources=[moving],
        lands=[] if added else [moving.shape],
        inner=(7,) if added else (),
        closing=functools.partial(ff_close, added=added),
    )


def add_kernel(*refs):
    refs[-1][...] = sum(ref[...].astype(f32) for ref in refs[:-1]).astype(refs[-1].dtype)


def add(terms, kind=bf16, deps=(), **beside):
    count, width = terms[0].shape
    step = 128 if count % 128 == 0 else 64 if count % 64 == 0 else count
    given = blocks((step, width), lambda i: (i, 0))
    return call(
        add_kernel,
        terms,
        [given] * len(terms),
        shaped((count, width), kind),
        given,
        grid=(count // step,),
        deps=deps,
        moved=count * width * 8,
        name="add",
        **beside,
    )


def outer_kernel(first_ref, second_ref, *outs):
    first = first_ref[...]
    if len(first.shape) == 3:
        first = first[0]
    product = dot(first, second_ref[...], 0, 0).astype(bf16)
    each = pl.num_programs(0) // len(outs)
    for k, out_ref in enumerate(outs):

        @pl.when(pl.program_id(0) // each == k)
        def _(out_ref=out_ref):
            out_ref[...] = product


def outer(first, second, split=1, deps=(), **beside):
    rows, width = second.shape
    if len(first.shape) == 3:
        groups, _, step = first.shape
        height = groups * step
        taken = blocks((1, rows, step), lambda i: (i, 0, 0))
    else:
        height = first.shape[1]
        step = next(k for k in (512, 384, 256, 192, LANES) if height % (k * split) == 0)
        taken = blocks((rows, step), lambda i: (0, i))
    each = height // step // split
    return call(
        outer_kernel,
        [first, second],
        [taken, blocks((rows, width), lambda i: (0, 0))],
        [shaped((height // split, width))] * split,
        [
            blocks((step, width), lambda i, k=k: (jnp.clip(i - k * each, 0, each - 1), 0))
            for k in range(split)
        ],
        grid=(height // step,),
        deps=deps,
        mib=56,
        flops=2 * rows * height * width,
        **beside,
        name="outer",
    )


def outer_pair_kernel(first_ref, second_ref, rows_ref, *outs):
    for part, (taken_ref, out_ref) in enumerate(zip((first_ref, second_ref), outs)):

        @pl.when(pl.program_id(0) == part)
        def _(taken_ref=taken_ref, out_ref=out_ref):
            out_ref[...] = dot(taken_ref[...], rows_ref[...], 0, 0).astype(bf16)


def outer_pair(firsts, second, deps=(), **beside):
    rows, height = firsts[0].shape
    width = second.shape[1]
    taken = blocks((rows, height), lambda i: (0, 0))
    return call(
        outer_pair_kernel,
        [*firsts, second],
        [taken, taken, blocks((rows, width), lambda i: (0, 0))],
        [shaped((height, width))] * 2,
        [blocks((height, width), lambda i: (0, 0))] * 2,
        grid=(2,),
        deps=deps,
        flops=4 * rows * height * width,
        name="outer_pair",
        mib=60,
        **beside,
    )


def pass_kernel(*refs):
    pass


def after(value, *deps):
    return call(
        pass_kernel, [value], [ANY], shaped(value.shape, value.dtype), ANY, deps=deps,
        aliases={0: 0}, name="after",
    )


def shift(count, step=1):
    return [(i, (i + step) % count) for i in range(count)]


def flip(value, bits):
    return lax.ppermute(value, "wide", [(i, i ^ bits) for i in range(8)])


def nothing(*refs):
    pass


def sum_places_kernel(place_ref, own_ref, others_ref, out_ref):
    total = jnp.zeros(own_ref.shape, f32)
    for k in range(others_ref.shape[0]):
        total = total + jnp.where(place_ref[0] == k, own_ref[...], others_ref[k])
    out_ref[...] = total


def sum_places(place, own, others):
    return call(
        sum_places_kernel,
        [place, own, others],
        [SMEM, VMEM, VMEM],
        shaped(own.shape, f32),
        VMEM,
        name="sum_places",
    )


def move(sends, sources, lands, deps=()):
    return call(
        nothing, [], [], [], [], sends=sends, sources=sources, lands=lands, deps=deps, name="move"
    )


def rows_at(first, count):
    return lambda wide, narrow: pl.ds(first, count)


def exchange_units(turned):
    return move(
        [
            Send(
                0, 0, "wide", e,
                lambda wide, narrow, e=e: jnp.bitwise_xor(wide, e),
                lambda wide, narrow: wide,
            )
            for e in range(1, turned.shape[0])
        ],
        [turned],
        [turned.shape],
    )[0]


def near_and_across(source, land, at=None, needs=()):
    return [
        Send(source, land, "wide", 2, at, needs=needs),
        Send(source, land + 1, "wide", 4, at, needs=needs),
    ]


def sum_entries_kernel(first_ref, second_ref, *outs):
    total = (first_ref[0].astype(f32) + second_ref[0].astype(f32)).astype(bf16)
    for r, out_ref in enumerate(outs):

        @pl.when(pl.program_id(0) == r)
        def _(out_ref=out_ref):
            out_ref[...] = total


def sum_entries(first, second):
    count, rows, width = first.shape
    given = blocks((1, rows, width), lambda i: (i, 0, 0))
    return call(
        sum_entries_kernel,
        [first, second],
        [given, given],
        [shaped((rows, width))] * count,
        [blocks((rows, width), lambda i: (0, 0))] * count,
        grid=(count,),
        moved=first.size * 6,
        name="sum_entries",
    )


def ff_meet_kernel(own_ref, other_ref, *outs):
    total = (own_ref[...].astype(f32) + other_ref[...].astype(f32)).astype(bf16)
    half = total.shape[0] // 2
    for r in range(3):

        @pl.when(pl.program_id(0) == r)
        def _(r=r):
            outs[r][...] = total

    @pl.when(pl.program_id(0) == 3)
    def _():
        outs[3][...] = total[:half]
        outs[4][...] = total[half:]


def ff_meet(own, other, deps=()):
    height, width = own.shape
    rows = height // 4
    given = blocks((rows, width), lambda i: (i, 0))
    sizes = [rows, rows, rows, rows // 2, rows // 2]
    return call(
        ff_meet_kernel,
        [own, other],
        [given, given],
        [shaped((size, width)) for size in sizes],
        [blocks((size, width), lambda i: (0, 0)) for size in sizes],
        grid=(4,),
        deps=deps,
        moved=own.size * 6,
        name="ff_meet",
    )


def ff_join_kernel(x_ref, first_ref, y_ref, second_ref, x_out, y_out):
    half = first_ref.shape[0]
    x_out[:half] = (x_ref[:half].astype(f32) + first_ref[...].astype(f32)).astype(bf16)
    x_out[half:] = x_ref[half:]
    y_out[:half] = y_ref[:half]
    y_out[half:] = (y_ref[half:].astype(f32) + second_ref[...].astype(f32)).astype(bf16)


def ff_join(met, first, second, deps=()):
    shape = shaped(met[1].shape)
    return call(
        ff_join_kernel,
        [met[1], first, met[2], second],
        [VMEM] * 4,
        [shape, shape],
        [VMEM] * 2,
        deps=deps,
        moved=met[1].size * 8,
        name="ff_join",
    )


def shaped_rows(array, parts):
    return (array.shape[0] // parts, array.shape[1])


def across_sends(source, land):
    return [Send(source, land, "wide", 4), Send(source + 1, land + 1, "wide", 2)]


def near_sends(source, land):
    return [Send(source, land, "wide", 2), Send(source + 1, land + 1, "wide", 4)]


def unit_row(col, query_width, kv_width, by_head, group_width):
    start, offset = col
    if start < query_width:
        return start // by_head * group_width + start % by_head + offset
    start -= query_width
    last = start >= kv_width
    if last:
        start -= kv_width
    head = (start + offset) // HD
    return head * group_width + by_head + last * HD + (start + offset) % HD


def assemble_qkv_kernel(
    turn_ref, own_ref, near_ref, other_ref, out_ref, *, piece, unit_cols, sizes
):
    height = near_ref.shape[1]
    for e in range(8):
        j = jnp.bitwise_xor(turn_ref[0], e)
        for c in range(height // piece):
            here = slice(c * piece, (c + 1) * piece)
            row = unit_row((c * unit_cols, j * piece), *sizes)
            if e % 2:
                value = other_ref[e // 2, here, :]
            elif e:
                value = near_ref[e // 2 - 1, here, :]
            else:
                value = own_ref[here, :]
            out_ref[pl.ds(pl.multiple_of(row, piece), piece), :] = value


def assemble_qkv(turn, rows, near, other, piece, unit_cols, sizes):
    _, height, _ = near.shape
    return call(
        functools.partial(
            assemble_qkv_kernel, piece=piece, unit_cols=unit_cols, sizes=sizes
        ),
        [turn, rows, near, other],
        [SMEM, blocks((height, D), lambda i: (0, 0)), whole_block(near), whole_block(other)],
        shaped((height * 8, D)),
        blocks((height * 8, D), lambda i: (0, 0)),
        grid=(1,),
        mib=32,
        moved=height * 8 * D * 4,
        name="assemble_qkv",
    )


def whole_block(array):
    return blocks(array.shape, lambda i: (0,) * len(array.shape))


def arrange_attn_kernel(turn_ref, *refs, piece, unit_cols, sizes):
    *grads, own_ref, other_ref = refs
    query_width, kv_width, _, group_width = sizes
    out_first = query_width + 2 * kv_width
    for j in range(unit_cols // piece):
        e = jnp.bitwise_xor(turn_ref[0], j)
        for core, out_ref in enumerate((own_ref, other_ref)):

            @pl.when(e % 2 == core)
            def _(j=j, e=e, out_ref=out_ref):
                for c in range(out_ref.shape[1] // piece):
                    if c * unit_cols < out_first:
                        row = unit_row((c * unit_cols, j * piece), *sizes)
                        grad_ref = grads[row // group_width]
                        row = row % group_width
                    else:
                        row = c * unit_cols - out_first + j * piece
                        grad_ref = grads[-1]
                    out_ref[e // 2, c * piece : (c + 1) * piece, :] = grad_ref[
                        row : row + piece, :
                    ]


def arrange_attn(turn, grads, piece, unit_cols, sizes):
    count = unit_cols // piece
    rows = sum(grad.shape[0] for grad in grads) // count
    shape = shaped((count // 2, rows, D))
    return call(
        functools.partial(arrange_attn_kernel, piece=piece, unit_cols=unit_cols, sizes=sizes),
        [turn, *grads],
        [SMEM] + [VMEM] * len(grads),
        [shape, shape],
        [VMEM] * 2,
        mib=32,
        moved=rows * count * D * 4,
        name="arrange_attn",
    )


def out_row(turn_ref, k, c, j, parts, piece, unit_cols, sign):
    n = lax.rem(turn_ref[1] + sign * k + parts, parts)
    return n * (D // parts) + c * unit_cols + j * piece


def assemble_out_kernel(
    turn_ref, rows_ref, z_ref, x_ref, y_ref, across_ref, other_ref, out_ref, *, first, piece,
    unit_cols, parts,
):
    height = z_ref.shape[1]
    for e in range(8):
        j = jnp.bitwise_xor(turn_ref[0], e)
        for k in range(parts):
            for c in range(height // piece):
                here = slice(c * piece, (c + 1) * piece)
                row = out_row(turn_ref, k, c, j, parts, piece, unit_cols, -1)
                if e % 2:
                    value = other_ref[e // 2, k, here, :]
                elif e:
                    value = (x_ref, y_ref, across_ref)[e // 2 - 1][k, here, :]
                elif k:
                    value = z_ref[k - 1, here, :]
                else:
                    value = rows_ref[first + c * piece : first + (c + 1) * piece, :]
                out_ref[pl.ds(pl.multiple_of(row, piece), piece), :] = value


def assemble_out(turn, rows, first, given, piece, unit_cols, parts, deps=()):
    height = given[0].shape[1]
    return call(
        functools.partial(
            assemble_out_kernel, first=first, piece=piece, unit_cols=unit_cols, parts=parts
        ),
        [turn, rows, *given],
        [SMEM, blocks((first + height, D), lambda i: (0, 0))] + [whole_block(a) for a in given],
        shaped((D, D)),
        blocks((D, D), lambda i: (0, 0)),
        grid=(1,),
        mib=52,
        deps=deps,
        moved=D * D * 4,
        name="assemble_out",
    )


def local(
    tokens, cotangent, lengths, owners, master, moment_one, moment_two, norm_gains, gain_first,
    gain_second,
):
    wide_count = lax.axis_size("wide")
    narrow_count = lax.axis_size("narrow")
    capacity, _, unit_rows, unit_cols = master.shape
    unit_count = owners.shape[0]
    row_count = tokens.shape[0]
    seq_len = row_count * narrow_count
    row_blocks = D // unit_rows
    col_blocks = unit_count // row_blocks
    piece = unit_cols // wide_count
    query_width = H // narrow_count * HD
    kv_width = KV // narrow_count * HD
    ff_width = FF // narrow_count
    qkv_width = query_width + 2 * kv_width
    groups = KV // narrow_count
    group_width = qkv_width // groups
    by_head = group_width - 2 * HD
    wide_index = lax.axis_index("wide")
    narrow_index = lax.axis_index("narrow")
    turn = jnp.stack([wide_index, narrow_index]).astype(jnp.int32)
    length = lax.dynamic_slice(lengths, (wide_index,), (1,))
    block = min(256, seq_len)
    qkv_blocks = qkv_width // unit_cols
    out_blocks = query_width // unit_cols
    attn_blocks = qkv_blocks + out_blocks
    sizes = (query_width, kv_width, by_head, group_width)
    back_by = (narrow_index - jnp.arange(narrow_count, dtype=jnp.int32)) % narrow_count

    inputs = tokens.astype(f32)
    normed = rmsnorm(inputs, norm_gains[0]).astype(bf16)
    normed_all = lax.all_gather(normed, "narrow", axis=0, tiled=True)

    slot_place, counts = positions(owners, wide_count, capacity)
    turned = turn_units(master, wide_count, ())
    got = exchange_units(turned)
    rows = pick_units(turn, slot_place, turned, got, row_blocks)
    qkv_rows = qkv_blocks * piece
    out_rows = out_blocks * piece
    ff_first = qkv_rows + out_rows
    ff_rows = 3 * ff_width // wide_count

    qkv_at, out_at = rows_at(0, qkv_rows), rows_at(qkv_rows, out_rows)

    def entry(k):
        return lambda wide, narrow: k

    near_qkv, other_qkv = move(
        [Send(0, 0, "wide", 2 * r, qkv_at, entry(r - 1)) for r in (1, 2, 3)]
        + [Send(0, 1, "wide", 1, qkv_at, entry(0))]
        + [
            Send(0, 1, "wide", 1, entry(r - 1), entry(r), landed=True, needs=(r - 1,))
            for r in (1, 2, 3)
        ],
        [rows],
        [(3, qkv_rows, D), (4, qkv_rows, D)],
    )
    w_qkv = assemble_qkv(turn, rows, near_qkv, other_qkv, piece, unit_cols, sizes)

    cos_table, sin_table = tables(seq_len, HD)
    cos_all = jnp.concatenate([cos_table] * (LANES // HD), axis=1)
    sin_all = jnp.concatenate([sin_table] * (LANES // HD), axis=1)
    low_rows = row_count // 2
    cotangent_then = after(cotangent[:low_rows], normed_all, w_qkv)
    back_low = lax.all_gather(cotangent_then, "narrow", axis=0, tiled=True)
    qkv = project(
        normed_all, w_qkv, cos_all, sin_all, group_width, row_count, (cotangent_then,)
    )
    out_shape = (narrow_count, out_rows, D)

    def first_entry(wide, narrow):
        return 0

    def later_entries(wide, narrow):
        return pl.ds(1, narrow_count - 1)

    third = ff_rows // 3
    attended, logs, narrow_out, x_first, y_first = attend_forward(
        length, qkv, groups, block,
        sends=[
            Send(0, 0, "narrow", k, out_at, entry(k - 1)) for k in range(1, narrow_count)
        ]
        + near_and_across(0, 1, rows_at(ff_first, third)),
        sources=[rows],
        lands=[(narrow_count - 1, out_rows, D), (third, D), (third, D)],
    )

    half = narrow_count // 2

    def heads_of(k):
        return lambda wide, narrow: pl.ds(
            pl.multiple_of(lax.rem(narrow + k, narrow_count) * row_count, row_count), row_count
        )

    def part_of(k, at):
        return lambda wide, narrow: (k, at)

    low_part, high_part = pl.ds(0, half), pl.ds(half, narrow_count - half)
    first_sends = narrow_count - 1
    attended_others, out_x, out_y, out_across, out_other = move(
        [Send(0, 0, "narrow", k, heads_of(k), entry(k - 1)) for k in range(1, narrow_count)]
        + [
            Send(1, 1, "wide", 2, out_at, first_entry),
            Send(2, 1, "wide", 2, None, later_entries),
            Send(1, 2, "wide", 4, out_at, first_entry),
            Send(2, 2, "wide", 4, None, later_entries),
            Send(1, 4, "wide", 1, out_at, lambda w, n: (0, 0)),
            Send(2, 4, "wide", 1, None, lambda w, n: (0, later_entries(w, n))),
            Send(
                1, 3, "wide", 4, lambda w, n: low_part, lambda w, n: low_part, landed=True,
                needs=(first_sends, first_sends + 1),
            ),
            Send(
                2, 3, "wide", 2, lambda w, n: high_part, lambda w, n: high_part, landed=True,
                needs=(first_sends + 2, first_sends + 3),
            ),
            Send(1, 4, "wide", 1, None, entry(1), landed=True),
            Send(2, 4, "wide", 1, None, entry(2), landed=True),
            Send(
                3, 4, "wide", 1, None, entry(3), landed=True,
                needs=(first_sends + 6, first_sends + 7),
            ),
        ],
        [attended, rows, narrow_out],
        [(narrow_count - 1, row_count, query_width)]
        + [out_shape] * 3
        + [(4, *out_shape)],
    )
    back_high = lax.all_gather(
        after(cotangent[low_rows:], attended_others, back_low), "narrow", axis=0, tiled=True
    )
    w_out = assemble_out(
        turn, rows, qkv_rows, [narrow_out, out_x, out_y, out_across, out_other], piece,
        unit_cols, narrow_count,
    )
    sixth = third // 2
    residual, normed_two, x_second, y_second = branch(
        attended, attended_others, w_out, tokens, norm_gains[1:2],
        sends=near_and_across(0, 0, rows_at(ff_first + third, sixth)),
        sources=[rows],
        lands=[(sixth, D), (sixth, D)],
    )

    rest = ff_rows - third - sixth
    block_one, x_third, y_third, *swapped = move(
        [Send(0, 0, "narrow", 1)]
        + near_and_across(1, 1, rows_at(ff_first + third + sixth, rest))
        + [Send(1, 3, "wide", 1, rows_at(ff_first, ff_rows))]
        + [Send(2 + k, 4 + k, "wide", 1) for k in range(4)]
        + [
            Send(1, 8, "wide", 1, landed=True, needs=(1,)),
            Send(2, 9, "wide", 1, landed=True, needs=(2,)),
        ],
        [normed_two, rows, x_first, x_second, y_first, y_second],
        [normed_two.shape, (rest, D), (rest, D), (ff_rows, D)]
        + [(third, D), (sixth, D)] * 2
        + [(rest, D)] * 2,
    )
    own_swap, x_first_swap, x_second_swap, y_first_swap, y_second_swap = swapped[:5]
    x_third_swap, y_third_swap = swapped[5:]
    block_two, across_first, across_second, across_third, *swapped = move(
        [
            Send(0, 0, "narrow", 1),
            Send(1, 1, "wide", 4),
            Send(2, 2, "wide", 4),
            Send(3, 3, "wide", 2),
            Send(1, 4, "wide", 1, landed=True, needs=(1,)),
            Send(2, 5, "wide", 1, landed=True, needs=(2,)),
            Send(3, 6, "wide", 1, landed=True, needs=(3,)),
        ],
        [block_one, x_first, x_second, y_third],
        [block_one.shape] + [(third, D), (sixth, D), (rest, D)] * 2,
    )
    across_swap = swapped

    def pieces(first, second, last):
        return [(first, 0, third), (second, 0, sixth), (last, 0, rest)]

    entries = [
        [(rows, ff_first, ff_rows)],
        pieces(x_first, x_second, x_third),
        pieces(y_first, y_second, y_third),
        pieces(across_first, across_second, across_third),
        [(own_swap, 0, ff_rows)],
        pieces(x_first_swap, x_second_swap, x_third_swap),
        pieces(y_first_swap, y_second_swap, y_third_swap),
        pieces(*across_swap),
    ]

    *kept, total, block_three = ff_step(1, block_one, back_low, back_high, entries, (), block_two)
    *kept, total = ff_step(2, block_two, back_low, back_high, entries, kept, total, True)
    *kept, total = ff_step(3, block_three, back_low, back_high, entries, kept, total, True)
    *kept, norm_two_back = ff_step(0, normed_two, back_low, back_high, entries, kept, total, True, True)
    hidden, dgate, dup, mlp_all, back_kept, ff_term = kept

    _, norm_two_pull = jax.vjp(rmsnorm, residual, norm_gains[1])
    resid_part, gain_two = norm_two_pull(norm_two_back)
    resid_back = cotangent.astype(f32) + resid_part
    attn_back = resid_back.astype(bf16)
    by_heads = spread(turn, attn_back, w_out, narrow_count)

    def heads_send(k, land):
        return Send(0, land, "narrow", k, entry(k))

    heads_shape = (row_count, query_width)
    *grad_down, heads_one, heads_three = outer(
        hidden, back_kept, 2,
        sends=[heads_send(1, 0), heads_send(3, 1)],
        sources=[by_heads],
        lands=[heads_shape, heads_shape],
    )
    half_shape, near_shape = shaped_rows(grad_down[0], 8), shaped_rows(grad_down[0], 4)
    *grad_gate, heads_two, down_swap = outer(
        dgate, mlp_all, 2,
        sends=[heads_send(2, 0), Send(1, 1, "wide", 1)],
        sources=[by_heads, grad_down[1]],
        lands=[heads_shape, grad_down[1].shape],
    )
    out_back = jnp.stack([by_heads[0], heads_one, heads_two, heads_three])
    out_back = jnp.take(out_back, back_by, axis=0).reshape(seq_len, query_width)
    attn_back_all = lax.all_gather(after(attn_back, heads_two), "narrow", axis=0, tiled=True)
    output = residual + lax.psum_scatter(
        after(ff_term, attn_back_all), "narrow", scatter_dimension=0, tiled=True
    ).astype(f32)
    met_down = ff_meet(grad_down[0], down_swap)
    *grad_upper, gate_swap, down_a, down_b = outer(
        dup, mlp_all, 2,
        sends=[Send(0, 0, "wide", 1)] + across_sends(1, 1),
        sources=[grad_gate[1], *met_down[3:]],
        lands=[grad_gate[1].shape, half_shape, half_shape],
    )
    joined_down = ff_join(met_down, down_a, down_b)
    met_gate = ff_meet(grad_gate[0], gate_swap)

    qkv_back = [None, None]
    qkv_back[0], upper_swap, gate_a, gate_b, down_x, down_y = attend_backward(
        0, groups, length, qkv, out_back, attended, logs, cos_all, sin_all, block,
        sends=[Send(0, 0, "wide", 1)] + across_sends(1, 1) + near_sends(3, 3),
        sources=[grad_upper[1], *met_gate[3:], *joined_down],
        lands=[grad_upper[1].shape, half_shape, half_shape, near_shape, near_shape],
    )
    joined_gate = ff_join(met_gate, gate_a, gate_b)
    met_upper = ff_meet(grad_upper[0], upper_swap)
    qkv_back[1], upper_a, upper_b, gate_x, gate_y = attend_backward(
        1, groups, length, qkv, out_back, attended, logs, cos_all, sin_all, block,
        sends=across_sends(0, 0) + near_sends(2, 2),
        sources=[*met_upper[3:], *joined_gate],
        lands=[half_shape] * 2 + [near_shape] * 2,
    )
    joined_upper = ff_join(met_upper, upper_a, upper_b)
    half_rows = near_shape[0] // 2
    halves = [
        [
            Send(0, 0, "wide", 2, rows_at(k * half_rows, half_rows)),
            Send(1, 1, "wide", 4, rows_at(k * half_rows, half_rows)),
        ]
        for k in range(2)
    ]
    norm_one_term, upper_xa, upper_ya = first_back(
        qkv_back, w_qkv, row_count,
        sends=halves[0], sources=list(joined_upper), lands=[half_shape] * 2,
    )
    *grad_qkv, upper_xb, upper_yb = outer_pair(
        qkv_back, normed_all, (norm_one_term,),
        sends=halves[1], sources=list(joined_upper), lands=[half_shape] * 2,
    )
    ff_sums = [
        add([met_gate[0], gate_x, gate_y], deps=(norm_one_term,)),
        add([met_upper[0][:half_rows], upper_xa, upper_ya], deps=(grad_qkv[0],)),
        add([met_upper[0][half_rows:], upper_xb, upper_yb]),
        add([met_down[0], down_x, down_y], deps=(norm_one_term,)),
    ]

    slots = wide_count * capacity
    unit_of = jnp.zeros((slots,), jnp.int32).at[slot_place].set(
        jnp.arange(unit_count, dtype=jnp.int32)
    )
    half_of = unit_of // col_blocks
    block_of = unit_of - half_of * col_blocks
    low, high = unpick_units(
        jnp.concatenate(ff_sums, axis=0),
        jnp.maximum(block_of - attn_blocks, 0),
        half_of,
        wide_count,
        piece,
        unit_rows,
    )

    def by_wide(wide, narrow):
        return wide

    def by_narrow(wide, narrow):
        return narrow

    (grad_out,) = outer(attended, attn_back_all, 1, (grad_qkv[0],))
    own_attn, other_attn = arrange_attn(
        turn, [*grad_qkv, grad_out], piece, unit_cols, sizes
    )
    gain_one = sum(
        jnp.sum(
            w_qkv[g * group_width : (g + 1) * group_width].astype(f32) * grad_qkv[g].astype(f32),
            axis=0,
        )
        for g in range(groups)
    )
    gain_terms = jnp.stack([gain_one / norm_gains[0], gain_two])
    owned_high = lax.all_to_all(high, "wide", split_axis=0, concat_axis=0)
    owned_low, attn_swap, gain_others = move(
        [
            Send(
                0, 0, "wide", e,
                lambda wide, narrow, e=e: jnp.bitwise_xor(wide, e),
                by_wide,
            )
            for e in range(1, wide_count)
        ]
        + [Send(1, 1, "wide", 1)]
        + [Send(2, 2, "wide", e, None, by_wide) for e in range(1, wide_count)],
        [low, other_attn, gain_terms],
        [low.shape, other_attn.shape, ((wide_count, *gain_terms.shape), f32)],
    )
    met_attn = sum_entries(own_attn, attn_swap)
    gain_plane = sum_places(wide_index.reshape(1), gain_terms, gain_others)
    filled = jnp.concatenate(
        [lax.dynamic_slice(counts, (wide_index,), (1,)), wide_index.reshape(1)]
    ).astype(jnp.int32)
    arrived = [flip(met_attn[r], 2 * r) for r in (1, 2, 3)]
    updated = update_units(
        filled, owned_low, low, 0, master, moment_one, moment_two, (), (met_attn[0],)
    )
    gain_others = jnp.stack(
        [gain_plane]
        + [
            after(lax.ppermute(gain_plane, "narrow", shift(narrow_count, k)), updated[0])
            for k in range(1, narrow_count)
        ]
    )
    gain_grads = sum_places(
        narrow_index.reshape(1), gain_plane, jnp.take(gain_others, back_by, axis=0)
    )
    attn_sum = add([met_attn[0]] + arrived, deps=(updated[0],))
    updated = update_units(
        filled, owned_high, owned_high, capacity // 2, master, moment_one, moment_two, updated
    )
    near = [attn_sum] + [
        after(flip(attn_sum, 2 * r), updated[0]) for r in (1, 2, 3)
    ]
    other = [flip(part, 1) for part in near]
    attn_grads = [attn_sum.reshape(attn_blocks, piece, D)] + [
        jnp.stack(part).reshape(wide_count // 2, attn_blocks, piece, D)
        for part in (near, other)
    ]

    first_slot = wide_index * capacity
    own_block = lax.dynamic_slice(block_of, (first_slot,), (capacity,))
    own_half = lax.dynamic_slice(half_of, (first_slot,), (capacity,))
    slot = jnp.arange(capacity, dtype=jnp.int32)
    is_attn = (own_block < attn_blocks) & (slot < filled[0])
    attn_count = jnp.sum(is_attn.astype(jnp.int32))
    rank = jnp.cumsum(is_attn.astype(jnp.int32)) - 1
    listed = min(capacity, attn_blocks * row_blocks)
    wanted = jnp.minimum(jnp.arange(listed, dtype=jnp.int32), jnp.maximum(attn_count - 1, 0))
    chosen = is_attn[None, :] & (rank[None, :] == wanted[:, None])

    def entries_of(values):
        return jnp.sum(jnp.where(chosen, values[None, :], 0), axis=1)

    owned_grads, new_master, new_copy, new_first, new_second = update_attn(
        entries_of(slot), entries_of(own_block), entries_of(own_half),
        jnp.stack([attn_count, filled[0], wide_index]).astype(jnp.int32),
        attn_grads, owned_low, low, master, moment_one, moment_two, updated,
    )

    norm_one_back = lax.psum_scatter(
        norm_one_term, "narrow", scatter_dimension=0, tiled=True
    ).astype(f32)
    _, norm_one_pull = jax.vjp(lambda values: rmsnorm(values, norm_gains[0]), inputs)
    (input_part,) = norm_one_pull(norm_one_back)
    input_grad = (resid_back + input_part).astype(bf16)
    new_gains, _, gain_second_new = adamw(
        norm_gains, gain_grads, gain_first, gain_second, 0.5, 0.0
    )
    return (
        output.astype(bf16),
        input_grad,
        owned_grads,
        new_master,
        new_copy,
        new_first,
        new_second,
        gain_grads,
        gain_second_new,
        new_gains,
    )


def rotate(values, cos_table, sin_table):
    middle = values.shape[-1] // 2
    turned = jnp.concatenate([-values[..., middle:], values[..., :middle]], axis=-1)
    return values * cos_table + turned * sin_table


def unrotate(gradient, cos_table, sin_table):
    middle = gradient.shape[-1] // 2
    weighted = gradient * sin_table
    turned = jnp.concatenate([weighted[..., middle:], -weighted[..., :middle]], axis=-1)
    return gradient * cos_table + turned


def matmul_rows(first_op, second_op):
    return lax.dot_general(
        first_op, second_op, (((0,), (0,)), ((), ())), preferred_element_type=jnp.float32
    )


def matmul_cols(first_op, second_op):
    return lax.dot_general(
        first_op, second_op, (((1,), (1,)), ((), ())), preferred_element_type=jnp.float32
    )


def project_any(normed_all, w_qkv, cos_heads, sin_heads, heads_here, kv_here):
    seq_len = normed_all.shape[0]
    projected = jnp.dot(normed_all, w_qkv, preferred_element_type=jnp.float32)
    query_width = heads_here * HD
    kv_width = kv_here * HD
    group_size = heads_here // kv_here
    query_heads = rotate(
        projected[:, :query_width].reshape(seq_len, heads_here, HD), cos_heads, sin_heads
    )
    key_heads = rotate(
        projected[:, query_width : query_width + kv_width].reshape(seq_len, kv_here, HD),
        cos_heads,
        sin_heads,
    )
    value_heads = projected[:, query_width + kv_width :].reshape(seq_len, kv_here, HD)
    query_heads = jnp.transpose(query_heads.astype(jnp.bfloat16), (1, 0, 2)).reshape(
        kv_here, group_size, seq_len, HD
    )
    key_heads = jnp.transpose(key_heads.astype(jnp.bfloat16), (1, 0, 2))
    value_heads = jnp.transpose(value_heads.astype(jnp.bfloat16), (1, 0, 2))
    return (query_heads, key_heads, value_heads)


def masked_scores(query_block, key_heads, row_start, length):
    block_rows = query_block.shape[2]
    seq_len = key_heads.shape[1]
    scores = jnp.einsum(
        "kgqd,ksd->kgqs", query_block, key_heads, preferred_element_type=jnp.float32
    ) * HD ** (-0.5)
    row_pos = row_start + jnp.arange(block_rows, dtype=jnp.int32)
    key_pos = jnp.arange(seq_len, dtype=jnp.int32)
    allowed = (key_pos[None, :] <= row_pos[:, None]) & (key_pos[None, :] < length)
    return jnp.where(allowed, scores, -1e30)


def attend_forward_any(query_heads, key_heads, value_heads, length, block_rows):
    seq_len = query_heads.shape[2]
    outputs = []
    log_sums = []
    for row_start in range(0, seq_len, block_rows):
        query_block = query_heads[:, :, row_start : row_start + block_rows]
        scores = masked_scores(query_block, key_heads, row_start, length)
        row_peak = jnp.max(scores, axis=-1, keepdims=True)
        raised = jnp.exp(scores - row_peak)
        row_total = jnp.sum(raised, axis=-1, keepdims=True)
        attn_probs = (raised / row_total).astype(jnp.bfloat16)
        outputs.append(
            jnp.einsum(
                "kgqs,ksd->kgqd", attn_probs, value_heads, preferred_element_type=jnp.float32
            )
        )
        log_sums.append((row_peak + jnp.log(row_total))[..., 0])
    return (jnp.concatenate(outputs, axis=2), jnp.concatenate(log_sums, axis=2))


def attend_backward_any(query_heads, key_heads, value_heads, out_back, log_sums, length, block_rows):
    seq_len = query_heads.shape[2]
    query_grads = []
    key_grad = jnp.zeros(key_heads.shape, jnp.float32)
    value_grad = jnp.zeros(value_heads.shape, jnp.float32)
    for row_start in range(0, seq_len, block_rows):
        query_block = query_heads[:, :, row_start : row_start + block_rows]
        back_block = out_back[:, :, row_start : row_start + block_rows]
        scores = masked_scores(query_block, key_heads, row_start, length)
        attn_probs = jnp.exp(scores - log_sums[:, :, row_start : row_start + block_rows, None])
        probs_back = jnp.einsum(
            "kgqd,ksd->kgqs", back_block, value_heads, preferred_element_type=jnp.float32
        )
        row_shift = jnp.sum(attn_probs * probs_back, axis=-1, keepdims=True)
        scores_back = (HD ** (-0.5) * attn_probs * (probs_back - row_shift)).astype(jnp.bfloat16)
        query_grads.append(
            jnp.einsum("kgqs,ksd->kgqd", scores_back, key_heads, preferred_element_type=jnp.float32)
        )
        key_grad = key_grad + jnp.einsum(
            "kgqs,kgqd->ksd", scores_back, query_block, preferred_element_type=jnp.float32
        )
        value_grad = value_grad + jnp.einsum(
            "kgqs,kgqd->ksd",
            attn_probs.astype(jnp.bfloat16),
            back_block,
            preferred_element_type=jnp.float32,
        )
    return (jnp.concatenate(query_grads, axis=2), key_grad, value_grad)


def local_any(
    tokens,
    cotangent,
    lengths,
    owners,
    master,
    moment_one,
    moment_two,
    norm_gains,
    gain_first,
    gain_second,
):
    wide_count = lax.axis_size("wide")
    narrow_count = lax.axis_size("narrow")
    capacity = master.shape[0]
    unit_rows = master.shape[2]
    unit_cols = master.shape[3]
    unit_count = owners.shape[0]
    row_count = tokens.shape[0]
    seq_len = row_count * narrow_count
    slot_place, _ = positions(owners, wide_count, capacity)
    own_slots = master[:, 0].astype(jnp.bfloat16)
    all_slots = lax.all_gather(own_slots, "wide", axis=0, tiled=True)
    unit_data = jnp.take(all_slots, slot_place, axis=0)
    row_blocks = D // unit_rows
    col_blocks = unit_count // row_blocks
    packed = jnp.transpose(
        unit_data.reshape(row_blocks, col_blocks, unit_rows, unit_cols), (0, 2, 1, 3)
    ).reshape(D, col_blocks * unit_cols)
    heads_here = H // narrow_count
    kv_here = KV // narrow_count
    group_size = heads_here // kv_here
    query_width = heads_here * HD
    kv_width = kv_here * HD
    ff_width = FF // narrow_count
    qkv_end = query_width + 2 * kv_width
    out_end = qkv_end + query_width
    gate_end = out_end + 2 * ff_width
    w_qkv = packed[:, :qkv_end]
    w_out_t = packed[:, qkv_end:out_end]
    w_gate_up = packed[:, out_end:gate_end]
    w_down_t = packed[:, gate_end:]
    cos_table, sin_table = tables(seq_len, HD)
    cos_heads = cos_table[:, None, :]
    sin_heads = sin_table[:, None, :]
    block_rows = min(512, seq_len)
    wide_index = lax.axis_index("wide")
    length = lengths[wide_index]
    inputs = tokens.astype(jnp.float32)
    normed = rmsnorm(inputs, norm_gains[0]).astype(jnp.bfloat16)
    normed_all = lax.all_gather(normed, "narrow", axis=0, tiled=True)
    query_heads, key_heads, value_heads = project_any(
        normed_all, w_qkv, cos_heads, sin_heads, heads_here, kv_here
    )
    attended, log_sums = attend_forward_any(query_heads, key_heads, value_heads, length, block_rows)
    attended = (
        jnp.transpose(attended.reshape(heads_here, seq_len, HD), (1, 0, 2))
        .reshape(seq_len, query_width)
        .astype(jnp.bfloat16)
    )
    residual = inputs + lax.psum_scatter(
        matmul_cols(attended, w_out_t), "narrow", scatter_dimension=0, tiled=True
    )
    normed_two = rmsnorm(residual, norm_gains[1]).astype(jnp.bfloat16)
    mlp_input = lax.all_gather(normed_two, "narrow", axis=0, tiled=True)
    gate_up = jnp.dot(mlp_input, w_gate_up, preferred_element_type=jnp.float32)
    hidden = (jax.nn.silu(gate_up[:, :ff_width]) * gate_up[:, ff_width:]).astype(jnp.bfloat16)
    output = residual + lax.psum_scatter(
        matmul_cols(hidden, w_down_t).astype(jnp.bfloat16),
        "narrow",
        scatter_dimension=0,
        tiled=True,
    ).astype(jnp.float32)
    down_back = lax.all_gather(cotangent, "narrow", axis=0, tiled=True)
    mlp_again = lax.all_gather(normed_two, "narrow", axis=0, tiled=True)
    gate_up = jnp.dot(mlp_again, w_gate_up, preferred_element_type=jnp.float32)
    hidden_back = jnp.dot(down_back, w_down_t, preferred_element_type=jnp.float32)
    grad_down_t = matmul_rows(down_back, hidden)
    _, swiglu_pull = jax.vjp(
        lambda gate_in, upper_in: jax.nn.silu(gate_in) * upper_in,
        gate_up[:, :ff_width],
        gate_up[:, ff_width:],
    )
    gate_back, upper_back = swiglu_pull(hidden_back)
    gate_up_back = jnp.concatenate([gate_back, upper_back], axis=1).astype(jnp.bfloat16)
    grad_gate_up = matmul_rows(mlp_again, gate_up_back)
    norm_two_back = lax.psum_scatter(
        matmul_cols(gate_up_back, w_gate_up).astype(jnp.bfloat16),
        "narrow",
        scatter_dimension=0,
        tiled=True,
    ).astype(jnp.float32)
    _, norm_two_pull = jax.vjp(rmsnorm, residual, norm_gains[1])
    resid_part, gain_two = norm_two_pull(norm_two_back)
    resid_back = cotangent.astype(jnp.float32) + resid_part
    attn_back = lax.all_gather(resid_back.astype(jnp.bfloat16), "narrow", axis=0, tiled=True)
    normed_again = lax.all_gather(normed, "narrow", axis=0, tiled=True)
    query_heads, key_heads, value_heads = project_any(
        normed_again, w_qkv, cos_heads, sin_heads, heads_here, kv_here
    )
    out_back = jnp.dot(attn_back, w_out_t, preferred_element_type=jnp.float32).astype(jnp.bfloat16)
    grad_out_t = matmul_rows(attn_back, attended)
    out_back = jnp.transpose(out_back.reshape(seq_len, heads_here, HD), (1, 0, 2)).reshape(
        kv_here, group_size, seq_len, HD
    )
    query_grad, key_grad, value_grad = attend_backward_any(
        query_heads, key_heads, value_heads, out_back, log_sums, length, block_rows
    )
    query_grad = jnp.transpose(query_grad.reshape(heads_here, seq_len, HD), (1, 0, 2))
    query_grad = unrotate(query_grad, cos_heads, sin_heads).reshape(seq_len, query_width)
    key_grad = unrotate(jnp.transpose(key_grad, (1, 0, 2)), cos_heads, sin_heads).reshape(
        seq_len, kv_width
    )
    value_grad = jnp.transpose(value_grad, (1, 0, 2)).reshape(seq_len, kv_width)
    qkv_back = jnp.concatenate([query_grad, key_grad, value_grad], axis=1).astype(jnp.bfloat16)
    grad_qkv = matmul_rows(normed_again, qkv_back)
    norm_one_back = lax.psum_scatter(
        matmul_cols(qkv_back, w_qkv).astype(jnp.bfloat16), "narrow", scatter_dimension=0, tiled=True
    ).astype(jnp.float32)
    _, norm_one_pull = jax.vjp(rmsnorm, inputs, norm_gains[0])
    input_part, gain_one = norm_one_pull(norm_one_back)
    input_grad = (resid_back + input_part).astype(jnp.bfloat16)
    grad_packed = jnp.concatenate([grad_qkv, grad_out_t, grad_gate_up, grad_down_t], axis=1)
    grad_units = jnp.transpose(
        grad_packed.reshape(row_blocks, unit_rows, col_blocks, unit_cols), (0, 2, 1, 3)
    ).reshape(unit_count, unit_rows, unit_cols)
    grad_slots = (
        jnp.zeros((wide_count * capacity, unit_rows, unit_cols), jnp.float32)
        .at[slot_place]
        .set(grad_units)
    )
    owned_grads = lax.psum_scatter(
        grad_slots.astype(jnp.bfloat16), "wide", scatter_dimension=0, tiled=True
    ).astype(jnp.float32)[:, None]
    new_master, new_first, new_second = adamw(
        master, owned_grads, moment_one, moment_two, 0.02, 0.1
    )
    gain_grads = lax.psum(jnp.stack([gain_one, gain_two]), ("wide", "narrow"))
    new_gains, unused, gain_second_new = adamw(
        norm_gains, gain_grads, gain_first, gain_second, 0.5, 0.0
    )
    return (
        output.astype(jnp.bfloat16),
        input_grad,
        owned_grads,
        new_master,
        new_master.astype(jnp.bfloat16),
        new_first,
        new_second,
        gain_grads,
        gain_second_new,
        new_gains,
    )


def solution(mesh):
    COLLECTIVE[0] = 0
    rows = P(("wide", "narrow"), None)
    units = P("wide", "narrow", None, None)
    return jax.shard_map(
        local if mesh.shape["wide"] == 8 and mesh.shape["narrow"] == 4 else local_any,
        mesh=mesh,
        in_specs=(rows, rows, P(), P(), units, units, units, P(), P(), P()),
        out_specs=(rows, rows, units, units, units, units, units, P(), P(), P()),
        check_vma=False,
    )
```

```python
import functools

import jax
import jax.numpy as jnp
import numpy as np
from jax import lax
from jax.experimental import pallas as pl
from jax.experimental.pallas import tpu as pltpu
from jax.sharding import PartitionSpec as P

D = 2048
H = 32
KV = 8
HD = 64
FF = 8192
STEP = 5
LANES = 128
MIB = 1 << 20
ANY = pl.BlockSpec(memory_space=pl.ANY)
VMEM = pl.BlockSpec(memory_space=pltpu.VMEM)
SMEM = pl.BlockSpec(memory_space=pltpu.SMEM)

f32 = jnp.float32
bf16 = jnp.bfloat16


def dot(first_op, second_op, first_dim, second_dim):
    return lax.dot_general(
        first_op,
        second_op,
        (((first_dim,), (second_dim,)), ((), ())),
        preferred_element_type=f32,
    )


def shaped(shape, kind=bf16):
    return jax.ShapeDtypeStruct(shape, kind)


def blocks(shape, place):
    return pl.BlockSpec(shape, place)


class Send:
    def __init__(self, source, land, axis, step, source_at=None, land_at=None, landed=False, needs=()):
        self.source, self.land, self.axis, self.step = source, land, axis, step
        self.source_at, self.land_at = source_at, land_at
        self.landed, self.needs = landed, needs


COLLECTIVE = [0]


def run_sends(sends, sources, lands, send_sem, recv_sem):
    count = lax.axis_size("narrow")
    wide, narrow = lax.axis_index("wide"), lax.axis_index("narrow")

    def target(axis, step):
        if axis == "wide":
            return {"wide": jnp.bitwise_xor(wide, step)}
        return {"narrow": lax.rem(narrow + step, count)}

    copies = []
    for k, send in enumerate(sends):
        ref = (lands if send.landed else sources)[send.source]
        if send.source_at is not None:
            ref = ref.at[send.source_at(wide, narrow)]
        land = lands[send.land]
        if send.land_at is not None:
            land = land.at[send.land_at(wide, narrow)]
        copies.append(
            pltpu.make_async_remote_copy(
                src_ref=ref,
                dst_ref=land,
                send_sem=send_sem.at[k],
                recv_sem=recv_sem.at[k],
                device_id=target(send.axis, send.step),
                device_id_type=pl.DeviceIdType.MESH,
            )
        )

    def start():
        partners = set()
        for send in sends:
            if send.axis == "wide":
                partners.add(("wide", send.step))
            else:
                partners.add(("narrow", send.step % count))
                partners.add(("narrow", -send.step % count))
        barrier = pltpu.get_barrier_semaphore()
        for axis, step in sorted(partners):
            pl.semaphore_signal(
                barrier, inc=1, device_id=target(axis, step), device_id_type=pl.DeviceIdType.MESH
            )
        pl.semaphore_wait(barrier, len(partners))
        for send, copy in zip(sends, copies):
            if not send.needs and not send.landed:
                copy.start()

    def finish():
        arrived = set()
        for send, copy in zip(sends, copies):
            for k in send.needs:
                if k not in arrived:
                    copies[k].wait_recv()
                    arrived.add(k)
            if send.needs or send.landed:
                copy.start()
        for k, copy in enumerate(copies):
            copy.wait_send()
            if k not in arrived:
                copy.wait_recv()

    return start, finish


def call(
    body, ins, in_specs, out_shape, out_specs, *, name, grid=(), prefetch=(), scratch=(), deps=(),
    aliases=None, mib=56, flops=0, moved=0, sends=(), sources=(), lands=(), inner=(), closing=None,
):
    first = len(prefetch) + len(ins)
    single = not isinstance(out_shape, (list, tuple))
    out_shapes = [out_shape] if single else list(out_shape)
    specs = [out_specs] if single else list(out_specs)
    out_count = len(out_shapes)
    land_count = len(lands)

    def wrapped(*refs):
        given = refs[:first]
        refs = refs[first:]
        source_refs = refs[: len(sources)]
        refs = refs[len(sources) + len(deps) :]
        outs, refs = refs[:out_count], refs[out_count:]
        land_refs, refs = refs[:land_count], refs[land_count:]
        if not sends:
            body(*given, *outs, *refs)
            return
        own, (send_sem, recv_sem) = refs[:-2], refs[-2:]
        start, finish = run_sends(
            sends, source_refs, [*land_refs, *[own[k] for k in inner]], send_sem, recv_sem
        )

        def last():
            finish()
            if closing is not None:
                closing(land_refs, (*given, *outs, *own))

        if grid:
            steps = [pl.program_id(k) for k in range(len(grid))]
            begins = functools.reduce(jnp.logical_and, [step == 0 for step in steps])
            ends = functools.reduce(
                jnp.logical_and, [step == size - 1 for step, size in zip(steps, grid)]
            )
            pl.when(begins)(start)
            body(*given, *outs, *own)
            pl.when(ends)(last)
        else:
            start()
            body(*given, *outs, *own)
            last()

    extra = {}
    if sends:
        COLLECTIVE[0] += 1
        extra = {"collective_id": COLLECTIVE[0], "has_side_effects": True}
        scratch = [*scratch] + [pltpu.SemaphoreType.DMA((len(sends),))] * 2
    results = pl.pallas_call(
        wrapped,
        grid_spec=pltpu.PrefetchScalarGridSpec(
            num_scalar_prefetch=len(prefetch),
            grid=grid,
            in_specs=list(in_specs) + [ANY] * (len(sources) + len(deps)),
            out_specs=specs + [ANY] * land_count,
            scratch_shapes=list(scratch),
        ),
        out_shape=out_shapes + [shaped(*land) if isinstance(land[0], tuple) else shaped(land) for land in lands],
        input_output_aliases=aliases or {},
        compiler_params=pltpu.CompilerParams(vmem_limit_bytes=mib * MIB, **extra),
        cost_estimate=pl.CostEstimate(
            flops=int(flops), bytes_accessed=int(moved), transcendentals=0
        ),
        name=name,
    )(*prefetch, *ins, *sources, *deps)
    return results[0] if single and not sends else list(results)


def tables(length_all, head_size):
    inverse = 500000.0 ** (-jnp.arange(0, head_size, 2, dtype=f32) / head_size)
    angles = jnp.arange(length_all, dtype=f32)[:, None] * inverse[None, :]
    angles = jnp.concatenate([angles, angles], axis=1)
    return (jnp.cos(angles), jnp.sin(angles))


def turn_tables(length_all):
    inverse = np.float32(500000.0) ** (-np.arange(0, HD, 2, dtype=np.float32) / np.float32(HD))
    angles = np.arange(length_all, dtype=np.float32)[:, None] * inverse[None, :]
    angles = np.concatenate([angles] * (2 * LANES // HD), axis=1).astype(np.float32)
    return jnp.asarray(np.cos(angles)), jnp.asarray(np.sin(angles))


def rmsnorm(values, weight_gain):
    return (
        values * lax.rsqrt(jnp.mean(values * values, axis=-1, keepdims=True) + 1e-05) * weight_gain
    )


def positions(owners, wide_count, capacity):
    onehot = (owners[:, None] == jnp.arange(wide_count, dtype=jnp.int32)[None, :]).astype(jnp.int32)
    before = jnp.cumsum(onehot, axis=0) - onehot
    return (owners * capacity + jnp.sum(before * onehot, axis=1), jnp.sum(onehot, axis=0))


def adamw(weight, gradient, moment_one, moment_two, rate, decay):
    moment_one = 0.5 * moment_one + 0.5 * gradient
    moment_two = 0.5 * moment_two + 0.5 * gradient * gradient
    correct = 1.0 - 0.5**STEP
    update = moment_one / correct / (jnp.sqrt(moment_two / correct) + 1e-08)
    return (weight - rate * (update + decay * weight), moment_one, moment_two)


def turn_kernel(unit_ref, out_ref):
    parts, step, piece, unit_rows = out_ref.shape
    for k in range(step):
        out_ref[:, k] = (
            jnp.transpose(unit_ref[k, 0], (1, 0)).reshape(parts, piece, unit_rows).astype(bf16)
        )


def turn_units(master, parts, deps):
    capacity, _, unit_rows, unit_cols = master.shape
    piece = unit_cols // parts
    step = 2 if capacity % 2 == 0 else 1
    return call(
        turn_kernel,
        [master],
        [blocks((step, 1, unit_rows, unit_cols), lambda s: (s, 0, 0, 0))],
        shaped((parts, capacity, piece, unit_rows)),
        blocks((parts, step, piece, unit_rows), lambda s: (0, s, 0, 0)),
        grid=(capacity // step,),
        deps=deps,
        mib=20,
        moved=master.size * 6,
        name="turn_units",
    )


def pick_kernel(turn_ref, place_ref, own_ref, got_ref, out_ref, sem, *, col_blocks):
    _, capacity, piece, unit_rows = got_ref.shape

    def start(unit, carry):
        half = unit // col_blocks
        block = unit - half * col_blocks
        owner = place_ref[unit] // capacity
        slot = place_ref[unit] - owner * capacity
        target = out_ref.at[
            pl.ds(pl.multiple_of(block * piece, piece), piece),
            pl.ds(pl.multiple_of(half * unit_rows, unit_rows), unit_rows),
        ]

        @pl.when(owner == turn_ref[0])
        def _():
            pltpu.make_async_copy(own_ref.at[owner, slot], target, sem).start()

        @pl.when(owner != turn_ref[0])
        def _():
            pltpu.make_async_copy(got_ref.at[owner, slot], target, sem).start()

        return carry

    lax.fori_loop(0, place_ref.shape[0], start, 0)
    pltpu.make_async_copy(out_ref, out_ref, sem).wait()


def pick_units(turn, slot_place, own, got, row_blocks):
    _, _, piece, unit_rows = got.shape
    unit_count = slot_place.shape[0]
    col_blocks = unit_count // row_blocks
    return call(
        functools.partial(pick_kernel, col_blocks=col_blocks),
        [turn, slot_place, own, got],
        [SMEM, SMEM, ANY, ANY],
        shaped((col_blocks * piece, row_blocks * unit_rows)),
        VMEM,
        scratch=[pltpu.SemaphoreType.DMA],
        moved=unit_count * piece * unit_rows * 12,
        name="pick_units",
    )


def unpick_kernel(block_ref, half_ref, rows_ref, low_ref, high_ref, sems, *, piece, unit_rows):
    owners, part, _, _ = low_ref.shape
    capacity = part + high_ref.shape[1]

    def start(owner, carry):
        for slot in range(capacity):
            out_ref = high_ref if slot >= part else low_ref
            place = owner * capacity + slot
            pltpu.make_async_copy(
                rows_ref.at[
                    pl.ds(pl.multiple_of(block_ref[place] * piece, piece), piece),
                    pl.ds(pl.multiple_of(half_ref[place] * unit_rows, unit_rows), unit_rows),
                ],
                out_ref.at[owner, slot - part if slot >= part else slot],
                sems.at[int(slot >= part)],
            ).start()
        return carry

    lax.fori_loop(0, owners, start, 0)
    pltpu.make_async_copy(low_ref, low_ref, sems.at[0]).wait()
    pltpu.make_async_copy(high_ref, high_ref, sems.at[1]).wait()


def unpick_units(rows, block_of, half_of, owners, piece, unit_rows):
    slots = block_of.shape[0]
    capacity = slots // owners
    low = capacity // 4 * 2
    sizes = (low, capacity - low)
    return call(
        functools.partial(unpick_kernel, piece=piece, unit_rows=unit_rows),
        [block_of, half_of, rows],
        [SMEM, SMEM, VMEM],
        [shaped((owners, size, piece, unit_rows)) for size in sizes],
        [ANY, ANY],
        scratch=[pltpu.SemaphoreType.DMA((2,))],
        moved=slots * piece * unit_rows * 8,
        name="unpick_units",
    )


def apply_update(gradient, master_ref, one_ref, two_ref, outs, k=0):
    grad_out, master_out, copy_out, one_out, two_out = outs
    weight, one, two = adamw(master_ref[k, 0], gradient, one_ref[k, 0], two_ref[k, 0], 0.02, 0.1)
    grad_out[k, 0] = gradient
    master_out[k, 0] = weight
    copy_out[k, 0] = weight.astype(bf16)
    one_out[k, 0] = one
    two_out[k, 0] = two


def unit_gradient(parts, piece, unit_rows):
    return jnp.transpose(parts.astype(f32).reshape(-1, unit_rows), (1, 0))


def all_pieces(grad_ref, own_ref, turn, k=0):
    place = lax.broadcasted_iota(jnp.int32, (grad_ref.shape[0], 1, 1), 0)
    own = own_ref[0, k : k + 1].astype(f32)
    return jnp.where(place == turn, own, grad_ref[:, k].astype(f32))


def update_kernel(filled_ref, grad_ref, own_ref, master_ref, one_ref, two_ref, *refs, first):
    _, step, piece, unit_rows = grad_ref.shape
    for k in range(step):
        pieces = all_pieces(grad_ref, own_ref, lax.axis_index("wide"), k)
        slot = jnp.zeros((unit_rows, 1), jnp.int32) + (pl.program_id(0) * step + k + first)
        gradient = jnp.where(
            slot < filled_ref[0], unit_gradient(pieces, piece, unit_rows), 0.0
        )
        apply_update(gradient, master_ref, one_ref, two_ref, refs[-5:], k)


def update_outs(master):
    whole = shaped(master.shape, f32)
    return [whole, whole, shaped(master.shape), whole, whole]


def update_units(filled, grads, own, first, master, moment_one, moment_two, done, deps=()):
    _, _, unit_rows, unit_cols = master.shape
    parts, slots, piece, _ = grads.shape
    step = 2 if slots % 2 == 0 and first % 2 == 0 else 1
    unit = blocks((step, 1, unit_rows, unit_cols), lambda s: (s + first // step, 0, 0, 0))
    return call(
        functools.partial(update_kernel, first=first),
        [filled, grads, own, master, moment_one, moment_two, *done],
        [
            SMEM,
            blocks((parts, step, piece, unit_rows), lambda s: (0, s, 0, 0)),
            blocks((1, step, piece, unit_rows), lambda s: (lax.axis_index("wide"), s, 0, 0)),
            unit,
            unit,
            unit,
        ]
        + [ANY] * len(done),
        update_outs(master),
        [unit] * 5,
        grid=(slots // step,),
        aliases={6 + k: k for k in range(len(done))},
        moved=master.size * 16,
        mib=40,
        deps=deps,
        name="update_units",
    )


def update_attn_kernel(
    slot_ref, block_ref, half_ref, count_ref, mine_ref, near_ref, other_ref, grad_ref, own_ref,
    master_ref, one_ref, two_ref, *refs,
):
    entry = pl.program_id(0)
    parts, _, piece, unit_rows = grad_ref.shape

    @pl.when((entry == 0) | (entry < count_ref[0]))
    def _():
        turn = count_ref[2]
        taken = []
        for j in range(parts):
            e = jnp.bitwise_xor(turn, j)
            near = jnp.where(
                e == 0, mine_ref[...].astype(f32), near_ref[pl.ds(e // 2, 1), 0].astype(f32)
            )
            other = other_ref[pl.ds(e // 2, 1), 0].astype(f32)
            taken.append(jnp.where(e % 2 == 0, near, other))
        attn = jnp.concatenate(taken, axis=0)
        gradient = jnp.where(count_ref[0] > 0, attn, all_pieces(grad_ref, own_ref, turn))
        gradient = unit_gradient(gradient, piece, unit_rows)
        gradient = jnp.where(slot_ref[entry] < count_ref[1], gradient, 0.0)
        apply_update(gradient, master_ref, one_ref, two_ref, refs[-5:])


def update_attn(
    slots, places, halves, count, attn, grads, own, master, moment_one, moment_two, done
):
    _, _, unit_rows, unit_cols = master.shape
    parts, low, piece, _ = grads.shape
    unit = blocks((1, 1, unit_rows, unit_cols), lambda k, slot, *refs: (slot[k], 0, 0, 0))
    given = blocks(
        (parts // 2, 1, piece, unit_rows),
        lambda k, slot, block, half, count: (0, block[k], 0, half[k]),
    )
    return call(
        update_attn_kernel,
        [*attn, grads, own, master, moment_one, moment_two, *done],
        [
            blocks(
                (1, piece, unit_rows),
                lambda k, slot, block, half, count: (block[k], 0, half[k]),
            ),
            given,
            given,
            blocks(
                (parts, 1, piece, unit_rows),
                lambda k, slot, *refs: (0, jnp.minimum(slot[k], low - 1), 0, 0),
            ),
            blocks(
                (1, 1, piece, unit_rows),
                lambda k, slot, block, half, count: (
                    count[2], jnp.minimum(slot[k], low - 1), 0, 0
                ),
            ),
            unit,
            unit,
            unit,
        ]
        + [ANY] * 5,
        update_outs(master),
        [unit] * 5,
        grid=(slots.shape[0],),
        prefetch=[slots, places, halves, count],
        aliases={12 + k: k for k in range(5)},
        moved=master.size * 6,
        mib=40,
        name="update_attn",
    )


def lane_index(shape):
    return lax.broadcasted_iota(jnp.int32, shape, 1)


def rope(tile, cos_tile, sin_tile):
    lower = lane_index(tile.shape) % HD < HD // 2
    ahead = pltpu.roll(tile, LANES - HD // 2, 1)
    behind = pltpu.roll(tile, HD // 2, 1)
    return tile * cos_tile + jnp.where(lower, -ahead, behind) * sin_tile


def unrope(tile, cos_tile, sin_tile):
    lower = lane_index(tile.shape) % HD < HD // 2
    weighted = tile * sin_tile
    ahead = pltpu.roll(weighted, LANES - HD // 2, 1)
    behind = pltpu.roll(weighted, HD // 2, 1)
    return tile * cos_tile + jnp.where(lower, ahead, -behind)


def project_kernel(rows_ref, w_ref, cos_ref, sin_ref, out_ref, *, group_width):
    product = dot(rows_ref[...], w_ref[...], 1, 1)
    for start in range(0, out_ref.shape[1], LANES):
        tile = product[:, start : start + LANES]
        turned = rope(tile, cos_ref[...], sin_ref[...])
        if (start + LANES) % group_width == 0:
            tile = jnp.where(lane_index(tile.shape) < HD, turned, tile).astype(bf16)
        else:
            tile = turned.astype(bf16) * HD ** (-0.5)
        out_ref[:, start : start + LANES] = tile


def project(rows, w_qkv, cos_all, sin_all, group_width, step, deps):
    count = rows.shape[0]
    width = w_qkv.shape[0]
    return call(
        functools.partial(project_kernel, group_width=group_width),
        [rows, w_qkv, cos_all, sin_all],
        [
            blocks((step, D), lambda i: (i, 0)),
            blocks((width, D), lambda i: (0, 0)),
            blocks((step, LANES), lambda i: (i, 0)),
            blocks((step, LANES), lambda i: (i, 0)),
        ],
        shaped((count, width)),
        blocks((step, width), lambda i: (i, 0)),
        grid=(count // step,),
        deps=deps,
        flops=2 * count * width * D,
        name="project",
    )


def extend(tile, kx, vx):
    tile = tile.astype(f32)
    other = pltpu.roll(tile, HD, 1)
    low = lane_index(tile.shape) < HD
    kx[0] = jnp.where(low, tile, 0.0).astype(bf16)
    kx[1] = jnp.where(low, 0.0, other).astype(bf16)
    vx[0] = jnp.where(low, other, 0.0).astype(bf16)
    vx[1] = jnp.where(low, 0.0, tile).astype(bf16)


def forward_kernel(length_ref, qkv_ref, out_ref, log_ref, kx, vx, *, block):
    length = length_ref[0]
    seq_len, group_width = qkv_ref.shape
    pairs = group_width // LANES - 1
    extend(qkv_ref[:, pairs * LANES :], kx, vx)
    row = lax.broadcasted_iota(jnp.int32, (block, block), 0)
    col = lax.broadcasted_iota(jnp.int32, (block, block), 1)
    causal = col <= row
    key_row = lax.broadcasted_iota(jnp.int32, (1, seq_len), 1)
    bias = jnp.where(key_row < length, 0.0, -1e30).astype(f32)
    low = lane_index((block, LANES)) < HD
    for pair in range(pairs):
        lanes = slice(pair * LANES, (pair + 1) * LANES)
        for start in range(0, seq_len, block):
            query = qkv_ref[start : start + block, lanes]
            total = None
            logs = []
            for half in range(2):
                diagonal = dot(query, kx[half, start : start + block, :], 1, 1)
                diagonal = jnp.where(causal, diagonal + bias[:, start : start + block], -1e30)
                peak = jnp.max(diagonal, axis=1, keepdims=True)
                if start:
                    before = dot(query, kx[half, :start, :], 1, 1) + bias[:, :start]
                    peak = jnp.maximum(peak, jnp.max(before, axis=1, keepdims=True))
                    before = jnp.exp(before - peak)
                diagonal = jnp.exp(diagonal - peak)
                row_sum = jnp.sum(diagonal, axis=1, keepdims=True)
                part = dot(diagonal.astype(bf16), vx[half, start : start + block, :], 1, 0)
                if start:
                    row_sum = row_sum + jnp.sum(before, axis=1, keepdims=True)
                    part = part + dot(before.astype(bf16), vx[half, :start, :], 1, 0)
                part = part / row_sum
                total = part if total is None else total + part
                logs.append(peak + jnp.log(row_sum))
            out_ref[start : start + block, lanes] = total.astype(bf16)
            tile = jnp.transpose(jnp.where(low, logs[0], logs[1]), (1, 0))
            log_ref[0, 2 * pair : 2 * pair + 1, start : start + block] = tile[0:1]
            log_ref[0, 2 * pair + 1 : 2 * pair + 2, start : start + block] = tile[HD : HD + 1]


def attend_forward(length, qkv, groups, block, deps=(), **beside):
    seq_len, width = qkv.shape
    group_width = width // groups
    query_width = group_width - LANES
    return call(
        functools.partial(forward_kernel, block=block),
        [length, qkv],
        [SMEM, blocks((seq_len, group_width), lambda g: (0, g))],
        [shaped((seq_len, groups * query_width)), shaped((groups, 8, seq_len), f32)],
        [
            blocks((seq_len, query_width), lambda g: (0, g)),
            blocks((1, 8, seq_len), lambda g: (g, 0, 0)),
        ],
        grid=(groups,),
        scratch=[pltpu.VMEM((2, seq_len, LANES), bf16), pltpu.VMEM((2, seq_len, LANES), bf16)],
        deps=deps,
        mib=48,
        flops=groups * seq_len * seq_len * 2048,
        **beside,
        name="attend_forward",
    )


def backward_kernel(
    length_ref, qkv_ref, back_ref, out_ref, log_ref, cos_ref, sin_ref, *refs, block
):
    grad_ref, kx, vx, dk, dv = refs
    length = length_ref[0]
    seq_len, group_width = qkv_ref.shape
    pairs = group_width // LANES - 1
    extend(qkv_ref[:, pairs * LANES :], kx, vx)
    dk[...] = jnp.zeros(dk.shape, f32)
    dv[...] = jnp.zeros(dv.shape, f32)
    key = lax.broadcasted_iota(jnp.int32, (block, block), 0)
    row = lax.broadcasted_iota(jnp.int32, (block, block), 1)
    causal = key <= row
    for pair in range(pairs):
        lanes = slice(pair * LANES, (pair + 1) * LANES)
        for start in range(0, seq_len, block):
            here = slice(start, start + block)
            query = qkv_ref[here, lanes]
            back = back_ref[here, lanes]
            turned = jnp.transpose(back.astype(f32) * out_ref[here, lanes].astype(f32), (1, 0))
            query_grad = None
            for half in range(2):
                log_row = log_ref[0, 2 * pair + half : 2 * pair + half + 1, here]
                shift = jnp.sum(turned[half * HD : half * HD + HD], axis=0, keepdims=True)
                for first in range(0, start + block, block):
                    keys = slice(first, first + block)
                    scores = dot(kx[half, keys, :], query, 1, 1)
                    probs = jnp.exp(scores - log_row)
                    if first + block > seq_len // 2:
                        probs = jnp.where(key + first < length, probs, 0.0)
                    if first == start:
                        probs = jnp.where(causal, probs, 0.0)
                    probs_back = dot(vx[half, keys, :], back, 1, 1)
                    scores_back = (probs * (probs_back - shift)).astype(bf16)
                    dv[half, keys, :] += dot(probs.astype(bf16), back, 1, 0)
                    dk[half, keys, :] += dot(scores_back, query, 1, 0)
                    part = dot(scores_back, kx[half, keys, :], 0, 0)
                    query_grad = part if query_grad is None else query_grad + part
            query_grad = unrope(query_grad * HD ** (-0.5), cos_ref[here, :], sin_ref[here, :])
            grad_ref[here, lanes] = query_grad.astype(bf16)

    low = lane_index((seq_len, LANES)) < HD
    key_grad = jnp.where(low, dk[0] + pltpu.roll(dk[1], HD, 1), 0.0)
    key_grad = unrope(key_grad, cos_ref[...], sin_ref[...])
    value_grad = pltpu.roll(dv[0], HD, 1) + dv[1]
    grad_ref[:, pairs * LANES :] = jnp.where(low, key_grad, value_grad).astype(bf16)


def attend_backward(group, groups, length, qkv, back, out, logs, cos_all, sin_all, block, deps=(), **beside):
    seq_len, width = qkv.shape
    group_width = width // groups
    query_width = group_width - LANES
    given = blocks((seq_len, query_width), lambda i: (0, group))
    table = blocks((seq_len, LANES), lambda i: (0, 0))
    return call(
        functools.partial(backward_kernel, block=block),
        [length, qkv, back, out, logs, cos_all, sin_all],
        [
            SMEM,
            blocks((seq_len, group_width), lambda i: (0, group)),
            given,
            given,
            blocks((1, 8, seq_len), lambda i: (group, 0, 0)),
            table,
            table,
        ],
        shaped((seq_len, group_width)),
        blocks((seq_len, group_width), lambda i: (0, 0)),
        grid=(1,),
        scratch=[
            pltpu.VMEM((2, seq_len, LANES), bf16),
            pltpu.VMEM((2, seq_len, LANES), bf16),
            pltpu.VMEM((2, seq_len, LANES), f32),
            pltpu.VMEM((2, seq_len, LANES), f32),
        ],
        deps=deps,
        mib=48,
        flops=seq_len * seq_len * 5120,
        **beside,
        name="attend_backward",
    )


def branch_kernel(
    attended_ref, others_ref, w_ref, tokens_ref, gain_ref, residual_ref, normed_ref
):
    parts = others_ref.shape[0] + 1
    step, width = others_ref.shape[1:]
    here = lax.axis_index("narrow")
    first = here * (attended_ref.shape[0] // parts) + pl.program_id(0) * step
    total = tokens_ref[...].astype(f32)
    for k in range(parts):
        part = (
            others_ref[k - 1]
            if k
            else attended_ref[pl.ds(pl.multiple_of(first, step), step), :]
        )
        place = lax.rem(here - k + parts, parts) * width
        total = total + dot(part, w_ref[pl.ds(pl.multiple_of(place, width), width), :], 1, 0)
    residual_ref[...] = total
    normed_ref[...] = rmsnorm(total, gain_ref[...]).astype(bf16)


def branch(attended, others, w_out, tokens, gain, **beside):
    groups, count, width = others.shape
    step = 128
    rows = blocks((step, D), lambda i: (i, 0))
    return call(
        branch_kernel,
        [attended, others, w_out, tokens, gain],
        [
            blocks(attended.shape, lambda i: (0, 0)),
            blocks((groups, step, width), lambda i: (0, i, 0)),
            blocks((D, D), lambda i: (0, 0)),
            rows,
            blocks((1, D), lambda i: (0, 0)),
        ],
        [shaped((count, D), f32), shaped((count, D))],
        [rows, rows],
        grid=(count // step,),
        flops=2 * count * D * D,
        name="branch",
        **beside,
    )


def spread_kernel(turn_ref, back_ref, w_ref, out_ref):
    out_ref[0] = dot(back_ref[...], w_ref[...], 1, 1).astype(bf16)


def spread(turn, back, w_out, groups, deps=()):
    count = back.shape[0]
    width = D // groups
    return call(
        spread_kernel,
        [back, w_out],
        [
            blocks((count, D), lambda i, t: (0, 0)),
            blocks((width, D), lambda i, t: (lax.rem(t[1] + i, groups), 0)),
        ],
        shaped((groups, count, width)),
        blocks((1, count, width), lambda i, t: (i, 0, 0)),
        grid=(groups,),
        prefetch=[turn],
        deps=deps,
        flops=2 * count * D * D,
        mib=32,
        name="spread",
    )


def first_back_kernel(*refs):
    groups = (len(refs) - 1) // 2
    total = sum(dot(refs[g][...], refs[groups + g][...], 1, 0) for g in range(groups))
    refs[-1][...] = total.astype(bf16)


def first_back(qkv_back, w_qkv, step, deps=(), **beside):
    groups = len(qkv_back)
    seq_len, width = qkv_back[0].shape
    return call(
        first_back_kernel,
        [*qkv_back, *([w_qkv] * groups)],
        [blocks((step, width), lambda i: (i, 0))] * groups
        + [blocks((width, D), lambda i, g=g: (g, 0)) for g in range(groups)],
        shaped((seq_len, D)),
        blocks((step, D), lambda i: (i, 0)),
        grid=(seq_len // step,),
        deps=deps,
        flops=2 * seq_len * width * groups * D,
        name="first_back",
        mib=60,
        **beside,
    )


def stream(entry_refs, layout, low, high, buffer, sems, use):
    def copies(i):
        found = []
        for part, (ref, start, end, offset) in enumerate(layout[i]):
            first, last = max(start, low), min(end, high)
            if first < last:
                found.append(
                    pltpu.make_async_copy(
                        entry_refs[ref].at[pl.ds(first - start + offset, last - first)],
                        buffer.at[i % 2, pl.ds(first - low, last - first)],
                        sems.at[i % 2, part],
                    )
                )
        return found

    for copy in copies(0):
        copy.start()
    for i in range(len(layout)):
        if i + 1 < len(layout):
            for copy in copies(i + 1):
                copy.start()
        for copy in copies(i):
            copy.wait()
        use(i, buffer.at[i % 2])


def stream_scratch(rows):
    return [pltpu.VMEM((2, rows, D), bf16), pltpu.SemaphoreType.DMA((2, 3))]


def entry_layout(entries):
    arrays, layout = [], []
    for entry in entries:
        start, parts = 0, []
        for array, offset, count in entry:
            known = [k for k, other in enumerate(arrays) if other is array]
            if not known:
                known = [len(arrays)]
                arrays.append(array)
            parts.append((known[0], start, start + count, offset))
            start += count
        layout.append(parts)
    return arrays, layout, start // 3


def ff_kernel(rows_all_ref, low_ref, high_ref, *refs, layout, size, s, parts):
    hid_all, dgate_all, dup_all, rows_kept, back_kept, term_all, _ = refs[-18:-11]
    total, down, rows_ref, back_ref, hid_ref, dgate_ref, dup_ref, _, buffer, sems, own = refs[-11:]
    count = rows_ref.shape[0]
    half = count // 2
    place = lax.rem(lax.axis_index("narrow") - s + parts, parts)
    low_place = pl.ds(pl.multiple_of(place * half, half), half)
    place = pl.ds(pl.multiple_of(place * count, count), count)
    here = pl.ds(s * count, count)
    copies = [
        pltpu.make_async_copy(rows_all_ref, rows_ref, own.at[0]),
        pltpu.make_async_copy(low_ref.at[low_place], back_ref.at[:half], own.at[1]),
        pltpu.make_async_copy(high_ref.at[low_place], back_ref.at[half:], own.at[4]),
    ]
    for copy in copies:
        copy.start()
    kept = [
        pltpu.make_async_copy(rows_ref, rows_kept.at[here], own.at[2]),
        pltpu.make_async_copy(back_ref, back_kept.at[here], own.at[3]),
    ]

    def use(i, weights):
        if i == 0:
            for copy in copies:
                copy.wait()
            for copy in kept:
                copy.start()
        gate = dot(rows_ref[...], weights[:size], 1, 1)
        up = dot(rows_ref[...], weights[size : 2 * size], 1, 1)
        hidden_back = dot(back_ref[...], weights[2 * size :], 1, 1)
        sig = 1.0 / (1.0 + jnp.exp(-gate))
        silu = gate * sig
        cols = slice(i * size, (i + 1) * size)
        hid = (silu * up).astype(bf16)
        dgate = (hidden_back * up * (sig * (1.0 + gate * (1.0 - sig)))).astype(bf16)
        dup = (hidden_back * silu).astype(bf16)
        hid_ref[:, cols] = hid
        dgate_ref[:, cols] = dgate
        dup_ref[:, cols] = dup
        part = dot(dgate, weights[:size], 1, 0) + dot(dup, weights[size : 2 * size], 1, 0)
        term = dot(hid, weights[2 * size :], 1, 0)
        if i:
            part = part + total[...]
            term = term + down[...]
        total[...] = part
        down[...] = term

    stream(refs, layout, 0, 3 * size, buffer, sems, use)
    for copy in kept:
        copy.wait()
    rows_ref[...] = down[...].astype(bf16)
    copies = [
        pltpu.make_async_copy(hid_ref, hid_all.at[here], own.at[0]),
        pltpu.make_async_copy(dgate_ref, dgate_all.at[here], own.at[1]),
        pltpu.make_async_copy(dup_ref, dup_all.at[here], own.at[2]),
        pltpu.make_async_copy(rows_ref, term_all.at[place], own.at[3]),
    ]
    for copy in copies:
        copy.start()
    for copy in copies:
        copy.wait()


def ff_close(lands, refs, *, added):
    out_ref, total = refs[-12:-10]
    arrived = refs[-4]
    value = total[...]
    if added:
        value = value + arrived[...].astype(f32)
    out_ref[...] = value.astype(out_ref.dtype)


def ff_step(s, rows, back_low, back_high, entries, kept, moving, added=False, last=False):
    count = rows.shape[0]
    seq_len = back_low.shape[0] + back_high.shape[0]
    arrays, layout, size = entry_layout(entries)
    ff_width = size * len(entries)
    return call(
        functools.partial(
            ff_kernel, layout=layout, size=size, s=s, parts=seq_len // count
        ),
        [rows, back_low, back_high, *arrays, *kept],
        [ANY] * (3 + len(arrays) + len(kept)),
        [shaped((seq_len, ff_width))] * 3
        + [shaped((seq_len, D))] * 3
        + [shaped((count, D), f32 if last else bf16)],
        [ANY] * 6 + [VMEM],
        scratch=[pltpu.VMEM((count, D), f32)] * 2
        + [pltpu.VMEM((count, D), bf16)] * 2
        + [pltpu.VMEM((count, ff_width), bf16)] * 3
        + [pltpu.VMEM((count, D), bf16)]
        + stream_scratch(3 * size)
        + [pltpu.SemaphoreType.DMA((5,))],
        aliases={3 + len(arrays) + k: k for k in range(len(kept))},
        mib=60,
        flops=10 * count * ff_width * D,
        name="ff_step",
        sends=[Send(0, 0, "narrow", 1)],
        sources=[moving],
        lands=[] if added else [moving.shape],
        inner=(7,) if added else (),
        closing=functools.partial(ff_close, added=added),
    )


def add_kernel(*refs):
    refs[-1][...] = sum(ref[...].astype(f32) for ref in refs[:-1]).astype(refs[-1].dtype)


def add(terms, kind=bf16, deps=(), **beside):
    count, width = terms[0].shape
    step = 128 if count % 128 == 0 else 64 if count % 64 == 0 else count
    given = blocks((step, width), lambda i: (i, 0))
    return call(
        add_kernel,
        terms,
        [given] * len(terms),
        shaped((count, width), kind),
        given,
        grid=(count // step,),
        deps=deps,
        moved=count * width * 8,
        name="add",
        **beside,
    )


def outer_kernel(first_ref, second_ref, *outs):
    first = first_ref[...]
    if len(first.shape) == 3:
        first = first[0]
    product = dot(first, second_ref[...], 0, 0).astype(bf16)
    each = pl.num_programs(0) // len(outs)
    for k, out_ref in enumerate(outs):

        @pl.when(pl.program_id(0) // each == k)
        def _(out_ref=out_ref):
            out_ref[...] = product


def outer(first, second, split=1, deps=(), **beside):
    rows, width = second.shape
    if len(first.shape) == 3:
        groups, _, step = first.shape
        height = groups * step
        taken = blocks((1, rows, step), lambda i: (i, 0, 0))
    else:
        height = first.shape[1]
        step = next(k for k in (512, 384, 256, 192, LANES) if height % (k * split) == 0)
        taken = blocks((rows, step), lambda i: (0, i))
    each = height // step // split
    return call(
        outer_kernel,
        [first, second],
        [taken, blocks((rows, width), lambda i: (0, 0))],
        [shaped((height // split, width))] * split,
        [
            blocks((step, width), lambda i, k=k: (jnp.clip(i - k * each, 0, each - 1), 0))
            for k in range(split)
        ],
        grid=(height // step,),
        deps=deps,
        mib=56,
        flops=2 * rows * height * width,
        **beside,
        name="outer",
    )


def outer_pair_kernel(first_ref, second_ref, rows_ref, *outs):
    for part, (taken_ref, out_ref) in enumerate(zip((first_ref, second_ref), outs)):

        @pl.when(pl.program_id(0) == part)
        def _(taken_ref=taken_ref, out_ref=out_ref):
            out_ref[...] = dot(taken_ref[...], rows_ref[...], 0, 0).astype(bf16)


def outer_pair(firsts, second, deps=(), **beside):
    rows, height = firsts[0].shape
    width = second.shape[1]
    taken = blocks((rows, height), lambda i: (0, 0))
    return call(
        outer_pair_kernel,
        [*firsts, second],
        [taken, taken, blocks((rows, width), lambda i: (0, 0))],
        [shaped((height, width))] * 2,
        [blocks((height, width), lambda i: (0, 0))] * 2,
        grid=(2,),
        deps=deps,
        flops=4 * rows * height * width,
        name="outer_pair",
        mib=60,
        **beside,
    )


def pass_kernel(*refs):
    pass


def after(value, *deps):
    return call(
        pass_kernel, [value], [ANY], shaped(value.shape, value.dtype), ANY, deps=deps,
        aliases={0: 0}, name="after",
    )


def shift(count, step=1):
    return [(i, (i + step) % count) for i in range(count)]


def flip(value, bits):
    return lax.ppermute(value, "wide", [(i, i ^ bits) for i in range(8)])


def nothing(*refs):
    pass


def sum_places_kernel(place_ref, own_ref, others_ref, out_ref):
    total = jnp.zeros(own_ref.shape, f32)
    for k in range(others_ref.shape[0]):
        total = total + jnp.where(place_ref[0] == k, own_ref[...], others_ref[k])
    out_ref[...] = total


def sum_places(place, own, others):
    return call(
        sum_places_kernel,
        [place, own, others],
        [SMEM, VMEM, VMEM],
        shaped(own.shape, f32),
        VMEM,
        name="sum_places",
    )


def move(sends, sources, lands, deps=()):
    return call(
        nothing, [], [], [], [], sends=sends, sources=sources, lands=lands, deps=deps, name="move"
    )


def rows_at(first, count):
    return lambda wide, narrow: pl.ds(first, count)


def exchange_units(turned):
    return move(
        [
            Send(
                0, 0, "wide", e,
                lambda wide, narrow, e=e: jnp.bitwise_xor(wide, e),
                lambda wide, narrow: wide,
            )
            for e in range(1, turned.shape[0])
        ],
        [turned],
        [turned.shape],
    )[0]


def near_and_across(source, land, at=None, needs=()):
    return [
        Send(source, land, "wide", 2, at, needs=needs),
        Send(source, land + 1, "wide", 4, at, needs=needs),
    ]


def sum_entries_kernel(first_ref, second_ref, *outs):
    total = (first_ref[0].astype(f32) + second_ref[0].astype(f32)).astype(bf16)
    for r, out_ref in enumerate(outs):

        @pl.when(pl.program_id(0) == r)
        def _(out_ref=out_ref):
            out_ref[...] = total


def sum_entries(first, second, **beside):
    count, rows, width = first.shape
    given = blocks((1, rows, width), lambda i: (i, 0, 0))
    return call(
        sum_entries_kernel,
        [first, second],
        [given, given],
        [shaped((rows, width))] * count,
        [blocks((rows, width), lambda i: (0, 0))] * count,
        grid=(count,),
        moved=first.size * 6,
        name="sum_entries",
        **beside,
    )


def ff_meet_kernel(own_ref, other_ref, first_out, second_out):
    total = (own_ref[...].astype(f32) + other_ref[...].astype(f32)).astype(bf16)
    half = first_out.shape[0]
    first_out[...] = total[:half]
    second_out[...] = total[half:]


def ff_meet(own, other, deps=()):
    rows, width = own.shape[0] // 4, own.shape[1]
    last = blocks((rows, width), lambda i: (3, 0))
    half = blocks((rows // 2, width), lambda i: (0, 0))
    return call(
        ff_meet_kernel,
        [own, other],
        [last, last],
        [shaped((rows // 2, width))] * 2,
        [half, half],
        grid=(1,),
        deps=deps,
        moved=own.size * 2,
        name="ff_meet",
    )


def ff_join_kernel(
    own_x, other_x, first_ref, own_y, other_y, second_ref, x_out, y_out
):
    half = first_ref.shape[0]
    x = own_x[...].astype(f32) + other_x[...].astype(f32)
    y = own_y[...].astype(f32) + other_y[...].astype(f32)
    x_out[:half] = (x[:half] + first_ref[...].astype(f32)).astype(bf16)
    x_out[half:] = x[half:].astype(bf16)
    y_out[:half] = y[:half].astype(bf16)
    y_out[half:] = (y[half:] + second_ref[...].astype(f32)).astype(bf16)


def ff_join(own, other, first, second, deps=()):
    rows, width = own.shape[0] // 4, own.shape[1]

    def quarter(k):
        return blocks((rows, width), lambda i: (k, 0))

    half = blocks((rows // 2, width), lambda i: (0, 0))
    shape = shaped((rows, width))
    return call(
        ff_join_kernel,
        [own, other, first, own, other, second],
        [quarter(1), quarter(1), half, quarter(2), quarter(2), half],
        [shape, shape],
        [quarter(0), quarter(0)],
        grid=(1,),
        deps=deps,
        moved=own.size * 4,
        name="ff_join",
    )


def ff_end_kernel(*refs):
    refs[-1][...] = sum(ref[...].astype(f32) for ref in refs[:-1]).astype(bf16)


def ff_end(own, other, near, deps=()):
    rows, width = own.shape[0] // 4, own.shape[1]
    first = blocks((rows, width), lambda i: (0, 0))
    return call(
        ff_end_kernel,
        [own, other, *near],
        [first] * (2 + len(near)),
        shaped((rows, width)),
        first,
        grid=(1,),
        deps=deps,
        moved=own.size * 2,
        name="ff_end",
    )


def shaped_rows(array, parts):
    return (array.shape[0] // parts, array.shape[1])


def across_sends(source, land):
    return [Send(source, land, "wide", 4), Send(source + 1, land + 1, "wide", 2)]


def near_sends(source, land):
    return [Send(source, land, "wide", 2), Send(source + 1, land + 1, "wide", 4)]


def unit_row(col, query_width, kv_width, by_head, group_width):
    start, offset = col
    if start < query_width:
        return start // by_head * group_width + start % by_head + offset
    start -= query_width
    last = start >= kv_width
    if last:
        start -= kv_width
    head = (start + offset) // HD
    return head * group_width + by_head + last * HD + (start + offset) % HD


def assemble_qkv_kernel(
    turn_ref, own_ref, near_ref, other_ref, out_ref, *, piece, unit_cols, sizes
):
    height = near_ref.shape[1]
    for e in range(8):
        j = jnp.bitwise_xor(turn_ref[0], e)
        for c in range(height // piece):
            here = slice(c * piece, (c + 1) * piece)
            row = unit_row((c * unit_cols, j * piece), *sizes)
            if e % 2:
                value = other_ref[e // 2, here, :]
            elif e:
                value = near_ref[e // 2 - 1, here, :]
            else:
                value = own_ref[here, :]
            out_ref[pl.ds(pl.multiple_of(row, piece), piece), :] = value


def assemble_qkv(turn, rows, near, other, piece, unit_cols, sizes):
    _, height, _ = near.shape
    return call(
        functools.partial(
            assemble_qkv_kernel, piece=piece, unit_cols=unit_cols, sizes=sizes
        ),
        [turn, rows, near, other],
        [SMEM, blocks((height, D), lambda i: (0, 0)), whole_block(near), whole_block(other)],
        shaped((height * 8, D)),
        blocks((height * 8, D), lambda i: (0, 0)),
        grid=(1,),
        mib=32,
        moved=height * 8 * D * 4,
        name="assemble_qkv",
    )


def whole_block(array):
    return blocks(array.shape, lambda i: (0,) * len(array.shape))


def arrange_attn_kernel(turn_ref, *refs, piece, unit_cols, sizes):
    *grads, own_ref, other_ref = refs
    query_width, kv_width, _, group_width = sizes
    out_first = query_width + 2 * kv_width
    for j in range(unit_cols // piece):
        e = jnp.bitwise_xor(turn_ref[0], j)
        for core, out_ref in enumerate((own_ref, other_ref)):

            @pl.when(e % 2 == core)
            def _(j=j, e=e, out_ref=out_ref):
                for c in range(out_ref.shape[1] // piece):
                    if c * unit_cols < out_first:
                        row = unit_row((c * unit_cols, j * piece), *sizes)
                        grad_ref = grads[row // group_width]
                        row = row % group_width
                    else:
                        row = c * unit_cols - out_first + j * piece
                        grad_ref = grads[-1]
                    out_ref[e // 2, c * piece : (c + 1) * piece, :] = grad_ref[
                        row : row + piece, :
                    ]


def arrange_attn(turn, grads, piece, unit_cols, sizes):
    count = unit_cols // piece
    rows = sum(grad.shape[0] for grad in grads) // count
    shape = shaped((count // 2, rows, D))
    return call(
        functools.partial(arrange_attn_kernel, piece=piece, unit_cols=unit_cols, sizes=sizes),
        [turn, *grads],
        [SMEM] + [VMEM] * len(grads),
        [shape, shape],
        [VMEM] * 2,
        mib=32,
        moved=rows * count * D * 4,
        name="arrange_attn",
    )


def out_row(turn_ref, k, c, j, parts, piece, unit_cols, sign):
    n = lax.rem(turn_ref[1] + sign * k + parts, parts)
    return n * (D // parts) + c * unit_cols + j * piece


def assemble_out_kernel(
    turn_ref, rows_ref, z_ref, x_ref, y_ref, across_ref, other_ref, out_ref, *, first, piece,
    unit_cols, parts,
):
    height = z_ref.shape[1]
    for e in range(8):
        j = jnp.bitwise_xor(turn_ref[0], e)
        for k in range(parts):
            for c in range(height // piece):
                here = slice(c * piece, (c + 1) * piece)
                row = out_row(turn_ref, k, c, j, parts, piece, unit_cols, -1)
                if e % 2:
                    value = other_ref[e // 2, k, here, :]
                elif e:
                    value = (x_ref, y_ref, across_ref)[e // 2 - 1][k, here, :]
                elif k:
                    value = z_ref[k - 1, here, :]
                else:
                    value = rows_ref[first + c * piece : first + (c + 1) * piece, :]
                out_ref[pl.ds(pl.multiple_of(row, piece), piece), :] = value


def assemble_out(turn, rows, first, given, piece, unit_cols, parts, deps=()):
    height = given[0].shape[1]
    return call(
        functools.partial(
            assemble_out_kernel, first=first, piece=piece, unit_cols=unit_cols, parts=parts
        ),
        [turn, rows, *given],
        [SMEM, blocks((first + height, D), lambda i: (0, 0))] + [whole_block(a) for a in given],
        shaped((D, D)),
        blocks((D, D), lambda i: (0, 0)),
        grid=(1,),
        mib=52,
        deps=deps,
        moved=D * D * 4,
        name="assemble_out",
    )


def local(
    tokens, cotangent, lengths, owners, master, moment_one, moment_two, norm_gains, gain_first,
    gain_second,
):
    wide_count = lax.axis_size("wide")
    narrow_count = lax.axis_size("narrow")
    capacity, _, unit_rows, unit_cols = master.shape
    unit_count = owners.shape[0]
    row_count = tokens.shape[0]
    seq_len = row_count * narrow_count
    row_blocks = D // unit_rows
    col_blocks = unit_count // row_blocks
    piece = unit_cols // wide_count
    query_width = H // narrow_count * HD
    kv_width = KV // narrow_count * HD
    ff_width = FF // narrow_count
    qkv_width = query_width + 2 * kv_width
    groups = KV // narrow_count
    group_width = qkv_width // groups
    by_head = group_width - 2 * HD
    wide_index = lax.axis_index("wide")
    narrow_index = lax.axis_index("narrow")
    turn = jnp.stack([wide_index, narrow_index]).astype(jnp.int32)
    length = lax.dynamic_slice(lengths, (wide_index,), (1,))
    block = min(256, seq_len)
    qkv_blocks = qkv_width // unit_cols
    out_blocks = query_width // unit_cols
    attn_blocks = qkv_blocks + out_blocks
    sizes = (query_width, kv_width, by_head, group_width)
    back_by = (narrow_index - jnp.arange(narrow_count, dtype=jnp.int32)) % narrow_count

    inputs = tokens.astype(f32)
    normed = rmsnorm(inputs, norm_gains[0]).astype(bf16)
    normed_all = lax.all_gather(normed, "narrow", axis=0, tiled=True)

    slot_place, counts = positions(owners, wide_count, capacity)
    turned = turn_units(master, wide_count, ())
    got = exchange_units(turned)
    rows = pick_units(turn, slot_place, turned, got, row_blocks)
    qkv_rows = qkv_blocks * piece
    out_rows = out_blocks * piece
    ff_first = qkv_rows + out_rows
    ff_rows = 3 * ff_width // wide_count

    qkv_at, out_at = rows_at(0, qkv_rows), rows_at(qkv_rows, out_rows)

    def entry(k):
        return lambda wide, narrow: k

    near_qkv, other_qkv = move(
        [Send(0, 0, "wide", 2 * r, qkv_at, entry(r - 1)) for r in (1, 2, 3)]
        + [Send(0, 1, "wide", 1, qkv_at, entry(0))]
        + [
            Send(0, 1, "wide", 1, entry(r - 1), entry(r), landed=True, needs=(r - 1,))
            for r in (1, 2, 3)
        ],
        [rows],
        [(3, qkv_rows, D), (4, qkv_rows, D)],
    )
    w_qkv = assemble_qkv(turn, rows, near_qkv, other_qkv, piece, unit_cols, sizes)

    cos_all, sin_all = turn_tables(seq_len)
    low_rows = row_count // 2
    cotangent_then = after(cotangent[:low_rows], normed_all, w_qkv)
    back_low = lax.all_gather(cotangent_then, "narrow", axis=0, tiled=True)
    qkv = project(
        normed_all, w_qkv, cos_all, sin_all, group_width, row_count, (cotangent_then,)
    )
    out_shape = (narrow_count, out_rows, D)

    def first_entry(wide, narrow):
        return 0

    def later_entries(wide, narrow):
        return pl.ds(1, narrow_count - 1)

    third = ff_rows // 3
    attended, logs, narrow_out, x_first, y_first = attend_forward(
        length, qkv, groups, block,
        sends=[
            Send(0, 0, "narrow", k, out_at, entry(k - 1)) for k in range(1, narrow_count)
        ]
        + near_and_across(0, 1, rows_at(ff_first, third)),
        sources=[rows],
        lands=[(narrow_count - 1, out_rows, D), (third, D), (third, D)],
    )

    half = narrow_count // 2

    def heads_of(k):
        return lambda wide, narrow: pl.ds(
            pl.multiple_of(lax.rem(narrow + k, narrow_count) * row_count, row_count), row_count
        )

    def part_of(k, at):
        return lambda wide, narrow: (k, at)

    low_part, high_part = pl.ds(0, half), pl.ds(half, narrow_count - half)
    first_sends = narrow_count - 1
    attended_others, out_x, out_y, out_across, out_other = move(
        [Send(0, 0, "narrow", k, heads_of(k), entry(k - 1)) for k in range(1, narrow_count)]
        + [
            Send(1, 1, "wide", 2, out_at, first_entry),
            Send(2, 1, "wide", 2, None, later_entries),
            Send(1, 2, "wide", 4, out_at, first_entry),
            Send(2, 2, "wide", 4, None, later_entries),
            Send(1, 4, "wide", 1, out_at, lambda w, n: (0, 0)),
            Send(2, 4, "wide", 1, None, lambda w, n: (0, later_entries(w, n))),
            Send(
                1, 3, "wide", 4, lambda w, n: low_part, lambda w, n: low_part, landed=True,
                needs=(first_sends, first_sends + 1),
            ),
            Send(
                2, 3, "wide", 2, lambda w, n: high_part, lambda w, n: high_part, landed=True,
                needs=(first_sends + 2, first_sends + 3),
            ),
            Send(1, 4, "wide", 1, None, entry(1), landed=True),
            Send(2, 4, "wide", 1, None, entry(2), landed=True),
            Send(
                3, 4, "wide", 1, None, entry(3), landed=True,
                needs=(first_sends + 6, first_sends + 7),
            ),
        ],
        [attended, rows, narrow_out],
        [(narrow_count - 1, row_count, query_width)]
        + [out_shape] * 3
        + [(4, *out_shape)],
    )
    back_high = lax.all_gather(
        after(cotangent[low_rows:], attended_others, back_low), "narrow", axis=0, tiled=True
    )
    w_out = assemble_out(
        turn, rows, qkv_rows, [narrow_out, out_x, out_y, out_across, out_other], piece,
        unit_cols, narrow_count,
    )
    residual, normed_two = branch(
        attended, attended_others, w_out, tokens, norm_gains[1:2]
    )

    rest = ff_rows - third
    half_rest = ff_rows // 2 - third
    block_one, x_last, y_last, own_swap, x_first_swap, y_first_swap, x_last_swap, y_last_swap = move(
        [Send(0, 0, "narrow", 1)]
        + near_and_across(1, 1, rows_at(ff_first + third, rest))
        + [Send(1, 3, "wide", 1, rows_at(ff_first, ff_rows))]
        + [Send(2, 4, "wide", 1), Send(3, 5, "wide", 1)]
        + [
            Send(1, 6, "wide", 1, landed=True, needs=(1,)),
            Send(2, 7, "wide", 1, landed=True, needs=(2,)),
        ],
        [normed_two, rows, x_first, y_first],
        [normed_two.shape, (rest, D), (rest, D), (ff_rows, D)]
        + [(third, D)] * 2
        + [(rest, D)] * 2,
    )
    block_two, *across = move(
        [
            Send(0, 0, "narrow", 1),
            Send(1, 1, "wide", 4),
            Send(2, 2, "wide", 4, rows_at(0, half_rest)),
            Send(3, 3, "wide", 2, rows_at(half_rest, ff_rows // 2)),
            Send(1, 4, "wide", 1, landed=True, needs=(1,)),
            Send(2, 5, "wide", 1, landed=True, needs=(2,)),
            Send(3, 6, "wide", 1, landed=True, needs=(3,)),
        ],
        [block_one, x_first, x_last, y_last],
        [block_one.shape] + [(third, D), (half_rest, D), (ff_rows // 2, D)] * 2,
    )

    def pieces(*arrays):
        return [(array, 0, array.shape[0]) for array in arrays]

    entries = [
        [(rows, ff_first, ff_rows)],
        pieces(x_first, x_last),
        pieces(y_first, y_last),
        pieces(*across[:3]),
        [(own_swap, 0, ff_rows)],
        pieces(x_first_swap, x_last_swap),
        pieces(y_first_swap, y_last_swap),
        pieces(*across[3:]),
    ]

    *kept, total, block_three = ff_step(1, block_one, back_low, back_high, entries, (), block_two)
    *kept, total = ff_step(2, block_two, back_low, back_high, entries, kept, total, True)
    *kept, total = ff_step(3, block_three, back_low, back_high, entries, kept, total, True)
    *kept, norm_two_back = ff_step(0, normed_two, back_low, back_high, entries, kept, total, True, True)
    hidden, dgate, dup, mlp_all, back_kept, ff_term = kept

    _, norm_two_pull = jax.vjp(rmsnorm, residual, norm_gains[1])
    resid_part, gain_two = norm_two_pull(norm_two_back)
    resid_back = cotangent.astype(f32) + resid_part
    attn_back = resid_back.astype(bf16)
    by_heads = spread(turn, attn_back, w_out, narrow_count)

    def heads_send(k, land):
        return Send(0, land, "narrow", k, entry(k))

    heads_shape = (row_count, query_width)
    *grad_down, heads_one, heads_three = outer(
        hidden, back_kept, 2,
        sends=[heads_send(1, 0), heads_send(3, 1)],
        sources=[by_heads],
        lands=[heads_shape, heads_shape],
    )
    half_shape, near_shape = shaped_rows(grad_down[0], 8), shaped_rows(grad_down[0], 4)
    *grad_gate, heads_two, down_swap = outer(
        dgate, mlp_all, 2,
        sends=[heads_send(2, 0), Send(1, 1, "wide", 1)],
        sources=[by_heads, grad_down[1]],
        lands=[heads_shape, grad_down[1].shape],
    )
    out_back = jnp.stack([by_heads[0], heads_one, heads_two, heads_three])
    out_back = jnp.take(out_back, back_by, axis=0).reshape(seq_len, query_width)
    ff_sum = lax.psum_scatter(
        after(ff_term, heads_two), "narrow", scatter_dimension=0, tiled=True
    )
    output = residual + ff_sum.astype(f32)
    down_across = ff_meet(grad_down[0], down_swap)
    *grad_upper, gate_swap, down_a, down_b = outer(
        dup, mlp_all, 2,
        sends=[Send(0, 0, "wide", 1)] + across_sends(1, 1),
        sources=[grad_gate[1], *down_across],
        lands=[grad_gate[1].shape, half_shape, half_shape],
    )
    joined_down = ff_join(grad_down[0], down_swap, down_a, down_b)
    gate_across = ff_meet(grad_gate[0], gate_swap)

    qkv_back = [None, None]
    qkv_back[0], upper_swap, gate_a, gate_b, down_x, down_y = attend_backward(
        0, groups, length, qkv, out_back, attended, logs, cos_all, sin_all, block,
        sends=[Send(0, 0, "wide", 1)] + across_sends(1, 1) + near_sends(3, 3),
        sources=[grad_upper[1], *gate_across, *joined_down],
        lands=[grad_upper[1].shape, half_shape, half_shape, near_shape, near_shape],
    )
    upper_across = ff_meet(grad_upper[0], upper_swap)
    joined_gate = ff_join(grad_gate[0], gate_swap, gate_a, gate_b)
    qkv_back[1], upper_a, upper_b, gate_x, gate_y = attend_backward(
        1, groups, length, qkv, out_back, attended, logs, cos_all, sin_all, block,
        sends=across_sends(0, 0) + near_sends(2, 2),
        sources=[*upper_across, *joined_gate],
        lands=[half_shape] * 2 + [near_shape] * 2,
    )
    attn_back_all = lax.all_gather(
        after(attn_back, ff_sum, qkv_back[1]), "narrow", axis=0, tiled=True
    )
    joined_upper = ff_join(grad_upper[0], upper_swap, upper_a, upper_b)
    half_rows = near_shape[0] // 2
    halves = [
        [
            Send(0, 0, "wide", 2, rows_at(k * half_rows, half_rows)),
            Send(1, 1, "wide", 4, rows_at(k * half_rows, half_rows)),
        ]
        for k in range(2)
    ]
    norm_one_term, upper_xa, upper_ya = first_back(
        qkv_back, w_qkv, row_count,
        sends=halves[0], sources=list(joined_upper), lands=[half_shape] * 2,
    )
    down_sum = ff_end(grad_down[0], down_swap, [down_x, down_y], (norm_one_term,))
    gate_sum = ff_end(grad_gate[0], gate_swap, [gate_x, gate_y], (norm_one_term,))
    *grad_qkv, upper_xb, upper_yb = outer_pair(
        qkv_back, normed_all, (norm_one_term,),
        sends=halves[1], sources=list(joined_upper), lands=[half_shape] * 2,
    )
    upper_sum = ff_end(
        grad_upper[0], upper_swap,
        [
            jnp.concatenate([upper_xa, upper_xb], axis=0),
            jnp.concatenate([upper_ya, upper_yb], axis=0),
        ],
    )
    ff_sums = [gate_sum, upper_sum, down_sum]

    slots = wide_count * capacity
    unit_of = jnp.zeros((slots,), jnp.int32).at[slot_place].set(
        jnp.arange(unit_count, dtype=jnp.int32)
    )
    half_of = unit_of // col_blocks
    block_of = unit_of - half_of * col_blocks
    low, high = unpick_units(
        jnp.concatenate(ff_sums, axis=0),
        jnp.maximum(block_of - attn_blocks, 0),
        half_of,
        wide_count,
        piece,
        unit_rows,
    )

    def by_wide(wide, narrow):
        return wide

    def by_narrow(wide, narrow):
        return narrow

    gain_one = sum(
        jnp.sum(
            w_qkv[g * group_width : (g + 1) * group_width].astype(f32) * grad_qkv[g].astype(f32),
            axis=0,
        )
        for g in range(groups)
    )
    gain_terms = jnp.stack([gain_one / norm_gains[0], gain_two])
    owned_low, gain_others = move(
        [
            Send(
                0, 0, "wide", e,
                lambda wide, narrow, e=e: jnp.bitwise_xor(wide, e),
                by_wide,
            )
            for e in range(1, wide_count)
        ]
        + [Send(1, 1, "wide", e, None, by_wide) for e in range(1, wide_count)],
        [low, gain_terms],
        [low.shape, ((wide_count, *gain_terms.shape), f32)],
    )
    owned_high = lax.all_to_all(after(high, owned_low), "wide", split_axis=0, concat_axis=0)
    gain_plane = sum_places(wide_index.reshape(1), gain_terms, gain_others)
    (grad_out,) = outer(attended, attn_back_all, 1, (owned_low,))
    own_attn, other_attn = arrange_attn(
        turn, [*grad_qkv, grad_out], piece, unit_cols, sizes
    )
    attn_swap, gain_others = move(
        [Send(0, 0, "wide", 1)]
        + [Send(1, 1, "narrow", k, None, by_narrow) for k in range(1, narrow_count)],
        [other_attn, gain_plane],
        [other_attn.shape, ((narrow_count, *gain_terms.shape), f32)],
    )
    met_attn = sum_entries(own_attn, attn_swap)
    gain_grads = sum_places(narrow_index.reshape(1), gain_plane, gain_others)
    filled = jnp.concatenate(
        [lax.dynamic_slice(counts, (wide_index,), (1,)), wide_index.reshape(1)]
    ).astype(jnp.int32)
    arrived = [flip(met_attn[r], 2 * r) for r in (1, 2, 3)]
    updated = update_units(
        filled, owned_low, low, 0, master, moment_one, moment_two, (), (met_attn[0],)
    )
    attn_sum = add([met_attn[0]] + [after(part, updated[0]) for part in arrived])
    near = [flip(attn_sum, 2 * r) for r in (1, 2, 3)]
    updated = update_units(
        filled, owned_high, owned_high, low.shape[1], master, moment_one, moment_two, updated,
        (attn_sum,),
    )
    near = [attn_sum] + [after(part, updated[0]) for part in near]
    other = [flip(part, 1) for part in near]
    attn_grads = [attn_sum.reshape(attn_blocks, piece, D)] + [
        jnp.stack(part).reshape(wide_count // 2, attn_blocks, piece, D)
        for part in (near, other)
    ]

    first_slot = wide_index * capacity
    own_block = lax.dynamic_slice(block_of, (first_slot,), (capacity,))
    own_half = lax.dynamic_slice(half_of, (first_slot,), (capacity,))
    slot = jnp.arange(capacity, dtype=jnp.int32)
    is_attn = (own_block < attn_blocks) & (slot < filled[0])
    attn_count = jnp.sum(is_attn.astype(jnp.int32))
    rank = jnp.cumsum(is_attn.astype(jnp.int32)) - 1
    listed = min(capacity, attn_blocks * row_blocks)
    wanted = jnp.minimum(jnp.arange(listed, dtype=jnp.int32), jnp.maximum(attn_count - 1, 0))
    chosen = is_attn[None, :] & (rank[None, :] == wanted[:, None])

    def entries_of(values):
        return jnp.sum(jnp.where(chosen, values[None, :], 0), axis=1)

    owned_grads, new_master, new_copy, new_first, new_second = update_attn(
        entries_of(slot), entries_of(own_block), entries_of(own_half),
        jnp.stack([attn_count, filled[0], wide_index]).astype(jnp.int32),
        attn_grads, owned_low, low, master, moment_one, moment_two, updated,
    )

    norm_one_back = lax.psum_scatter(
        norm_one_term, "narrow", scatter_dimension=0, tiled=True
    )
    norm_one_back = after(norm_one_back, owned_grads).astype(f32)
    _, norm_one_pull = jax.vjp(lambda values: rmsnorm(values, norm_gains[0]), inputs)
    (input_part,) = norm_one_pull(norm_one_back)
    input_grad = (resid_back + input_part).astype(bf16)
    new_gains, _, gain_second_new = adamw(
        norm_gains, gain_grads, gain_first, gain_second, 0.5, 0.0
    )
    return (
        output.astype(bf16),
        input_grad,
        owned_grads,
        new_master,
        new_copy,
        new_first,
        new_second,
        gain_grads,
        gain_second_new,
        new_gains,
    )


def rotate(values, cos_table, sin_table):
    middle = values.shape[-1] // 2
    turned = jnp.concatenate([-values[..., middle:], values[..., :middle]], axis=-1)
    return values * cos_table + turned * sin_table


def unrotate(gradient, cos_table, sin_table):
    middle = gradient.shape[-1] // 2
    weighted = gradient * sin_table
    turned = jnp.concatenate([weighted[..., middle:], -weighted[..., :middle]], axis=-1)
    return gradient * cos_table + turned


def matmul_rows(first_op, second_op):
    return lax.dot_general(
        first_op, second_op, (((0,), (0,)), ((), ())), preferred_element_type=jnp.float32
    )


def matmul_cols(first_op, second_op):
    return lax.dot_general(
        first_op, second_op, (((1,), (1,)), ((), ())), preferred_element_type=jnp.float32
    )


def project_any(normed_all, w_qkv, cos_heads, sin_heads, heads_here, kv_here):
    seq_len = normed_all.shape[0]
    projected = jnp.dot(normed_all, w_qkv, preferred_element_type=jnp.float32)
    query_width = heads_here * HD
    kv_width = kv_here * HD
    group_size = heads_here // kv_here
    query_heads = rotate(
        projected[:, :query_width].reshape(seq_len, heads_here, HD), cos_heads, sin_heads
    )
    key_heads = rotate(
        projected[:, query_width : query_width + kv_width].reshape(seq_len, kv_here, HD),
        cos_heads,
        sin_heads,
    )
    value_heads = projected[:, query_width + kv_width :].reshape(seq_len, kv_here, HD)
    query_heads = jnp.transpose(query_heads.astype(jnp.bfloat16), (1, 0, 2)).reshape(
        kv_here, group_size, seq_len, HD
    )
    key_heads = jnp.transpose(key_heads.astype(jnp.bfloat16), (1, 0, 2))
    value_heads = jnp.transpose(value_heads.astype(jnp.bfloat16), (1, 0, 2))
    return (query_heads, key_heads, value_heads)


def masked_scores(query_block, key_heads, row_start, length):
    block_rows = query_block.shape[2]
    seq_len = key_heads.shape[1]
    scores = jnp.einsum(
        "kgqd,ksd->kgqs", query_block, key_heads, preferred_element_type=jnp.float32
    ) * HD ** (-0.5)
    row_pos = row_start + jnp.arange(block_rows, dtype=jnp.int32)
    key_pos = jnp.arange(seq_len, dtype=jnp.int32)
    allowed = (key_pos[None, :] <= row_pos[:, None]) & (key_pos[None, :] < length)
    return jnp.where(allowed, scores, -1e30)


def attend_forward_any(query_heads, key_heads, value_heads, length, block_rows):
    seq_len = query_heads.shape[2]
    outputs = []
    log_sums = []
    for row_start in range(0, seq_len, block_rows):
        query_block = query_heads[:, :, row_start : row_start + block_rows]
        scores = masked_scores(query_block, key_heads, row_start, length)
        row_peak = jnp.max(scores, axis=-1, keepdims=True)
        raised = jnp.exp(scores - row_peak)
        row_total = jnp.sum(raised, axis=-1, keepdims=True)
        attn_probs = (raised / row_total).astype(jnp.bfloat16)
        outputs.append(
            jnp.einsum(
                "kgqs,ksd->kgqd", attn_probs, value_heads, preferred_element_type=jnp.float32
            )
        )
        log_sums.append((row_peak + jnp.log(row_total))[..., 0])
    return (jnp.concatenate(outputs, axis=2), jnp.concatenate(log_sums, axis=2))


def attend_backward_any(query_heads, key_heads, value_heads, out_back, log_sums, length, block_rows):
    seq_len = query_heads.shape[2]
    query_grads = []
    key_grad = jnp.zeros(key_heads.shape, jnp.float32)
    value_grad = jnp.zeros(value_heads.shape, jnp.float32)
    for row_start in range(0, seq_len, block_rows):
        query_block = query_heads[:, :, row_start : row_start + block_rows]
        back_block = out_back[:, :, row_start : row_start + block_rows]
        scores = masked_scores(query_block, key_heads, row_start, length)
        attn_probs = jnp.exp(scores - log_sums[:, :, row_start : row_start + block_rows, None])
        probs_back = jnp.einsum(
            "kgqd,ksd->kgqs", back_block, value_heads, preferred_element_type=jnp.float32
        )
        row_shift = jnp.sum(attn_probs * probs_back, axis=-1, keepdims=True)
        scores_back = (HD ** (-0.5) * attn_probs * (probs_back - row_shift)).astype(jnp.bfloat16)
        query_grads.append(
            jnp.einsum("kgqs,ksd->kgqd", scores_back, key_heads, preferred_element_type=jnp.float32)
        )
        key_grad = key_grad + jnp.einsum(
            "kgqs,kgqd->ksd", scores_back, query_block, preferred_element_type=jnp.float32
        )
        value_grad = value_grad + jnp.einsum(
            "kgqs,kgqd->ksd",
            attn_probs.astype(jnp.bfloat16),
            back_block,
            preferred_element_type=jnp.float32,
        )
    return (jnp.concatenate(query_grads, axis=2), key_grad, value_grad)


def local_any(
    tokens,
    cotangent,
    lengths,
    owners,
    master,
    moment_one,
    moment_two,
    norm_gains,
    gain_first,
    gain_second,
):
    wide_count = lax.axis_size("wide")
    narrow_count = lax.axis_size("narrow")
    capacity = master.shape[0]
    unit_rows = master.shape[2]
    unit_cols = master.shape[3]
    unit_count = owners.shape[0]
    row_count = tokens.shape[0]
    seq_len = row_count * narrow_count
    slot_place, _ = positions(owners, wide_count, capacity)
    own_slots = master[:, 0].astype(jnp.bfloat16)
    all_slots = lax.all_gather(own_slots, "wide", axis=0, tiled=True)
    unit_data = jnp.take(all_slots, slot_place, axis=0)
    row_blocks = D // unit_rows
    col_blocks = unit_count // row_blocks
    packed = jnp.transpose(
        unit_data.reshape(row_blocks, col_blocks, unit_rows, unit_cols), (0, 2, 1, 3)
    ).reshape(D, col_blocks * unit_cols)
    heads_here = H // narrow_count
    kv_here = KV // narrow_count
    group_size = heads_here // kv_here
    query_width = heads_here * HD
    kv_width = kv_here * HD
    ff_width = FF // narrow_count
    qkv_end = query_width + 2 * kv_width
    out_end = qkv_end + query_width
    gate_end = out_end + 2 * ff_width
    w_qkv = packed[:, :qkv_end]
    w_out_t = packed[:, qkv_end:out_end]
    w_gate_up = packed[:, out_end:gate_end]
    w_down_t = packed[:, gate_end:]
    cos_table, sin_table = tables(seq_len, HD)
    cos_heads = cos_table[:, None, :]
    sin_heads = sin_table[:, None, :]
    block_rows = min(512, seq_len)
    wide_index = lax.axis_index("wide")
    length = lengths[wide_index]
    inputs = tokens.astype(jnp.float32)
    normed = rmsnorm(inputs, norm_gains[0]).astype(jnp.bfloat16)
    normed_all = lax.all_gather(normed, "narrow", axis=0, tiled=True)
    query_heads, key_heads, value_heads = project_any(
        normed_all, w_qkv, cos_heads, sin_heads, heads_here, kv_here
    )
    attended, log_sums = attend_forward_any(query_heads, key_heads, value_heads, length, block_rows)
    attended = (
        jnp.transpose(attended.reshape(heads_here, seq_len, HD), (1, 0, 2))
        .reshape(seq_len, query_width)
        .astype(jnp.bfloat16)
    )
    residual = inputs + lax.psum_scatter(
        matmul_cols(attended, w_out_t), "narrow", scatter_dimension=0, tiled=True
    )
    normed_two = rmsnorm(residual, norm_gains[1]).astype(jnp.bfloat16)
    mlp_input = lax.all_gather(normed_two, "narrow", axis=0, tiled=True)
    gate_up = jnp.dot(mlp_input, w_gate_up, preferred_element_type=jnp.float32)
    hidden = (jax.nn.silu(gate_up[:, :ff_width]) * gate_up[:, ff_width:]).astype(jnp.bfloat16)
    output = residual + lax.psum_scatter(
        matmul_cols(hidden, w_down_t).astype(jnp.bfloat16),
        "narrow",
        scatter_dimension=0,
        tiled=True,
    ).astype(jnp.float32)
    down_back = lax.all_gather(cotangent, "narrow", axis=0, tiled=True)
    mlp_again = lax.all_gather(normed_two, "narrow", axis=0, tiled=True)
    gate_up = jnp.dot(mlp_again, w_gate_up, preferred_element_type=jnp.float32)
    hidden_back = jnp.dot(down_back, w_down_t, preferred_element_type=jnp.float32)
    grad_down_t = matmul_rows(down_back, hidden)
    _, swiglu_pull = jax.vjp(
        lambda gate_in, upper_in: jax.nn.silu(gate_in) * upper_in,
        gate_up[:, :ff_width],
        gate_up[:, ff_width:],
    )
    gate_back, upper_back = swiglu_pull(hidden_back)
    gate_up_back = jnp.concatenate([gate_back, upper_back], axis=1).astype(jnp.bfloat16)
    grad_gate_up = matmul_rows(mlp_again, gate_up_back)
    norm_two_back = lax.psum_scatter(
        matmul_cols(gate_up_back, w_gate_up).astype(jnp.bfloat16),
        "narrow",
        scatter_dimension=0,
        tiled=True,
    ).astype(jnp.float32)
    _, norm_two_pull = jax.vjp(rmsnorm, residual, norm_gains[1])
    resid_part, gain_two = norm_two_pull(norm_two_back)
    resid_back = cotangent.astype(jnp.float32) + resid_part
    attn_back = lax.all_gather(resid_back.astype(jnp.bfloat16), "narrow", axis=0, tiled=True)
    normed_again = lax.all_gather(normed, "narrow", axis=0, tiled=True)
    query_heads, key_heads, value_heads = project_any(
        normed_again, w_qkv, cos_heads, sin_heads, heads_here, kv_here
    )
    out_back = jnp.dot(attn_back, w_out_t, preferred_element_type=jnp.float32).astype(jnp.bfloat16)
    grad_out_t = matmul_rows(attn_back, attended)
    out_back = jnp.transpose(out_back.reshape(seq_len, heads_here, HD), (1, 0, 2)).reshape(
        kv_here, group_size, seq_len, HD
    )
    query_grad, key_grad, value_grad = attend_backward_any(
        query_heads, key_heads, value_heads, out_back, log_sums, length, block_rows
    )
    query_grad = jnp.transpose(query_grad.reshape(heads_here, seq_len, HD), (1, 0, 2))
    query_grad = unrotate(query_grad, cos_heads, sin_heads).reshape(seq_len, query_width)
    key_grad = unrotate(jnp.transpose(key_grad, (1, 0, 2)), cos_heads, sin_heads).reshape(
        seq_len, kv_width
    )
    value_grad = jnp.transpose(value_grad, (1, 0, 2)).reshape(seq_len, kv_width)
    qkv_back = jnp.concatenate([query_grad, key_grad, value_grad], axis=1).astype(jnp.bfloat16)
    grad_qkv = matmul_rows(normed_again, qkv_back)
    norm_one_back = lax.psum_scatter(
        matmul_cols(qkv_back, w_qkv).astype(jnp.bfloat16), "narrow", scatter_dimension=0, tiled=True
    ).astype(jnp.float32)
    _, norm_one_pull = jax.vjp(rmsnorm, inputs, norm_gains[0])
    input_part, gain_one = norm_one_pull(norm_one_back)
    input_grad = (resid_back + input_part).astype(jnp.bfloat16)
    grad_packed = jnp.concatenate([grad_qkv, grad_out_t, grad_gate_up, grad_down_t], axis=1)
    grad_units = jnp.transpose(
        grad_packed.reshape(row_blocks, unit_rows, col_blocks, unit_cols), (0, 2, 1, 3)
    ).reshape(unit_count, unit_rows, unit_cols)
    grad_slots = (
        jnp.zeros((wide_count * capacity, unit_rows, unit_cols), jnp.float32)
        .at[slot_place]
        .set(grad_units)
    )
    owned_grads = lax.psum_scatter(
        grad_slots.astype(jnp.bfloat16), "wide", scatter_dimension=0, tiled=True
    ).astype(jnp.float32)[:, None]
    new_master, new_first, new_second = adamw(
        master, owned_grads, moment_one, moment_two, 0.02, 0.1
    )
    gain_grads = lax.psum(jnp.stack([gain_one, gain_two]), ("wide", "narrow"))
    new_gains, unused, gain_second_new = adamw(
        norm_gains, gain_grads, gain_first, gain_second, 0.5, 0.0
    )
    return (
        output.astype(jnp.bfloat16),
        input_grad,
        owned_grads,
        new_master,
        new_master.astype(jnp.bfloat16),
        new_first,
        new_second,
        gain_grads,
        gain_second_new,
        new_gains,
    )


def solution(mesh):
    COLLECTIVE[0] = 0
    rows = P(("wide", "narrow"), None)
    units = P("wide", "narrow", None, None)
    return jax.shard_map(
        local if mesh.shape["wide"] == 8 and mesh.shape["narrow"] == 4 else local_any,
        mesh=mesh,
        in_specs=(rows, rows, P(), P(), units, units, units, P(), P(), P()),
        out_specs=(rows, rows, units, units, units, units, units, P(), P(), P()),
        check_vma=False,
    )
```

```python
import functools

import jax
import jax.numpy as jnp
import numpy as np
from jax import lax
from jax.experimental import pallas as pl
from jax.experimental.pallas import tpu as pltpu
from jax.sharding import PartitionSpec as P

D = 2048
H = 32
KV = 8
HD = 64
FF = 8192
STEP = 5
LANES = 128
MIB = 1 << 20
ANY = pl.BlockSpec(memory_space=pl.ANY)
VMEM = pl.BlockSpec(memory_space=pltpu.VMEM)
SMEM = pl.BlockSpec(memory_space=pltpu.SMEM)

f32 = jnp.float32
bf16 = jnp.bfloat16


def dot(first_op, second_op, first_dim, second_dim):
    return lax.dot_general(
        first_op,
        second_op,
        (((first_dim,), (second_dim,)), ((), ())),
        preferred_element_type=f32,
    )


def shaped(shape, kind=bf16):
    return jax.ShapeDtypeStruct(shape, kind)


def blocks(shape, place):
    return pl.BlockSpec(shape, place)


class Send:
    def __init__(self, source, land, axis, step, source_at=None, land_at=None, landed=False, needs=()):
        self.source, self.land, self.axis, self.step = source, land, axis, step
        self.source_at, self.land_at = source_at, land_at
        self.landed, self.needs = landed, needs


COLLECTIVE = [0]


def run_sends(sends, sources, lands, send_sem, recv_sem):
    count = lax.axis_size("narrow")
    wide, narrow = lax.axis_index("wide"), lax.axis_index("narrow")

    def target(axis, step):
        if axis == "wide":
            return {"wide": jnp.bitwise_xor(wide, step)}
        return {"narrow": lax.rem(narrow + step, count)}

    copies = []
    for k, send in enumerate(sends):
        ref = (lands if send.landed else sources)[send.source]
        if send.source_at is not None:
            ref = ref.at[send.source_at(wide, narrow)]
        land = lands[send.land]
        if send.land_at is not None:
            land = land.at[send.land_at(wide, narrow)]
        copies.append(
            pltpu.make_async_remote_copy(
                src_ref=ref,
                dst_ref=land,
                send_sem=send_sem.at[k],
                recv_sem=recv_sem.at[k],
                device_id=target(send.axis, send.step),
                device_id_type=pl.DeviceIdType.MESH,
            )
        )

    def start():
        partners = set()
        for send in sends:
            if send.axis == "wide":
                partners.add(("wide", send.step))
            else:
                partners.add(("narrow", send.step % count))
                partners.add(("narrow", -send.step % count))
        barrier = pltpu.get_barrier_semaphore()
        for axis, step in sorted(partners):
            pl.semaphore_signal(
                barrier, inc=1, device_id=target(axis, step), device_id_type=pl.DeviceIdType.MESH
            )
        pl.semaphore_wait(barrier, len(partners))
        for send, copy in zip(sends, copies):
            if not send.needs and not send.landed:
                copy.start()

    def finish():
        arrived = set()
        for send, copy in zip(sends, copies):
            for k in send.needs:
                if k not in arrived:
                    copies[k].wait_recv()
                    arrived.add(k)
            if send.needs or send.landed:
                copy.start()
        for k, copy in enumerate(copies):
            copy.wait_send()
            if k not in arrived:
                copy.wait_recv()

    return start, finish


def call(
    body, ins, in_specs, out_shape, out_specs, *, name, grid=(), prefetch=(), scratch=(), deps=(),
    aliases=None, mib=56, flops=0, moved=0, sends=(), sources=(), lands=(), inner=(), closing=None,
):
    first = len(prefetch) + len(ins)
    single = not isinstance(out_shape, (list, tuple))
    out_shapes = [out_shape] if single else list(out_shape)
    specs = [out_specs] if single else list(out_specs)
    out_count = len(out_shapes)
    land_count = len(lands)

    def wrapped(*refs):
        given = refs[:first]
        refs = refs[first:]
        source_refs = refs[: len(sources)]
        refs = refs[len(sources) + len(deps) :]
        outs, refs = refs[:out_count], refs[out_count:]
        land_refs, refs = refs[:land_count], refs[land_count:]
        if not sends:
            body(*given, *outs, *refs)
            return
        own, (send_sem, recv_sem) = refs[:-2], refs[-2:]
        start, finish = run_sends(
            sends, source_refs, [*land_refs, *[own[k] for k in inner]], send_sem, recv_sem
        )

        def last():
            finish()
            if closing is not None:
                closing(land_refs, (*given, *outs, *own))

        if grid:
            steps = [pl.program_id(k) for k in range(len(grid))]
            begins = functools.reduce(jnp.logical_and, [step == 0 for step in steps])
            ends = functools.reduce(
                jnp.logical_and, [step == size - 1 for step, size in zip(steps, grid)]
            )
            pl.when(begins)(start)
            body(*given, *outs, *own)
            pl.when(ends)(last)
        else:
            start()
            body(*given, *outs, *own)
            last()

    extra = {}
    if sends:
        COLLECTIVE[0] += 1
        extra = {"collective_id": COLLECTIVE[0], "has_side_effects": True}
        scratch = [*scratch] + [pltpu.SemaphoreType.DMA((len(sends),))] * 2
    results = pl.pallas_call(
        wrapped,
        grid_spec=pltpu.PrefetchScalarGridSpec(
            num_scalar_prefetch=len(prefetch),
            grid=grid,
            in_specs=list(in_specs) + [ANY] * (len(sources) + len(deps)),
            out_specs=specs + [ANY] * land_count,
            scratch_shapes=list(scratch),
        ),
        out_shape=out_shapes + [shaped(*land) if isinstance(land[0], tuple) else shaped(land) for land in lands],
        input_output_aliases=aliases or {},
        compiler_params=pltpu.CompilerParams(vmem_limit_bytes=mib * MIB, **extra),
        cost_estimate=pl.CostEstimate(
            flops=int(flops), bytes_accessed=int(moved), transcendentals=0
        ),
        name=name,
    )(*prefetch, *ins, *sources, *deps)
    return results[0] if single and not sends else list(results)


def tables(length_all, head_size):
    inverse = 500000.0 ** (-jnp.arange(0, head_size, 2, dtype=f32) / head_size)
    angles = jnp.arange(length_all, dtype=f32)[:, None] * inverse[None, :]
    angles = jnp.concatenate([angles, angles], axis=1)
    return (jnp.cos(angles), jnp.sin(angles))


def turn_tables(length_all):
    inverse = np.float32(500000.0) ** (-np.arange(0, HD, 2, dtype=np.float32) / np.float32(HD))
    angles = np.arange(length_all, dtype=np.float32)[:, None] * inverse[None, :]
    angles = np.concatenate([angles] * (2 * LANES // HD), axis=1).astype(np.float32)
    return jnp.asarray(np.cos(angles)), jnp.asarray(np.sin(angles))


def rmsnorm(values, weight_gain):
    return (
        values * lax.rsqrt(jnp.mean(values * values, axis=-1, keepdims=True) + 1e-05) * weight_gain
    )


def positions(owners, wide_count, capacity):
    onehot = (owners[:, None] == jnp.arange(wide_count, dtype=jnp.int32)[None, :]).astype(jnp.int32)
    before = jnp.cumsum(onehot, axis=0) - onehot
    return (owners * capacity + jnp.sum(before * onehot, axis=1), jnp.sum(onehot, axis=0))


def adamw(weight, gradient, moment_one, moment_two, rate, decay):
    moment_one = 0.5 * moment_one + 0.5 * gradient
    moment_two = 0.5 * moment_two + 0.5 * gradient * gradient
    correct = 1.0 - 0.5**STEP
    update = moment_one / correct / (jnp.sqrt(moment_two / correct) + 1e-08)
    return (weight - rate * (update + decay * weight), moment_one, moment_two)


def turn_kernel(unit_ref, out_ref):
    parts, step, piece, unit_rows = out_ref.shape
    for k in range(step):
        out_ref[:, k] = (
            jnp.transpose(unit_ref[k, 0], (1, 0)).reshape(parts, piece, unit_rows).astype(bf16)
        )


def turn_units(master, parts, deps):
    capacity, _, unit_rows, unit_cols = master.shape
    piece = unit_cols // parts
    step = capacity // 2 if capacity % 2 == 0 else 1
    return call(
        turn_kernel,
        [master],
        [blocks((step, 1, unit_rows, unit_cols), lambda s: (s, 0, 0, 0))],
        shaped((parts, capacity, piece, unit_rows)),
        blocks((parts, step, piece, unit_rows), lambda s: (0, s, 0, 0)),
        grid=(capacity // step,),
        deps=deps,
        mib=60,
        moved=master.size * 6,
        name="turn_units",
    )


def pick_kernel(turn_ref, place_ref, own_ref, got_ref, out_ref, sem, *, col_blocks):
    _, capacity, piece, unit_rows = got_ref.shape

    def start(unit, carry):
        half = unit // col_blocks
        block = unit - half * col_blocks
        owner = place_ref[unit] // capacity
        slot = place_ref[unit] - owner * capacity
        target = out_ref.at[
            pl.ds(pl.multiple_of(block * piece, piece), piece),
            pl.ds(pl.multiple_of(half * unit_rows, unit_rows), unit_rows),
        ]

        @pl.when(owner == turn_ref[0])
        def _():
            pltpu.make_async_copy(own_ref.at[owner, slot], target, sem).start()

        @pl.when(owner != turn_ref[0])
        def _():
            pltpu.make_async_copy(got_ref.at[owner, slot], target, sem).start()

        return carry

    lax.fori_loop(0, place_ref.shape[0], start, 0)
    pltpu.make_async_copy(out_ref, out_ref, sem).wait()


def pick_units(turn, slot_place, own, got, row_blocks):
    _, _, piece, unit_rows = got.shape
    unit_count = slot_place.shape[0]
    col_blocks = unit_count // row_blocks
    return call(
        functools.partial(pick_kernel, col_blocks=col_blocks),
        [turn, slot_place, own, got],
        [SMEM, SMEM, ANY, ANY],
        shaped((col_blocks * piece, row_blocks * unit_rows)),
        VMEM,
        scratch=[pltpu.SemaphoreType.DMA],
        moved=unit_count * piece * unit_rows * 12,
        name="pick_units",
    )


def unpick_kernel(block_ref, half_ref, rows_ref, low_ref, high_ref, sems, *, piece, unit_rows):
    owners, part, _, _ = low_ref.shape
    capacity = part + high_ref.shape[1]

    def start(owner, carry):
        for slot in range(capacity):
            out_ref = high_ref if slot >= part else low_ref
            place = owner * capacity + slot
            pltpu.make_async_copy(
                rows_ref.at[
                    pl.ds(pl.multiple_of(block_ref[place] * piece, piece), piece),
                    pl.ds(pl.multiple_of(half_ref[place] * unit_rows, unit_rows), unit_rows),
                ],
                out_ref.at[owner, slot - part if slot >= part else slot],
                sems.at[int(slot >= part)],
            ).start()
        return carry

    lax.fori_loop(0, owners, start, 0)
    pltpu.make_async_copy(low_ref, low_ref, sems.at[0]).wait()
    pltpu.make_async_copy(high_ref, high_ref, sems.at[1]).wait()


def unpick_units(rows, block_of, half_of, owners, piece, unit_rows):
    slots = block_of.shape[0]
    capacity = slots // owners
    low = capacity // 4 * 2
    sizes = (low, capacity - low)
    return call(
        functools.partial(unpick_kernel, piece=piece, unit_rows=unit_rows),
        [block_of, half_of, rows],
        [SMEM, SMEM, VMEM],
        [shaped((owners, size, piece, unit_rows)) for size in sizes],
        [ANY, ANY],
        scratch=[pltpu.SemaphoreType.DMA((2,))],
        moved=slots * piece * unit_rows * 8,
        name="unpick_units",
    )


def apply_update(gradient, master_ref, one_ref, two_ref, outs, k=0):
    grad_out, master_out, copy_out, one_out, two_out = outs
    weight, one, two = adamw(master_ref[k, 0], gradient, one_ref[k, 0], two_ref[k, 0], 0.02, 0.1)
    grad_out[k, 0] = gradient
    master_out[k, 0] = weight
    copy_out[k, 0] = weight.astype(bf16)
    one_out[k, 0] = one
    two_out[k, 0] = two


def unit_gradient(parts, piece, unit_rows):
    return jnp.transpose(parts.astype(f32).reshape(-1, unit_rows), (1, 0))


def all_pieces(grad_ref, own_ref, turn, k=0):
    place = lax.broadcasted_iota(jnp.int32, (grad_ref.shape[0], 1, 1), 0)
    own = own_ref[0, k : k + 1].astype(f32)
    return jnp.where(place == turn, own, grad_ref[:, k].astype(f32))


def update_kernel(filled_ref, grad_ref, own_ref, master_ref, one_ref, two_ref, *refs, first):
    _, step, piece, unit_rows = grad_ref.shape
    for k in range(step):
        pieces = all_pieces(grad_ref, own_ref, lax.axis_index("wide"), k)
        slot = jnp.zeros((unit_rows, 1), jnp.int32) + (pl.program_id(0) * step + k + first)
        gradient = jnp.where(
            slot < filled_ref[0], unit_gradient(pieces, piece, unit_rows), 0.0
        )
        apply_update(gradient, master_ref, one_ref, two_ref, refs[-5:], k)


def update_outs(master):
    whole = shaped(master.shape, f32)
    return [whole, whole, shaped(master.shape), whole, whole]


def update_units(filled, grads, own, first, master, moment_one, moment_two, done, deps=()):
    _, _, unit_rows, unit_cols = master.shape
    parts, slots, piece, _ = grads.shape
    step = 2 if slots % 2 == 0 and first % 2 == 0 else 1
    unit = blocks((step, 1, unit_rows, unit_cols), lambda s: (s + first // step, 0, 0, 0))
    return call(
        functools.partial(update_kernel, first=first),
        [filled, grads, own, master, moment_one, moment_two, *done],
        [
            SMEM,
            blocks((parts, step, piece, unit_rows), lambda s: (0, s, 0, 0)),
            blocks((1, step, piece, unit_rows), lambda s: (lax.axis_index("wide"), s, 0, 0)),
            unit,
            unit,
            unit,
        ]
        + [ANY] * len(done),
        update_outs(master),
        [unit] * 5,
        grid=(slots // step,),
        aliases={6 + k: k for k in range(len(done))},
        moved=master.size * 16,
        mib=40,
        deps=deps,
        name="update_units",
    )


def lane_index(shape):
    return lax.broadcasted_iota(jnp.int32, shape, 1)


def rope(tile, cos_tile, sin_tile):
    lower = lane_index(tile.shape) % HD < HD // 2
    ahead = pltpu.roll(tile, LANES - HD // 2, 1)
    behind = pltpu.roll(tile, HD // 2, 1)
    return tile * cos_tile + jnp.where(lower, -ahead, behind) * sin_tile


def unrope(tile, cos_tile, sin_tile):
    lower = lane_index(tile.shape) % HD < HD // 2
    weighted = tile * sin_tile
    ahead = pltpu.roll(weighted, LANES - HD // 2, 1)
    behind = pltpu.roll(weighted, HD // 2, 1)
    return tile * cos_tile + jnp.where(lower, ahead, -behind)


def project_kernel(rows_ref, w_ref, cos_ref, sin_ref, out_ref, *, group_width):
    product = dot(rows_ref[...], w_ref[...], 1, 1)
    for start in range(0, out_ref.shape[1], LANES):
        tile = product[:, start : start + LANES]
        turned = rope(tile, cos_ref[...], sin_ref[...])
        if (start + LANES) % group_width == 0:
            tile = jnp.where(lane_index(tile.shape) < HD, turned, tile).astype(bf16)
        else:
            tile = turned.astype(bf16) * HD ** (-0.5)
        out_ref[:, start : start + LANES] = tile


def project(rows, w_qkv, cos_all, sin_all, group_width, step, deps):
    count = rows.shape[0]
    width = w_qkv.shape[0]
    return call(
        functools.partial(project_kernel, group_width=group_width),
        [rows, w_qkv, cos_all, sin_all],
        [
            blocks((step, D), lambda i: (i, 0)),
            blocks((width, D), lambda i: (0, 0)),
            blocks((step, LANES), lambda i: (i, 0)),
            blocks((step, LANES), lambda i: (i, 0)),
        ],
        shaped((count, width)),
        blocks((step, width), lambda i: (i, 0)),
        grid=(count // step,),
        deps=deps,
        flops=2 * count * width * D,
        name="project",
    )


def extend(tile, kx, vx):
    tile = tile.astype(f32)
    other = pltpu.roll(tile, HD, 1)
    low = lane_index(tile.shape) < HD
    kx[0] = jnp.where(low, tile, 0.0).astype(bf16)
    kx[1] = jnp.where(low, 0.0, other).astype(bf16)
    vx[0] = jnp.where(low, other, 0.0).astype(bf16)
    vx[1] = jnp.where(low, 0.0, tile).astype(bf16)


def forward_kernel(length_ref, qkv_ref, out_ref, log_ref, kx, vx, *, block):
    length = length_ref[0]
    seq_len, group_width = qkv_ref.shape
    pairs = group_width // LANES - 1
    extend(qkv_ref[:, pairs * LANES :], kx, vx)
    row = lax.broadcasted_iota(jnp.int32, (block, block), 0)
    col = lax.broadcasted_iota(jnp.int32, (block, block), 1)
    causal = col <= row
    key_row = lax.broadcasted_iota(jnp.int32, (1, seq_len), 1)
    bias = jnp.where(key_row < length, 0.0, -1e30).astype(f32)
    low = lane_index((block, LANES)) < HD
    for pair in range(pairs):
        lanes = slice(pair * LANES, (pair + 1) * LANES)
        for start in range(0, seq_len, block):
            query = qkv_ref[start : start + block, lanes]
            total = None
            logs = []
            for half in range(2):
                diagonal = dot(query, kx[half, start : start + block, :], 1, 1)
                diagonal = jnp.where(causal, diagonal + bias[:, start : start + block], -1e30)
                peak = jnp.max(diagonal, axis=1, keepdims=True)
                if start:
                    before = dot(query, kx[half, :start, :], 1, 1) + bias[:, :start]
                    peak = jnp.maximum(peak, jnp.max(before, axis=1, keepdims=True))
                    before = jnp.exp(before - peak)
                diagonal = jnp.exp(diagonal - peak)
                row_sum = jnp.sum(diagonal, axis=1, keepdims=True)
                part = dot(diagonal.astype(bf16), vx[half, start : start + block, :], 1, 0)
                if start:
                    row_sum = row_sum + jnp.sum(before, axis=1, keepdims=True)
                    part = part + dot(before.astype(bf16), vx[half, :start, :], 1, 0)
                part = part / row_sum
                total = part if total is None else total + part
                logs.append(peak + jnp.log(row_sum))
            out_ref[start : start + block, lanes] = total.astype(bf16)
            tile = jnp.transpose(jnp.where(low, logs[0], logs[1]), (1, 0))
            log_ref[0, 2 * pair : 2 * pair + 1, start : start + block] = tile[0:1]
            log_ref[0, 2 * pair + 1 : 2 * pair + 2, start : start + block] = tile[HD : HD + 1]


def attend_forward(length, qkv, groups, block, deps=(), **beside):
    seq_len, width = qkv.shape
    group_width = width // groups
    query_width = group_width - LANES
    return call(
        functools.partial(forward_kernel, block=block),
        [length, qkv],
        [SMEM, blocks((seq_len, group_width), lambda g: (0, g))],
        [shaped((seq_len, groups * query_width)), shaped((groups, 8, seq_len), f32)],
        [
            blocks((seq_len, query_width), lambda g: (0, g)),
            blocks((1, 8, seq_len), lambda g: (g, 0, 0)),
        ],
        grid=(groups,),
        scratch=[pltpu.VMEM((2, seq_len, LANES), bf16), pltpu.VMEM((2, seq_len, LANES), bf16)],
        deps=deps,
        mib=48,
        flops=groups * seq_len * seq_len * 2048,
        **beside,
        name="attend_forward",
    )


def backward_kernel(
    length_ref, qkv_ref, back_ref, out_ref, log_ref, cos_ref, sin_ref, *refs, block
):
    grad_ref, kx, vx, dk, dv = refs
    length = length_ref[0]
    seq_len, group_width = qkv_ref.shape
    pairs = group_width // LANES - 1
    extend(qkv_ref[:, pairs * LANES :], kx, vx)
    dk[...] = jnp.zeros(dk.shape, f32)
    dv[...] = jnp.zeros(dv.shape, f32)
    key = lax.broadcasted_iota(jnp.int32, (block, block), 0)
    row = lax.broadcasted_iota(jnp.int32, (block, block), 1)
    causal = key <= row
    for pair in range(pairs):
        lanes = slice(pair * LANES, (pair + 1) * LANES)
        for start in range(0, seq_len, block):
            here = slice(start, start + block)
            query = qkv_ref[here, lanes]
            back = back_ref[here, lanes]
            turned = jnp.transpose(back.astype(f32) * out_ref[here, lanes].astype(f32), (1, 0))
            query_grad = None
            for half in range(2):
                log_row = log_ref[0, 2 * pair + half : 2 * pair + half + 1, here]
                shift = jnp.sum(turned[half * HD : half * HD + HD], axis=0, keepdims=True)
                for first in range(0, start + block, block):
                    keys = slice(first, first + block)
                    scores = dot(kx[half, keys, :], query, 1, 1)
                    probs = jnp.exp(scores - log_row)
                    if first + block > seq_len // 2:
                        probs = jnp.where(key + first < length, probs, 0.0)
                    if first == start:
                        probs = jnp.where(causal, probs, 0.0)
                    probs_back = dot(vx[half, keys, :], back, 1, 1)
                    scores_back = (probs * (probs_back - shift)).astype(bf16)
                    dv[half, keys, :] += dot(probs.astype(bf16), back, 1, 0)
                    dk[half, keys, :] += dot(scores_back, query, 1, 0)
                    part = dot(scores_back, kx[half, keys, :], 0, 0)
                    query_grad = part if query_grad is None else query_grad + part
            query_grad = unrope(query_grad * HD ** (-0.5), cos_ref[here, :], sin_ref[here, :])
            grad_ref[here, lanes] = query_grad.astype(bf16)

    low = lane_index((seq_len, LANES)) < HD
    key_grad = jnp.where(low, dk[0] + pltpu.roll(dk[1], HD, 1), 0.0)
    key_grad = unrope(key_grad, cos_ref[...], sin_ref[...])
    value_grad = pltpu.roll(dv[0], HD, 1) + dv[1]
    grad_ref[:, pairs * LANES :] = jnp.where(low, key_grad, value_grad).astype(bf16)


def attend_backward(group, groups, length, qkv, back, out, logs, cos_all, sin_all, block, deps=(), **beside):
    seq_len, width = qkv.shape
    group_width = width // groups
    query_width = group_width - LANES
    given = blocks((seq_len, query_width), lambda i: (0, group))
    table = blocks((seq_len, LANES), lambda i: (0, 0))
    return call(
        functools.partial(backward_kernel, block=block),
        [length, qkv, back, out, logs, cos_all, sin_all],
        [
            SMEM,
            blocks((seq_len, group_width), lambda i: (0, group)),
            given,
            given,
            blocks((1, 8, seq_len), lambda i: (group, 0, 0)),
            table,
            table,
        ],
        shaped((seq_len, group_width)),
        blocks((seq_len, group_width), lambda i: (0, 0)),
        grid=(1,),
        scratch=[
            pltpu.VMEM((2, seq_len, LANES), bf16),
            pltpu.VMEM((2, seq_len, LANES), bf16),
            pltpu.VMEM((2, seq_len, LANES), f32),
            pltpu.VMEM((2, seq_len, LANES), f32),
        ],
        deps=deps,
        mib=48,
        flops=seq_len * seq_len * 5120,
        **beside,
        name="attend_backward",
    )


def branch_kernel(
    attended_ref, others_ref, w_ref, tokens_ref, gain_ref, residual_ref, normed_ref
):
    parts = others_ref.shape[0] + 1
    step, width = others_ref.shape[1:]
    here = lax.axis_index("narrow")
    first = here * (attended_ref.shape[0] // parts) + pl.program_id(0) * step
    total = tokens_ref[...].astype(f32)
    for k in range(parts):
        part = (
            others_ref[k - 1]
            if k
            else attended_ref[pl.ds(pl.multiple_of(first, step), step), :]
        )
        place = lax.rem(here - k + parts, parts) * width
        total = total + dot(part, w_ref[pl.ds(pl.multiple_of(place, width), width), :], 1, 0)
    residual_ref[...] = total
    normed_ref[...] = rmsnorm(total, gain_ref[...]).astype(bf16)


def branch(attended, others, w_out, tokens, gain, **beside):
    groups, count, width = others.shape
    step = 128
    rows = blocks((step, D), lambda i: (i, 0))
    return call(
        branch_kernel,
        [attended, others, w_out, tokens, gain],
        [
            blocks(attended.shape, lambda i: (0, 0)),
            blocks((groups, step, width), lambda i: (0, i, 0)),
            blocks((D, D), lambda i: (0, 0)),
            rows,
            blocks((1, D), lambda i: (0, 0)),
        ],
        [shaped((count, D), f32), shaped((count, D))],
        [rows, rows],
        grid=(count // step,),
        flops=2 * count * D * D,
        name="branch",
        **beside,
    )


def spread_kernel(turn_ref, back_ref, w_ref, out_ref):
    out_ref[0] = dot(back_ref[...], w_ref[...], 1, 1).astype(bf16)


def spread(turn, back, w_out, groups, deps=()):
    count = back.shape[0]
    width = D // groups
    return call(
        spread_kernel,
        [back, w_out],
        [
            blocks((count, D), lambda i, t: (0, 0)),
            blocks((width, D), lambda i, t: (lax.rem(t[1] + i, groups), 0)),
        ],
        shaped((groups, count, width)),
        blocks((1, count, width), lambda i, t: (i, 0, 0)),
        grid=(groups,),
        prefetch=[turn],
        deps=deps,
        flops=2 * count * D * D,
        mib=32,
        name="spread",
    )


def first_back_kernel(*refs):
    groups = (len(refs) - 1) // 2
    total = sum(dot(refs[g][...], refs[groups + g][...], 1, 0) for g in range(groups))
    refs[-1][...] = total.astype(bf16)


def first_back(qkv_back, w_qkv, step, deps=(), **beside):
    groups = len(qkv_back)
    seq_len, width = qkv_back[0].shape
    return call(
        first_back_kernel,
        [*qkv_back, *([w_qkv] * groups)],
        [blocks((step, width), lambda i: (i, 0))] * groups
        + [blocks((width, D), lambda i, g=g: (g, 0)) for g in range(groups)],
        shaped((seq_len, D)),
        blocks((step, D), lambda i: (i, 0)),
        grid=(seq_len // step,),
        deps=deps,
        flops=2 * seq_len * width * groups * D,
        name="first_back",
        mib=60,
        **beside,
    )


def stream(entry_refs, layout, low, high, buffer, sems, use):
    def copies(i):
        found = []
        for part, (ref, start, end, offset) in enumerate(layout[i]):
            first, last = max(start, low), min(end, high)
            if first < last:
                found.append(
                    pltpu.make_async_copy(
                        entry_refs[ref].at[pl.ds(first - start + offset, last - first)],
                        buffer.at[i % 2, pl.ds(first - low, last - first)],
                        sems.at[i % 2, part],
                    )
                )
        return found

    for copy in copies(0):
        copy.start()
    for i in range(len(layout)):
        if i + 1 < len(layout):
            for copy in copies(i + 1):
                copy.start()
        for copy in copies(i):
            copy.wait()
        use(i, buffer.at[i % 2])


def stream_scratch(rows):
    return [pltpu.VMEM((2, rows, D), bf16), pltpu.SemaphoreType.DMA((2, 3))]


def entry_layout(entries):
    arrays, layout = [], []
    for entry in entries:
        start, parts = 0, []
        for array, offset, count in entry:
            known = [k for k, other in enumerate(arrays) if other is array]
            if not known:
                known = [len(arrays)]
                arrays.append(array)
            parts.append((known[0], start, start + count, offset))
            start += count
        layout.append(parts)
    return arrays, layout, start // 3


def ff_kernel(rows_all_ref, low_ref, high_ref, *refs, layout, size, s, parts):
    hid_all, dgate_all, dup_all, rows_kept, back_kept, term_all, _ = refs[-18:-11]
    total, down, rows_ref, back_ref, hid_ref, dgate_ref, dup_ref, _, buffer, sems, own = refs[-11:]
    count = rows_ref.shape[0]
    low = low_ref.shape[0] // parts
    place = lax.rem(lax.axis_index("narrow") - s + parts, parts)
    low_place = pl.ds(pl.multiple_of(place * low, low), low)
    high_place = pl.ds(pl.multiple_of(place * (count - low), count - low), count - low)
    place = pl.ds(pl.multiple_of(place * count, count), count)
    here = pl.ds(s * count, count)
    copies = [
        pltpu.make_async_copy(rows_all_ref, rows_ref, own.at[0]),
        pltpu.make_async_copy(low_ref.at[low_place], back_ref.at[:low], own.at[1]),
        pltpu.make_async_copy(high_ref.at[high_place], back_ref.at[low:], own.at[4]),
    ]
    for copy in copies:
        copy.start()
    kept = [
        pltpu.make_async_copy(rows_ref, rows_kept.at[here], own.at[2]),
        pltpu.make_async_copy(back_ref, back_kept.at[here], own.at[3]),
    ]

    def use(i, weights):
        if i == 0:
            for copy in copies:
                copy.wait()
            for copy in kept:
                copy.start()
        gate = dot(rows_ref[...], weights[:size], 1, 1)
        up = dot(rows_ref[...], weights[size : 2 * size], 1, 1)
        hidden_back = dot(back_ref[...], weights[2 * size :], 1, 1)
        sig = 1.0 / (1.0 + jnp.exp(-gate))
        silu = gate * sig
        cols = slice(i * size, (i + 1) * size)
        hid = (silu * up).astype(bf16)
        dgate = (hidden_back * up * (sig * (1.0 + gate * (1.0 - sig)))).astype(bf16)
        dup = (hidden_back * silu).astype(bf16)
        hid_ref[:, cols] = hid
        dgate_ref[:, cols] = dgate
        dup_ref[:, cols] = dup
        part = dot(dgate, weights[:size], 1, 0) + dot(dup, weights[size : 2 * size], 1, 0)
        term = dot(hid, weights[2 * size :], 1, 0)
        if i:
            part = part + total[...]
            term = term + down[...]
        total[...] = part
        down[...] = term

    stream(refs, layout, 0, 3 * size, buffer, sems, use)
    for copy in kept:
        copy.wait()
    rows_ref[...] = down[...].astype(bf16)
    copies = [
        pltpu.make_async_copy(hid_ref, hid_all.at[here], own.at[0]),
        pltpu.make_async_copy(dgate_ref, dgate_all.at[here], own.at[1]),
        pltpu.make_async_copy(dup_ref, dup_all.at[here], own.at[2]),
        pltpu.make_async_copy(rows_ref, term_all.at[place], own.at[3]),
    ]
    for copy in copies:
        copy.start()
    for copy in copies:
        copy.wait()


def ff_close(lands, refs, *, added):
    out_ref, total = refs[-12:-10]
    arrived = refs[-4]
    value = total[...]
    if added:
        value = value + arrived[...].astype(f32)
    out_ref[...] = value.astype(out_ref.dtype)


def ff_step(s, rows, back_low, back_high, entries, kept, moving, added=False, last=False):
    count = rows.shape[0]
    seq_len = back_low.shape[0] + back_high.shape[0]
    arrays, layout, size = entry_layout(entries)
    ff_width = size * len(entries)
    return call(
        functools.partial(
            ff_kernel, layout=layout, size=size, s=s, parts=seq_len // count
        ),
        [rows, back_low, back_high, *arrays, *kept],
        [ANY] * (3 + len(arrays) + len(kept)),
        [shaped((seq_len, ff_width))] * 3
        + [shaped((seq_len, D))] * 3
        + [shaped((count, D), f32 if last else bf16)],
        [ANY] * 6 + [VMEM],
        scratch=[pltpu.VMEM((count, D), f32)] * 2
        + [pltpu.VMEM((count, D), bf16)] * 2
        + [pltpu.VMEM((count, ff_width), bf16)] * 3
        + [pltpu.VMEM((count, D), bf16)]
        + stream_scratch(3 * size)
        + [pltpu.SemaphoreType.DMA((5,))],
        aliases={3 + len(arrays) + k: k for k in range(len(kept))},
        mib=60,
        flops=10 * count * ff_width * D,
        name="ff_step",
        sends=[Send(0, 0, "narrow", 1)],
        sources=[moving],
        lands=[] if added else [moving.shape],
        inner=(7,) if added else (),
        closing=functools.partial(ff_close, added=added),
    )


def add_kernel(*refs):
    refs[-1][...] = sum(ref[...].astype(f32) for ref in refs[:-1]).astype(refs[-1].dtype)


def add(terms, kind=bf16, deps=(), **beside):
    count, width = terms[0].shape
    step = 128 if count % 128 == 0 else 64 if count % 64 == 0 else count
    given = blocks((step, width), lambda i: (i, 0))
    return call(
        add_kernel,
        terms,
        [given] * len(terms),
        shaped((count, width), kind),
        given,
        grid=(count // step,),
        deps=deps,
        moved=count * width * 8,
        name="add",
        **beside,
    )


def outer_kernel(first_ref, second_ref, *outs):
    first = first_ref[...]
    if len(first.shape) == 3:
        first = first[0]
    product = dot(first, second_ref[...], 0, 0).astype(bf16)
    each = pl.num_programs(0) // len(outs)
    for k, out_ref in enumerate(outs):

        @pl.when(pl.program_id(0) // each == k)
        def _(out_ref=out_ref):
            out_ref[...] = product


def outer(first, second, split=1, deps=(), **beside):
    rows, width = second.shape
    if len(first.shape) == 3:
        groups, _, step = first.shape
        height = groups * step
        taken = blocks((1, rows, step), lambda i: (i, 0, 0))
    else:
        height = first.shape[1]
        step = next(k for k in (512, 384, 256, 192, LANES) if height % (k * split) == 0)
        taken = blocks((rows, step), lambda i: (0, i))
    each = height // step // split
    return call(
        outer_kernel,
        [first, second],
        [taken, blocks((rows, width), lambda i: (0, 0))],
        [shaped((height // split, width))] * split,
        [
            blocks((step, width), lambda i, k=k: (jnp.clip(i - k * each, 0, each - 1), 0))
            for k in range(split)
        ],
        grid=(height // step,),
        deps=deps,
        mib=56,
        flops=2 * rows * height * width,
        **beside,
        name="outer",
    )


def outer_pair_kernel(first_ref, second_ref, rows_ref, *outs):
    for part, (taken_ref, out_ref) in enumerate(zip((first_ref, second_ref), outs)):

        @pl.when(pl.program_id(0) == part)
        def _(taken_ref=taken_ref, out_ref=out_ref):
            out_ref[...] = dot(taken_ref[...], rows_ref[...], 0, 0).astype(bf16)


def outer_pair(firsts, second, deps=(), **beside):
    rows, height = firsts[0].shape
    width = second.shape[1]
    taken = blocks((rows, height), lambda i: (0, 0))
    return call(
        outer_pair_kernel,
        [*firsts, second],
        [taken, taken, blocks((rows, width), lambda i: (0, 0))],
        [shaped((height, width))] * 2,
        [blocks((height, width), lambda i: (0, 0))] * 2,
        grid=(2,),
        deps=deps,
        flops=4 * rows * height * width,
        name="outer_pair",
        mib=60,
        **beside,
    )


def pass_kernel(*refs):
    pass


def after(value, *deps):
    return call(
        pass_kernel, [value], [ANY], shaped(value.shape, value.dtype), ANY, deps=deps,
        aliases={0: 0}, name="after",
    )


def shift(count, step=1):
    return [(i, (i + step) % count) for i in range(count)]


def nothing(*refs):
    pass


def sum_places_kernel(place_ref, own_ref, others_ref, out_ref):
    total = jnp.zeros(own_ref.shape, f32)
    for k in range(others_ref.shape[0]):
        total = total + jnp.where(place_ref[0] == k, own_ref[...], others_ref[k])
    out_ref[...] = total


def sum_places(place, own, others):
    return call(
        sum_places_kernel,
        [place, own, others],
        [SMEM, VMEM, VMEM],
        shaped(own.shape, f32),
        VMEM,
        name="sum_places",
    )


def move(sends, sources, lands, deps=()):
    return call(
        nothing, [], [], [], [], sends=sends, sources=sources, lands=lands, deps=deps, name="move"
    )


def rows_at(first, count):
    return lambda wide, narrow: pl.ds(first, count)


def exchange_units(turned):
    return move(
        [
            Send(
                0, 0, "wide", e,
                lambda wide, narrow, e=e: jnp.bitwise_xor(wide, e),
                lambda wide, narrow: wide,
            )
            for e in range(1, turned.shape[0])
        ],
        [turned],
        [turned.shape],
    )[0]


def near_and_across(source, land, at=None, needs=()):
    return [
        Send(source, land, "wide", 2, at, needs=needs),
        Send(source, land + 1, "wide", 4, at, needs=needs),
    ]


def sum_entries_kernel(first_ref, second_ref, *outs):
    total = (first_ref[0].astype(f32) + second_ref[0].astype(f32)).astype(bf16)
    for r, out_ref in enumerate(outs):

        @pl.when(pl.program_id(0) == r)
        def _(out_ref=out_ref):
            out_ref[...] = total


def sum_entries(first, second, **beside):
    count, rows, width = first.shape
    given = blocks((1, rows, width), lambda i: (i, 0, 0))
    return call(
        sum_entries_kernel,
        [first, second],
        [given, given],
        [shaped((rows, width))] * count,
        [blocks((rows, width), lambda i: (0, 0))] * count,
        grid=(count,),
        moved=first.size * 6,
        name="sum_entries",
        **beside,
    )


def ff_meet_kernel(own_ref, other_ref, first_out, second_out):
    total = (own_ref[...].astype(f32) + other_ref[...].astype(f32)).astype(bf16)
    half = first_out.shape[0]
    first_out[...] = total[:half]
    second_out[...] = total[half:]


def ff_meet(own, other, deps=()):
    rows, width = own.shape[0] // 4, own.shape[1]
    last = blocks((rows, width), lambda i: (3, 0))
    half = blocks((rows // 2, width), lambda i: (0, 0))
    return call(
        ff_meet_kernel,
        [own, other],
        [last, last],
        [shaped((rows // 2, width))] * 2,
        [half, half],
        grid=(1,),
        deps=deps,
        moved=own.size * 2,
        name="ff_meet",
    )


def ff_join_kernel(
    own_x, other_x, first_ref, own_y, other_y, second_ref, x_out, y_out
):
    half = first_ref.shape[0]
    x = own_x[...].astype(f32) + other_x[...].astype(f32)
    y = own_y[...].astype(f32) + other_y[...].astype(f32)
    x_out[:half] = (x[:half] + first_ref[...].astype(f32)).astype(bf16)
    x_out[half:] = x[half:].astype(bf16)
    y_out[:half] = y[:half].astype(bf16)
    y_out[half:] = (y[half:] + second_ref[...].astype(f32)).astype(bf16)


def ff_join(own, other, first, second, deps=()):
    rows, width = own.shape[0] // 4, own.shape[1]

    def quarter(k):
        return blocks((rows, width), lambda i: (k, 0))

    half = blocks((rows // 2, width), lambda i: (0, 0))
    shape = shaped((rows, width))
    return call(
        ff_join_kernel,
        [own, other, first, own, other, second],
        [quarter(1), quarter(1), half, quarter(2), quarter(2), half],
        [shape, shape],
        [quarter(0), quarter(0)],
        grid=(1,),
        deps=deps,
        moved=own.size * 4,
        name="ff_join",
    )


def ff_end_kernel(*refs):
    refs[-1][...] = sum(ref[...].astype(f32) for ref in refs[:-1]).astype(bf16)


def ff_end(own, other, near, deps=(), **beside):
    rows, width = own.shape[0] // 4, own.shape[1]
    first = blocks((rows, width), lambda i: (0, 0))
    return call(
        ff_end_kernel,
        [own, other, *near],
        [first] * (2 + len(near)),
        shaped((rows, width)),
        first,
        grid=(1,),
        deps=deps,
        moved=own.size * 2,
        name="ff_end",
        **beside,
    )


def shaped_rows(array, parts):
    return (array.shape[0] // parts, array.shape[1])


def across_sends(source, land):
    return [Send(source, land, "wide", 4), Send(source + 1, land + 1, "wide", 2)]


def near_sends(source, land):
    return [Send(source, land, "wide", 2), Send(source + 1, land + 1, "wide", 4)]


def unit_row(col, query_width, kv_width, by_head, group_width):
    start, offset = col
    if start < query_width:
        return start // by_head * group_width + start % by_head + offset
    start -= query_width
    last = start >= kv_width
    if last:
        start -= kv_width
    head = (start + offset) // HD
    return head * group_width + by_head + last * HD + (start + offset) % HD


def assemble_qkv_kernel(
    turn_ref, own_ref, near_ref, other_ref, out_ref, *, piece, unit_cols, sizes
):
    height = near_ref.shape[1]
    for e in range(8):
        j = jnp.bitwise_xor(turn_ref[0], e)
        for c in range(height // piece):
            here = slice(c * piece, (c + 1) * piece)
            row = unit_row((c * unit_cols, j * piece), *sizes)
            if e % 2:
                value = other_ref[e // 2, here, :]
            elif e:
                value = near_ref[e // 2 - 1, here, :]
            else:
                value = own_ref[here, :]
            out_ref[pl.ds(pl.multiple_of(row, piece), piece), :] = value


def assemble_qkv(turn, rows, near, other, piece, unit_cols, sizes):
    _, height, _ = near.shape
    return call(
        functools.partial(
            assemble_qkv_kernel, piece=piece, unit_cols=unit_cols, sizes=sizes
        ),
        [turn, rows, near, other],
        [SMEM, blocks((height, D), lambda i: (0, 0)), whole_block(near), whole_block(other)],
        shaped((height * 8, D)),
        blocks((height * 8, D), lambda i: (0, 0)),
        grid=(1,),
        mib=32,
        moved=height * 8 * D * 4,
        name="assemble_qkv",
    )


def whole_block(array):
    return blocks(array.shape, lambda i: (0,) * len(array.shape))


def arrange_attn_kernel(turn_ref, *refs, piece, unit_cols, sizes):
    *grads, own_ref, other_ref = refs
    query_width, kv_width, _, group_width = sizes
    out_first = query_width + 2 * kv_width
    for j in range(unit_cols // piece):
        e = jnp.bitwise_xor(turn_ref[0], j)
        for core, out_ref in enumerate((own_ref, other_ref)):

            @pl.when(e % 2 == core)
            def _(j=j, e=e, out_ref=out_ref):
                for c in range(out_ref.shape[1] // piece):
                    if c * unit_cols < out_first:
                        row = unit_row((c * unit_cols, j * piece), *sizes)
                        grad_ref = grads[row // group_width]
                        row = row % group_width
                    else:
                        row = c * unit_cols - out_first + j * piece
                        grad_ref = grads[-1]
                    out_ref[e // 2, c * piece : (c + 1) * piece, :] = grad_ref[
                        row : row + piece, :
                    ]


def arrange_attn(turn, grads, piece, unit_cols, sizes):
    count = unit_cols // piece
    rows = sum(grad.shape[0] for grad in grads) // count
    shape = shaped((count // 2, rows, D))
    return call(
        functools.partial(arrange_attn_kernel, piece=piece, unit_cols=unit_cols, sizes=sizes),
        [turn, *grads],
        [SMEM] + [VMEM] * len(grads),
        [shape, shape],
        [VMEM] * 2,
        mib=32,
        moved=rows * count * D * 4,
        name="arrange_attn",
    )


def out_row(turn_ref, k, c, j, parts, piece, unit_cols, sign):
    n = lax.rem(turn_ref[1] + sign * k + parts, parts)
    return n * (D // parts) + c * unit_cols + j * piece


def assemble_out_kernel(
    turn_ref, rows_ref, z_ref, x_ref, y_ref, across_ref, other_ref, out_ref, *, first, piece,
    unit_cols, parts,
):
    height = z_ref.shape[1]
    for e in range(8):
        j = jnp.bitwise_xor(turn_ref[0], e)
        for k in range(parts):
            for c in range(height // piece):
                here = slice(c * piece, (c + 1) * piece)
                row = out_row(turn_ref, k, c, j, parts, piece, unit_cols, -1)
                if e % 2:
                    value = other_ref[e // 2, k, here, :]
                elif e:
                    value = (x_ref, y_ref, across_ref)[e // 2 - 1][k, here, :]
                elif k:
                    value = z_ref[k - 1, here, :]
                else:
                    value = rows_ref[first + c * piece : first + (c + 1) * piece, :]
                out_ref[pl.ds(pl.multiple_of(row, piece), piece), :] = value


def assemble_out(turn, rows, first, given, piece, unit_cols, parts, deps=()):
    height = given[0].shape[1]
    return call(
        functools.partial(
            assemble_out_kernel, first=first, piece=piece, unit_cols=unit_cols, parts=parts
        ),
        [turn, rows, *given],
        [SMEM, blocks((first + height, D), lambda i: (0, 0))] + [whole_block(a) for a in given],
        shaped((D, D)),
        blocks((D, D), lambda i: (0, 0)),
        grid=(1,),
        mib=52,
        deps=deps,
        moved=D * D * 4,
        name="assemble_out",
    )


def local(
    tokens, cotangent, lengths, owners, master, moment_one, moment_two, norm_gains, gain_first,
    gain_second,
):
    wide_count = lax.axis_size("wide")
    narrow_count = lax.axis_size("narrow")
    capacity, _, unit_rows, unit_cols = master.shape
    unit_count = owners.shape[0]
    row_count = tokens.shape[0]
    seq_len = row_count * narrow_count
    row_blocks = D // unit_rows
    col_blocks = unit_count // row_blocks
    piece = unit_cols // wide_count
    query_width = H // narrow_count * HD
    kv_width = KV // narrow_count * HD
    ff_width = FF // narrow_count
    qkv_width = query_width + 2 * kv_width
    groups = KV // narrow_count
    group_width = qkv_width // groups
    by_head = group_width - 2 * HD
    wide_index = lax.axis_index("wide")
    narrow_index = lax.axis_index("narrow")
    turn = jnp.stack([wide_index, narrow_index]).astype(jnp.int32)
    length = lax.dynamic_slice(lengths, (wide_index,), (1,))
    block = min(256, seq_len)
    qkv_blocks = qkv_width // unit_cols
    out_blocks = query_width // unit_cols
    attn_blocks = qkv_blocks + out_blocks
    sizes = (query_width, kv_width, by_head, group_width)
    back_by = (narrow_index - jnp.arange(narrow_count, dtype=jnp.int32)) % narrow_count

    inputs = tokens.astype(f32)
    normed = rmsnorm(inputs, norm_gains[0]).astype(bf16)
    normed_all = lax.all_gather(normed, "narrow", axis=0, tiled=True)

    slot_place, counts = positions(owners, wide_count, capacity)
    turned = turn_units(master, wide_count, ())
    got = exchange_units(turned)
    rows = pick_units(turn, slot_place, turned, got, row_blocks)
    qkv_rows = qkv_blocks * piece
    out_rows = out_blocks * piece
    ff_first = qkv_rows + out_rows
    ff_rows = 3 * ff_width // wide_count

    qkv_at, out_at = rows_at(0, qkv_rows), rows_at(qkv_rows, out_rows)

    def entry(k):
        return lambda wide, narrow: k

    near_qkv, other_qkv, narrow_out = move(
        [Send(0, 0, "wide", 2 * r, qkv_at, entry(r - 1)) for r in (1, 2, 3)]
        + [Send(0, 1, "wide", 1, qkv_at, entry(0))]
        + [Send(0, 2, "narrow", k, out_at, entry(k - 1)) for k in range(1, narrow_count)]
        + [
            Send(0, 1, "wide", 1, entry(r - 1), entry(r), landed=True, needs=(r - 1,))
            for r in (1, 2, 3)
        ],
        [rows],
        [
            (3, qkv_rows, D),
            (4, qkv_rows, D),
            (narrow_count - 1, out_rows, D),
        ],
    )
    w_qkv = assemble_qkv(turn, rows, near_qkv, other_qkv, piece, unit_cols, sizes)

    cos_all, sin_all = turn_tables(seq_len)
    low_rows = row_count // 2
    cotangent_then = after(cotangent[:low_rows], normed_all, w_qkv)
    back_low = lax.all_gather(cotangent_then, "narrow", axis=0, tiled=True)
    qkv = project(
        normed_all, w_qkv, cos_all, sin_all, group_width, row_count, (cotangent_then,)
    )
    out_shape = (narrow_count, out_rows, D)

    def first_entry(wide, narrow):
        return 0

    def later_entries(wide, narrow):
        return pl.ds(1, narrow_count - 1)

    attended, logs, out_x, out_y = attend_forward(
        length, qkv, groups, block,
        sends=[
            Send(0, 0, "wide", 2, out_at, first_entry),
            Send(0, 1, "wide", 4, out_at, first_entry),
            Send(1, 0, "wide", 2, None, later_entries),
            Send(1, 1, "wide", 4, None, later_entries),
        ],
        sources=[rows, narrow_out],
        lands=[out_shape, out_shape],
    )

    half = narrow_count // 2
    third = ff_rows // 3

    def heads_of(k):
        return lambda wide, narrow: pl.ds(
            pl.multiple_of(lax.rem(narrow + k, narrow_count) * row_count, row_count), row_count
        )

    def part_of(k, at):
        return lambda wide, narrow: (k, at)

    low_part, high_part = pl.ds(0, half), pl.ds(half, narrow_count - half)
    attended_others, out_across, out_other, x_first, y_first = move(
        [Send(0, 0, "narrow", k, heads_of(k), entry(k - 1)) for k in range(1, narrow_count)]
        + [
            Send(2, 1, "wide", 4, lambda w, n: low_part, lambda w, n: low_part),
            Send(3, 1, "wide", 2, lambda w, n: high_part, lambda w, n: high_part),
            Send(1, 2, "wide", 1, out_at, lambda w, n: (0, 0)),
            Send(4, 2, "wide", 1, None, lambda w, n: (0, pl.ds(1, narrow_count - 1))),
            Send(2, 2, "wide", 1, None, entry(1)),
            Send(3, 2, "wide", 1, None, entry(2)),
            Send(1, 3, "wide", 2, rows_at(ff_first, third)),
            Send(1, 4, "wide", 4, rows_at(ff_first, third)),
            Send(
                1, 2, "wide", 1, None, entry(3), landed=True,
                needs=(narrow_count - 1, narrow_count),
            ),
        ],
        [attended, rows, out_x, out_y, narrow_out],
        [
            (narrow_count - 1, row_count, query_width),
            out_shape,
            (4, *out_shape),
            (third, D),
            (third, D),
        ],
    )
    back_high = lax.all_gather(
        after(cotangent[low_rows:], attended_others, back_low), "narrow", axis=0, tiled=True
    )
    w_out = assemble_out(
        turn, rows, qkv_rows, [narrow_out, out_x, out_y, out_across, out_other], piece,
        unit_cols, narrow_count,
    )
    residual, normed_two = branch(
        attended, attended_others, w_out, tokens, norm_gains[1:2]
    )

    rest = ff_rows - third
    half_rest = ff_rows // 2 - third
    (
        block_one, x_last, y_last, own_swap, x_first_swap, y_first_swap, x_last_swap, y_last_swap,
        across_first,
    ) = move(
        [Send(0, 0, "narrow", 1)]
        + near_and_across(1, 1, rows_at(ff_first + third, rest))
        + [Send(1, 3, "wide", 1, rows_at(ff_first, ff_rows))]
        + [Send(2, 4, "wide", 1), Send(3, 5, "wide", 1)]
        + [
            Send(1, 6, "wide", 1, landed=True, needs=(1,)),
            Send(2, 7, "wide", 1, landed=True, needs=(2,)),
            Send(2, 8, "wide", 4),
        ],
        [normed_two, rows, x_first, y_first],
        [normed_two.shape, (rest, D), (rest, D), (ff_rows, D)]
        + [(third, D)] * 2
        + [(rest, D)] * 2
        + [(third, D)],
    )
    block_two, *across = move(
        [
            Send(0, 0, "narrow", 1),
            Send(2, 1, "wide", 4, rows_at(0, half_rest)),
            Send(3, 2, "wide", 2, rows_at(half_rest, ff_rows // 2)),
            Send(1, 3, "wide", 1),
            Send(1, 4, "wide", 1, landed=True, needs=(1,)),
            Send(2, 5, "wide", 1, landed=True, needs=(2,)),
        ],
        [block_one, across_first, x_last, y_last],
        [block_one.shape, (half_rest, D), (ff_rows // 2, D)]
        + [(third, D), (half_rest, D), (ff_rows // 2, D)],
    )
    across = [across_first, *across]

    def pieces(*arrays):
        return [(array, 0, array.shape[0]) for array in arrays]

    entries = [
        [(rows, ff_first, ff_rows)],
        pieces(x_first, x_last),
        pieces(y_first, y_last),
        pieces(*across[:3]),
        [(own_swap, 0, ff_rows)],
        pieces(x_first_swap, x_last_swap),
        pieces(y_first_swap, y_last_swap),
        pieces(*across[3:]),
    ]

    *kept, total, block_three = ff_step(1, block_one, back_low, back_high, entries, (), block_two)
    *kept, total = ff_step(2, block_two, back_low, back_high, entries, kept, total, True)
    *kept, total = ff_step(3, block_three, back_low, back_high, entries, kept, total, True)
    *kept, norm_two_back = ff_step(0, normed_two, back_low, back_high, entries, kept, total, True, True)
    hidden, dgate, dup, mlp_all, back_kept, ff_term = kept

    _, norm_two_pull = jax.vjp(rmsnorm, residual, norm_gains[1])
    resid_part, gain_two = norm_two_pull(norm_two_back)
    resid_back = cotangent.astype(f32) + resid_part
    attn_back = resid_back.astype(bf16)
    by_heads = spread(turn, attn_back, w_out, narrow_count)

    def heads_send(k, land):
        return Send(0, land, "narrow", k, entry(k))

    heads_shape = (row_count, query_width)
    *grad_down, heads_one, heads_three = outer(
        hidden, back_kept, 2,
        sends=[heads_send(1, 0), heads_send(3, 1)],
        sources=[by_heads],
        lands=[heads_shape, heads_shape],
    )
    half_shape, near_shape = shaped_rows(grad_down[0], 8), shaped_rows(grad_down[0], 4)
    *grad_gate, heads_two, down_swap = outer(
        dgate, mlp_all, 2,
        sends=[heads_send(2, 0), Send(1, 1, "wide", 1)],
        sources=[by_heads, grad_down[1]],
        lands=[heads_shape, grad_down[1].shape],
    )
    out_back = jnp.stack([by_heads[0], heads_one, heads_two, heads_three])
    out_back = jnp.take(out_back, back_by, axis=0).reshape(seq_len, query_width)
    attn_back_all = lax.all_gather(after(attn_back, heads_two), "narrow", axis=0, tiled=True)
    ff_sum = lax.psum_scatter(
        after(ff_term, heads_two), "narrow", scatter_dimension=0, tiled=True
    )
    output = residual + ff_sum.astype(f32)
    down_across = ff_meet(grad_down[0], down_swap)
    *grad_upper, gate_swap, down_a, down_b = outer(
        dup, mlp_all, 2,
        sends=[Send(0, 0, "wide", 1)] + across_sends(1, 1),
        sources=[grad_gate[1], *down_across],
        lands=[grad_gate[1].shape, half_shape, half_shape],
    )
    joined_down = ff_join(grad_down[0], down_swap, down_a, down_b)
    gate_across = ff_meet(grad_gate[0], gate_swap)

    qkv_back = [None, None]
    qkv_back[0], upper_swap, gate_a, gate_b, down_x, down_y = attend_backward(
        0, groups, length, qkv, out_back, attended, logs, cos_all, sin_all, block,
        sends=[Send(0, 0, "wide", 1)] + across_sends(1, 1) + near_sends(3, 3),
        sources=[grad_upper[1], *gate_across, *joined_down],
        lands=[grad_upper[1].shape, half_shape, half_shape, near_shape, near_shape],
    )
    upper_across = ff_meet(grad_upper[0], upper_swap)
    joined_gate = ff_join(grad_gate[0], gate_swap, gate_a, gate_b)
    qkv_back[1], upper_a, upper_b, gate_x, gate_y = attend_backward(
        1, groups, length, qkv, out_back, attended, logs, cos_all, sin_all, block,
        sends=across_sends(0, 0) + near_sends(2, 2),
        sources=[*upper_across, *joined_gate],
        lands=[half_shape] * 2 + [near_shape] * 2,
    )
    joined_upper = ff_join(grad_upper[0], upper_swap, upper_a, upper_b)
    *grad_qkv, upper_x, upper_y = outer_pair(
        qkv_back, normed_all, (joined_upper[0],),
        sends=near_sends(0, 0), sources=list(joined_upper), lands=[near_shape] * 2,
    )
    (grad_out,) = outer(attended, attn_back_all, 1, (grad_qkv[0],))
    own_attn, other_attn = arrange_attn(
        turn, [*grad_qkv, grad_out], piece, unit_cols, sizes
    )
    gate_sum, attn_swap = ff_end(
        grad_gate[0], gate_swap, [gate_x, gate_y],
        sends=[Send(0, 0, "wide", 1)], sources=[other_attn], lands=[other_attn.shape],
    )
    down_sum = ff_end(grad_down[0], down_swap, [down_x, down_y], (grad_qkv[0],))
    upper_sum = ff_end(grad_upper[0], upper_swap, [upper_x, upper_y])
    met_attn = sum_entries(own_attn, attn_swap)
    norm_one_term, *arrived = first_back(
        qkv_back, w_qkv, row_count, (down_sum, upper_sum),
        sends=[Send(r - 1, r - 1, "wide", 2 * r) for r in (1, 2, 3)],
        sources=met_attn[1:],
        lands=[met_attn[0].shape] * 3,
    )
    attn_sum = add([met_attn[0]] + arrived)

    slots = wide_count * capacity
    unit_of = jnp.zeros((slots,), jnp.int32).at[slot_place].set(
        jnp.arange(unit_count, dtype=jnp.int32)
    )
    half_of = unit_of // col_blocks
    low, high = unpick_units(
        jnp.concatenate([attn_sum, gate_sum, upper_sum, down_sum], axis=0),
        unit_of - half_of * col_blocks,
        half_of,
        wide_count,
        piece,
        unit_rows,
    )
    gain_one = sum(
        jnp.sum(
            w_qkv[g * group_width : (g + 1) * group_width].astype(f32) * grad_qkv[g].astype(f32),
            axis=0,
        )
        for g in range(groups)
    )
    gain_terms = jnp.stack([gain_one / norm_gains[0], gain_two])
    owned_low, gain_others = move(
        [
            Send(
                0, 0, "wide", e,
                lambda wide, narrow, e=e: jnp.bitwise_xor(wide, e),
                lambda wide, narrow: wide,
            )
            for e in range(1, wide_count)
        ]
        + [
            Send(1, 1, "wide", e, None, lambda wide, narrow: wide) for e in range(1, wide_count)
        ],
        [low, gain_terms],
        [low.shape, ((wide_count, *gain_terms.shape), f32)],
    )
    owned_high = lax.all_to_all(after(high, owned_low), "wide", split_axis=0, concat_axis=0)
    gain_plane = sum_places(wide_index.reshape(1), gain_terms, gain_others)
    filled = jnp.concatenate(
        [lax.dynamic_slice(counts, (wide_index,), (1,)), wide_index.reshape(1)]
    ).astype(jnp.int32)
    updated = update_units(
        filled, owned_low, low, 0, master, moment_one, moment_two, ()
    )
    owned_grads, new_master, new_copy, new_first, new_second = update_units(
        filled, owned_high, owned_high, low.shape[1], master, moment_one, moment_two, updated
    )
    gain_others = jnp.stack(
        [gain_plane]
        + [
            after(lax.ppermute(gain_plane, "narrow", shift(narrow_count, k)), owned_grads)
            for k in range(1, narrow_count)
        ]
    )
    gain_grads = sum_places(
        narrow_index.reshape(1), gain_plane, jnp.take(gain_others, back_by, axis=0)
    )

    norm_one_back = lax.psum_scatter(
        after(norm_one_term, ff_sum, attn_sum), "narrow", scatter_dimension=0, tiled=True
    )
    norm_one_back = after(norm_one_back, owned_grads).astype(f32)
    _, norm_one_pull = jax.vjp(lambda values: rmsnorm(values, norm_gains[0]), inputs)
    (input_part,) = norm_one_pull(norm_one_back)
    input_grad = (resid_back + input_part).astype(bf16)
    new_gains, _, gain_second_new = adamw(
        norm_gains, gain_grads, gain_first, gain_second, 0.5, 0.0
    )
    return (
        output.astype(bf16),
        input_grad,
        owned_grads,
        new_master,
        new_copy,
        new_first,
        new_second,
        gain_grads,
        gain_second_new,
        new_gains,
    )


def rotate(values, cos_table, sin_table):
    middle = values.shape[-1] // 2
    turned = jnp.concatenate([-values[..., middle:], values[..., :middle]], axis=-1)
    return values * cos_table + turned * sin_table


def unrotate(gradient, cos_table, sin_table):
    middle = gradient.shape[-1] // 2
    weighted = gradient * sin_table
    turned = jnp.concatenate([weighted[..., middle:], -weighted[..., :middle]], axis=-1)
    return gradient * cos_table + turned


def matmul_rows(first_op, second_op):
    return lax.dot_general(
        first_op, second_op, (((0,), (0,)), ((), ())), preferred_element_type=jnp.float32
    )


def matmul_cols(first_op, second_op):
    return lax.dot_general(
        first_op, second_op, (((1,), (1,)), ((), ())), preferred_element_type=jnp.float32
    )


def project_any(normed_all, w_qkv, cos_heads, sin_heads, heads_here, kv_here):
    seq_len = normed_all.shape[0]
    projected = jnp.dot(normed_all, w_qkv, preferred_element_type=jnp.float32)
    query_width = heads_here * HD
    kv_width = kv_here * HD
    group_size = heads_here // kv_here
    query_heads = rotate(
        projected[:, :query_width].reshape(seq_len, heads_here, HD), cos_heads, sin_heads
    )
    key_heads = rotate(
        projected[:, query_width : query_width + kv_width].reshape(seq_len, kv_here, HD),
        cos_heads,
        sin_heads,
    )
    value_heads = projected[:, query_width + kv_width :].reshape(seq_len, kv_here, HD)
    query_heads = jnp.transpose(query_heads.astype(jnp.bfloat16), (1, 0, 2)).reshape(
        kv_here, group_size, seq_len, HD
    )
    key_heads = jnp.transpose(key_heads.astype(jnp.bfloat16), (1, 0, 2))
    value_heads = jnp.transpose(value_heads.astype(jnp.bfloat16), (1, 0, 2))
    return (query_heads, key_heads, value_heads)


def masked_scores(query_block, key_heads, row_start, length):
    block_rows = query_block.shape[2]
    seq_len = key_heads.shape[1]
    scores = jnp.einsum(
        "kgqd,ksd->kgqs", query_block, key_heads, preferred_element_type=jnp.float32
    ) * HD ** (-0.5)
    row_pos = row_start + jnp.arange(block_rows, dtype=jnp.int32)
    key_pos = jnp.arange(seq_len, dtype=jnp.int32)
    allowed = (key_pos[None, :] <= row_pos[:, None]) & (key_pos[None, :] < length)
    return jnp.where(allowed, scores, -1e30)


def attend_forward_any(query_heads, key_heads, value_heads, length, block_rows):
    seq_len = query_heads.shape[2]
    outputs = []
    log_sums = []
    for row_start in range(0, seq_len, block_rows):
        query_block = query_heads[:, :, row_start : row_start + block_rows]
        scores = masked_scores(query_block, key_heads, row_start, length)
        row_peak = jnp.max(scores, axis=-1, keepdims=True)
        raised = jnp.exp(scores - row_peak)
        row_total = jnp.sum(raised, axis=-1, keepdims=True)
        attn_probs = (raised / row_total).astype(jnp.bfloat16)
        outputs.append(
            jnp.einsum(
                "kgqs,ksd->kgqd", attn_probs, value_heads, preferred_element_type=jnp.float32
            )
        )
        log_sums.append((row_peak + jnp.log(row_total))[..., 0])
    return (jnp.concatenate(outputs, axis=2), jnp.concatenate(log_sums, axis=2))


def attend_backward_any(query_heads, key_heads, value_heads, out_back, log_sums, length, block_rows):
    seq_len = query_heads.shape[2]
    query_grads = []
    key_grad = jnp.zeros(key_heads.shape, jnp.float32)
    value_grad = jnp.zeros(value_heads.shape, jnp.float32)
    for row_start in range(0, seq_len, block_rows):
        query_block = query_heads[:, :, row_start : row_start + block_rows]
        back_block = out_back[:, :, row_start : row_start + block_rows]
        scores = masked_scores(query_block, key_heads, row_start, length)
        attn_probs = jnp.exp(scores - log_sums[:, :, row_start : row_start + block_rows, None])
        probs_back = jnp.einsum(
            "kgqd,ksd->kgqs", back_block, value_heads, preferred_element_type=jnp.float32
        )
        row_shift = jnp.sum(attn_probs * probs_back, axis=-1, keepdims=True)
        scores_back = (HD ** (-0.5) * attn_probs * (probs_back - row_shift)).astype(jnp.bfloat16)
        query_grads.append(
            jnp.einsum("kgqs,ksd->kgqd", scores_back, key_heads, preferred_element_type=jnp.float32)
        )
        key_grad = key_grad + jnp.einsum(
            "kgqs,kgqd->ksd", scores_back, query_block, preferred_element_type=jnp.float32
        )
        value_grad = value_grad + jnp.einsum(
            "kgqs,kgqd->ksd",
            attn_probs.astype(jnp.bfloat16),
            back_block,
            preferred_element_type=jnp.float32,
        )
    return (jnp.concatenate(query_grads, axis=2), key_grad, value_grad)


def local_any(
    tokens,
    cotangent,
    lengths,
    owners,
    master,
    moment_one,
    moment_two,
    norm_gains,
    gain_first,
    gain_second,
):
    wide_count = lax.axis_size("wide")
    narrow_count = lax.axis_size("narrow")
    capacity = master.shape[0]
    unit_rows = master.shape[2]
    unit_cols = master.shape[3]
    unit_count = owners.shape[0]
    row_count = tokens.shape[0]
    seq_len = row_count * narrow_count
    slot_place, _ = positions(owners, wide_count, capacity)
    own_slots = master[:, 0].astype(jnp.bfloat16)
    all_slots = lax.all_gather(own_slots, "wide", axis=0, tiled=True)
    unit_data = jnp.take(all_slots, slot_place, axis=0)
    row_blocks = D // unit_rows
    col_blocks = unit_count // row_blocks
    packed = jnp.transpose(
        unit_data.reshape(row_blocks, col_blocks, unit_rows, unit_cols), (0, 2, 1, 3)
    ).reshape(D, col_blocks * unit_cols)
    heads_here = H // narrow_count
    kv_here = KV // narrow_count
    group_size = heads_here // kv_here
    query_width = heads_here * HD
    kv_width = kv_here * HD
    ff_width = FF // narrow_count
    qkv_end = query_width + 2 * kv_width
    out_end = qkv_end + query_width
    gate_end = out_end + 2 * ff_width
    w_qkv = packed[:, :qkv_end]
    w_out_t = packed[:, qkv_end:out_end]
    w_gate_up = packed[:, out_end:gate_end]
    w_down_t = packed[:, gate_end:]
    cos_table, sin_table = tables(seq_len, HD)
    cos_heads = cos_table[:, None, :]
    sin_heads = sin_table[:, None, :]
    block_rows = min(512, seq_len)
    wide_index = lax.axis_index("wide")
    length = lengths[wide_index]
    inputs = tokens.astype(jnp.float32)
    normed = rmsnorm(inputs, norm_gains[0]).astype(jnp.bfloat16)
    normed_all = lax.all_gather(normed, "narrow", axis=0, tiled=True)
    query_heads, key_heads, value_heads = project_any(
        normed_all, w_qkv, cos_heads, sin_heads, heads_here, kv_here
    )
    attended, log_sums = attend_forward_any(query_heads, key_heads, value_heads, length, block_rows)
    attended = (
        jnp.transpose(attended.reshape(heads_here, seq_len, HD), (1, 0, 2))
        .reshape(seq_len, query_width)
        .astype(jnp.bfloat16)
    )
    residual = inputs + lax.psum_scatter(
        matmul_cols(attended, w_out_t), "narrow", scatter_dimension=0, tiled=True
    )
    normed_two = rmsnorm(residual, norm_gains[1]).astype(jnp.bfloat16)
    mlp_input = lax.all_gather(normed_two, "narrow", axis=0, tiled=True)
    gate_up = jnp.dot(mlp_input, w_gate_up, preferred_element_type=jnp.float32)
    hidden = (jax.nn.silu(gate_up[:, :ff_width]) * gate_up[:, ff_width:]).astype(jnp.bfloat16)
    output = residual + lax.psum_scatter(
        matmul_cols(hidden, w_down_t).astype(jnp.bfloat16),
        "narrow",
        scatter_dimension=0,
        tiled=True,
    ).astype(jnp.float32)
    down_back = lax.all_gather(cotangent, "narrow", axis=0, tiled=True)
    mlp_again = lax.all_gather(normed_two, "narrow", axis=0, tiled=True)
    gate_up = jnp.dot(mlp_again, w_gate_up, preferred_element_type=jnp.float32)
    hidden_back = jnp.dot(down_back, w_down_t, preferred_element_type=jnp.float32)
    grad_down_t = matmul_rows(down_back, hidden)
    _, swiglu_pull = jax.vjp(
        lambda gate_in, upper_in: jax.nn.silu(gate_in) * upper_in,
        gate_up[:, :ff_width],
        gate_up[:, ff_width:],
    )
    gate_back, upper_back = swiglu_pull(hidden_back)
    gate_up_back = jnp.concatenate([gate_back, upper_back], axis=1).astype(jnp.bfloat16)
    grad_gate_up = matmul_rows(mlp_again, gate_up_back)
    norm_two_back = lax.psum_scatter(
        matmul_cols(gate_up_back, w_gate_up).astype(jnp.bfloat16),
        "narrow",
        scatter_dimension=0,
        tiled=True,
    ).astype(jnp.float32)
    _, norm_two_pull = jax.vjp(rmsnorm, residual, norm_gains[1])
    resid_part, gain_two = norm_two_pull(norm_two_back)
    resid_back = cotangent.astype(jnp.float32) + resid_part
    attn_back = lax.all_gather(resid_back.astype(jnp.bfloat16), "narrow", axis=0, tiled=True)
    normed_again = lax.all_gather(normed, "narrow", axis=0, tiled=True)
    query_heads, key_heads, value_heads = project_any(
        normed_again, w_qkv, cos_heads, sin_heads, heads_here, kv_here
    )
    out_back = jnp.dot(attn_back, w_out_t, preferred_element_type=jnp.float32).astype(jnp.bfloat16)
    grad_out_t = matmul_rows(attn_back, attended)
    out_back = jnp.transpose(out_back.reshape(seq_len, heads_here, HD), (1, 0, 2)).reshape(
        kv_here, group_size, seq_len, HD
    )
    query_grad, key_grad, value_grad = attend_backward_any(
        query_heads, key_heads, value_heads, out_back, log_sums, length, block_rows
    )
    query_grad = jnp.transpose(query_grad.reshape(heads_here, seq_len, HD), (1, 0, 2))
    query_grad = unrotate(query_grad, cos_heads, sin_heads).reshape(seq_len, query_width)
    key_grad = unrotate(jnp.transpose(key_grad, (1, 0, 2)), cos_heads, sin_heads).reshape(
        seq_len, kv_width
    )
    value_grad = jnp.transpose(value_grad, (1, 0, 2)).reshape(seq_len, kv_width)
    qkv_back = jnp.concatenate([query_grad, key_grad, value_grad], axis=1).astype(jnp.bfloat16)
    grad_qkv = matmul_rows(normed_again, qkv_back)
    norm_one_back = lax.psum_scatter(
        matmul_cols(qkv_back, w_qkv).astype(jnp.bfloat16), "narrow", scatter_dimension=0, tiled=True
    ).astype(jnp.float32)
    _, norm_one_pull = jax.vjp(rmsnorm, inputs, norm_gains[0])
    input_part, gain_one = norm_one_pull(norm_one_back)
    input_grad = (resid_back + input_part).astype(jnp.bfloat16)
    grad_packed = jnp.concatenate([grad_qkv, grad_out_t, grad_gate_up, grad_down_t], axis=1)
    grad_units = jnp.transpose(
        grad_packed.reshape(row_blocks, unit_rows, col_blocks, unit_cols), (0, 2, 1, 3)
    ).reshape(unit_count, unit_rows, unit_cols)
    grad_slots = (
        jnp.zeros((wide_count * capacity, unit_rows, unit_cols), jnp.float32)
        .at[slot_place]
        .set(grad_units)
    )
    owned_grads = lax.psum_scatter(
        grad_slots.astype(jnp.bfloat16), "wide", scatter_dimension=0, tiled=True
    ).astype(jnp.float32)[:, None]
    new_master, new_first, new_second = adamw(
        master, owned_grads, moment_one, moment_two, 0.02, 0.1
    )
    gain_grads = lax.psum(jnp.stack([gain_one, gain_two]), ("wide", "narrow"))
    new_gains, unused, gain_second_new = adamw(
        norm_gains, gain_grads, gain_first, gain_second, 0.5, 0.0
    )
    return (
        output.astype(jnp.bfloat16),
        input_grad,
        owned_grads,
        new_master,
        new_master.astype(jnp.bfloat16),
        new_first,
        new_second,
        gain_grads,
        gain_second_new,
        new_gains,
    )


def solution(mesh):
    COLLECTIVE[0] = 0
    rows = P(("wide", "narrow"), None)
    units = P("wide", "narrow", None, None)
    return jax.shard_map(
        local if mesh.shape["wide"] == 8 and mesh.shape["narrow"] == 4 else local_any,
        mesh=mesh,
        in_specs=(rows, rows, P(), P(), units, units, units, P(), P(), P()),
        out_specs=(rows, rows, units, units, units, units, units, P(), P(), P()),
        check_vma=False,
    )
```

```python
import functools

import jax
import jax.numpy as jnp
import numpy as np
from jax import lax
from jax.experimental import pallas as pl
from jax.experimental.pallas import tpu as pltpu
from jax.sharding import PartitionSpec as P

D = 2048
H = 32
KV = 8
HD = 64
FF = 8192
STEP = 5
LANES = 128
MIB = 1 << 20
ANY = pl.BlockSpec(memory_space=pl.ANY)
VMEM = pl.BlockSpec(memory_space=pltpu.VMEM)
SMEM = pl.BlockSpec(memory_space=pltpu.SMEM)

f32 = jnp.float32
bf16 = jnp.bfloat16


def dot(first_op, second_op, first_dim, second_dim):
    return lax.dot_general(
        first_op,
        second_op,
        (((first_dim,), (second_dim,)), ((), ())),
        preferred_element_type=f32,
    )


def shaped(shape, kind=bf16):
    return jax.ShapeDtypeStruct(shape, kind)


def blocks(shape, place):
    return pl.BlockSpec(shape, place)


class Send:
    def __init__(self, source, land, axis, step, source_at=None, land_at=None, landed=False, needs=()):
        self.source, self.land, self.axis, self.step = source, land, axis, step
        self.source_at, self.land_at = source_at, land_at
        self.landed, self.needs = landed, needs


COLLECTIVE = [0]


def run_sends(sends, sources, lands, send_sem, recv_sem):
    count = lax.axis_size("narrow")
    wide, narrow = lax.axis_index("wide"), lax.axis_index("narrow")

    def target(axis, step):
        if axis == "wide":
            return {"wide": jnp.bitwise_xor(wide, step)}
        return {"narrow": lax.rem(narrow + step, count)}

    copies = []
    for k, send in enumerate(sends):
        ref = (lands if send.landed else sources)[send.source]
        if send.source_at is not None:
            ref = ref.at[send.source_at(wide, narrow)]
        land = lands[send.land]
        if send.land_at is not None:
            land = land.at[send.land_at(wide, narrow)]
        copies.append(
            pltpu.make_async_remote_copy(
                src_ref=ref,
                dst_ref=land,
                send_sem=send_sem.at[k],
                recv_sem=recv_sem.at[k],
                device_id=target(send.axis, send.step),
                device_id_type=pl.DeviceIdType.MESH,
            )
        )

    def start():
        partners = set()
        for send in sends:
            if send.axis == "wide":
                partners.add(("wide", send.step))
            else:
                partners.add(("narrow", send.step % count))
                partners.add(("narrow", -send.step % count))
        barrier = pltpu.get_barrier_semaphore()
        for axis, step in sorted(partners):
            pl.semaphore_signal(
                barrier, inc=1, device_id=target(axis, step), device_id_type=pl.DeviceIdType.MESH
            )
        pl.semaphore_wait(barrier, len(partners))
        for send, copy in zip(sends, copies):
            if not send.needs and not send.landed:
                copy.start()

    def finish():
        arrived = set()
        for send, copy in zip(sends, copies):
            for k in send.needs:
                if k not in arrived:
                    copies[k].wait_recv()
                    arrived.add(k)
            if send.needs or send.landed:
                copy.start()
        for k, copy in enumerate(copies):
            copy.wait_send()
            if k not in arrived:
                copy.wait_recv()

    return start, finish


def call(
    body, ins, in_specs, out_shape, out_specs, *, name, grid=(), prefetch=(), scratch=(), deps=(),
    aliases=None, mib=56, flops=0, moved=0, sends=(), sources=(), lands=(), inner=(), closing=None,
):
    first = len(prefetch) + len(ins)
    single = not isinstance(out_shape, (list, tuple))
    out_shapes = [out_shape] if single else list(out_shape)
    specs = [out_specs] if single else list(out_specs)
    out_count = len(out_shapes)
    land_count = len(lands)

    def wrapped(*refs):
        given = refs[:first]
        refs = refs[first:]
        source_refs = refs[: len(sources)]
        refs = refs[len(sources) + len(deps) :]
        outs, refs = refs[:out_count], refs[out_count:]
        land_refs, refs = refs[:land_count], refs[land_count:]
        if not sends:
            body(*given, *outs, *refs)
            return
        own, (send_sem, recv_sem) = refs[:-2], refs[-2:]
        start, finish = run_sends(
            sends, source_refs, [*land_refs, *[own[k] for k in inner]], send_sem, recv_sem
        )

        def last():
            finish()
            if closing is not None:
                closing(land_refs, (*given, *outs, *own))

        if grid:
            steps = [pl.program_id(k) for k in range(len(grid))]
            begins = functools.reduce(jnp.logical_and, [step == 0 for step in steps])
            ends = functools.reduce(
                jnp.logical_and, [step == size - 1 for step, size in zip(steps, grid)]
            )
            pl.when(begins)(start)
            body(*given, *outs, *own)
            pl.when(ends)(last)
        else:
            start()
            body(*given, *outs, *own)
            last()

    extra = {}
    if sends:
        COLLECTIVE[0] += 1
        extra = {"collective_id": COLLECTIVE[0], "has_side_effects": True}
        scratch = [*scratch] + [pltpu.SemaphoreType.DMA((len(sends),))] * 2
    results = pl.pallas_call(
        wrapped,
        grid_spec=pltpu.PrefetchScalarGridSpec(
            num_scalar_prefetch=len(prefetch),
            grid=grid,
            in_specs=list(in_specs) + [ANY] * (len(sources) + len(deps)),
            out_specs=specs + [ANY] * land_count,
            scratch_shapes=list(scratch),
        ),
        out_shape=out_shapes + [shaped(*land) if isinstance(land[0], tuple) else shaped(land) for land in lands],
        input_output_aliases=aliases or {},
        compiler_params=pltpu.CompilerParams(vmem_limit_bytes=mib * MIB, **extra),
        cost_estimate=pl.CostEstimate(
            flops=int(flops), bytes_accessed=int(moved), transcendentals=0
        ),
        name=name,
    )(*prefetch, *ins, *sources, *deps)
    return results[0] if single and not sends else list(results)


def tables(length_all, head_size):
    inverse = 500000.0 ** (-jnp.arange(0, head_size, 2, dtype=f32) / head_size)
    angles = jnp.arange(length_all, dtype=f32)[:, None] * inverse[None, :]
    angles = jnp.concatenate([angles, angles], axis=1)
    return (jnp.cos(angles), jnp.sin(angles))


def turn_tables(length_all):
    inverse = np.float32(500000.0) ** (-np.arange(0, HD, 2, dtype=np.float32) / np.float32(HD))
    angles = np.arange(length_all, dtype=np.float32)[:, None] * inverse[None, :]
    angles = np.concatenate([angles] * (2 * LANES // HD), axis=1).astype(np.float32)
    return jnp.asarray(np.cos(angles)), jnp.asarray(np.sin(angles))


def rmsnorm(values, weight_gain):
    return (
        values * lax.rsqrt(jnp.mean(values * values, axis=-1, keepdims=True) + 1e-05) * weight_gain
    )


def positions(owners, wide_count, capacity):
    onehot = (owners[:, None] == jnp.arange(wide_count, dtype=jnp.int32)[None, :]).astype(jnp.int32)
    before = jnp.cumsum(onehot, axis=0) - onehot
    return (owners * capacity + jnp.sum(before * onehot, axis=1), jnp.sum(onehot, axis=0))


def adamw(weight, gradient, moment_one, moment_two, rate, decay):
    moment_one = 0.5 * moment_one + 0.5 * gradient
    moment_two = 0.5 * moment_two + 0.5 * gradient * gradient
    correct = 1.0 - 0.5**STEP
    update = moment_one / correct / (jnp.sqrt(moment_two / correct) + 1e-08)
    return (weight - rate * (update + decay * weight), moment_one, moment_two)


def turn_kernel(unit_ref, out_ref):
    parts, step, piece, unit_rows = out_ref.shape
    for k in range(step):
        out_ref[:, k] = (
            jnp.transpose(unit_ref[k, 0], (1, 0)).reshape(parts, piece, unit_rows).astype(bf16)
        )


def turn_units(master, parts, deps):
    capacity, _, unit_rows, unit_cols = master.shape
    piece = unit_cols // parts
    step = capacity // 2 if capacity % 2 == 0 else 1
    return call(
        turn_kernel,
        [master],
        [blocks((step, 1, unit_rows, unit_cols), lambda s: (s, 0, 0, 0))],
        shaped((parts, capacity, piece, unit_rows)),
        blocks((parts, step, piece, unit_rows), lambda s: (0, s, 0, 0)),
        grid=(capacity // step,),
        deps=deps,
        mib=60,
        moved=master.size * 6,
        name="turn_units",
    )


def pick_kernel(turn_ref, place_ref, own_ref, got_ref, out_ref, sem, *, col_blocks):
    _, capacity, piece, unit_rows = got_ref.shape

    def start(unit, carry):
        half = unit // col_blocks
        block = unit - half * col_blocks
        owner = place_ref[unit] // capacity
        slot = place_ref[unit] - owner * capacity
        target = out_ref.at[
            pl.ds(pl.multiple_of(block * piece, piece), piece),
            pl.ds(pl.multiple_of(half * unit_rows, unit_rows), unit_rows),
        ]

        @pl.when(owner == turn_ref[0])
        def _():
            pltpu.make_async_copy(own_ref.at[owner, slot], target, sem).start()

        @pl.when(owner != turn_ref[0])
        def _():
            pltpu.make_async_copy(got_ref.at[owner, slot], target, sem).start()

        return carry

    lax.fori_loop(0, place_ref.shape[0], start, 0)
    pltpu.make_async_copy(out_ref, out_ref, sem).wait()


def pick_units(turn, slot_place, own, got, row_blocks):
    _, _, piece, unit_rows = got.shape
    unit_count = slot_place.shape[0]
    col_blocks = unit_count // row_blocks
    return call(
        functools.partial(pick_kernel, col_blocks=col_blocks),
        [turn, slot_place, own, got],
        [SMEM, SMEM, ANY, ANY],
        shaped((col_blocks * piece, row_blocks * unit_rows)),
        VMEM,
        scratch=[pltpu.SemaphoreType.DMA],
        moved=unit_count * piece * unit_rows * 12,
        name="pick_units",
    )


def unpick_kernel(block_ref, half_ref, rows_ref, low_ref, high_ref, sems, *, piece, unit_rows):
    owners, part, _, _ = low_ref.shape
    capacity = part + high_ref.shape[1]

    def start(owner, carry):
        for slot in range(capacity):
            out_ref = high_ref if slot >= part else low_ref
            place = owner * capacity + slot
            pltpu.make_async_copy(
                rows_ref.at[
                    pl.ds(pl.multiple_of(block_ref[place] * piece, piece), piece),
                    pl.ds(pl.multiple_of(half_ref[place] * unit_rows, unit_rows), unit_rows),
                ],
                out_ref.at[owner, slot - part if slot >= part else slot],
                sems.at[int(slot >= part)],
            ).start()
        return carry

    lax.fori_loop(0, owners, start, 0)
    pltpu.make_async_copy(low_ref, low_ref, sems.at[0]).wait()
    pltpu.make_async_copy(high_ref, high_ref, sems.at[1]).wait()


def unpick_units(rows, block_of, half_of, owners, piece, unit_rows):
    slots = block_of.shape[0]
    capacity = slots // owners
    low = capacity * 5 // 16 * 2
    sizes = (low, capacity - low)
    return call(
        functools.partial(unpick_kernel, piece=piece, unit_rows=unit_rows),
        [block_of, half_of, rows],
        [SMEM, SMEM, VMEM],
        [shaped((owners, size, piece, unit_rows)) for size in sizes],
        [ANY, ANY],
        scratch=[pltpu.SemaphoreType.DMA((2,))],
        moved=slots * piece * unit_rows * 8,
        name="unpick_units",
    )


def apply_update(gradient, master_ref, one_ref, two_ref, outs, k=0):
    grad_out, master_out, copy_out, one_out, two_out = outs
    weight, one, two = adamw(master_ref[k, 0], gradient, one_ref[k, 0], two_ref[k, 0], 0.02, 0.1)
    grad_out[k, 0] = gradient
    master_out[k, 0] = weight
    copy_out[k, 0] = weight.astype(bf16)
    one_out[k, 0] = one
    two_out[k, 0] = two


def unit_gradient(parts, piece, unit_rows):
    return jnp.transpose(parts.astype(f32).reshape(-1, unit_rows), (1, 0))


def all_pieces(grad_ref, own_ref, turn, k=0):
    place = lax.broadcasted_iota(jnp.int32, (grad_ref.shape[0], 1, 1), 0)
    own = own_ref[0, k : k + 1].astype(f32)
    return jnp.where(place == turn, own, grad_ref[:, k].astype(f32))


def update_kernel(filled_ref, grad_ref, own_ref, master_ref, one_ref, two_ref, *refs, first):
    _, step, piece, unit_rows = grad_ref.shape
    for k in range(step):
        pieces = all_pieces(grad_ref, own_ref, lax.axis_index("wide"), k)
        slot = jnp.zeros((unit_rows, 1), jnp.int32) + (pl.program_id(0) * step + k + first)
        gradient = jnp.where(
            slot < filled_ref[0], unit_gradient(pieces, piece, unit_rows), 0.0
        )
        apply_update(gradient, master_ref, one_ref, two_ref, refs[-5:], k)


def update_outs(master):
    whole = shaped(master.shape, f32)
    return [whole, whole, shaped(master.shape), whole, whole]


def update_units(filled, grads, own, first, master, moment_one, moment_two, done, deps=()):
    _, _, unit_rows, unit_cols = master.shape
    parts, slots, piece, _ = grads.shape
    step = 2 if slots % 2 == 0 and first % 2 == 0 else 1
    unit = blocks((step, 1, unit_rows, unit_cols), lambda s: (s + first // step, 0, 0, 0))
    return call(
        functools.partial(update_kernel, first=first),
        [filled, grads, own, master, moment_one, moment_two, *done],
        [
            SMEM,
            blocks((parts, step, piece, unit_rows), lambda s: (0, s, 0, 0)),
            blocks((1, step, piece, unit_rows), lambda s: (lax.axis_index("wide"), s, 0, 0)),
            unit,
            unit,
            unit,
        ]
        + [ANY] * len(done),
        update_outs(master),
        [unit] * 5,
        grid=(slots // step,),
        aliases={6 + k: k for k in range(len(done))},
        moved=master.size * 16,
        mib=40,
        deps=deps,
        name="update_units",
    )


def lane_index(shape):
    return lax.broadcasted_iota(jnp.int32, shape, 1)


def rope(tile, cos_tile, sin_tile):
    lower = lane_index(tile.shape) % HD < HD // 2
    ahead = pltpu.roll(tile, LANES - HD // 2, 1)
    behind = pltpu.roll(tile, HD // 2, 1)
    return tile * cos_tile + jnp.where(lower, -ahead, behind) * sin_tile


def unrope(tile, cos_tile, sin_tile):
    lower = lane_index(tile.shape) % HD < HD // 2
    weighted = tile * sin_tile
    ahead = pltpu.roll(weighted, LANES - HD // 2, 1)
    behind = pltpu.roll(weighted, HD // 2, 1)
    return tile * cos_tile + jnp.where(lower, ahead, -behind)


def project_kernel(rows_ref, w_ref, cos_ref, sin_ref, out_ref, *, group_width):
    product = dot(rows_ref[...], w_ref[...], 1, 1)
    for start in range(0, out_ref.shape[1], LANES):
        tile = product[:, start : start + LANES]
        turned = rope(tile, cos_ref[...], sin_ref[...])
        if (start + LANES) % group_width == 0:
            tile = jnp.where(lane_index(tile.shape) < HD, turned, tile).astype(bf16)
        else:
            tile = turned.astype(bf16) * HD ** (-0.5)
        out_ref[:, start : start + LANES] = tile


def project(rows, w_qkv, cos_all, sin_all, group_width, step, deps):
    count = rows.shape[0]
    width = w_qkv.shape[0]
    return call(
        functools.partial(project_kernel, group_width=group_width),
        [rows, w_qkv, cos_all, sin_all],
        [
            blocks((step, D), lambda i: (i, 0)),
            blocks((width, D), lambda i: (0, 0)),
            blocks((step, LANES), lambda i: (i, 0)),
            blocks((step, LANES), lambda i: (i, 0)),
        ],
        shaped((count, width)),
        blocks((step, width), lambda i: (i, 0)),
        grid=(count // step,),
        deps=deps,
        flops=2 * count * width * D,
        name="project",
    )


def extend(tile, kx, vx):
    tile = tile.astype(f32)
    other = pltpu.roll(tile, HD, 1)
    low = lane_index(tile.shape) < HD
    kx[0] = jnp.where(low, tile, 0.0).astype(bf16)
    kx[1] = jnp.where(low, 0.0, other).astype(bf16)
    vx[0] = jnp.where(low, other, 0.0).astype(bf16)
    vx[1] = jnp.where(low, 0.0, tile).astype(bf16)


def forward_kernel(length_ref, qkv_ref, out_ref, log_ref, kx, vx, *, block):
    length = length_ref[0]
    seq_len, group_width = qkv_ref.shape
    pairs = group_width // LANES - 1
    extend(qkv_ref[:, pairs * LANES :], kx, vx)
    row = lax.broadcasted_iota(jnp.int32, (block, block), 0)
    col = lax.broadcasted_iota(jnp.int32, (block, block), 1)
    causal = col <= row
    key_row = lax.broadcasted_iota(jnp.int32, (1, seq_len), 1)
    bias = jnp.where(key_row < length, 0.0, -1e30).astype(f32)
    low = lane_index((block, LANES)) < HD
    for pair in range(pairs):
        lanes = slice(pair * LANES, (pair + 1) * LANES)
        for start in range(0, seq_len, block):
            query = qkv_ref[start : start + block, lanes]
            total = None
            logs = []
            for half in range(2):
                diagonal = dot(query, kx[half, start : start + block, :], 1, 1)
                diagonal = jnp.where(causal, diagonal + bias[:, start : start + block], -1e30)
                peak = jnp.max(diagonal, axis=1, keepdims=True)
                if start:
                    before = dot(query, kx[half, :start, :], 1, 1) + bias[:, :start]
                    peak = jnp.maximum(peak, jnp.max(before, axis=1, keepdims=True))
                    before = jnp.exp(before - peak)
                diagonal = jnp.exp(diagonal - peak)
                row_sum = jnp.sum(diagonal, axis=1, keepdims=True)
                part = dot(diagonal.astype(bf16), vx[half, start : start + block, :], 1, 0)
                if start:
                    row_sum = row_sum + jnp.sum(before, axis=1, keepdims=True)
                    part = part + dot(before.astype(bf16), vx[half, :start, :], 1, 0)
                part = part / row_sum
                total = part if total is None else total + part
                logs.append(peak + jnp.log(row_sum))
            out_ref[start : start + block, lanes] = total.astype(bf16)
            tile = jnp.transpose(jnp.where(low, logs[0], logs[1]), (1, 0))
            log_ref[0, 2 * pair : 2 * pair + 1, start : start + block] = tile[0:1]
            log_ref[0, 2 * pair + 1 : 2 * pair + 2, start : start + block] = tile[HD : HD + 1]


def attend_forward(length, qkv, groups, block, deps=(), **beside):
    seq_len, width = qkv.shape
    group_width = width // groups
    query_width = group_width - LANES
    return call(
        functools.partial(forward_kernel, block=block),
        [length, qkv],
        [SMEM, blocks((seq_len, group_width), lambda g: (0, g))],
        [shaped((seq_len, groups * query_width)), shaped((groups, 8, seq_len), f32)],
        [
            blocks((seq_len, query_width), lambda g: (0, g)),
            blocks((1, 8, seq_len), lambda g: (g, 0, 0)),
        ],
        grid=(groups,),
        scratch=[pltpu.VMEM((2, seq_len, LANES), bf16), pltpu.VMEM((2, seq_len, LANES), bf16)],
        deps=deps,
        mib=48,
        flops=groups * seq_len * seq_len * 2048,
        **beside,
        name="attend_forward",
    )


def backward_kernel(
    length_ref, qkv_ref, back_ref, out_ref, log_ref, cos_ref, sin_ref, *refs, block
):
    grad_ref, kx, vx, dk, dv = refs
    length = length_ref[0]
    seq_len, group_width = qkv_ref.shape
    pairs = group_width // LANES - 1
    extend(qkv_ref[:, pairs * LANES :], kx, vx)
    dk[...] = jnp.zeros(dk.shape, f32)
    dv[...] = jnp.zeros(dv.shape, f32)
    key = lax.broadcasted_iota(jnp.int32, (block, block), 0)
    row = lax.broadcasted_iota(jnp.int32, (block, block), 1)
    causal = key <= row
    for pair in range(pairs):
        lanes = slice(pair * LANES, (pair + 1) * LANES)
        for start in range(0, seq_len, block):
            here = slice(start, start + block)
            query = qkv_ref[here, lanes]
            back = back_ref[here, lanes]
            turned = jnp.transpose(back.astype(f32) * out_ref[here, lanes].astype(f32), (1, 0))
            query_grad = None
            for half in range(2):
                log_row = log_ref[0, 2 * pair + half : 2 * pair + half + 1, here]
                shift = jnp.sum(turned[half * HD : half * HD + HD], axis=0, keepdims=True)
                for first in range(0, start + block, block):
                    keys = slice(first, first + block)
                    scores = dot(kx[half, keys, :], query, 1, 1)
                    probs = jnp.exp(scores - log_row)
                    if first + block > seq_len // 2:
                        probs = jnp.where(key + first < length, probs, 0.0)
                    if first == start:
                        probs = jnp.where(causal, probs, 0.0)
                    probs_back = dot(vx[half, keys, :], back, 1, 1)
                    scores_back = (probs * (probs_back - shift)).astype(bf16)
                    dv[half, keys, :] += dot(probs.astype(bf16), back, 1, 0)
                    dk[half, keys, :] += dot(scores_back, query, 1, 0)
                    part = dot(scores_back, kx[half, keys, :], 0, 0)
                    query_grad = part if query_grad is None else query_grad + part
            query_grad = unrope(query_grad * HD ** (-0.5), cos_ref[here, :], sin_ref[here, :])
            grad_ref[here, lanes] = query_grad.astype(bf16)

    low = lane_index((seq_len, LANES)) < HD
    key_grad = jnp.where(low, dk[0] + pltpu.roll(dk[1], HD, 1), 0.0)
    key_grad = unrope(key_grad, cos_ref[...], sin_ref[...])
    value_grad = pltpu.roll(dv[0], HD, 1) + dv[1]
    grad_ref[:, pairs * LANES :] = jnp.where(low, key_grad, value_grad).astype(bf16)


def attend_backward(group, groups, length, qkv, back, out, logs, cos_all, sin_all, block, deps=(), **beside):
    seq_len, width = qkv.shape
    group_width = width // groups
    query_width = group_width - LANES
    given = blocks((seq_len, query_width), lambda i: (0, group))
    table = blocks((seq_len, LANES), lambda i: (0, 0))
    return call(
        functools.partial(backward_kernel, block=block),
        [length, qkv, back, out, logs, cos_all, sin_all],
        [
            SMEM,
            blocks((seq_len, group_width), lambda i: (0, group)),
            given,
            given,
            blocks((1, 8, seq_len), lambda i: (group, 0, 0)),
            table,
            table,
        ],
        shaped((seq_len, group_width)),
        blocks((seq_len, group_width), lambda i: (0, 0)),
        grid=(1,),
        scratch=[
            pltpu.VMEM((2, seq_len, LANES), bf16),
            pltpu.VMEM((2, seq_len, LANES), bf16),
            pltpu.VMEM((2, seq_len, LANES), f32),
            pltpu.VMEM((2, seq_len, LANES), f32),
        ],
        deps=deps,
        mib=48,
        flops=seq_len * seq_len * 5120,
        **beside,
        name="attend_backward",
    )


def branch_kernel(
    attended_ref, others_ref, w_ref, tokens_ref, gain_ref, residual_ref, normed_ref
):
    parts = others_ref.shape[0] + 1
    step, width = others_ref.shape[1:]
    here = lax.axis_index("narrow")
    first = here * (attended_ref.shape[0] // parts) + pl.program_id(0) * step
    total = tokens_ref[...].astype(f32)
    for k in range(parts):
        part = (
            others_ref[k - 1]
            if k
            else attended_ref[pl.ds(pl.multiple_of(first, step), step), :]
        )
        place = lax.rem(here - k + parts, parts) * width
        total = total + dot(part, w_ref[pl.ds(pl.multiple_of(place, width), width), :], 1, 0)
    residual_ref[...] = total
    normed_ref[...] = rmsnorm(total, gain_ref[...]).astype(bf16)


def branch(attended, others, w_out, tokens, gain, **beside):
    groups, count, width = others.shape
    step = 128
    rows = blocks((step, D), lambda i: (i, 0))
    return call(
        branch_kernel,
        [attended, others, w_out, tokens, gain],
        [
            blocks(attended.shape, lambda i: (0, 0)),
            blocks((groups, step, width), lambda i: (0, i, 0)),
            blocks((D, D), lambda i: (0, 0)),
            rows,
            blocks((1, D), lambda i: (0, 0)),
        ],
        [shaped((count, D), f32), shaped((count, D))],
        [rows, rows],
        grid=(count // step,),
        flops=2 * count * D * D,
        name="branch",
        **beside,
    )


def spread_kernel(turn_ref, back_ref, w_ref, out_ref):
    out_ref[0] = dot(back_ref[...], w_ref[...], 1, 1).astype(bf16)


def spread(turn, back, w_out, groups, deps=()):
    count = back.shape[0]
    width = D // groups
    return call(
        spread_kernel,
        [back, w_out],
        [
            blocks((count, D), lambda i, t: (0, 0)),
            blocks((width, D), lambda i, t: (lax.rem(t[1] + i, groups), 0)),
        ],
        shaped((groups, count, width)),
        blocks((1, count, width), lambda i, t: (i, 0, 0)),
        grid=(groups,),
        prefetch=[turn],
        deps=deps,
        flops=2 * count * D * D,
        mib=32,
        name="spread",
    )


def first_back_kernel(*refs, groups, sums):
    taken, weights, grads = refs[:groups], refs[groups : 2 * groups], refs[2 * groups : 3 * groups]
    terms, outs = refs[3 * groups : -2 - sums], refs[-2 - sums :]
    outs[0][...] = sum(dot(taken[g][...], weights[g][...], 1, 0) for g in range(groups)).astype(bf16)

    @pl.when(pl.program_id(0) == 0)
    def _():
        outs[1][...] = sum(
            jnp.sum(weights[g][...].astype(f32) * grads[g][...].astype(f32), axis=0, keepdims=True)
            for g in range(groups)
        )

    each = len(terms) // sums
    for k in range(sums):

        @pl.when(pl.program_id(0) == k + 1)
        def _(k=k):
            parts = terms[k * each : (k + 1) * each]
            outs[2 + k][...] = sum(part[...].astype(f32) for part in parts).astype(bf16)


def first_back(qkv_back, w_qkv, step, grads, ends, deps=(), **beside):
    groups = len(qkv_back)
    seq_len, width = qkv_back[0].shape
    rows = ends[0][2].shape[0]
    end = blocks((rows, D), lambda i: (0, 0))
    return call(
        functools.partial(first_back_kernel, groups=groups, sums=len(ends)),
        [*qkv_back, *([w_qkv] * groups), *grads, *[term for terms in ends for term in terms]],
        [blocks((step, width), lambda i: (i, 0))] * groups
        + [blocks((width, D), lambda i, g=g: (g, 0)) for g in range(groups)]
        + [blocks((width, D), lambda i: (0, 0))] * groups
        + [end] * sum(len(terms) for terms in ends),
        [shaped((seq_len, D)), shaped((1, D), f32)] + [shaped((rows, D))] * len(ends),
        [blocks((step, D), lambda i: (i, 0)), blocks((1, D), lambda i: (0, 0))]
        + [end] * len(ends),
        grid=(seq_len // step,),
        deps=deps,
        mib=60,
        flops=2 * seq_len * width * groups * D,
        name="first_back",
        **beside,
    )


def stream(entry_refs, layout, low, high, buffer, sems, use):
    def copies(i):
        found = []
        for part, (ref, start, end, offset) in enumerate(layout[i]):
            first, last = max(start, low), min(end, high)
            if first < last:
                found.append(
                    pltpu.make_async_copy(
                        entry_refs[ref].at[pl.ds(first - start + offset, last - first)],
                        buffer.at[i % 2, pl.ds(first - low, last - first)],
                        sems.at[i % 2, part],
                    )
                )
        return found

    for copy in copies(0):
        copy.start()
    for i in range(len(layout)):
        if i + 1 < len(layout):
            for copy in copies(i + 1):
                copy.start()
        for copy in copies(i):
            copy.wait()
        use(i, buffer.at[i % 2])


def stream_scratch(rows):
    return [pltpu.VMEM((2, rows, D), bf16), pltpu.SemaphoreType.DMA((2, 3))]


def entry_layout(entries):
    arrays, layout = [], []
    for entry in entries:
        start, parts = 0, []
        for array, offset, count in entry:
            known = [k for k, other in enumerate(arrays) if other is array]
            if not known:
                known = [len(arrays)]
                arrays.append(array)
            parts.append((known[0], start, start + count, offset))
            start += count
        layout.append(parts)
    return arrays, layout, start // 3


def ff_kernel(rows_all_ref, low_ref, high_ref, *refs, layout, size, s, parts):
    hid_all, dgate_all, dup_all, rows_kept, back_kept, term_all, _ = refs[-18:-11]
    total, down, rows_ref, back_ref, hid_ref, dgate_ref, dup_ref, _, buffer, sems, own = refs[-11:]
    count = rows_ref.shape[0]
    low = low_ref.shape[0] // parts
    place = lax.rem(lax.axis_index("narrow") - s + parts, parts)
    low_place = pl.ds(pl.multiple_of(place * low, low), low)
    high_place = pl.ds(pl.multiple_of(place * (count - low), count - low), count - low)
    place = pl.ds(pl.multiple_of(place * count, count), count)
    here = pl.ds(s * count, count)
    copies = [
        pltpu.make_async_copy(rows_all_ref, rows_ref, own.at[0]),
        pltpu.make_async_copy(low_ref.at[low_place], back_ref.at[:low], own.at[1]),
        pltpu.make_async_copy(high_ref.at[high_place], back_ref.at[low:], own.at[4]),
    ]
    for copy in copies:
        copy.start()
    kept = [
        pltpu.make_async_copy(rows_ref, rows_kept.at[here], own.at[2]),
        pltpu.make_async_copy(back_ref, back_kept.at[here], own.at[3]),
    ]

    def use(i, weights):
        if i == 0:
            for copy in copies:
                copy.wait()
            for copy in kept:
                copy.start()
        gate = dot(rows_ref[...], weights[:size], 1, 1)
        up = dot(rows_ref[...], weights[size : 2 * size], 1, 1)
        hidden_back = dot(back_ref[...], weights[2 * size :], 1, 1)
        sig = 1.0 / (1.0 + jnp.exp(-gate))
        silu = gate * sig
        cols = slice(i * size, (i + 1) * size)
        hid = (silu * up).astype(bf16)
        dgate = (hidden_back * up * (sig * (1.0 + gate * (1.0 - sig)))).astype(bf16)
        dup = (hidden_back * silu).astype(bf16)
        hid_ref[:, cols] = hid
        dgate_ref[:, cols] = dgate
        dup_ref[:, cols] = dup
        part = dot(dgate, weights[:size], 1, 0) + dot(dup, weights[size : 2 * size], 1, 0)
        term = dot(hid, weights[2 * size :], 1, 0)
        if i:
            part = part + total[...]
            term = term + down[...]
        total[...] = part
        down[...] = term

    stream(refs, layout, 0, 3 * size, buffer, sems, use)
    for copy in kept:
        copy.wait()
    rows_ref[...] = down[...].astype(bf16)
    copies = [
        pltpu.make_async_copy(hid_ref, hid_all.at[here], own.at[0]),
        pltpu.make_async_copy(dgate_ref, dgate_all.at[here], own.at[1]),
        pltpu.make_async_copy(dup_ref, dup_all.at[here], own.at[2]),
        pltpu.make_async_copy(rows_ref, term_all.at[place], own.at[3]),
    ]
    for copy in copies:
        copy.start()
    for copy in copies:
        copy.wait()


def ff_close(lands, refs, *, added):
    out_ref, total = refs[-12:-10]
    arrived = refs[-4]
    value = total[...]
    if added:
        value = value + arrived[...].astype(f32)
    out_ref[...] = value.astype(out_ref.dtype)


def ff_step(s, rows, back_low, back_high, entries, kept, moving, added=False, last=False):
    count = rows.shape[0]
    seq_len = back_low.shape[0] + back_high.shape[0]
    arrays, layout, size = entry_layout(entries)
    ff_width = size * len(entries)
    return call(
        functools.partial(
            ff_kernel, layout=layout, size=size, s=s, parts=seq_len // count
        ),
        [rows, back_low, back_high, *arrays, *kept],
        [ANY] * (3 + len(arrays) + len(kept)),
        [shaped((seq_len, ff_width))] * 3
        + [shaped((seq_len, D))] * 3
        + [shaped((count, D), f32 if last else bf16)],
        [ANY] * 6 + [VMEM],
        scratch=[pltpu.VMEM((count, D), f32)] * 2
        + [pltpu.VMEM((count, D), bf16)] * 2
        + [pltpu.VMEM((count, ff_width), bf16)] * 3
        + [pltpu.VMEM((count, D), bf16)]
        + stream_scratch(3 * size)
        + [pltpu.SemaphoreType.DMA((5,))],
        aliases={3 + len(arrays) + k: k for k in range(len(kept))},
        mib=60,
        flops=10 * count * ff_width * D,
        name="ff_step",
        sends=[Send(0, 0, "narrow", 1)],
        sources=[moving],
        lands=[] if added else [moving.shape],
        inner=(7,) if added else (),
        closing=functools.partial(ff_close, added=added),
    )


def add_kernel(*refs):
    refs[-1][...] = sum(ref[...].astype(f32) for ref in refs[:-1]).astype(refs[-1].dtype)


def add(terms, kind=bf16, deps=(), **beside):
    count, width = terms[0].shape
    step = 128 if count % 128 == 0 else 64 if count % 64 == 0 else count
    given = blocks((step, width), lambda i: (i, 0))
    return call(
        add_kernel,
        terms,
        [given] * len(terms),
        shaped((count, width), kind),
        given,
        grid=(count // step,),
        deps=deps,
        moved=count * width * 8,
        name="add",
        **beside,
    )


def outer_kernel(first_ref, second_ref, *outs):
    first = first_ref[...]
    if len(first.shape) == 3:
        first = first[0]
    product = dot(first, second_ref[...], 0, 0).astype(bf16)
    each = pl.num_programs(0) // len(outs)
    for k, out_ref in enumerate(outs):

        @pl.when(pl.program_id(0) // each == k)
        def _(out_ref=out_ref):
            out_ref[...] = product


def outer(first, second, split=1, deps=(), **beside):
    rows, width = second.shape
    if len(first.shape) == 3:
        groups, _, step = first.shape
        height = groups * step
        taken = blocks((1, rows, step), lambda i: (i, 0, 0))
    else:
        height = first.shape[1]
        step = next(k for k in (512, 384, 256, 192, LANES) if height % (k * split) == 0)
        taken = blocks((rows, step), lambda i: (0, i))
    each = height // step // split
    return call(
        outer_kernel,
        [first, second],
        [taken, blocks((rows, width), lambda i: (0, 0))],
        [shaped((height // split, width))] * split,
        [
            blocks((step, width), lambda i, k=k: (jnp.clip(i - k * each, 0, each - 1), 0))
            for k in range(split)
        ],
        grid=(height // step,),
        deps=deps,
        mib=56,
        flops=2 * rows * height * width,
        **beside,
        name="outer",
    )


def outer_pair_kernel(first_ref, second_ref, rows_ref, *outs):
    for part, (taken_ref, out_ref) in enumerate(zip((first_ref, second_ref), outs)):

        @pl.when(pl.program_id(0) == part)
        def _(taken_ref=taken_ref, out_ref=out_ref):
            out_ref[...] = dot(taken_ref[...], rows_ref[...], 0, 0).astype(bf16)


def outer_pair(firsts, second, deps=(), **beside):
    rows, height = firsts[0].shape
    width = second.shape[1]
    taken = blocks((rows, height), lambda i: (0, 0))
    return call(
        outer_pair_kernel,
        [*firsts, second],
        [taken, taken, blocks((rows, width), lambda i: (0, 0))],
        [shaped((height, width))] * 2,
        [blocks((height, width), lambda i: (0, 0))] * 2,
        grid=(2,),
        deps=deps,
        flops=4 * rows * height * width,
        name="outer_pair",
        mib=60,
        **beside,
    )


def pass_kernel(*refs):
    pass


def after(value, *deps):
    return call(
        pass_kernel, [value], [ANY], shaped(value.shape, value.dtype), ANY, deps=deps,
        aliases={0: 0}, name="after",
    )


def shift(count, step=1):
    return [(i, (i + step) % count) for i in range(count)]


def nothing(*refs):
    pass


def sum_places_kernel(place_ref, own_ref, others_ref, out_ref):
    total = jnp.zeros(own_ref.shape, f32)
    for k in range(others_ref.shape[0]):
        total = total + jnp.where(place_ref[0] == k, own_ref[...], others_ref[k])
    out_ref[...] = total


def sum_places(place, own, others):
    return call(
        sum_places_kernel,
        [place, own, others],
        [SMEM, VMEM, VMEM],
        shaped(own.shape, f32),
        VMEM,
        name="sum_places",
    )


def move(sends, sources, lands, deps=()):
    return call(
        nothing, [], [], [], [], sends=sends, sources=sources, lands=lands, deps=deps, name="move"
    )


def rows_at(first, count):
    return lambda wide, narrow: pl.ds(first, count)


def exchange_units(turned):
    return move(
        [
            Send(
                0, 0, "wide", e,
                lambda wide, narrow, e=e: jnp.bitwise_xor(wide, e),
                lambda wide, narrow: wide,
            )
            for e in range(1, turned.shape[0])
        ],
        [turned],
        [turned.shape],
    )[0]


def near_and_across(source, land, at=None, needs=()):
    return [
        Send(source, land, "wide", 2, at, needs=needs),
        Send(source, land + 1, "wide", 4, at, needs=needs),
    ]


def sum_entries_kernel(first_ref, second_ref, *outs):
    total = (first_ref[0].astype(f32) + second_ref[0].astype(f32)).astype(bf16)
    for r, out_ref in enumerate(outs):

        @pl.when(pl.program_id(0) == r)
        def _(out_ref=out_ref):
            out_ref[...] = total


def sum_entries(first, second, **beside):
    count, rows, width = first.shape
    given = blocks((1, rows, width), lambda i: (i, 0, 0))
    return call(
        sum_entries_kernel,
        [first, second],
        [given, given],
        [shaped((rows, width))] * count,
        [blocks((rows, width), lambda i: (0, 0))] * count,
        grid=(count,),
        moved=first.size * 6,
        name="sum_entries",
        **beside,
    )


def ff_meet_kernel(own_ref, other_ref, first_out, second_out):
    total = (own_ref[...].astype(f32) + other_ref[...].astype(f32)).astype(bf16)
    half = first_out.shape[0]
    first_out[...] = total[:half]
    second_out[...] = total[half:]


def ff_meet(own, other, deps=()):
    rows, width = own.shape[0] // 4, own.shape[1]
    last = blocks((rows, width), lambda i: (3, 0))
    half = blocks((rows // 2, width), lambda i: (0, 0))
    return call(
        ff_meet_kernel,
        [own, other],
        [last, last],
        [shaped((rows // 2, width))] * 2,
        [half, half],
        grid=(1,),
        deps=deps,
        moved=own.size * 2,
        name="ff_meet",
    )


def ff_join_kernel(
    own_x, other_x, first_ref, own_y, other_y, second_ref, x_out, y_out
):
    half = first_ref.shape[0]
    x = own_x[...].astype(f32) + other_x[...].astype(f32)
    y = own_y[...].astype(f32) + other_y[...].astype(f32)
    x_out[:half] = (x[:half] + first_ref[...].astype(f32)).astype(bf16)
    x_out[half:] = x[half:].astype(bf16)
    y_out[:half] = y[:half].astype(bf16)
    y_out[half:] = (y[half:] + second_ref[...].astype(f32)).astype(bf16)


def ff_join(own, other, first, second, deps=()):
    rows, width = own.shape[0] // 4, own.shape[1]

    def quarter(k):
        return blocks((rows, width), lambda i: (k, 0))

    half = blocks((rows // 2, width), lambda i: (0, 0))
    shape = shaped((rows, width))
    return call(
        ff_join_kernel,
        [own, other, first, own, other, second],
        [quarter(1), quarter(1), half, quarter(2), quarter(2), half],
        [shape, shape],
        [quarter(0), quarter(0)],
        grid=(1,),
        deps=deps,
        moved=own.size * 4,
        name="ff_join",
    )


def ff_end_kernel(*refs):
    refs[-1][...] = sum(ref[...].astype(f32) for ref in refs[:-1]).astype(bf16)


def ff_end(own, other, near, deps=(), **beside):
    rows, width = own.shape[0] // 4, own.shape[1]
    first = blocks((rows, width), lambda i: (0, 0))
    return call(
        ff_end_kernel,
        [own, other, *near],
        [first] * (2 + len(near)),
        shaped((rows, width)),
        first,
        grid=(1,),
        deps=deps,
        moved=own.size * 2,
        name="ff_end",
        **beside,
    )


def shaped_rows(array, parts):
    return (array.shape[0] // parts, array.shape[1])


def across_sends(source, land):
    return [Send(source, land, "wide", 4), Send(source + 1, land + 1, "wide", 2)]


def near_sends(source, land):
    return [Send(source, land, "wide", 2), Send(source + 1, land + 1, "wide", 4)]


def unit_row(col, query_width, kv_width, by_head, group_width):
    start, offset = col
    if start < query_width:
        return start // by_head * group_width + start % by_head + offset
    start -= query_width
    last = start >= kv_width
    if last:
        start -= kv_width
    head = (start + offset) // HD
    return head * group_width + by_head + last * HD + (start + offset) % HD


def assemble_qkv_kernel(
    turn_ref, own_ref, near_ref, other_ref, out_ref, *, piece, unit_cols, sizes
):
    height = near_ref.shape[1]
    for e in range(8):
        j = jnp.bitwise_xor(turn_ref[0], e)
        for c in range(height // piece):
            here = slice(c * piece, (c + 1) * piece)
            row = unit_row((c * unit_cols, j * piece), *sizes)
            if e % 2:
                value = other_ref[e // 2, here, :]
            elif e:
                value = near_ref[e // 2 - 1, here, :]
            else:
                value = own_ref[here, :]
            out_ref[pl.ds(pl.multiple_of(row, piece), piece), :] = value


def assemble_qkv(turn, rows, near, other, piece, unit_cols, sizes):
    _, height, _ = near.shape
    return call(
        functools.partial(
            assemble_qkv_kernel, piece=piece, unit_cols=unit_cols, sizes=sizes
        ),
        [turn, rows, near, other],
        [SMEM, blocks((height, D), lambda i: (0, 0)), whole_block(near), whole_block(other)],
        shaped((height * 8, D)),
        blocks((height * 8, D), lambda i: (0, 0)),
        grid=(1,),
        mib=32,
        moved=height * 8 * D * 4,
        name="assemble_qkv",
    )


def whole_block(array):
    return blocks(array.shape, lambda i: (0,) * len(array.shape))


def arrange_attn_kernel(turn_ref, *refs, piece, unit_cols, sizes):
    *grads, own_ref, other_ref = refs
    query_width, kv_width, _, group_width = sizes
    out_first = query_width + 2 * kv_width
    for j in range(unit_cols // piece):
        e = jnp.bitwise_xor(turn_ref[0], j)
        for core, out_ref in enumerate((own_ref, other_ref)):

            @pl.when(e % 2 == core)
            def _(j=j, e=e, out_ref=out_ref):
                for c in range(out_ref.shape[1] // piece):
                    if c * unit_cols < out_first:
                        row = unit_row((c * unit_cols, j * piece), *sizes)
                        grad_ref = grads[row // group_width]
                        row = row % group_width
                    else:
                        row = c * unit_cols - out_first + j * piece
                        grad_ref = grads[-1]
                    out_ref[e // 2, c * piece : (c + 1) * piece, :] = grad_ref[
                        row : row + piece, :
                    ]


def arrange_attn(turn, grads, piece, unit_cols, sizes):
    count = unit_cols // piece
    rows = sum(grad.shape[0] for grad in grads) // count
    shape = shaped((count // 2, rows, D))
    return call(
        functools.partial(arrange_attn_kernel, piece=piece, unit_cols=unit_cols, sizes=sizes),
        [turn, *grads],
        [SMEM] + [VMEM] * len(grads),
        [shape, shape],
        [VMEM] * 2,
        mib=32,
        moved=rows * count * D * 4,
        name="arrange_attn",
    )


def out_row(turn_ref, k, c, j, parts, piece, unit_cols, sign):
    n = lax.rem(turn_ref[1] + sign * k + parts, parts)
    return n * (D // parts) + c * unit_cols + j * piece


def assemble_out_kernel(
    turn_ref, rows_ref, z_ref, x_ref, y_ref, across_ref, other_ref, out_ref, *, first, piece,
    unit_cols, parts,
):
    height = z_ref.shape[1]
    for e in range(8):
        j = jnp.bitwise_xor(turn_ref[0], e)
        for k in range(parts):
            for c in range(height // piece):
                here = slice(c * piece, (c + 1) * piece)
                row = out_row(turn_ref, k, c, j, parts, piece, unit_cols, -1)
                if e % 2:
                    value = other_ref[e // 2, k, here, :]
                elif e:
                    value = (x_ref, y_ref, across_ref)[e // 2 - 1][k, here, :]
                elif k:
                    value = z_ref[k - 1, here, :]
                else:
                    value = rows_ref[first + c * piece : first + (c + 1) * piece, :]
                out_ref[pl.ds(pl.multiple_of(row, piece), piece), :] = value


def assemble_out(turn, rows, first, given, piece, unit_cols, parts, deps=()):
    height = given[0].shape[1]
    return call(
        functools.partial(
            assemble_out_kernel, first=first, piece=piece, unit_cols=unit_cols, parts=parts
        ),
        [turn, rows, *given],
        [SMEM, blocks((first + height, D), lambda i: (0, 0))] + [whole_block(a) for a in given],
        shaped((D, D)),
        blocks((D, D), lambda i: (0, 0)),
        grid=(1,),
        mib=52,
        deps=deps,
        moved=D * D * 4,
        name="assemble_out",
    )


def local(
    tokens, cotangent, lengths, owners, master, moment_one, moment_two, norm_gains, gain_first,
    gain_second,
):
    wide_count = lax.axis_size("wide")
    narrow_count = lax.axis_size("narrow")
    capacity, _, unit_rows, unit_cols = master.shape
    unit_count = owners.shape[0]
    row_count = tokens.shape[0]
    seq_len = row_count * narrow_count
    row_blocks = D // unit_rows
    col_blocks = unit_count // row_blocks
    piece = unit_cols // wide_count
    query_width = H // narrow_count * HD
    kv_width = KV // narrow_count * HD
    ff_width = FF // narrow_count
    qkv_width = query_width + 2 * kv_width
    groups = KV // narrow_count
    group_width = qkv_width // groups
    by_head = group_width - 2 * HD
    wide_index = lax.axis_index("wide")
    narrow_index = lax.axis_index("narrow")
    turn = jnp.stack([wide_index, narrow_index]).astype(jnp.int32)
    length = lax.dynamic_slice(lengths, (wide_index,), (1,))
    block = min(256, seq_len)
    qkv_blocks = qkv_width // unit_cols
    out_blocks = query_width // unit_cols
    attn_blocks = qkv_blocks + out_blocks
    sizes = (query_width, kv_width, by_head, group_width)
    back_by = (narrow_index - jnp.arange(narrow_count, dtype=jnp.int32)) % narrow_count

    inputs = tokens.astype(f32)
    normed = rmsnorm(inputs, norm_gains[0]).astype(bf16)
    normed_all = lax.all_gather(normed, "narrow", axis=0, tiled=True)

    slot_place, counts = positions(owners, wide_count, capacity)
    turned = turn_units(master, wide_count, ())
    got = exchange_units(turned)
    rows = pick_units(turn, slot_place, turned, got, row_blocks)
    qkv_rows = qkv_blocks * piece
    out_rows = out_blocks * piece
    ff_first = qkv_rows + out_rows
    ff_rows = 3 * ff_width // wide_count

    qkv_at, out_at = rows_at(0, qkv_rows), rows_at(qkv_rows, out_rows)

    def entry(k):
        return lambda wide, narrow: k

    near_qkv, other_qkv, narrow_out = move(
        [Send(0, 0, "wide", 2 * r, qkv_at, entry(r - 1)) for r in (1, 2, 3)]
        + [Send(0, 1, "wide", 1, qkv_at, entry(0))]
        + [Send(0, 2, "narrow", k, out_at, entry(k - 1)) for k in range(1, narrow_count)]
        + [
            Send(0, 1, "wide", 1, entry(r - 1), entry(r), landed=True, needs=(r - 1,))
            for r in (1, 2, 3)
        ],
        [rows],
        [
            (3, qkv_rows, D),
            (4, qkv_rows, D),
            (narrow_count - 1, out_rows, D),
        ],
    )
    w_qkv = assemble_qkv(turn, rows, near_qkv, other_qkv, piece, unit_cols, sizes)

    cos_all, sin_all = turn_tables(seq_len)
    low_rows = row_count // 2
    cotangent_then = after(cotangent[:low_rows], normed_all, w_qkv)
    back_low = lax.all_gather(cotangent_then, "narrow", axis=0, tiled=True)
    qkv = project(
        normed_all, w_qkv, cos_all, sin_all, group_width, row_count, (cotangent_then,)
    )
    out_shape = (narrow_count, out_rows, D)

    def first_entry(wide, narrow):
        return 0

    def later_entries(wide, narrow):
        return pl.ds(1, narrow_count - 1)

    attended, logs, out_x, out_y = attend_forward(
        length, qkv, groups, block,
        sends=[
            Send(0, 0, "wide", 2, out_at, first_entry),
            Send(0, 1, "wide", 4, out_at, first_entry),
            Send(1, 0, "wide", 2, None, later_entries),
            Send(1, 1, "wide", 4, None, later_entries),
        ],
        sources=[rows, narrow_out],
        lands=[out_shape, out_shape],
    )

    half = narrow_count // 2
    third = ff_rows // 3

    def heads_of(k):
        return lambda wide, narrow: pl.ds(
            pl.multiple_of(lax.rem(narrow + k, narrow_count) * row_count, row_count), row_count
        )

    def part_of(k, at):
        return lambda wide, narrow: (k, at)

    low_part, high_part = pl.ds(0, half), pl.ds(half, narrow_count - half)
    attended_others, out_across, out_other, x_first, y_first = move(
        [Send(0, 0, "narrow", k, heads_of(k), entry(k - 1)) for k in range(1, narrow_count)]
        + [
            Send(2, 1, "wide", 4, lambda w, n: low_part, lambda w, n: low_part),
            Send(3, 1, "wide", 2, lambda w, n: high_part, lambda w, n: high_part),
            Send(1, 2, "wide", 1, out_at, lambda w, n: (0, 0)),
            Send(4, 2, "wide", 1, None, lambda w, n: (0, pl.ds(1, narrow_count - 1))),
            Send(2, 2, "wide", 1, None, entry(1)),
            Send(3, 2, "wide", 1, None, entry(2)),
            Send(1, 3, "wide", 2, rows_at(ff_first, third)),
            Send(1, 4, "wide", 4, rows_at(ff_first, third)),
            Send(
                1, 2, "wide", 1, None, entry(3), landed=True,
                needs=(narrow_count - 1, narrow_count),
            ),
        ],
        [attended, rows, out_x, out_y, narrow_out],
        [
            (narrow_count - 1, row_count, query_width),
            out_shape,
            (4, *out_shape),
            (third, D),
            (third, D),
        ],
    )
    back_high = lax.all_gather(
        after(cotangent[low_rows:], attended_others, back_low), "narrow", axis=0, tiled=True
    )
    w_out = assemble_out(
        turn, rows, qkv_rows, [narrow_out, out_x, out_y, out_across, out_other], piece,
        unit_cols, narrow_count,
    )
    residual, normed_two = branch(
        attended, attended_others, w_out, tokens, norm_gains[1:2]
    )

    rest = ff_rows - third
    half_rest = ff_rows // 2 - third
    (
        block_one, x_last, y_last, own_swap, x_first_swap, y_first_swap, x_last_swap, y_last_swap,
        across_first,
    ) = move(
        [Send(0, 0, "narrow", 1)]
        + near_and_across(1, 1, rows_at(ff_first + third, rest))
        + [Send(1, 3, "wide", 1, rows_at(ff_first, ff_rows))]
        + [Send(2, 4, "wide", 1), Send(3, 5, "wide", 1)]
        + [
            Send(1, 6, "wide", 1, landed=True, needs=(1,)),
            Send(2, 7, "wide", 1, landed=True, needs=(2,)),
            Send(2, 8, "wide", 4),
        ],
        [normed_two, rows, x_first, y_first],
        [normed_two.shape, (rest, D), (rest, D), (ff_rows, D)]
        + [(third, D)] * 2
        + [(rest, D)] * 2
        + [(third, D)],
    )
    block_two, *across = move(
        [
            Send(0, 0, "narrow", 1),
            Send(2, 1, "wide", 4, rows_at(0, half_rest)),
            Send(3, 2, "wide", 2, rows_at(half_rest, ff_rows // 2)),
            Send(1, 3, "wide", 1),
            Send(1, 4, "wide", 1, landed=True, needs=(1,)),
            Send(2, 5, "wide", 1, landed=True, needs=(2,)),
        ],
        [block_one, across_first, x_last, y_last],
        [block_one.shape, (half_rest, D), (ff_rows // 2, D)]
        + [(third, D), (half_rest, D), (ff_rows // 2, D)],
    )
    across = [across_first, *across]

    def pieces(*arrays):
        return [(array, 0, array.shape[0]) for array in arrays]

    entries = [
        [(rows, ff_first, ff_rows)],
        pieces(x_first, x_last),
        pieces(y_first, y_last),
        pieces(*across[:3]),
        [(own_swap, 0, ff_rows)],
        pieces(x_first_swap, x_last_swap),
        pieces(y_first_swap, y_last_swap),
        pieces(*across[3:]),
    ]

    *kept, total, block_three = ff_step(1, block_one, back_low, back_high, entries, (), block_two)
    *kept, total = ff_step(2, block_two, back_low, back_high, entries, kept, total, True)
    *kept, total = ff_step(3, block_three, back_low, back_high, entries, kept, total, True)
    *kept, norm_two_back = ff_step(0, normed_two, back_low, back_high, entries, kept, total, True, True)
    hidden, dgate, dup, mlp_all, back_kept, ff_term = kept

    _, norm_two_pull = jax.vjp(rmsnorm, residual, norm_gains[1])
    resid_part, gain_two = norm_two_pull(norm_two_back)
    resid_back = cotangent.astype(f32) + resid_part
    attn_back = resid_back.astype(bf16)
    by_heads = spread(turn, attn_back, w_out, narrow_count)

    def heads_send(k, land):
        return Send(0, land, "narrow", k, entry(k))

    heads_shape = (row_count, query_width)
    *grad_down, heads_one, heads_three = outer(
        hidden, back_kept, 2,
        sends=[heads_send(1, 0), heads_send(3, 1)],
        sources=[by_heads],
        lands=[heads_shape, heads_shape],
    )
    half_shape, near_shape = shaped_rows(grad_down[0], 8), shaped_rows(grad_down[0], 4)
    *grad_gate, heads_two, down_swap = outer(
        dgate, mlp_all, 2,
        sends=[heads_send(2, 0), Send(1, 1, "wide", 1)],
        sources=[by_heads, grad_down[1]],
        lands=[heads_shape, grad_down[1].shape],
    )
    out_back = jnp.stack([by_heads[0], heads_one, heads_two, heads_three])
    out_back = jnp.take(out_back, back_by, axis=0).reshape(seq_len, query_width)
    attn_back_all = lax.all_gather(after(attn_back, heads_two), "narrow", axis=0, tiled=True)
    ff_sum = lax.psum_scatter(
        after(ff_term, heads_two), "narrow", scatter_dimension=0, tiled=True
    )
    output = residual + ff_sum.astype(f32)
    down_across = ff_meet(grad_down[0], down_swap)
    *grad_upper, gate_swap, down_a, down_b = outer(
        dup, mlp_all, 2,
        sends=[Send(0, 0, "wide", 1)] + across_sends(1, 1),
        sources=[grad_gate[1], *down_across],
        lands=[grad_gate[1].shape, half_shape, half_shape],
    )
    joined_down = ff_join(grad_down[0], down_swap, down_a, down_b)
    gate_across = ff_meet(grad_gate[0], gate_swap)

    qkv_back = [None, None]
    qkv_back[0], upper_swap, gate_a, gate_b, down_x, down_y = attend_backward(
        0, groups, length, qkv, out_back, attended, logs, cos_all, sin_all, block,
        sends=[Send(0, 0, "wide", 1)] + across_sends(1, 1) + near_sends(3, 3),
        sources=[grad_upper[1], *gate_across, *joined_down],
        lands=[grad_upper[1].shape, half_shape, half_shape, near_shape, near_shape],
    )
    upper_across = ff_meet(grad_upper[0], upper_swap)
    joined_gate = ff_join(grad_gate[0], gate_swap, gate_a, gate_b)
    qkv_back[1], upper_a, upper_b, gate_x, gate_y = attend_backward(
        1, groups, length, qkv, out_back, attended, logs, cos_all, sin_all, block,
        sends=across_sends(0, 0) + near_sends(2, 2),
        sources=[*upper_across, *joined_gate],
        lands=[half_shape] * 2 + [near_shape] * 2,
    )
    joined_upper = ff_join(grad_upper[0], upper_swap, upper_a, upper_b)
    *grad_qkv, upper_x, upper_y = outer_pair(
        qkv_back, normed_all, (joined_upper[0],),
        sends=near_sends(0, 0), sources=list(joined_upper), lands=[near_shape] * 2,
    )
    (grad_out,) = outer(attended, attn_back_all, 1, (grad_qkv[0],))
    own_attn, other_attn = arrange_attn(
        turn, [*grad_qkv, grad_out], piece, unit_cols, sizes
    )
    gate_sum, attn_swap = ff_end(
        grad_gate[0], gate_swap, [gate_x, gate_y],
        sends=[Send(0, 0, "wide", 1)], sources=[other_attn], lands=[other_attn.shape],
    )
    met_attn = sum_entries(own_attn, attn_swap)
    norm_one_term, gain_one, down_sum, upper_sum, *arrived = first_back(
        qkv_back, w_qkv, row_count, grad_qkv,
        [
            [grad_down[0], down_swap, down_x, down_y],
            [grad_upper[0], upper_swap, upper_x, upper_y],
        ],
        sends=[Send(r - 1, r - 1, "wide", 2 * r) for r in (1, 2, 3)],
        sources=met_attn[1:],
        lands=[met_attn[0].shape] * 3,
    )
    attn_sum = add([met_attn[0]] + arrived)

    slots = wide_count * capacity
    unit_of = jnp.zeros((slots,), jnp.int32).at[slot_place].set(
        jnp.arange(unit_count, dtype=jnp.int32)
    )
    half_of = unit_of // col_blocks
    low, high = unpick_units(
        jnp.concatenate([attn_sum, gate_sum, upper_sum, down_sum], axis=0),
        unit_of - half_of * col_blocks,
        half_of,
        wide_count,
        piece,
        unit_rows,
    )
    gain_terms = jnp.stack([gain_one[0] / norm_gains[0], gain_two])
    owned_low, gain_others = move(
        [
            Send(
                0, 0, "wide", e,
                lambda wide, narrow, e=e: jnp.bitwise_xor(wide, e),
                lambda wide, narrow: wide,
            )
            for e in range(1, wide_count)
        ]
        + [
            Send(1, 1, "wide", e, None, lambda wide, narrow: wide) for e in range(1, wide_count)
        ],
        [low, gain_terms],
        [low.shape, ((wide_count, *gain_terms.shape), f32)],
    )
    owned_high = lax.all_to_all(after(high, owned_low), "wide", split_axis=0, concat_axis=0)
    gain_plane = sum_places(wide_index.reshape(1), gain_terms, gain_others)
    filled = jnp.concatenate(
        [lax.dynamic_slice(counts, (wide_index,), (1,)), wide_index.reshape(1)]
    ).astype(jnp.int32)
    updated = update_units(
        filled, owned_low, low, 0, master, moment_one, moment_two, ()
    )
    owned_grads, new_master, new_copy, new_first, new_second = update_units(
        filled, owned_high, owned_high, low.shape[1], master, moment_one, moment_two, updated
    )
    gain_others = jnp.stack(
        [gain_plane]
        + [
            after(lax.ppermute(gain_plane, "narrow", shift(narrow_count, k)), owned_grads)
            for k in range(1, narrow_count)
        ]
    )
    gain_grads = sum_places(
        narrow_index.reshape(1), gain_plane, jnp.take(gain_others, back_by, axis=0)
    )

    norm_one_back = lax.psum_scatter(
        after(norm_one_term, ff_sum, attn_sum), "narrow", scatter_dimension=0, tiled=True
    )
    norm_one_back = after(norm_one_back, owned_grads).astype(f32)
    _, norm_one_pull = jax.vjp(lambda values: rmsnorm(values, norm_gains[0]), inputs)
    (input_part,) = norm_one_pull(norm_one_back)
    input_grad = (resid_back + input_part).astype(bf16)
    new_gains, _, gain_second_new = adamw(
        norm_gains, gain_grads, gain_first, gain_second, 0.5, 0.0
    )
    return (
        output.astype(bf16),
        input_grad,
        owned_grads,
        new_master,
        new_copy,
        new_first,
        new_second,
        gain_grads,
        gain_second_new,
        new_gains,
    )


def rotate(values, cos_table, sin_table):
    middle = values.shape[-1] // 2
    turned = jnp.concatenate([-values[..., middle:], values[..., :middle]], axis=-1)
    return values * cos_table + turned * sin_table


def unrotate(gradient, cos_table, sin_table):
    middle = gradient.shape[-1] // 2
    weighted = gradient * sin_table
    turned = jnp.concatenate([weighted[..., middle:], -weighted[..., :middle]], axis=-1)
    return gradient * cos_table + turned


def matmul_rows(first_op, second_op):
    return lax.dot_general(
        first_op, second_op, (((0,), (0,)), ((), ())), preferred_element_type=jnp.float32
    )


def matmul_cols(first_op, second_op):
    return lax.dot_general(
        first_op, second_op, (((1,), (1,)), ((), ())), preferred_element_type=jnp.float32
    )


def project_any(normed_all, w_qkv, cos_heads, sin_heads, heads_here, kv_here):
    seq_len = normed_all.shape[0]
    projected = jnp.dot(normed_all, w_qkv, preferred_element_type=jnp.float32)
    query_width = heads_here * HD
    kv_width = kv_here * HD
    group_size = heads_here // kv_here
    query_heads = rotate(
        projected[:, :query_width].reshape(seq_len, heads_here, HD), cos_heads, sin_heads
    )
    key_heads = rotate(
        projected[:, query_width : query_width + kv_width].reshape(seq_len, kv_here, HD),
        cos_heads,
        sin_heads,
    )
    value_heads = projected[:, query_width + kv_width :].reshape(seq_len, kv_here, HD)
    query_heads = jnp.transpose(query_heads.astype(jnp.bfloat16), (1, 0, 2)).reshape(
        kv_here, group_size, seq_len, HD
    )
    key_heads = jnp.transpose(key_heads.astype(jnp.bfloat16), (1, 0, 2))
    value_heads = jnp.transpose(value_heads.astype(jnp.bfloat16), (1, 0, 2))
    return (query_heads, key_heads, value_heads)


def masked_scores(query_block, key_heads, row_start, length):
    block_rows = query_block.shape[2]
    seq_len = key_heads.shape[1]
    scores = jnp.einsum(
        "kgqd,ksd->kgqs", query_block, key_heads, preferred_element_type=jnp.float32
    ) * HD ** (-0.5)
    row_pos = row_start + jnp.arange(block_rows, dtype=jnp.int32)
    key_pos = jnp.arange(seq_len, dtype=jnp.int32)
    allowed = (key_pos[None, :] <= row_pos[:, None]) & (key_pos[None, :] < length)
    return jnp.where(allowed, scores, -1e30)


def attend_forward_any(query_heads, key_heads, value_heads, length, block_rows):
    seq_len = query_heads.shape[2]
    outputs = []
    log_sums = []
    for row_start in range(0, seq_len, block_rows):
        query_block = query_heads[:, :, row_start : row_start + block_rows]
        scores = masked_scores(query_block, key_heads, row_start, length)
        row_peak = jnp.max(scores, axis=-1, keepdims=True)
        raised = jnp.exp(scores - row_peak)
        row_total = jnp.sum(raised, axis=-1, keepdims=True)
        attn_probs = (raised / row_total).astype(jnp.bfloat16)
        outputs.append(
            jnp.einsum(
                "kgqs,ksd->kgqd", attn_probs, value_heads, preferred_element_type=jnp.float32
            )
        )
        log_sums.append((row_peak + jnp.log(row_total))[..., 0])
    return (jnp.concatenate(outputs, axis=2), jnp.concatenate(log_sums, axis=2))


def attend_backward_any(query_heads, key_heads, value_heads, out_back, log_sums, length, block_rows):
    seq_len = query_heads.shape[2]
    query_grads = []
    key_grad = jnp.zeros(key_heads.shape, jnp.float32)
    value_grad = jnp.zeros(value_heads.shape, jnp.float32)
    for row_start in range(0, seq_len, block_rows):
        query_block = query_heads[:, :, row_start : row_start + block_rows]
        back_block = out_back[:, :, row_start : row_start + block_rows]
        scores = masked_scores(query_block, key_heads, row_start, length)
        attn_probs = jnp.exp(scores - log_sums[:, :, row_start : row_start + block_rows, None])
        probs_back = jnp.einsum(
            "kgqd,ksd->kgqs", back_block, value_heads, preferred_element_type=jnp.float32
        )
        row_shift = jnp.sum(attn_probs * probs_back, axis=-1, keepdims=True)
        scores_back = (HD ** (-0.5) * attn_probs * (probs_back - row_shift)).astype(jnp.bfloat16)
        query_grads.append(
            jnp.einsum("kgqs,ksd->kgqd", scores_back, key_heads, preferred_element_type=jnp.float32)
        )
        key_grad = key_grad + jnp.einsum(
            "kgqs,kgqd->ksd", scores_back, query_block, preferred_element_type=jnp.float32
        )
        value_grad = value_grad + jnp.einsum(
            "kgqs,kgqd->ksd",
            attn_probs.astype(jnp.bfloat16),
            back_block,
            preferred_element_type=jnp.float32,
        )
    return (jnp.concatenate(query_grads, axis=2), key_grad, value_grad)


def local_any(
    tokens,
    cotangent,
    lengths,
    owners,
    master,
    moment_one,
    moment_two,
    norm_gains,
    gain_first,
    gain_second,
):
    wide_count = lax.axis_size("wide")
    narrow_count = lax.axis_size("narrow")
    capacity = master.shape[0]
    unit_rows = master.shape[2]
    unit_cols = master.shape[3]
    unit_count = owners.shape[0]
    row_count = tokens.shape[0]
    seq_len = row_count * narrow_count
    slot_place, _ = positions(owners, wide_count, capacity)
    own_slots = master[:, 0].astype(jnp.bfloat16)
    all_slots = lax.all_gather(own_slots, "wide", axis=0, tiled=True)
    unit_data = jnp.take(all_slots, slot_place, axis=0)
    row_blocks = D // unit_rows
    col_blocks = unit_count // row_blocks
    packed = jnp.transpose(
        unit_data.reshape(row_blocks, col_blocks, unit_rows, unit_cols), (0, 2, 1, 3)
    ).reshape(D, col_blocks * unit_cols)
    heads_here = H // narrow_count
    kv_here = KV // narrow_count
    group_size = heads_here // kv_here
    query_width = heads_here * HD
    kv_width = kv_here * HD
    ff_width = FF // narrow_count
    qkv_end = query_width + 2 * kv_width
    out_end = qkv_end + query_width
    gate_end = out_end + 2 * ff_width
    w_qkv = packed[:, :qkv_end]
    w_out_t = packed[:, qkv_end:out_end]
    w_gate_up = packed[:, out_end:gate_end]
    w_down_t = packed[:, gate_end:]
    cos_table, sin_table = tables(seq_len, HD)
    cos_heads = cos_table[:, None, :]
    sin_heads = sin_table[:, None, :]
    block_rows = min(512, seq_len)
    wide_index = lax.axis_index("wide")
    length = lengths[wide_index]
    inputs = tokens.astype(jnp.float32)
    normed = rmsnorm(inputs, norm_gains[0]).astype(jnp.bfloat16)
    normed_all = lax.all_gather(normed, "narrow", axis=0, tiled=True)
    query_heads, key_heads, value_heads = project_any(
        normed_all, w_qkv, cos_heads, sin_heads, heads_here, kv_here
    )
    attended, log_sums = attend_forward_any(query_heads, key_heads, value_heads, length, block_rows)
    attended = (
        jnp.transpose(attended.reshape(heads_here, seq_len, HD), (1, 0, 2))
        .reshape(seq_len, query_width)
        .astype(jnp.bfloat16)
    )
    residual = inputs + lax.psum_scatter(
        matmul_cols(attended, w_out_t), "narrow", scatter_dimension=0, tiled=True
    )
    normed_two = rmsnorm(residual, norm_gains[1]).astype(jnp.bfloat16)
    mlp_input = lax.all_gather(normed_two, "narrow", axis=0, tiled=True)
    gate_up = jnp.dot(mlp_input, w_gate_up, preferred_element_type=jnp.float32)
    hidden = (jax.nn.silu(gate_up[:, :ff_width]) * gate_up[:, ff_width:]).astype(jnp.bfloat16)
    output = residual + lax.psum_scatter(
        matmul_cols(hidden, w_down_t).astype(jnp.bfloat16),
        "narrow",
        scatter_dimension=0,
        tiled=True,
    ).astype(jnp.float32)
    down_back = lax.all_gather(cotangent, "narrow", axis=0, tiled=True)
    mlp_again = lax.all_gather(normed_two, "narrow", axis=0, tiled=True)
    gate_up = jnp.dot(mlp_again, w_gate_up, preferred_element_type=jnp.float32)
    hidden_back = jnp.dot(down_back, w_down_t, preferred_element_type=jnp.float32)
    grad_down_t = matmul_rows(down_back, hidden)
    _, swiglu_pull = jax.vjp(
        lambda gate_in, upper_in: jax.nn.silu(gate_in) * upper_in,
        gate_up[:, :ff_width],
        gate_up[:, ff_width:],
    )
    gate_back, upper_back = swiglu_pull(hidden_back)
    gate_up_back = jnp.concatenate([gate_back, upper_back], axis=1).astype(jnp.bfloat16)
    grad_gate_up = matmul_rows(mlp_again, gate_up_back)
    norm_two_back = lax.psum_scatter(
        matmul_cols(gate_up_back, w_gate_up).astype(jnp.bfloat16),
        "narrow",
        scatter_dimension=0,
        tiled=True,
    ).astype(jnp.float32)
    _, norm_two_pull = jax.vjp(rmsnorm, residual, norm_gains[1])
    resid_part, gain_two = norm_two_pull(norm_two_back)
    resid_back = cotangent.astype(jnp.float32) + resid_part
    attn_back = lax.all_gather(resid_back.astype(jnp.bfloat16), "narrow", axis=0, tiled=True)
    normed_again = lax.all_gather(normed, "narrow", axis=0, tiled=True)
    query_heads, key_heads, value_heads = project_any(
        normed_again, w_qkv, cos_heads, sin_heads, heads_here, kv_here
    )
    out_back = jnp.dot(attn_back, w_out_t, preferred_element_type=jnp.float32).astype(jnp.bfloat16)
    grad_out_t = matmul_rows(attn_back, attended)
    out_back = jnp.transpose(out_back.reshape(seq_len, heads_here, HD), (1, 0, 2)).reshape(
        kv_here, group_size, seq_len, HD
    )
    query_grad, key_grad, value_grad = attend_backward_any(
        query_heads, key_heads, value_heads, out_back, log_sums, length, block_rows
    )
    query_grad = jnp.transpose(query_grad.reshape(heads_here, seq_len, HD), (1, 0, 2))
    query_grad = unrotate(query_grad, cos_heads, sin_heads).reshape(seq_len, query_width)
    key_grad = unrotate(jnp.transpose(key_grad, (1, 0, 2)), cos_heads, sin_heads).reshape(
        seq_len, kv_width
    )
    value_grad = jnp.transpose(value_grad, (1, 0, 2)).reshape(seq_len, kv_width)
    qkv_back = jnp.concatenate([query_grad, key_grad, value_grad], axis=1).astype(jnp.bfloat16)
    grad_qkv = matmul_rows(normed_again, qkv_back)
    norm_one_back = lax.psum_scatter(
        matmul_cols(qkv_back, w_qkv).astype(jnp.bfloat16), "narrow", scatter_dimension=0, tiled=True
    ).astype(jnp.float32)
    _, norm_one_pull = jax.vjp(rmsnorm, inputs, norm_gains[0])
    input_part, gain_one = norm_one_pull(norm_one_back)
    input_grad = (resid_back + input_part).astype(jnp.bfloat16)
    grad_packed = jnp.concatenate([grad_qkv, grad_out_t, grad_gate_up, grad_down_t], axis=1)
    grad_units = jnp.transpose(
        grad_packed.reshape(row_blocks, unit_rows, col_blocks, unit_cols), (0, 2, 1, 3)
    ).reshape(unit_count, unit_rows, unit_cols)
    grad_slots = (
        jnp.zeros((wide_count * capacity, unit_rows, unit_cols), jnp.float32)
        .at[slot_place]
        .set(grad_units)
    )
    owned_grads = lax.psum_scatter(
        grad_slots.astype(jnp.bfloat16), "wide", scatter_dimension=0, tiled=True
    ).astype(jnp.float32)[:, None]
    new_master, new_first, new_second = adamw(
        master, owned_grads, moment_one, moment_two, 0.02, 0.1
    )
    gain_grads = lax.psum(jnp.stack([gain_one, gain_two]), ("wide", "narrow"))
    new_gains, unused, gain_second_new = adamw(
        norm_gains, gain_grads, gain_first, gain_second, 0.5, 0.0
    )
    return (
        output.astype(jnp.bfloat16),
        input_grad,
        owned_grads,
        new_master,
        new_master.astype(jnp.bfloat16),
        new_first,
        new_second,
        gain_grads,
        gain_second_new,
        new_gains,
    )


def solution(mesh):
    COLLECTIVE[0] = 0
    rows = P(("wide", "narrow"), None)
    units = P("wide", "narrow", None, None)
    return jax.shard_map(
        local if mesh.shape["wide"] == 8 and mesh.shape["narrow"] == 4 else local_any,
        mesh=mesh,
        in_specs=(rows, rows, P(), P(), units, units, units, P(), P(), P()),
        out_specs=(rows, rows, units, units, units, units, units, P(), P(), P()),
        check_vma=False,
    )
```

```python
import functools

import jax
import jax.numpy as jnp
import numpy as np
from jax import lax
from jax.experimental import pallas as pl
from jax.experimental.pallas import tpu as pltpu
from jax.sharding import PartitionSpec as P

D = 2048
H = 32
KV = 8
HD = 64
FF = 8192
STEP = 5
LANES = 128
MIB = 1 << 20
ANY = pl.BlockSpec(memory_space=pl.ANY)
VMEM = pl.BlockSpec(memory_space=pltpu.VMEM)
SMEM = pl.BlockSpec(memory_space=pltpu.SMEM)

f32 = jnp.float32
bf16 = jnp.bfloat16


def dot(first_op, second_op, first_dim, second_dim):
    return lax.dot_general(
        first_op,
        second_op,
        (((first_dim,), (second_dim,)), ((), ())),
        preferred_element_type=f32,
    )


def shaped(shape, kind=bf16):
    return jax.ShapeDtypeStruct(shape, kind)


def blocks(shape, place):
    return pl.BlockSpec(shape, place)


class Send:
    def __init__(self, source, land, axis, step, source_at=None, land_at=None, landed=False, needs=()):
        self.source, self.land, self.axis, self.step = source, land, axis, step
        self.source_at, self.land_at = source_at, land_at
        self.landed, self.needs = landed, needs


COLLECTIVE = [0]


def run_sends(sends, sources, lands, send_sem, recv_sem):
    count = lax.axis_size("narrow")
    wide, narrow = lax.axis_index("wide"), lax.axis_index("narrow")

    def target(axis, step):
        if axis == "wide":
            return {"wide": jnp.bitwise_xor(wide, step)}
        return {"narrow": lax.rem(narrow + step, count)}

    copies = []
    for k, send in enumerate(sends):
        ref = (lands if send.landed else sources)[send.source]
        if send.source_at is not None:
            ref = ref.at[send.source_at(wide, narrow)]
        land = lands[send.land]
        if send.land_at is not None:
            land = land.at[send.land_at(wide, narrow)]
        copies.append(
            pltpu.make_async_remote_copy(
                src_ref=ref,
                dst_ref=land,
                send_sem=send_sem.at[k],
                recv_sem=recv_sem.at[k],
                device_id=target(send.axis, send.step),
                device_id_type=pl.DeviceIdType.MESH,
            )
        )

    def start():
        partners = set()
        for send in sends:
            if send.axis == "wide":
                partners.add(("wide", send.step))
            else:
                partners.add(("narrow", send.step % count))
                partners.add(("narrow", -send.step % count))
        barrier = pltpu.get_barrier_semaphore()
        for axis, step in sorted(partners):
            pl.semaphore_signal(
                barrier, inc=1, device_id=target(axis, step), device_id_type=pl.DeviceIdType.MESH
            )
        pl.semaphore_wait(barrier, len(partners))
        for send, copy in zip(sends, copies):
            if not send.needs and not send.landed:
                copy.start()

    def finish():
        arrived = set()
        for send, copy in zip(sends, copies):
            for k in send.needs:
                if k not in arrived:
                    copies[k].wait_recv()
                    arrived.add(k)
            if send.needs or send.landed:
                copy.start()
        for k, copy in enumerate(copies):
            copy.wait_send()
            if k not in arrived:
                copy.wait_recv()

    return start, finish


def call(
    body, ins, in_specs, out_shape, out_specs, *, name, grid=(), prefetch=(), scratch=(), deps=(),
    aliases=None, mib=56, flops=0, moved=0, sends=(), sources=(), lands=(), inner=(), closing=None,
):
    first = len(prefetch) + len(ins)
    single = not isinstance(out_shape, (list, tuple))
    out_shapes = [out_shape] if single else list(out_shape)
    specs = [out_specs] if single else list(out_specs)
    out_count = len(out_shapes)
    land_count = len(lands)

    def wrapped(*refs):
        given = refs[:first]
        refs = refs[first:]
        source_refs = refs[: len(sources)]
        refs = refs[len(sources) + len(deps) :]
        outs, refs = refs[:out_count], refs[out_count:]
        land_refs, refs = refs[:land_count], refs[land_count:]
        if not sends:
            body(*given, *outs, *refs)
            return
        own, (send_sem, recv_sem) = refs[:-2], refs[-2:]
        start, finish = run_sends(
            sends, source_refs, [*land_refs, *[own[k] for k in inner]], send_sem, recv_sem
        )

        def last():
            finish()
            if closing is not None:
                closing(land_refs, (*given, *outs, *own))

        if grid:
            steps = [pl.program_id(k) for k in range(len(grid))]
            begins = functools.reduce(jnp.logical_and, [step == 0 for step in steps])
            ends = functools.reduce(
                jnp.logical_and, [step == size - 1 for step, size in zip(steps, grid)]
            )
            pl.when(begins)(start)
            body(*given, *outs, *own)
            pl.when(ends)(last)
        else:
            start()
            body(*given, *outs, *own)
            last()

    extra = {}
    if sends:
        COLLECTIVE[0] += 1
        extra = {"collective_id": COLLECTIVE[0], "has_side_effects": True}
        scratch = [*scratch] + [pltpu.SemaphoreType.DMA((len(sends),))] * 2
    results = pl.pallas_call(
        wrapped,
        grid_spec=pltpu.PrefetchScalarGridSpec(
            num_scalar_prefetch=len(prefetch),
            grid=grid,
            in_specs=list(in_specs) + [ANY] * (len(sources) + len(deps)),
            out_specs=specs + [ANY] * land_count,
            scratch_shapes=list(scratch),
        ),
        out_shape=out_shapes + [shaped(*land) if isinstance(land[0], tuple) else shaped(land) for land in lands],
        input_output_aliases=aliases or {},
        compiler_params=pltpu.CompilerParams(vmem_limit_bytes=mib * MIB, **extra),
        cost_estimate=pl.CostEstimate(
            flops=int(flops), bytes_accessed=int(moved), transcendentals=0
        ),
        name=name,
    )(*prefetch, *ins, *sources, *deps)
    return results[0] if single and not sends else list(results)


def tables(length_all, head_size):
    inverse = 500000.0 ** (-jnp.arange(0, head_size, 2, dtype=f32) / head_size)
    angles = jnp.arange(length_all, dtype=f32)[:, None] * inverse[None, :]
    angles = jnp.concatenate([angles, angles], axis=1)
    return (jnp.cos(angles), jnp.sin(angles))


def turn_tables(length_all):
    inverse = np.float32(500000.0) ** (-np.arange(0, HD, 2, dtype=np.float32) / np.float32(HD))
    angles = np.arange(length_all, dtype=np.float32)[:, None] * inverse[None, :]
    angles = np.concatenate([angles] * (2 * LANES // HD), axis=1).astype(np.float32)
    return jnp.asarray(np.cos(angles)), jnp.asarray(np.sin(angles))


def rmsnorm(values, weight_gain):
    return (
        values * lax.rsqrt(jnp.mean(values * values, axis=-1, keepdims=True) + 1e-05) * weight_gain
    )


def positions(owners, wide_count, capacity):
    onehot = (owners[:, None] == jnp.arange(wide_count, dtype=jnp.int32)[None, :]).astype(jnp.int32)
    before = jnp.cumsum(onehot, axis=0) - onehot
    return (owners * capacity + jnp.sum(before * onehot, axis=1), jnp.sum(onehot, axis=0))


def adamw(weight, gradient, moment_one, moment_two, rate, decay):
    moment_one = 0.5 * moment_one + 0.5 * gradient
    moment_two = 0.5 * moment_two + 0.5 * gradient * gradient
    correct = 1.0 - 0.5**STEP
    update = moment_one / correct / (jnp.sqrt(moment_two / correct) + 1e-08)
    return (weight - rate * (update + decay * weight), moment_one, moment_two)


def turn_kernel(unit_ref, out_ref):
    parts, step, piece, unit_rows = out_ref.shape
    for k in range(step):
        out_ref[:, k] = (
            jnp.transpose(unit_ref[k, 0], (1, 0)).reshape(parts, piece, unit_rows).astype(bf16)
        )


def turn_units(master, parts, deps):
    capacity, _, unit_rows, unit_cols = master.shape
    piece = unit_cols // parts
    step = capacity // 2 if capacity % 2 == 0 else 1
    return call(
        turn_kernel,
        [master],
        [blocks((step, 1, unit_rows, unit_cols), lambda s: (s, 0, 0, 0))],
        shaped((parts, capacity, piece, unit_rows)),
        blocks((parts, step, piece, unit_rows), lambda s: (0, s, 0, 0)),
        grid=(capacity // step,),
        deps=deps,
        mib=60,
        moved=master.size * 6,
        name="turn_units",
    )


def pick_kernel(turn_ref, place_ref, own_ref, got_ref, out_ref, sem, *, col_blocks):
    _, capacity, piece, unit_rows = got_ref.shape

    def start(unit, carry):
        half = unit // col_blocks
        block = unit - half * col_blocks
        owner = place_ref[unit] // capacity
        slot = place_ref[unit] - owner * capacity
        target = out_ref.at[
            pl.ds(pl.multiple_of(block * piece, piece), piece),
            pl.ds(pl.multiple_of(half * unit_rows, unit_rows), unit_rows),
        ]

        @pl.when(owner == turn_ref[0])
        def _():
            pltpu.make_async_copy(own_ref.at[owner, slot], target, sem).start()

        @pl.when(owner != turn_ref[0])
        def _():
            pltpu.make_async_copy(got_ref.at[owner, slot], target, sem).start()

        return carry

    lax.fori_loop(0, place_ref.shape[0], start, 0)
    pltpu.make_async_copy(out_ref, out_ref, sem).wait()


def pick_units(turn, slot_place, own, got, row_blocks):
    _, _, piece, unit_rows = got.shape
    unit_count = slot_place.shape[0]
    col_blocks = unit_count // row_blocks
    return call(
        functools.partial(pick_kernel, col_blocks=col_blocks),
        [turn, slot_place, own, got],
        [SMEM, SMEM, ANY, ANY],
        shaped((col_blocks * piece, row_blocks * unit_rows)),
        VMEM,
        scratch=[pltpu.SemaphoreType.DMA],
        moved=unit_count * piece * unit_rows * 12,
        name="pick_units",
    )


def unpick_kernel(block_ref, half_ref, rows_ref, low_ref, high_ref, sems, *, piece, unit_rows):
    owners, part, _, _ = low_ref.shape
    capacity = part + high_ref.shape[1]

    def start(owner, carry):
        for slot in range(capacity):
            out_ref = high_ref if slot >= part else low_ref
            place = owner * capacity + slot
            pltpu.make_async_copy(
                rows_ref.at[
                    pl.ds(pl.multiple_of(block_ref[place] * piece, piece), piece),
                    pl.ds(pl.multiple_of(half_ref[place] * unit_rows, unit_rows), unit_rows),
                ],
                out_ref.at[owner, slot - part if slot >= part else slot],
                sems.at[int(slot >= part)],
            ).start()
        return carry

    lax.fori_loop(0, owners, start, 0)
    pltpu.make_async_copy(low_ref, low_ref, sems.at[0]).wait()
    pltpu.make_async_copy(high_ref, high_ref, sems.at[1]).wait()


def unpick_units(rows, block_of, half_of, owners, piece, unit_rows):
    slots = block_of.shape[0]
    capacity = slots // owners
    low = capacity * 5 // 16 * 2
    sizes = (low, capacity - low)
    return call(
        functools.partial(unpick_kernel, piece=piece, unit_rows=unit_rows),
        [block_of, half_of, rows],
        [SMEM, SMEM, VMEM],
        [shaped((owners, size, piece, unit_rows)) for size in sizes],
        [ANY, ANY],
        scratch=[pltpu.SemaphoreType.DMA((2,))],
        moved=slots * piece * unit_rows * 8,
        name="unpick_units",
    )


def apply_update(gradient, master_ref, one_ref, two_ref, outs, k=0):
    grad_out, master_out, copy_out, one_out, two_out = outs
    weight, one, two = adamw(master_ref[k, 0], gradient, one_ref[k, 0], two_ref[k, 0], 0.02, 0.1)
    grad_out[k, 0] = gradient
    master_out[k, 0] = weight
    copy_out[k, 0] = weight.astype(bf16)
    one_out[k, 0] = one
    two_out[k, 0] = two


def unit_gradient(parts, piece, unit_rows):
    return jnp.transpose(parts.astype(f32).reshape(-1, unit_rows), (1, 0))


def all_pieces(grad_ref, own_ref, turn, k=0):
    place = lax.broadcasted_iota(jnp.int32, (grad_ref.shape[0], 1, 1), 0)
    own = own_ref[0, k : k + 1].astype(f32)
    return jnp.where(place == turn, own, grad_ref[:, k].astype(f32))


def update_kernel(filled_ref, grad_ref, own_ref, master_ref, one_ref, two_ref, *refs, first):
    _, step, piece, unit_rows = grad_ref.shape
    for k in range(step):
        pieces = all_pieces(grad_ref, own_ref, lax.axis_index("wide"), k)
        slot = jnp.zeros((unit_rows, 1), jnp.int32) + (pl.program_id(0) * step + k + first)
        gradient = jnp.where(
            slot < filled_ref[0], unit_gradient(pieces, piece, unit_rows), 0.0
        )
        apply_update(gradient, master_ref, one_ref, two_ref, refs[-5:], k)


def update_outs(master):
    whole = shaped(master.shape, f32)
    return [whole, whole, shaped(master.shape), whole, whole]


def update_units(filled, grads, own, first, master, moment_one, moment_two, done, deps=()):
    _, _, unit_rows, unit_cols = master.shape
    parts, slots, piece, _ = grads.shape
    step = 2 if slots % 2 == 0 and first % 2 == 0 else 1
    unit = blocks((step, 1, unit_rows, unit_cols), lambda s: (s + first // step, 0, 0, 0))
    return call(
        functools.partial(update_kernel, first=first),
        [filled, grads, own, master, moment_one, moment_two, *done],
        [
            SMEM,
            blocks((parts, step, piece, unit_rows), lambda s: (0, s, 0, 0)),
            blocks((1, step, piece, unit_rows), lambda s: (lax.axis_index("wide"), s, 0, 0)),
            unit,
            unit,
            unit,
        ]
        + [ANY] * len(done),
        update_outs(master),
        [unit] * 5,
        grid=(slots // step,),
        aliases={6 + k: k for k in range(len(done))},
        moved=master.size * 16,
        mib=60,
        deps=deps,
        name="update_units",
    )


def lane_index(shape):
    return lax.broadcasted_iota(jnp.int32, shape, 1)


def rope(tile, cos_tile, sin_tile):
    lower = lane_index(tile.shape) % HD < HD // 2
    ahead = pltpu.roll(tile, LANES - HD // 2, 1)
    behind = pltpu.roll(tile, HD // 2, 1)
    return tile * cos_tile + jnp.where(lower, -ahead, behind) * sin_tile


def unrope(tile, cos_tile, sin_tile):
    lower = lane_index(tile.shape) % HD < HD // 2
    weighted = tile * sin_tile
    ahead = pltpu.roll(weighted, LANES - HD // 2, 1)
    behind = pltpu.roll(weighted, HD // 2, 1)
    return tile * cos_tile + jnp.where(lower, ahead, -behind)


def project_kernel(rows_ref, w_ref, cos_ref, sin_ref, out_ref, *, group_width):
    product = dot(rows_ref[...], w_ref[...], 1, 1)
    for start in range(0, out_ref.shape[1], LANES):
        tile = product[:, start : start + LANES]
        turned = rope(tile, cos_ref[...], sin_ref[...])
        if (start + LANES) % group_width == 0:
            tile = jnp.where(lane_index(tile.shape) < HD, turned, tile).astype(bf16)
        else:
            tile = turned.astype(bf16) * HD ** (-0.5)
        out_ref[:, start : start + LANES] = tile


def project(rows, w_qkv, cos_all, sin_all, group_width, step, deps):
    count = rows.shape[0]
    width = w_qkv.shape[0]
    return call(
        functools.partial(project_kernel, group_width=group_width),
        [rows, w_qkv, cos_all, sin_all],
        [
            blocks((step, D), lambda i: (i, 0)),
            blocks((width, D), lambda i: (0, 0)),
            blocks((step, LANES), lambda i: (i, 0)),
            blocks((step, LANES), lambda i: (i, 0)),
        ],
        shaped((count, width)),
        blocks((step, width), lambda i: (i, 0)),
        grid=(count // step,),
        deps=deps,
        flops=2 * count * width * D,
        name="project",
    )


def extend(tile, kx, vx):
    tile = tile.astype(f32)
    other = pltpu.roll(tile, HD, 1)
    low = lane_index(tile.shape) < HD
    kx[0] = jnp.where(low, tile, 0.0).astype(bf16)
    kx[1] = jnp.where(low, 0.0, other).astype(bf16)
    vx[0] = jnp.where(low, other, 0.0).astype(bf16)
    vx[1] = jnp.where(low, 0.0, tile).astype(bf16)


def forward_kernel(length_ref, qkv_ref, out_ref, log_ref, kx, vx, *, block):
    length = length_ref[0]
    seq_len, group_width = qkv_ref.shape
    pairs = group_width // LANES - 1
    extend(qkv_ref[:, pairs * LANES :], kx, vx)
    row = lax.broadcasted_iota(jnp.int32, (block, block), 0)
    col = lax.broadcasted_iota(jnp.int32, (block, block), 1)
    causal = col <= row
    key_row = lax.broadcasted_iota(jnp.int32, (1, seq_len), 1)
    bias = jnp.where(key_row < length, 0.0, -1e30).astype(f32)
    low = lane_index((block, LANES)) < HD
    for pair in range(pairs):
        lanes = slice(pair * LANES, (pair + 1) * LANES)
        for start in range(0, seq_len, block):
            query = qkv_ref[start : start + block, lanes]
            total = None
            logs = []
            for half in range(2):
                diagonal = dot(query, kx[half, start : start + block, :], 1, 1)
                diagonal = jnp.where(causal, diagonal + bias[:, start : start + block], -1e30)
                peak = jnp.max(diagonal, axis=1, keepdims=True)
                if start:
                    before = dot(query, kx[half, :start, :], 1, 1) + bias[:, :start]
                    peak = jnp.maximum(peak, jnp.max(before, axis=1, keepdims=True))
                    before = jnp.exp(before - peak)
                diagonal = jnp.exp(diagonal - peak)
                row_sum = jnp.sum(diagonal, axis=1, keepdims=True)
                part = dot(diagonal.astype(bf16), vx[half, start : start + block, :], 1, 0)
                if start:
                    row_sum = row_sum + jnp.sum(before, axis=1, keepdims=True)
                    part = part + dot(before.astype(bf16), vx[half, :start, :], 1, 0)
                part = part / row_sum
                total = part if total is None else total + part
                logs.append(peak + jnp.log(row_sum))
            out_ref[start : start + block, lanes] = total.astype(bf16)
            tile = jnp.transpose(jnp.where(low, logs[0], logs[1]), (1, 0))
            log_ref[0, 2 * pair : 2 * pair + 1, start : start + block] = tile[0:1]
            log_ref[0, 2 * pair + 1 : 2 * pair + 2, start : start + block] = tile[HD : HD + 1]


def attend_forward(length, qkv, groups, block, deps=(), **beside):
    seq_len, width = qkv.shape
    group_width = width // groups
    query_width = group_width - LANES
    return call(
        functools.partial(forward_kernel, block=block),
        [length, qkv],
        [SMEM, blocks((seq_len, group_width), lambda g: (0, g))],
        [shaped((seq_len, groups * query_width)), shaped((groups, 8, seq_len), f32)],
        [
            blocks((seq_len, query_width), lambda g: (0, g)),
            blocks((1, 8, seq_len), lambda g: (g, 0, 0)),
        ],
        grid=(groups,),
        scratch=[pltpu.VMEM((2, seq_len, LANES), bf16), pltpu.VMEM((2, seq_len, LANES), bf16)],
        deps=deps,
        mib=48,
        flops=groups * seq_len * seq_len * 2048,
        **beside,
        name="attend_forward",
    )


def backward_kernel(
    length_ref, qkv_ref, back_ref, out_ref, log_ref, cos_ref, sin_ref, *refs, block
):
    grad_ref, kx, vx, dk, dv = refs
    length = length_ref[0]
    seq_len, group_width = qkv_ref.shape
    pairs = group_width // LANES - 1
    extend(qkv_ref[:, pairs * LANES :], kx, vx)
    dk[...] = jnp.zeros(dk.shape, f32)
    dv[...] = jnp.zeros(dv.shape, f32)
    key = lax.broadcasted_iota(jnp.int32, (block, block), 0)
    row = lax.broadcasted_iota(jnp.int32, (block, block), 1)
    causal = key <= row
    for pair in range(pairs):
        lanes = slice(pair * LANES, (pair + 1) * LANES)
        for start in range(0, seq_len, block):
            here = slice(start, start + block)
            query = qkv_ref[here, lanes]
            back = back_ref[here, lanes]
            turned = jnp.transpose(back.astype(f32) * out_ref[here, lanes].astype(f32), (1, 0))
            query_grad = None
            for half in range(2):
                log_row = log_ref[0, 2 * pair + half : 2 * pair + half + 1, here]
                shift = jnp.sum(turned[half * HD : half * HD + HD], axis=0, keepdims=True)
                for first in range(0, start + block, block):
                    keys = slice(first, first + block)
                    scores = dot(kx[half, keys, :], query, 1, 1)
                    probs = jnp.exp(scores - log_row)
                    if first + block > seq_len // 2:
                        probs = jnp.where(key + first < length, probs, 0.0)
                    if first == start:
                        probs = jnp.where(causal, probs, 0.0)
                    probs_back = dot(vx[half, keys, :], back, 1, 1)
                    scores_back = (probs * (probs_back - shift)).astype(bf16)
                    dv[half, keys, :] += dot(probs.astype(bf16), back, 1, 0)
                    dk[half, keys, :] += dot(scores_back, query, 1, 0)
                    part = dot(scores_back, kx[half, keys, :], 0, 0)
                    query_grad = part if query_grad is None else query_grad + part
            query_grad = unrope(query_grad * HD ** (-0.5), cos_ref[here, :], sin_ref[here, :])
            grad_ref[here, lanes] = query_grad.astype(bf16)

    low = lane_index((seq_len, LANES)) < HD
    key_grad = jnp.where(low, dk[0] + pltpu.roll(dk[1], HD, 1), 0.0)
    key_grad = unrope(key_grad, cos_ref[...], sin_ref[...])
    value_grad = pltpu.roll(dv[0], HD, 1) + dv[1]
    grad_ref[:, pairs * LANES :] = jnp.where(low, key_grad, value_grad).astype(bf16)


def attend_backward(group, groups, length, qkv, back, out, logs, cos_all, sin_all, block, deps=(), **beside):
    seq_len, width = qkv.shape
    group_width = width // groups
    query_width = group_width - LANES
    given = blocks((seq_len, query_width), lambda i: (0, group))
    table = blocks((seq_len, LANES), lambda i: (0, 0))
    return call(
        functools.partial(backward_kernel, block=block),
        [length, qkv, back, out, logs, cos_all, sin_all],
        [
            SMEM,
            blocks((seq_len, group_width), lambda i: (0, group)),
            given,
            given,
            blocks((1, 8, seq_len), lambda i: (group, 0, 0)),
            table,
            table,
        ],
        shaped((seq_len, group_width)),
        blocks((seq_len, group_width), lambda i: (0, 0)),
        grid=(1,),
        scratch=[
            pltpu.VMEM((2, seq_len, LANES), bf16),
            pltpu.VMEM((2, seq_len, LANES), bf16),
            pltpu.VMEM((2, seq_len, LANES), f32),
            pltpu.VMEM((2, seq_len, LANES), f32),
        ],
        deps=deps,
        mib=48,
        flops=seq_len * seq_len * 5120,
        **beside,
        name="attend_backward",
    )


def branch_kernel(
    attended_ref, others_ref, w_ref, tokens_ref, gain_ref, residual_ref, normed_ref
):
    parts = others_ref.shape[0] + 1
    step, width = others_ref.shape[1:]
    here = lax.axis_index("narrow")
    first = here * (attended_ref.shape[0] // parts) + pl.program_id(0) * step
    total = tokens_ref[...].astype(f32)
    for k in range(parts):
        part = (
            others_ref[k - 1]
            if k
            else attended_ref[pl.ds(pl.multiple_of(first, step), step), :]
        )
        place = lax.rem(here - k + parts, parts) * width
        total = total + dot(part, w_ref[pl.ds(pl.multiple_of(place, width), width), :], 1, 0)
    residual_ref[...] = total
    normed_ref[...] = rmsnorm(total, gain_ref[...]).astype(bf16)


def branch(attended, others, w_out, tokens, gain, **beside):
    groups, count, width = others.shape
    step = 128
    rows = blocks((step, D), lambda i: (i, 0))
    return call(
        branch_kernel,
        [attended, others, w_out, tokens, gain],
        [
            blocks(attended.shape, lambda i: (0, 0)),
            blocks((groups, step, width), lambda i: (0, i, 0)),
            blocks((D, D), lambda i: (0, 0)),
            rows,
            blocks((1, D), lambda i: (0, 0)),
        ],
        [shaped((count, D), f32), shaped((count, D))],
        [rows, rows],
        grid=(count // step,),
        flops=2 * count * D * D,
        name="branch",
        **beside,
    )


def spread_kernel(turn_ref, back_ref, w_ref, out_ref):
    out_ref[0] = dot(back_ref[...], w_ref[...], 1, 1).astype(bf16)


def spread(turn, back, w_out, groups, deps=()):
    count = back.shape[0]
    width = D // groups
    return call(
        spread_kernel,
        [back, w_out],
        [
            blocks((count, D), lambda i, t: (0, 0)),
            blocks((width, D), lambda i, t: (lax.rem(t[1] + i, groups), 0)),
        ],
        shaped((groups, count, width)),
        blocks((1, count, width), lambda i, t: (i, 0, 0)),
        grid=(groups,),
        prefetch=[turn],
        deps=deps,
        flops=2 * count * D * D,
        mib=32,
        name="spread",
    )


def first_back_kernel(*refs, groups, sums):
    taken, weights, grads = refs[:groups], refs[groups : 2 * groups], refs[2 * groups : 3 * groups]
    terms, outs = refs[3 * groups : -2 - sums], refs[-2 - sums :]
    outs[0][...] = sum(dot(taken[g][...], weights[g][...], 1, 0) for g in range(groups)).astype(bf16)

    @pl.when(pl.program_id(0) == 0)
    def _():
        outs[1][...] = sum(
            jnp.sum(weights[g][...].astype(f32) * grads[g][...].astype(f32), axis=0, keepdims=True)
            for g in range(groups)
        )

    each = len(terms) // sums
    for k in range(sums):

        @pl.when(pl.program_id(0) == k + 1)
        def _(k=k):
            parts = terms[k * each : (k + 1) * each]
            outs[2 + k][...] = sum(part[...].astype(f32) for part in parts).astype(bf16)


def first_back(qkv_back, w_qkv, step, grads, ends, deps=(), **beside):
    groups = len(qkv_back)
    seq_len, width = qkv_back[0].shape
    rows = ends[0][2].shape[0]
    end = blocks((rows, D), lambda i: (0, 0))
    return call(
        functools.partial(first_back_kernel, groups=groups, sums=len(ends)),
        [*qkv_back, *([w_qkv] * groups), *grads, *[term for terms in ends for term in terms]],
        [blocks((step, width), lambda i: (i, 0))] * groups
        + [blocks((width, D), lambda i, g=g: (g, 0)) for g in range(groups)]
        + [blocks((width, D), lambda i: (0, 0))] * groups
        + [end] * sum(len(terms) for terms in ends),
        [shaped((seq_len, D)), shaped((1, D), f32)] + [shaped((rows, D))] * len(ends),
        [blocks((step, D), lambda i: (i, 0)), blocks((1, D), lambda i: (0, 0))]
        + [end] * len(ends),
        grid=(seq_len // step,),
        deps=deps,
        mib=60,
        flops=2 * seq_len * width * groups * D,
        name="first_back",
        **beside,
    )


def stream(entry_refs, layout, low, high, buffer, sems, use):
    def copies(i):
        found = []
        for part, (ref, start, end, offset) in enumerate(layout[i]):
            first, last = max(start, low), min(end, high)
            if first < last:
                found.append(
                    pltpu.make_async_copy(
                        entry_refs[ref].at[pl.ds(first - start + offset, last - first)],
                        buffer.at[i % 2, pl.ds(first - low, last - first)],
                        sems.at[i % 2, part],
                    )
                )
        return found

    for copy in copies(0):
        copy.start()
    for i in range(len(layout)):
        if i + 1 < len(layout):
            for copy in copies(i + 1):
                copy.start()
        for copy in copies(i):
            copy.wait()
        use(i, buffer.at[i % 2])


def stream_scratch(rows):
    return [pltpu.VMEM((2, rows, D), bf16), pltpu.SemaphoreType.DMA((2, 3))]


def entry_layout(entries):
    arrays, layout = [], []
    for entry in entries:
        start, parts = 0, []
        for array, offset, count in entry:
            known = [k for k, other in enumerate(arrays) if other is array]
            if not known:
                known = [len(arrays)]
                arrays.append(array)
            parts.append((known[0], start, start + count, offset))
            start += count
        layout.append(parts)
    return arrays, layout, start // 3


def ff_kernel(rows_all_ref, low_ref, high_ref, *refs, layout, size, s, parts):
    hid_all, dgate_all, dup_all, rows_kept, back_kept, term_all, _ = refs[-18:-11]
    total, down, rows_ref, back_ref, hid_ref, dgate_ref, dup_ref, _, buffer, sems, own = refs[-11:]
    count = rows_ref.shape[0]
    low = low_ref.shape[0] // parts
    place = lax.rem(lax.axis_index("narrow") - s + parts, parts)
    low_place = pl.ds(pl.multiple_of(place * low, low), low)
    high_place = pl.ds(pl.multiple_of(place * (count - low), count - low), count - low)
    place = pl.ds(pl.multiple_of(place * count, count), count)
    here = pl.ds(s * count, count)
    copies = [
        pltpu.make_async_copy(rows_all_ref, rows_ref, own.at[0]),
        pltpu.make_async_copy(low_ref.at[low_place], back_ref.at[:low], own.at[1]),
        pltpu.make_async_copy(high_ref.at[high_place], back_ref.at[low:], own.at[4]),
    ]
    for copy in copies:
        copy.start()
    kept = [
        pltpu.make_async_copy(rows_ref, rows_kept.at[here], own.at[2]),
        pltpu.make_async_copy(back_ref, back_kept.at[here], own.at[3]),
    ]

    def use(i, weights):
        if i == 0:
            for copy in copies:
                copy.wait()
            for copy in kept:
                copy.start()
        gate = dot(rows_ref[...], weights[:size], 1, 1)
        up = dot(rows_ref[...], weights[size : 2 * size], 1, 1)
        hidden_back = dot(back_ref[...], weights[2 * size :], 1, 1)
        sig = 1.0 / (1.0 + jnp.exp(-gate))
        silu = gate * sig
        cols = slice(i * size, (i + 1) * size)
        hid = (silu * up).astype(bf16)
        dgate = (hidden_back * up * (sig * (1.0 + gate * (1.0 - sig)))).astype(bf16)
        dup = (hidden_back * silu).astype(bf16)
        hid_ref[:, cols] = hid
        dgate_ref[:, cols] = dgate
        dup_ref[:, cols] = dup
        part = dot(dgate, weights[:size], 1, 0) + dot(dup, weights[size : 2 * size], 1, 0)
        term = dot(hid, weights[2 * size :], 1, 0)
        if i:
            part = part + total[...]
            term = term + down[...]
        total[...] = part
        down[...] = term

    stream(refs, layout, 0, 3 * size, buffer, sems, use)
    for copy in kept:
        copy.wait()
    rows_ref[...] = down[...].astype(bf16)
    copies = [
        pltpu.make_async_copy(hid_ref, hid_all.at[here], own.at[0]),
        pltpu.make_async_copy(dgate_ref, dgate_all.at[here], own.at[1]),
        pltpu.make_async_copy(dup_ref, dup_all.at[here], own.at[2]),
        pltpu.make_async_copy(rows_ref, term_all.at[place], own.at[3]),
    ]
    for copy in copies:
        copy.start()
    for copy in copies:
        copy.wait()


def ff_close(lands, refs, *, added):
    out_ref, total = refs[-12:-10]
    arrived = refs[-4]
    value = total[...]
    if added:
        value = value + arrived[...].astype(f32)
    out_ref[...] = value.astype(out_ref.dtype)


def ff_step(s, rows, back_low, back_high, entries, kept, moving, added=False, last=False):
    count = rows.shape[0]
    seq_len = back_low.shape[0] + back_high.shape[0]
    arrays, layout, size = entry_layout(entries)
    ff_width = size * len(entries)
    return call(
        functools.partial(
            ff_kernel, layout=layout, size=size, s=s, parts=seq_len // count
        ),
        [rows, back_low, back_high, *arrays, *kept],
        [ANY] * (3 + len(arrays) + len(kept)),
        [shaped((seq_len, ff_width))] * 3
        + [shaped((seq_len, D))] * 3
        + [shaped((count, D), f32 if last else bf16)],
        [ANY] * 6 + [VMEM],
        scratch=[pltpu.VMEM((count, D), f32)] * 2
        + [pltpu.VMEM((count, D), bf16)] * 2
        + [pltpu.VMEM((count, ff_width), bf16)] * 3
        + [pltpu.VMEM((count, D), bf16)]
        + stream_scratch(3 * size)
        + [pltpu.SemaphoreType.DMA((5,))],
        aliases={3 + len(arrays) + k: k for k in range(len(kept))},
        mib=60,
        flops=10 * count * ff_width * D,
        name="ff_step",
        sends=[Send(0, 0, "narrow", 1)],
        sources=[moving],
        lands=[] if added else [moving.shape],
        inner=(7,) if added else (),
        closing=functools.partial(ff_close, added=added),
    )


def add_kernel(*refs):
    refs[-1][...] = sum(ref[...].astype(f32) for ref in refs[:-1]).astype(refs[-1].dtype)


def add(terms, kind=bf16, deps=(), **beside):
    count, width = terms[0].shape
    step = 128 if count % 128 == 0 else 64 if count % 64 == 0 else count
    given = blocks((step, width), lambda i: (i, 0))
    return call(
        add_kernel,
        terms,
        [given] * len(terms),
        shaped((count, width), kind),
        given,
        grid=(count // step,),
        deps=deps,
        moved=count * width * 8,
        name="add",
        **beside,
    )


def outer_kernel(first_ref, second_ref, *outs):
    first = first_ref[...]
    if len(first.shape) == 3:
        first = first[0]
    product = dot(first, second_ref[...], 0, 0).astype(bf16)
    each = pl.num_programs(0) // len(outs)
    for k, out_ref in enumerate(outs):

        @pl.when(pl.program_id(0) // each == k)
        def _(out_ref=out_ref):
            out_ref[...] = product


def outer(first, second, split=1, deps=(), **beside):
    rows, width = second.shape
    if len(first.shape) == 3:
        groups, _, step = first.shape
        height = groups * step
        taken = blocks((1, rows, step), lambda i: (i, 0, 0))
    else:
        height = first.shape[1]
        step = next(k for k in (512, 384, 256, 192, LANES) if height % (k * split) == 0)
        taken = blocks((rows, step), lambda i: (0, i))
    each = height // step // split
    return call(
        outer_kernel,
        [first, second],
        [taken, blocks((rows, width), lambda i: (0, 0))],
        [shaped((height // split, width))] * split,
        [
            blocks((step, width), lambda i, k=k: (jnp.clip(i - k * each, 0, each - 1), 0))
            for k in range(split)
        ],
        grid=(height // step,),
        deps=deps,
        mib=56,
        flops=2 * rows * height * width,
        **beside,
        name="outer",
    )


def outer_pair_kernel(first_ref, second_ref, rows_ref, *outs):
    for part, (taken_ref, out_ref) in enumerate(zip((first_ref, second_ref), outs)):

        @pl.when(pl.program_id(0) == part)
        def _(taken_ref=taken_ref, out_ref=out_ref):
            out_ref[...] = dot(taken_ref[...], rows_ref[...], 0, 0).astype(bf16)


def outer_pair(firsts, second, deps=(), **beside):
    rows, height = firsts[0].shape
    width = second.shape[1]
    taken = blocks((rows, height), lambda i: (0, 0))
    return call(
        outer_pair_kernel,
        [*firsts, second],
        [taken, taken, blocks((rows, width), lambda i: (0, 0))],
        [shaped((height, width))] * 2,
        [blocks((height, width), lambda i: (0, 0))] * 2,
        grid=(2,),
        deps=deps,
        flops=4 * rows * height * width,
        name="outer_pair",
        mib=60,
        **beside,
    )


def pass_kernel(*refs):
    pass


def after(value, *deps):
    return call(
        pass_kernel, [value], [ANY], shaped(value.shape, value.dtype), ANY, deps=deps,
        aliases={0: 0}, name="after",
    )


def shift(count, step=1):
    return [(i, (i + step) % count) for i in range(count)]


def nothing(*refs):
    pass


def sum_places_kernel(place_ref, own_ref, others_ref, out_ref):
    total = jnp.zeros(own_ref.shape, f32)
    for k in range(others_ref.shape[0]):
        total = total + jnp.where(place_ref[0] == k, own_ref[...], others_ref[k])
    out_ref[...] = total


def sum_places(place, own, others):
    return call(
        sum_places_kernel,
        [place, own, others],
        [SMEM, VMEM, VMEM],
        shaped(own.shape, f32),
        VMEM,
        name="sum_places",
    )


def move(sends, sources, lands, deps=()):
    return call(
        nothing, [], [], [], [], sends=sends, sources=sources, lands=lands, deps=deps, name="move"
    )


def rows_at(first, count):
    return lambda wide, narrow: pl.ds(first, count)


def exchange_units(turned):
    return move(
        [
            Send(
                0, 0, "wide", e,
                lambda wide, narrow, e=e: jnp.bitwise_xor(wide, e),
                lambda wide, narrow: wide,
            )
            for e in range(1, turned.shape[0])
        ],
        [turned],
        [turned.shape],
    )[0]


def near_and_across(source, land, at=None, needs=()):
    return [
        Send(source, land, "wide", 2, at, needs=needs),
        Send(source, land + 1, "wide", 4, at, needs=needs),
    ]


def sum_entries_kernel(first_ref, second_ref, *outs):
    total = (first_ref[0].astype(f32) + second_ref[0].astype(f32)).astype(bf16)
    for r, out_ref in enumerate(outs):

        @pl.when(pl.program_id(0) == r)
        def _(out_ref=out_ref):
            out_ref[...] = total


def sum_entries(first, second, **beside):
    count, rows, width = first.shape
    given = blocks((1, rows, width), lambda i: (i, 0, 0))
    return call(
        sum_entries_kernel,
        [first, second],
        [given, given],
        [shaped((rows, width))] * count,
        [blocks((rows, width), lambda i: (0, 0))] * count,
        grid=(count,),
        moved=first.size * 6,
        name="sum_entries",
        **beside,
    )


def ff_meet_kernel(own_ref, other_ref, first_out, second_out):
    total = (own_ref[...].astype(f32) + other_ref[...].astype(f32)).astype(bf16)
    half = first_out.shape[0]
    first_out[...] = total[:half]
    second_out[...] = total[half:]


def ff_meet(own, other, deps=()):
    rows, width = own.shape[0] // 4, own.shape[1]
    last = blocks((rows, width), lambda i: (3, 0))
    half = blocks((rows // 2, width), lambda i: (0, 0))
    return call(
        ff_meet_kernel,
        [own, other],
        [last, last],
        [shaped((rows // 2, width))] * 2,
        [half, half],
        grid=(1,),
        deps=deps,
        moved=own.size * 2,
        name="ff_meet",
    )


def ff_join_kernel(
    own_x, other_x, first_ref, own_y, other_y, second_ref, x_out, y_out
):
    half = first_ref.shape[0]
    x = own_x[...].astype(f32) + other_x[...].astype(f32)
    y = own_y[...].astype(f32) + other_y[...].astype(f32)
    x_out[:half] = (x[:half] + first_ref[...].astype(f32)).astype(bf16)
    x_out[half:] = x[half:].astype(bf16)
    y_out[:half] = y[:half].astype(bf16)
    y_out[half:] = (y[half:] + second_ref[...].astype(f32)).astype(bf16)


def ff_join(own, other, first, second, deps=()):
    rows, width = own.shape[0] // 4, own.shape[1]

    def quarter(k):
        return blocks((rows, width), lambda i: (k, 0))

    half = blocks((rows // 2, width), lambda i: (0, 0))
    shape = shaped((rows, width))
    return call(
        ff_join_kernel,
        [own, other, first, own, other, second],
        [quarter(1), quarter(1), half, quarter(2), quarter(2), half],
        [shape, shape],
        [quarter(0), quarter(0)],
        grid=(1,),
        deps=deps,
        moved=own.size * 4,
        name="ff_join",
    )


def ff_end_kernel(*refs):
    refs[-1][...] = sum(ref[...].astype(f32) for ref in refs[:-1]).astype(bf16)


def ff_end(own, other, near, deps=(), **beside):
    rows, width = own.shape[0] // 4, own.shape[1]
    first = blocks((rows, width), lambda i: (0, 0))
    return call(
        ff_end_kernel,
        [own, other, *near],
        [first] * (2 + len(near)),
        shaped((rows, width)),
        first,
        grid=(1,),
        deps=deps,
        moved=own.size * 2,
        name="ff_end",
        **beside,
    )


def shaped_rows(array, parts):
    return (array.shape[0] // parts, array.shape[1])


def across_sends(source, land):
    return [Send(source, land, "wide", 4), Send(source + 1, land + 1, "wide", 2)]


def near_sends(source, land):
    return [Send(source, land, "wide", 2), Send(source + 1, land + 1, "wide", 4)]


def unit_row(col, query_width, kv_width, by_head, group_width):
    start, offset = col
    if start < query_width:
        return start // by_head * group_width + start % by_head + offset
    start -= query_width
    last = start >= kv_width
    if last:
        start -= kv_width
    head = (start + offset) // HD
    return head * group_width + by_head + last * HD + (start + offset) % HD


def assemble_qkv_kernel(
    turn_ref, own_ref, near_ref, other_ref, out_ref, *, piece, unit_cols, sizes
):
    height = near_ref.shape[1]
    for e in range(8):
        j = jnp.bitwise_xor(turn_ref[0], e)
        for c in range(height // piece):
            here = slice(c * piece, (c + 1) * piece)
            row = unit_row((c * unit_cols, j * piece), *sizes)
            if e % 2:
                value = other_ref[e // 2, here, :]
            elif e:
                value = near_ref[e // 2 - 1, here, :]
            else:
                value = own_ref[here, :]
            out_ref[pl.ds(pl.multiple_of(row, piece), piece), :] = value


def assemble_qkv(turn, rows, near, other, piece, unit_cols, sizes):
    _, height, _ = near.shape
    return call(
        functools.partial(
            assemble_qkv_kernel, piece=piece, unit_cols=unit_cols, sizes=sizes
        ),
        [turn, rows, near, other],
        [SMEM, blocks((height, D), lambda i: (0, 0)), whole_block(near), whole_block(other)],
        shaped((height * 8, D)),
        blocks((height * 8, D), lambda i: (0, 0)),
        grid=(1,),
        mib=60,
        moved=height * 8 * D * 4,
        name="assemble_qkv",
    )


def whole_block(array):
    return blocks(array.shape, lambda i: (0,) * len(array.shape))


def arrange_attn_kernel(turn_ref, *refs, piece, unit_cols, sizes):
    *grads, own_ref, other_ref = refs
    query_width, kv_width, _, group_width = sizes
    out_first = query_width + 2 * kv_width
    for j in range(unit_cols // piece):
        e = jnp.bitwise_xor(turn_ref[0], j)
        for core, out_ref in enumerate((own_ref, other_ref)):

            @pl.when(e % 2 == core)
            def _(j=j, e=e, out_ref=out_ref):
                for c in range(out_ref.shape[1] // piece):
                    if c * unit_cols < out_first:
                        row = unit_row((c * unit_cols, j * piece), *sizes)
                        grad_ref = grads[row // group_width]
                        row = row % group_width
                    else:
                        row = c * unit_cols - out_first + j * piece
                        grad_ref = grads[-1]
                    out_ref[e // 2, c * piece : (c + 1) * piece, :] = grad_ref[
                        row : row + piece, :
                    ]


def arrange_attn(turn, grads, piece, unit_cols, sizes):
    count = unit_cols // piece
    rows = sum(grad.shape[0] for grad in grads) // count
    shape = shaped((count // 2, rows, D))
    return call(
        functools.partial(arrange_attn_kernel, piece=piece, unit_cols=unit_cols, sizes=sizes),
        [turn, *grads],
        [SMEM] + [VMEM] * len(grads),
        [shape, shape],
        [VMEM] * 2,
        mib=32,
        moved=rows * count * D * 4,
        name="arrange_attn",
    )


def out_row(turn_ref, k, c, j, parts, piece, unit_cols, sign):
    n = lax.rem(turn_ref[1] + sign * k + parts, parts)
    return n * (D // parts) + c * unit_cols + j * piece


def assemble_out_kernel(
    turn_ref, rows_ref, z_ref, x_ref, y_ref, across_ref, other_ref, out_ref, *, first, piece,
    unit_cols, parts,
):
    height = z_ref.shape[1]
    for e in range(8):
        j = jnp.bitwise_xor(turn_ref[0], e)
        for k in range(parts):
            for c in range(height // piece):
                here = slice(c * piece, (c + 1) * piece)
                row = out_row(turn_ref, k, c, j, parts, piece, unit_cols, -1)
                if e % 2:
                    value = other_ref[e // 2, k, here, :]
                elif e:
                    value = (x_ref, y_ref, across_ref)[e // 2 - 1][k, here, :]
                elif k:
                    value = z_ref[k - 1, here, :]
                else:
                    value = rows_ref[first + c * piece : first + (c + 1) * piece, :]
                out_ref[pl.ds(pl.multiple_of(row, piece), piece), :] = value


def assemble_out(turn, rows, first, given, piece, unit_cols, parts, deps=()):
    height = given[0].shape[1]
    return call(
        functools.partial(
            assemble_out_kernel, first=first, piece=piece, unit_cols=unit_cols, parts=parts
        ),
        [turn, rows, *given],
        [SMEM, blocks((first + height, D), lambda i: (0, 0))] + [whole_block(a) for a in given],
        shaped((D, D)),
        blocks((D, D), lambda i: (0, 0)),
        grid=(1,),
        mib=52,
        deps=deps,
        moved=D * D * 4,
        name="assemble_out",
    )


def local(
    tokens, cotangent, lengths, owners, master, moment_one, moment_two, norm_gains, gain_first,
    gain_second,
):
    wide_count = lax.axis_size("wide")
    narrow_count = lax.axis_size("narrow")
    capacity, _, unit_rows, unit_cols = master.shape
    unit_count = owners.shape[0]
    row_count = tokens.shape[0]
    seq_len = row_count * narrow_count
    row_blocks = D // unit_rows
    col_blocks = unit_count // row_blocks
    piece = unit_cols // wide_count
    query_width = H // narrow_count * HD
    kv_width = KV // narrow_count * HD
    ff_width = FF // narrow_count
    qkv_width = query_width + 2 * kv_width
    groups = KV // narrow_count
    group_width = qkv_width // groups
    by_head = group_width - 2 * HD
    wide_index = lax.axis_index("wide")
    narrow_index = lax.axis_index("narrow")
    turn = jnp.stack([wide_index, narrow_index]).astype(jnp.int32)
    length = lax.dynamic_slice(lengths, (wide_index,), (1,))
    block = min(256, seq_len)
    qkv_blocks = qkv_width // unit_cols
    out_blocks = query_width // unit_cols
    attn_blocks = qkv_blocks + out_blocks
    sizes = (query_width, kv_width, by_head, group_width)
    back_by = (narrow_index - jnp.arange(narrow_count, dtype=jnp.int32)) % narrow_count

    inputs = tokens.astype(f32)
    normed = rmsnorm(inputs, norm_gains[0]).astype(bf16)
    normed_all = lax.all_gather(normed, "narrow", axis=0, tiled=True)

    slot_place, counts = positions(owners, wide_count, capacity)
    turned = turn_units(master, wide_count, ())
    got = exchange_units(turned)
    rows = pick_units(turn, slot_place, turned, got, row_blocks)
    qkv_rows = qkv_blocks * piece
    out_rows = out_blocks * piece
    ff_first = qkv_rows + out_rows
    ff_rows = 3 * ff_width // wide_count

    qkv_at, out_at = rows_at(0, qkv_rows), rows_at(qkv_rows, out_rows)

    def entry(k):
        return lambda wide, narrow: k

    near_qkv, other_qkv, narrow_out = move(
        [Send(0, 0, "wide", 2 * r, qkv_at, entry(r - 1)) for r in (1, 2, 3)]
        + [Send(0, 1, "wide", 1, qkv_at, entry(0))]
        + [Send(0, 2, "narrow", k, out_at, entry(k - 1)) for k in range(1, narrow_count)]
        + [
            Send(0, 1, "wide", 1, entry(r - 1), entry(r), landed=True, needs=(r - 1,))
            for r in (1, 2, 3)
        ],
        [rows],
        [
            (3, qkv_rows, D),
            (4, qkv_rows, D),
            (narrow_count - 1, out_rows, D),
        ],
    )
    w_qkv = assemble_qkv(turn, rows, near_qkv, other_qkv, piece, unit_cols, sizes)

    cos_all, sin_all = turn_tables(seq_len)
    low_rows = row_count // 2
    cotangent_then = after(cotangent[:low_rows], normed_all, w_qkv)
    back_low = lax.all_gather(cotangent_then, "narrow", axis=0, tiled=True)
    qkv = project(
        normed_all, w_qkv, cos_all, sin_all, group_width, row_count, (cotangent_then,)
    )
    out_shape = (narrow_count, out_rows, D)

    def first_entry(wide, narrow):
        return 0

    def later_entries(wide, narrow):
        return pl.ds(1, narrow_count - 1)

    attended, logs, out_x, out_y = attend_forward(
        length, qkv, groups, block,
        sends=[
            Send(0, 0, "wide", 2, out_at, first_entry),
            Send(0, 1, "wide", 4, out_at, first_entry),
            Send(1, 0, "wide", 2, None, later_entries),
            Send(1, 1, "wide", 4, None, later_entries),
        ],
        sources=[rows, narrow_out],
        lands=[out_shape, out_shape],
    )

    half = narrow_count // 2
    third = ff_rows // 3

    def heads_of(k):
        return lambda wide, narrow: pl.ds(
            pl.multiple_of(lax.rem(narrow + k, narrow_count) * row_count, row_count), row_count
        )

    def part_of(k, at):
        return lambda wide, narrow: (k, at)

    low_part, high_part = pl.ds(0, half), pl.ds(half, narrow_count - half)
    attended_others, out_across, out_other, x_first, y_first = move(
        [Send(0, 0, "narrow", k, heads_of(k), entry(k - 1)) for k in range(1, narrow_count)]
        + [
            Send(2, 1, "wide", 4, lambda w, n: low_part, lambda w, n: low_part),
            Send(3, 1, "wide", 2, lambda w, n: high_part, lambda w, n: high_part),
            Send(1, 2, "wide", 1, out_at, lambda w, n: (0, 0)),
            Send(4, 2, "wide", 1, None, lambda w, n: (0, pl.ds(1, narrow_count - 1))),
            Send(2, 2, "wide", 1, None, entry(1)),
            Send(3, 2, "wide", 1, None, entry(2)),
            Send(1, 3, "wide", 2, rows_at(ff_first, third)),
            Send(1, 4, "wide", 4, rows_at(ff_first, third)),
            Send(
                1, 2, "wide", 1, None, entry(3), landed=True,
                needs=(narrow_count - 1, narrow_count),
            ),
        ],
        [attended, rows, out_x, out_y, narrow_out],
        [
            (narrow_count - 1, row_count, query_width),
            out_shape,
            (4, *out_shape),
            (third, D),
            (third, D),
        ],
    )
    back_high = lax.all_gather(
        after(cotangent[low_rows:], attended_others, back_low), "narrow", axis=0, tiled=True
    )
    w_out = assemble_out(
        turn, rows, qkv_rows, [narrow_out, out_x, out_y, out_across, out_other], piece,
        unit_cols, narrow_count,
    )
    residual, normed_two = branch(
        attended, attended_others, w_out, tokens, norm_gains[1:2]
    )

    rest = ff_rows - third
    half_rest = ff_rows // 2 - third
    (
        block_one, x_last, y_last, own_swap, x_first_swap, y_first_swap, x_last_swap, y_last_swap,
        across_first,
    ) = move(
        [Send(0, 0, "narrow", 1)]
        + near_and_across(1, 1, rows_at(ff_first + third, rest))
        + [Send(1, 3, "wide", 1, rows_at(ff_first, ff_rows))]
        + [Send(2, 4, "wide", 1), Send(3, 5, "wide", 1)]
        + [
            Send(1, 6, "wide", 1, landed=True, needs=(1,)),
            Send(2, 7, "wide", 1, landed=True, needs=(2,)),
            Send(2, 8, "wide", 4),
        ],
        [normed_two, rows, x_first, y_first],
        [normed_two.shape, (rest, D), (rest, D), (ff_rows, D)]
        + [(third, D)] * 2
        + [(rest, D)] * 2
        + [(third, D)],
    )
    block_two, *across = move(
        [
            Send(0, 0, "narrow", 1),
            Send(2, 1, "wide", 4, rows_at(0, half_rest)),
            Send(3, 2, "wide", 2, rows_at(half_rest, ff_rows // 2)),
            Send(1, 3, "wide", 1),
            Send(1, 4, "wide", 1, landed=True, needs=(1,)),
            Send(2, 5, "wide", 1, landed=True, needs=(2,)),
        ],
        [block_one, across_first, x_last, y_last],
        [block_one.shape, (half_rest, D), (ff_rows // 2, D)]
        + [(third, D), (half_rest, D), (ff_rows // 2, D)],
    )
    across = [across_first, *across]

    def pieces(*arrays):
        return [(array, 0, array.shape[0]) for array in arrays]

    entries = [
        [(rows, ff_first, ff_rows)],
        pieces(x_first, x_last),
        pieces(y_first, y_last),
        pieces(*across[:3]),
        [(own_swap, 0, ff_rows)],
        pieces(x_first_swap, x_last_swap),
        pieces(y_first_swap, y_last_swap),
        pieces(*across[3:]),
    ]

    *kept, total, block_three = ff_step(1, block_one, back_low, back_high, entries, (), block_two)
    *kept, total = ff_step(2, block_two, back_low, back_high, entries, kept, total, True)
    *kept, total = ff_step(3, block_three, back_low, back_high, entries, kept, total, True)
    *kept, norm_two_back = ff_step(0, normed_two, back_low, back_high, entries, kept, total, True, True)
    hidden, dgate, dup, mlp_all, back_kept, ff_term = kept

    _, norm_two_pull = jax.vjp(rmsnorm, residual, norm_gains[1])
    resid_part, gain_two = norm_two_pull(norm_two_back)
    resid_back = cotangent.astype(f32) + resid_part
    attn_back = resid_back.astype(bf16)
    by_heads = spread(turn, attn_back, w_out, narrow_count)

    def heads_send(k, land):
        return Send(0, land, "narrow", k, entry(k))

    heads_shape = (row_count, query_width)
    *grad_down, heads_one, heads_three = outer(
        hidden, back_kept, 2,
        sends=[heads_send(1, 0), heads_send(3, 1)],
        sources=[by_heads],
        lands=[heads_shape, heads_shape],
    )
    half_shape, near_shape = shaped_rows(grad_down[0], 8), shaped_rows(grad_down[0], 4)
    *grad_gate, heads_two, down_swap = outer(
        dgate, mlp_all, 2,
        sends=[heads_send(2, 0), Send(1, 1, "wide", 1)],
        sources=[by_heads, grad_down[1]],
        lands=[heads_shape, grad_down[1].shape],
    )
    out_back = jnp.stack([by_heads[0], heads_one, heads_two, heads_three])
    out_back = jnp.take(out_back, back_by, axis=0).reshape(seq_len, query_width)
    attn_back_all = lax.all_gather(after(attn_back, heads_two), "narrow", axis=0, tiled=True)
    ff_sum = lax.psum_scatter(
        after(ff_term, heads_two), "narrow", scatter_dimension=0, tiled=True
    )
    output = residual + ff_sum.astype(f32)
    down_across = ff_meet(grad_down[0], down_swap)
    *grad_upper, gate_swap, down_a, down_b = outer(
        dup, mlp_all, 2,
        sends=[Send(0, 0, "wide", 1)] + across_sends(1, 1),
        sources=[grad_gate[1], *down_across],
        lands=[grad_gate[1].shape, half_shape, half_shape],
    )
    joined_down = ff_join(grad_down[0], down_swap, down_a, down_b)
    gate_across = ff_meet(grad_gate[0], gate_swap)

    qkv_back = [None, None]
    qkv_back[0], upper_swap, gate_a, gate_b, down_x, down_y = attend_backward(
        0, groups, length, qkv, out_back, attended, logs, cos_all, sin_all, block,
        sends=[Send(0, 0, "wide", 1)] + across_sends(1, 1) + near_sends(3, 3),
        sources=[grad_upper[1], *gate_across, *joined_down],
        lands=[grad_upper[1].shape, half_shape, half_shape, near_shape, near_shape],
    )
    upper_across = ff_meet(grad_upper[0], upper_swap)
    joined_gate = ff_join(grad_gate[0], gate_swap, gate_a, gate_b)
    qkv_back[1], upper_a, upper_b, gate_x, gate_y = attend_backward(
        1, groups, length, qkv, out_back, attended, logs, cos_all, sin_all, block,
        sends=across_sends(0, 0) + near_sends(2, 2),
        sources=[*upper_across, *joined_gate],
        lands=[half_shape] * 2 + [near_shape] * 2,
    )
    joined_upper = ff_join(grad_upper[0], upper_swap, upper_a, upper_b)
    *grad_qkv, upper_x, upper_y = outer_pair(
        qkv_back, normed_all, (joined_upper[0],),
        sends=near_sends(0, 0), sources=list(joined_upper), lands=[near_shape] * 2,
    )
    (grad_out,) = outer(attended, attn_back_all, 1, (grad_qkv[0],))
    own_attn, other_attn = arrange_attn(
        turn, [*grad_qkv, grad_out], piece, unit_cols, sizes
    )
    gate_sum, attn_swap = ff_end(
        grad_gate[0], gate_swap, [gate_x, gate_y],
        sends=[Send(0, 0, "wide", 1)], sources=[other_attn], lands=[other_attn.shape],
    )
    met_attn = sum_entries(own_attn, attn_swap)
    norm_one_term, gain_one, down_sum, upper_sum, *arrived = first_back(
        qkv_back, w_qkv, row_count, grad_qkv,
        [
            [grad_down[0], down_swap, down_x, down_y],
            [grad_upper[0], upper_swap, upper_x, upper_y],
        ],
        sends=[Send(r - 1, r - 1, "wide", 2 * r) for r in (1, 2, 3)],
        sources=met_attn[1:],
        lands=[met_attn[0].shape] * 3,
    )
    attn_sum = add([met_attn[0]] + arrived)

    slots = wide_count * capacity
    unit_of = jnp.zeros((slots,), jnp.int32).at[slot_place].set(
        jnp.arange(unit_count, dtype=jnp.int32)
    )
    half_of = unit_of // col_blocks
    low, high = unpick_units(
        jnp.concatenate([attn_sum, gate_sum, upper_sum, down_sum], axis=0),
        unit_of - half_of * col_blocks,
        half_of,
        wide_count,
        piece,
        unit_rows,
    )
    gain_terms = jnp.stack([gain_one[0] / norm_gains[0], gain_two])
    owned_low, gain_others = move(
        [
            Send(
                0, 0, "wide", e,
                lambda wide, narrow, e=e: jnp.bitwise_xor(wide, e),
                lambda wide, narrow: wide,
            )
            for e in range(1, wide_count)
        ]
        + [
            Send(1, 1, "wide", e, None, lambda wide, narrow: wide) for e in range(1, wide_count)
        ],
        [low, gain_terms],
        [low.shape, ((wide_count, *gain_terms.shape), f32)],
    )
    owned_high = lax.all_to_all(after(high, owned_low), "wide", split_axis=0, concat_axis=0)
    gain_plane = sum_places(wide_index.reshape(1), gain_terms, gain_others)
    filled = jnp.concatenate(
        [lax.dynamic_slice(counts, (wide_index,), (1,)), wide_index.reshape(1)]
    ).astype(jnp.int32)
    updated = update_units(
        filled, owned_low, low, 0, master, moment_one, moment_two, ()
    )
    owned_grads, new_master, new_copy, new_first, new_second = update_units(
        filled, owned_high, owned_high, low.shape[1], master, moment_one, moment_two, updated
    )
    gain_others = jnp.stack(
        [gain_plane]
        + [
            after(lax.ppermute(gain_plane, "narrow", shift(narrow_count, k)), owned_grads)
            for k in range(1, narrow_count)
        ]
    )
    gain_grads = sum_places(
        narrow_index.reshape(1), gain_plane, jnp.take(gain_others, back_by, axis=0)
    )

    norm_one_back = lax.psum_scatter(
        after(norm_one_term, ff_sum, attn_sum), "narrow", scatter_dimension=0, tiled=True
    )
    norm_one_back = after(norm_one_back, owned_grads).astype(f32)
    _, norm_one_pull = jax.vjp(lambda values: rmsnorm(values, norm_gains[0]), inputs)
    (input_part,) = norm_one_pull(norm_one_back)
    input_grad = (resid_back + input_part).astype(bf16)
    new_gains, _, gain_second_new = adamw(
        norm_gains, gain_grads, gain_first, gain_second, 0.5, 0.0
    )
    return (
        output.astype(bf16),
        input_grad,
        owned_grads,
        new_master,
        new_copy,
        new_first,
        new_second,
        gain_grads,
        gain_second_new,
        new_gains,
    )


def rotate(values, cos_table, sin_table):
    middle = values.shape[-1] // 2
    turned = jnp.concatenate([-values[..., middle:], values[..., :middle]], axis=-1)
    return values * cos_table + turned * sin_table


def unrotate(gradient, cos_table, sin_table):
    middle = gradient.shape[-1] // 2
    weighted = gradient * sin_table
    turned = jnp.concatenate([weighted[..., middle:], -weighted[..., :middle]], axis=-1)
    return gradient * cos_table + turned


def matmul_rows(first_op, second_op):
    return lax.dot_general(
        first_op, second_op, (((0,), (0,)), ((), ())), preferred_element_type=jnp.float32
    )


def matmul_cols(first_op, second_op):
    return lax.dot_general(
        first_op, second_op, (((1,), (1,)), ((), ())), preferred_element_type=jnp.float32
    )


def project_any(normed_all, w_qkv, cos_heads, sin_heads, heads_here, kv_here):
    seq_len = normed_all.shape[0]
    projected = jnp.dot(normed_all, w_qkv, preferred_element_type=jnp.float32)
    query_width = heads_here * HD
    kv_width = kv_here * HD
    group_size = heads_here // kv_here
    query_heads = rotate(
        projected[:, :query_width].reshape(seq_len, heads_here, HD), cos_heads, sin_heads
    )
    key_heads = rotate(
        projected[:, query_width : query_width + kv_width].reshape(seq_len, kv_here, HD),
        cos_heads,
        sin_heads,
    )
    value_heads = projected[:, query_width + kv_width :].reshape(seq_len, kv_here, HD)
    query_heads = jnp.transpose(query_heads.astype(jnp.bfloat16), (1, 0, 2)).reshape(
        kv_here, group_size, seq_len, HD
    )
    key_heads = jnp.transpose(key_heads.astype(jnp.bfloat16), (1, 0, 2))
    value_heads = jnp.transpose(value_heads.astype(jnp.bfloat16), (1, 0, 2))
    return (query_heads, key_heads, value_heads)


def masked_scores(query_block, key_heads, row_start, length):
    block_rows = query_block.shape[2]
    seq_len = key_heads.shape[1]
    scores = jnp.einsum(
        "kgqd,ksd->kgqs", query_block, key_heads, preferred_element_type=jnp.float32
    ) * HD ** (-0.5)
    row_pos = row_start + jnp.arange(block_rows, dtype=jnp.int32)
    key_pos = jnp.arange(seq_len, dtype=jnp.int32)
    allowed = (key_pos[None, :] <= row_pos[:, None]) & (key_pos[None, :] < length)
    return jnp.where(allowed, scores, -1e30)


def attend_forward_any(query_heads, key_heads, value_heads, length, block_rows):
    seq_len = query_heads.shape[2]
    outputs = []
    log_sums = []
    for row_start in range(0, seq_len, block_rows):
        query_block = query_heads[:, :, row_start : row_start + block_rows]
        scores = masked_scores(query_block, key_heads, row_start, length)
        row_peak = jnp.max(scores, axis=-1, keepdims=True)
        raised = jnp.exp(scores - row_peak)
        row_total = jnp.sum(raised, axis=-1, keepdims=True)
        attn_probs = (raised / row_total).astype(jnp.bfloat16)
        outputs.append(
            jnp.einsum(
                "kgqs,ksd->kgqd", attn_probs, value_heads, preferred_element_type=jnp.float32
            )
        )
        log_sums.append((row_peak + jnp.log(row_total))[..., 0])
    return (jnp.concatenate(outputs, axis=2), jnp.concatenate(log_sums, axis=2))


def attend_backward_any(query_heads, key_heads, value_heads, out_back, log_sums, length, block_rows):
    seq_len = query_heads.shape[2]
    query_grads = []
    key_grad = jnp.zeros(key_heads.shape, jnp.float32)
    value_grad = jnp.zeros(value_heads.shape, jnp.float32)
    for row_start in range(0, seq_len, block_rows):
        query_block = query_heads[:, :, row_start : row_start + block_rows]
        back_block = out_back[:, :, row_start : row_start + block_rows]
        scores = masked_scores(query_block, key_heads, row_start, length)
        attn_probs = jnp.exp(scores - log_sums[:, :, row_start : row_start + block_rows, None])
        probs_back = jnp.einsum(
            "kgqd,ksd->kgqs", back_block, value_heads, preferred_element_type=jnp.float32
        )
        row_shift = jnp.sum(attn_probs * probs_back, axis=-1, keepdims=True)
        scores_back = (HD ** (-0.5) * attn_probs * (probs_back - row_shift)).astype(jnp.bfloat16)
        query_grads.append(
            jnp.einsum("kgqs,ksd->kgqd", scores_back, key_heads, preferred_element_type=jnp.float32)
        )
        key_grad = key_grad + jnp.einsum(
            "kgqs,kgqd->ksd", scores_back, query_block, preferred_element_type=jnp.float32
        )
        value_grad = value_grad + jnp.einsum(
            "kgqs,kgqd->ksd",
            attn_probs.astype(jnp.bfloat16),
            back_block,
            preferred_element_type=jnp.float32,
        )
    return (jnp.concatenate(query_grads, axis=2), key_grad, value_grad)


def local_any(
    tokens,
    cotangent,
    lengths,
    owners,
    master,
    moment_one,
    moment_two,
    norm_gains,
    gain_first,
    gain_second,
):
    wide_count = lax.axis_size("wide")
    narrow_count = lax.axis_size("narrow")
    capacity = master.shape[0]
    unit_rows = master.shape[2]
    unit_cols = master.shape[3]
    unit_count = owners.shape[0]
    row_count = tokens.shape[0]
    seq_len = row_count * narrow_count
    slot_place, _ = positions(owners, wide_count, capacity)
    own_slots = master[:, 0].astype(jnp.bfloat16)
    all_slots = lax.all_gather(own_slots, "wide", axis=0, tiled=True)
    unit_data = jnp.take(all_slots, slot_place, axis=0)
    row_blocks = D // unit_rows
    col_blocks = unit_count // row_blocks
    packed = jnp.transpose(
        unit_data.reshape(row_blocks, col_blocks, unit_rows, unit_cols), (0, 2, 1, 3)
    ).reshape(D, col_blocks * unit_cols)
    heads_here = H // narrow_count
    kv_here = KV // narrow_count
    group_size = heads_here // kv_here
    query_width = heads_here * HD
    kv_width = kv_here * HD
    ff_width = FF // narrow_count
    qkv_end = query_width + 2 * kv_width
    out_end = qkv_end + query_width
    gate_end = out_end + 2 * ff_width
    w_qkv = packed[:, :qkv_end]
    w_out_t = packed[:, qkv_end:out_end]
    w_gate_up = packed[:, out_end:gate_end]
    w_down_t = packed[:, gate_end:]
    cos_table, sin_table = tables(seq_len, HD)
    cos_heads = cos_table[:, None, :]
    sin_heads = sin_table[:, None, :]
    block_rows = min(512, seq_len)
    wide_index = lax.axis_index("wide")
    length = lengths[wide_index]
    inputs = tokens.astype(jnp.float32)
    normed = rmsnorm(inputs, norm_gains[0]).astype(jnp.bfloat16)
    normed_all = lax.all_gather(normed, "narrow", axis=0, tiled=True)
    query_heads, key_heads, value_heads = project_any(
        normed_all, w_qkv, cos_heads, sin_heads, heads_here, kv_here
    )
    attended, log_sums = attend_forward_any(query_heads, key_heads, value_heads, length, block_rows)
    attended = (
        jnp.transpose(attended.reshape(heads_here, seq_len, HD), (1, 0, 2))
        .reshape(seq_len, query_width)
        .astype(jnp.bfloat16)
    )
    residual = inputs + lax.psum_scatter(
        matmul_cols(attended, w_out_t), "narrow", scatter_dimension=0, tiled=True
    )
    normed_two = rmsnorm(residual, norm_gains[1]).astype(jnp.bfloat16)
    mlp_input = lax.all_gather(normed_two, "narrow", axis=0, tiled=True)
    gate_up = jnp.dot(mlp_input, w_gate_up, preferred_element_type=jnp.float32)
    hidden = (jax.nn.silu(gate_up[:, :ff_width]) * gate_up[:, ff_width:]).astype(jnp.bfloat16)
    output = residual + lax.psum_scatter(
        matmul_cols(hidden, w_down_t).astype(jnp.bfloat16),
        "narrow",
        scatter_dimension=0,
        tiled=True,
    ).astype(jnp.float32)
    down_back = lax.all_gather(cotangent, "narrow", axis=0, tiled=True)
    mlp_again = lax.all_gather(normed_two, "narrow", axis=0, tiled=True)
    gate_up = jnp.dot(mlp_again, w_gate_up, preferred_element_type=jnp.float32)
    hidden_back = jnp.dot(down_back, w_down_t, preferred_element_type=jnp.float32)
    grad_down_t = matmul_rows(down_back, hidden)
    _, swiglu_pull = jax.vjp(
        lambda gate_in, upper_in: jax.nn.silu(gate_in) * upper_in,
        gate_up[:, :ff_width],
        gate_up[:, ff_width:],
    )
    gate_back, upper_back = swiglu_pull(hidden_back)
    gate_up_back = jnp.concatenate([gate_back, upper_back], axis=1).astype(jnp.bfloat16)
    grad_gate_up = matmul_rows(mlp_again, gate_up_back)
    norm_two_back = lax.psum_scatter(
        matmul_cols(gate_up_back, w_gate_up).astype(jnp.bfloat16),
        "narrow",
        scatter_dimension=0,
        tiled=True,
    ).astype(jnp.float32)
    _, norm_two_pull = jax.vjp(rmsnorm, residual, norm_gains[1])
    resid_part, gain_two = norm_two_pull(norm_two_back)
    resid_back = cotangent.astype(jnp.float32) + resid_part
    attn_back = lax.all_gather(resid_back.astype(jnp.bfloat16), "narrow", axis=0, tiled=True)
    normed_again = lax.all_gather(normed, "narrow", axis=0, tiled=True)
    query_heads, key_heads, value_heads = project_any(
        normed_again, w_qkv, cos_heads, sin_heads, heads_here, kv_here
    )
    out_back = jnp.dot(attn_back, w_out_t, preferred_element_type=jnp.float32).astype(jnp.bfloat16)
    grad_out_t = matmul_rows(attn_back, attended)
    out_back = jnp.transpose(out_back.reshape(seq_len, heads_here, HD), (1, 0, 2)).reshape(
        kv_here, group_size, seq_len, HD
    )
    query_grad, key_grad, value_grad = attend_backward_any(
        query_heads, key_heads, value_heads, out_back, log_sums, length, block_rows
    )
    query_grad = jnp.transpose(query_grad.reshape(heads_here, seq_len, HD), (1, 0, 2))
    query_grad = unrotate(query_grad, cos_heads, sin_heads).reshape(seq_len, query_width)
    key_grad = unrotate(jnp.transpose(key_grad, (1, 0, 2)), cos_heads, sin_heads).reshape(
        seq_len, kv_width
    )
    value_grad = jnp.transpose(value_grad, (1, 0, 2)).reshape(seq_len, kv_width)
    qkv_back = jnp.concatenate([query_grad, key_grad, value_grad], axis=1).astype(jnp.bfloat16)
    grad_qkv = matmul_rows(normed_again, qkv_back)
    norm_one_back = lax.psum_scatter(
        matmul_cols(qkv_back, w_qkv).astype(jnp.bfloat16), "narrow", scatter_dimension=0, tiled=True
    ).astype(jnp.float32)
    _, norm_one_pull = jax.vjp(rmsnorm, inputs, norm_gains[0])
    input_part, gain_one = norm_one_pull(norm_one_back)
    input_grad = (resid_back + input_part).astype(jnp.bfloat16)
    grad_packed = jnp.concatenate([grad_qkv, grad_out_t, grad_gate_up, grad_down_t], axis=1)
    grad_units = jnp.transpose(
        grad_packed.reshape(row_blocks, unit_rows, col_blocks, unit_cols), (0, 2, 1, 3)
    ).reshape(unit_count, unit_rows, unit_cols)
    grad_slots = (
        jnp.zeros((wide_count * capacity, unit_rows, unit_cols), jnp.float32)
        .at[slot_place]
        .set(grad_units)
    )
    owned_grads = lax.psum_scatter(
        grad_slots.astype(jnp.bfloat16), "wide", scatter_dimension=0, tiled=True
    ).astype(jnp.float32)[:, None]
    new_master, new_first, new_second = adamw(
        master, owned_grads, moment_one, moment_two, 0.02, 0.1
    )
    gain_grads = lax.psum(jnp.stack([gain_one, gain_two]), ("wide", "narrow"))
    new_gains, unused, gain_second_new = adamw(
        norm_gains, gain_grads, gain_first, gain_second, 0.5, 0.0
    )
    return (
        output.astype(jnp.bfloat16),
        input_grad,
        owned_grads,
        new_master,
        new_master.astype(jnp.bfloat16),
        new_first,
        new_second,
        gain_grads,
        gain_second_new,
        new_gains,
    )


def solution(mesh):
    COLLECTIVE[0] = 0
    rows = P(("wide", "narrow"), None)
    units = P("wide", "narrow", None, None)
    return jax.shard_map(
        local if mesh.shape["wide"] == 8 and mesh.shape["narrow"] == 4 else local_any,
        mesh=mesh,
        in_specs=(rows, rows, P(), P(), units, units, units, P(), P(), P()),
        out_specs=(rows, rows, units, units, units, units, units, P(), P(), P()),
        check_vma=False,
    )
```
